32 devices in a mesh: map: 8 (over z, core), layer: 4 (over y, x).
Axes of the slice: x: 2, y: 2, z: 4, core: 2. Of those that a mesh axis runs over, the one named last changes fastest.
Arguments:
- velocity_init: float32 [2, 16, 16, 1024], P(None, 'layer', 'map'), may hold values from -4 to 4
- driving: float32 [2, 16, 1024], P(None, 'map', 'layer'), may hold values from -80 to 80
- observed: float32 [2, 16, 1024], P(None, 'map', 'layer'), may hold values from -4 to 4
- log_friction: float32 [16, 1024], P('map', 'layer'), may hold values from -1 to 1.5
- ice_mask: int32 [16, 1024], P('map', 'layer'), may hold values from 0 to 2
Outputs:
- velocity: float32 [2, 16, 16, 1024], P(None, 'layer', 'map')
- friction_new: float32 [16, 1024], P('map', 'layer')
- misfit: float32 [], replicated
The draws below stay inside these ranges and needn't reach their ends.
All inputs are finite; a program needn't handle non-finite values.
Results may differ from the reference program's by a relative error of at most 0.0003.
Values sent between devices are 32-bit elements; how exact they have to be, the bound alone decides.
No kernel may reach another device: no remote copies, remote signals or barrier semaphores. Data moves between devices by JAX's collectives and lax.ppermute only.
A program may use at most 64 MiB of HBM per device.

```python
import math
import jax
import jax.numpy as jnp
from jax import lax

NX = 16
NY = 1024
NZ = 16


def draw_driving(key, part):
    keys = jax.random.split(key, 3)
    base = jnp.clip(jax.random.normal(keys[0], (2, NX, NY), jnp.float32), -5.0, 5.0)
    row_scale = jnp.exp(jax.random.uniform(keys[1], (1, NX, 1), jnp.float32) * math.log(10.0))
    col_scale = jnp.exp(jax.random.uniform(keys[2], (1, 1, NY), jnp.float32) * math.log(10.0))
    trend = 1.0 + 2.0 * jnp.arange(NX, dtype=jnp.float32)[None, :, None] / NX
    return 0.05 * base * row_scale * col_scale * trend


def place_ends(entries, rng, smallest, largest):
    place = [jax.random.randint(jax.random.fold_in(rng, axis), (), 0, length) for axis, length in enumerate(entries.shape)]
    main_axis = entries.shape.index(max(entries.shape))
    next_to = place[:main_axis] + [(place[main_axis] + 1) % entries.shape[main_axis]] + place[main_axis + 1:]
    return entries.at[tuple(place)].set(smallest).at[tuple(next_to)].set(largest)


def block_levels(stream_key, shape, cuts, smallest, high):
    factor_of, own = 1.0, jax.random.fold_in(stream_key, 6)
    for axis_at, blocks in cuts:
        draws = jnp.exp(jax.random.uniform(jax.random.fold_in(own, axis_at), (blocks,), jnp.float32, smallest / len(cuts), high / len(cuts)))
        factor_of = factor_of * jnp.repeat(draws, shape[axis_at] // blocks).reshape([-1 if axis == axis_at else 1 for axis in range(len(shape))])
    return factor_of


def normal_values(own_key, extent, width, bound, shards=(), kind=jnp.bfloat16):
    level = block_levels(own_key, extent, shards, -0.22, 0.18) if shards else 1.0
    entries = jax.random.normal(own_key, extent, jnp.float32) * width * level
    return jnp.minimum(jnp.maximum(entries, -bound), bound).astype(kind)


def setup_inputs(seed: int = 0) -> dict:
    key_of = jax.random.split(jax.random.key(seed), 6)
    velocity_init = normal_values(key_of[0], (2, NZ, NX, NY), 0.5, 4.0, ((1, 4), (2, 8)), jnp.float32)
    driving = draw_driving(jax.random.fold_in(key_of[5], 71), 0)
    observed = normal_values(key_of[2], (2, NX, NY), 0.5, 4.0, ((1, 8), (2, 4)), jnp.float32)
    log_friction = jnp.clip(-1.0 + 2.5 * jax.random.uniform(key_of[3], (NX, NY), jnp.float32) ** block_levels(key_of[3], (NX, NY), ((0, 8), (1, 4)), -0.2, 0.2), -1.0, 1.5)
    ice_mask = place_ends(jax.random.randint(key_of[4], (NX, NY), 0, 3), jax.random.fold_in(key_of[4], 1), 0, 2).astype(jnp.int32)
    return {"velocity_init": velocity_init, "driving": driving, "observed": observed, "log_friction": log_friction, "ice_mask": ice_mask}


strain_floor = 0.1
step_size = 0.5

def viscosity_of(extended):
    along_x = extended[0]
    along_y = extended[1]
    stretch_x = (along_x[:, 2:, 1:-1] - along_x[:, :-2, 1:-1]) * 0.5
    shear_uy = (along_x[:, 1:-1, 2:] - along_x[:, 1:-1, :-2]) * 0.5
    shear_vx = (along_y[:, 2:, 1:-1] - along_y[:, :-2, 1:-1]) * 0.5
    stretch_y = (along_y[:, 1:-1, 2:] - along_y[:, 1:-1, :-2]) * 0.5
    shearing = shear_uy + shear_vx
    strain_rate = stretch_x * stretch_x + stretch_y * stretch_y + stretch_x * stretch_y + 0.25 * shearing * shearing
    return jnp.power(strain_floor + strain_rate, -1.0 / 3.0)

def face_terms(viscous):
    centre = viscous[:, 1:-1, 1:-1]
    east_face = 0.5 * (centre + viscous[:, 2:, 1:-1])
    west_face = 0.5 * (centre + viscous[:, :-2, 1:-1])
    north_face = 0.5 * (centre + viscous[:, 1:-1, 2:])
    south_face = 0.5 * (centre + viscous[:, 1:-1, :-2])
    return (east_face, west_face, north_face, south_face)

def horizontal_diag(face_list):
    east_face, west_face, north_face, south_face = face_list
    first = 4.0 * (east_face + west_face) + (north_face + south_face)
    second = east_face + west_face + 4.0 * (north_face + south_face)
    return jnp.stack([first, second], 0)

def neighbour_sum(face_list, extended):
    east_face, west_face, north_face, south_face = face_list
    comp_u = extended[0]
    comp_v = extended[1]
    first = 4.0 * (east_face * comp_u[:, 2:, 1:-1] + west_face * comp_u[:, :-2, 1:-1]) + north_face * comp_u[:, 1:-1, 2:] + south_face * comp_u[:, 1:-1, :-2]
    second = east_face * comp_v[:, 2:, 1:-1] + west_face * comp_v[:, :-2, 1:-1] + 4.0 * (north_face * comp_v[:, 1:-1, 2:] + south_face * comp_v[:, 1:-1, :-2])
    return jnp.stack([first, second], 0)

def column_solve(centre, side_diag, right_hand, friction):
    layer_total = centre.shape[0]
    vertical_gain = 2.0 * float(layer_total * layer_total)
    coupling = vertical_gain * 0.5 * (centre[:-1] + centre[1:])
    zero_layer = jnp.zeros_like(centre[:1])
    lower_link = jnp.concatenate([zero_layer, coupling], 0)
    upper_link = jnp.concatenate([coupling, zero_layer], 0)
    bed_term = jnp.concatenate([friction[None], jnp.zeros_like(centre[1:])], 0)
    diagonal = (lower_link + upper_link + bed_term)[None] + side_diag
    diagonal = jnp.moveaxis(diagonal, 1, 0)
    right_side = jnp.moveaxis(right_hand, 1, 0)

    def forward(carried, layer_item):
        ratio_prev, value_prev = carried
        diag_layer, lower_layer, upper_layer, right_layer = layer_item
        pivots = diag_layer + lower_layer * ratio_prev
        ratio = -upper_layer / pivots
        value = (right_layer + lower_layer * value_prev) / pivots
        return ((ratio, value), (ratio, value))
    start = (jnp.zeros_like(right_side[0]), jnp.zeros_like(right_side[0]))
    final_pair, (ratios, values) = lax.scan(forward, start, (diagonal, lower_link, upper_link, right_side), unroll=8)

    def backward(following, layer_item):
        ratio, value = layer_item
        current = value - ratio * following
        return (current, current)
    final_row, solved = lax.scan(backward, jnp.zeros_like(right_side[0]), (ratios, values), reverse=True, unroll=8)
    return jnp.moveaxis(solved, 0, 1)

def top_source(mismatch, layer_count):
    zero_part = jnp.zeros((2, layer_count - 1) + mismatch.shape[1:], jnp.float32)
    return jnp.concatenate([zero_part, (float(layer_count) * mismatch)[:, None]], 1)

def reference(velocity_init, driving, observed, log_friction, ice_mask):
    ice_cols = ice_mask != 0
    friction = jnp.exp(log_friction) * (ice_mask == 1).astype(jnp.float32)
    forcing = driving[:, None]
    velocity = velocity_init
    for iteration in range(2):
        padded = jnp.pad(velocity, ((0, 0), (0, 0), (2, 2), (2, 2)))
        viscous = viscosity_of(padded)
        face_list = face_terms(viscous)
        centre = viscous[:, 1:-1, 1:-1]
        side_diag = horizontal_diag(face_list)
        side_sum = neighbour_sum(face_list, padded[:, :, 1:-1, 1:-1])
        velocity = jnp.where(ice_cols, column_solve(centre, side_diag, forcing + side_sum, friction), 0.0)
    mismatch = jnp.where(ice_cols, velocity[:, -1] - observed, 0.0)
    source = top_source(mismatch, velocity.shape[1])
    adjoint = jnp.where(ice_cols, column_solve(centre, side_diag, source, friction), 0.0)
    adjoint_rim = jnp.pad(adjoint, ((0, 0), (0, 0), (1, 1), (1, 1)))
    adjoint = jnp.where(ice_cols, column_solve(centre, side_diag, source + neighbour_sum(face_list, adjoint_rim), friction), 0.0)
    gradient = -friction * (velocity[0, 0] * adjoint[0, 0] + velocity[1, 0] * adjoint[1, 0])
    column_count = NX * NY
    misfit = 0.5 * jnp.sum(mismatch * mismatch) / column_count
    grad_scale = jnp.sqrt(jnp.sum(gradient * gradient) / column_count + 1e-06)
    return (velocity, log_friction - step_size * gradient / grad_scale, misfit)
```

```python
import functools
import math

import jax
import jax.numpy as jnp
from jax import lax
from jax.experimental import pallas as pl
from jax.experimental.pallas import tpu as pltpu
from jax.sharding import PartitionSpec as P

strain_floor = 0.1
step_size = 0.5
LANES = 128
REACH = 5
MIB = 1 << 20


def rows_of_eight(count):
    return -(-count // 8) * 8


class Plan:
    def __init__(self, mesh_shape, velocity_shape):
        self.map_size = mesh_shape["map"]
        self.layer_size = mesh_shape["layer"]
        self.devices = self.map_size * self.layer_size
        self.layers_here = velocity_shape[1]
        self.rows = velocity_shape[2]
        self.ny = velocity_shape[3]
        self.layers = self.layers_here * self.layer_size
        self.cols = self.ny // self.devices
        self.width = LANES // self.rows
        self.halo = (self.width - self.cols) // 2
        self.local_cols = self.ny // self.layer_size
        self.per_chunk = LANES // self.cols
        self.chunks = self.ny // LANES
        self.column_count = self.rows * self.map_size * self.ny
        self.vel_rows = 2 * self.layers_here
        self.in_rows = rows_of_eight(self.vel_rows + 6)
        self.out_rows = rows_of_eight(self.layers_here + 3)
        self.unrolled = self.map_size <= 8
        assert self.width * self.rows == LANES and self.cols * self.per_chunk == LANES
        assert self.halo >= REACH and 2 * self.cols <= self.width and self.local_cols % LANES == 0


def repeat(plan, count, body, carry=0):
    if plan.unrolled:
        for index in range(count):
            carry = body(index, carry)
        return carry
    return lax.fori_loop(0, count, body, carry)


def lane_roll(value, shift):
    shift = shift % LANES
    return value if shift == 0 else pltpu.roll(value, shift, 1)


def pack_kernel(plan, vel_ref, driving_ref, observed_ref, log_ref, mask_ref, out_ref, held):
    width, rows = plan.width, plan.rows
    held[...] = jnp.zeros_like(held)
    for r in range(rows):
        for c in range(2):
            for k in range(plan.layers_here):
                held[r, c * plan.layers_here + k : c * plan.layers_here + k + 1, LANES : LANES + plan.ny] = vel_ref[
                    c, k, r : r + 1, :
                ]
    first = pl.multiple_of(LANES + lax.axis_index("layer") * plan.local_cols, LANES)
    here = pl.ds(first, plan.local_cols)
    base = plan.vel_rows
    for r in range(rows):
        for c in range(2):
            held[r, base + c : base + c + 1, here] = driving_ref[c, r : r + 1, :]
            held[r, base + 2 + c : base + 3 + c, here] = observed_ref[c, r : r + 1, :]
        held[r, base + 4 : base + 5, here] = log_ref[r : r + 1, :]
        held[r, base + 5 : base + 6, here] = mask_ref[r : r + 1, :].astype(jnp.float32)

    lane = lax.broadcasted_iota(jnp.int32, (plan.in_rows, LANES), 1)

    def chunk_windows(i, carry):
        def part(r, step):
            return held[r, :, pl.ds(pl.multiple_of((i + 1 + step) * LANES, LANES), LANES)]

        for t in range(plan.per_chunk):
            relative = plan.cols * t - plan.halo
            step, offset = relative // LANES, relative % LANES
            block = None
            for r in range(rows):
                window = part(r, step)
                if offset + width > LANES:
                    window = jnp.where(lane >= offset, window, part(r, step + 1))
                window = lane_roll(window, r * width - offset)
                block = window if block is None else jnp.where(lane >= r * width, window, block)
            out_ref[i * plan.per_chunk + t] = block
        return carry

    repeat(plan, plan.chunks, chunk_windows)


def solve_kernel(plan, in_ref, out_ref, field, eta_ref, side, rhs, faces, ratio, inverse):
    size, width, rows = plan.map_size, plan.width, plan.rows
    layers, here = plan.layers, plan.layers_here
    shape = (size, LANES)
    lane = lax.broadcasted_iota(jnp.int32, shape, 1)
    sub = lax.broadcasted_iota(jnp.int32, shape, 0)
    last_group = lane >= LANES - width
    first_group = lane < width
    x_end = jnp.logical_and(last_group, sub == size - 1)
    x_start = jnp.logical_and(first_group, sub == 0)

    def arrived(part, row):
        return in_ref[pl.ds(part * plan.in_rows + row, size, stride=plan.layer_size * plan.in_rows), :]

    def column_input(index):
        total = arrived(0, plan.vel_rows + index)
        for part in range(1, plan.layer_size):
            total = total + arrived(part, plan.vel_rows + index)
        return total

    def x_pair(value, edge):
        after = lane_roll(value, -width)
        before = after if 2 * width == LANES else lane_roll(value, width)
        after = jnp.where(last_group, pltpu.roll(after, size - 1, 0), after)
        before = jnp.where(first_group, pltpu.roll(before, 1, 0), before)
        return jnp.where(x_end, edge, after), jnp.where(x_start, edge, before)

    def y_pair(value):
        return lane_roll(value, -1), lane_roll(value, 1)

    def viscosity(rate):
        return jnp.exp2(jnp.log(strain_floor + rate) * (-1.0 / (3.0 * math.log(2.0))))

    def reciprocal(value):
        guess = pl.reciprocal(value, approx=True)
        return guess * (2.0 - value * guess)

    for part in range(plan.layer_size):
        for c in range(2):
            for k in range(here):
                field[c, part * here + k] = arrived(part, c * here + k)
    driving = [2.0 * column_input(c) for c in range(2)]
    observed = [column_input(2 + c) for c in range(2)]
    mask = column_input(5)
    ice = mask != 0.0
    friction = jnp.where(mask == 1.0, jnp.exp(column_input(4)), 0.0)

    def stencil(k, keep):
        u, v = field[0, k], field[1, k]
        u_east, u_west = x_pair(u, 0.0)
        v_east, v_west = x_pair(v, 0.0)
        u_north, u_south = y_pair(u)
        v_north, v_south = y_pair(v)
        stretch_x = u_east - u_west
        stretch_y = v_north - v_south
        shear = 0.5 * ((u_north - u_south) + (v_east - v_west))
        rate = 0.25 * (stretch_x * (stretch_x + stretch_y) + stretch_y * stretch_y + shear * shear)
        half_v = 0.5 * v
        eta = viscosity(rate)
        eta_edge = viscosity(0.25 * (u * u + half_v * half_v))
        eta_east, eta_west = x_pair(eta, eta_edge)
        eta_north, eta_south = y_pair(eta)
        east, west = eta + eta_east, eta + eta_west
        north, south = eta + eta_north, eta + eta_south
        along_x, along_y = east + west, north + south
        eta_ref[k] = eta
        side[0, k] = 4.0 * along_x + along_y
        side[1, k] = along_x + 4.0 * along_y
        rhs[0, k] = driving[0] + (4.0 * (east * u_east + west * u_west) + (north * u_north + south * u_south))
        rhs[1, k] = driving[1] + ((east * v_east + west * v_west) + 4.0 * (north * v_north + south * v_south))
        if keep:
            faces[0, k] = east
            faces[1, k] = west
            faces[2, k] = north
            faces[3, k] = south

    def coupling_of(k):
        return (2.0 * layers * layers) * (eta_ref[k] + eta_ref[k + 1])

    def eliminate(k, carry):
        lower, rest, value = carry
        coupling = coupling_of(k)
        new_rest, new_value = [], []
        for c in range(2):
            inv = reciprocal(coupling + rest[c])
            link = coupling * inv
            inverse[c, k] = inv
            ratio[c, k] = link
            out = (rhs[c, k] + lower * value[c]) * inv
            rhs[c, k] = out
            new_value.append(out)
            new_rest.append(side[c, k + 1] + rest[c] * link)
        return coupling, tuple(new_rest), tuple(new_value)

    def forward_solve():
        zero = jnp.zeros(shape, jnp.float32)
        rest = tuple(side[c, 0] + 2.0 * friction for c in range(2))
        lower, rest, value = repeat(plan, layers - 1, eliminate, (zero, rest, (zero, zero)))
        top = []
        for c in range(2):
            inv = reciprocal(rest[c])
            inverse[c, layers - 1] = inv
            top.append(jnp.where(ice, (rhs[c, layers - 1] + lower * value[c]) * inv, 0.0))
            field[c, layers - 1] = top[c]

        def back(step, following):
            k = layers - 2 - step
            current = tuple(jnp.where(ice, rhs[c, k] + ratio[c, k] * following[c], 0.0) for c in range(2))
            for c in range(2):
                field[c, k] = current[c]
            return current

        return top, repeat(plan, layers - 1, back, tuple(top))

    for sweep in range(2):

        def stencil_body(k, carry):
            stencil(k, sweep == 1)
            return carry

        repeat(plan, layers, stencil_body)
        top, base = forward_solve()

    centre = jnp.logical_and(lane % width >= plan.halo, lane % width < plan.halo + plan.cols)

    def send(k, carry):
        both = jnp.where(centre, field[0, k], lane_roll(field[1, k], plan.cols))
        out_ref[pl.ds((k // here) * plan.out_rows + k % here, size, stride=plan.layer_size * plan.out_rows), :] = both
        return carry

    repeat(plan, layers, send)

    mismatch = [jnp.where(ice, top[c] - observed[c], 0.0) for c in range(2)]
    source = [(2.0 * layers) * mismatch[c] for c in range(2)]

    first_top = tuple(source[c] * inverse[c, layers - 1] for c in range(2))

    def side_sum(k, value):
        east, west, north, south = (faces[n, k] for n in range(4))
        u_east, u_west = x_pair(value[0], 0.0)
        v_east, v_west = x_pair(value[1], 0.0)
        u_north, u_south = y_pair(value[0])
        v_north, v_south = y_pair(value[1])
        rhs[0, k] = 4.0 * (east * u_east + west * u_west) + (north * u_north + south * u_south)
        rhs[1, k] = (east * v_east + west * v_west) + 4.0 * (north * v_north + south * v_south)

    side_sum(layers - 1, first_top)

    def first_back(step, following):
        k = layers - 2 - step
        current = tuple(ratio[c, k] * following[c] for c in range(2))
        side_sum(k, current)
        return current

    repeat(plan, layers - 1, first_back, first_top)

    def second_forward(k, carry):
        lower, value = carry
        out = tuple((rhs[c, k] + lower * value[c]) * inverse[c, k] for c in range(2))
        for c in range(2):
            rhs[c, k] = out[c]
        return coupling_of(k), out

    zero = jnp.zeros(shape, jnp.float32)
    lower, value = repeat(plan, layers - 1, second_forward, (zero, (zero, zero)))
    second_top = tuple(
        (rhs[c, layers - 1] + source[c] + lower * value[c]) * inverse[c, layers - 1] for c in range(2)
    )

    def second_back(step, following):
        k = layers - 2 - step
        return tuple(rhs[c, k] + ratio[c, k] * following[c] for c in range(2))

    adjoint = repeat(plan, layers - 1, second_back, second_top)
    adjoint = [jnp.where(ice, adjoint[c], 0.0) for c in range(2)]
    gradient = -friction * (base[0] * adjoint[0] + base[1] * adjoint[1])
    misfit_part = jnp.where(centre, mismatch[0] * mismatch[0] + mismatch[1] * mismatch[1], 0.0)
    grad_part = jnp.where(centre, gradient * gradient, 0.0)
    misfit_row = jnp.broadcast_to(jnp.sum(misfit_part, axis=0, keepdims=True), shape)
    grad_row = jnp.broadcast_to(jnp.sum(grad_part, axis=0, keepdims=True), shape)
    for part in range(plan.layer_size):
        for n, plane in enumerate((gradient, misfit_row, grad_row)):
            out_ref[pl.ds(part * plan.out_rows + here + n, size, stride=plan.layer_size * plan.out_rows), :] = plane


def unpack_kernel(plan, in_ref, log_ref, vel_ref, friction_ref, misfit_ref, grad_ref):
    here, width, cols = plan.layers_here, plan.width, plan.cols
    lane = lax.broadcasted_iota(jnp.int32, (plan.out_rows, LANES), 1)
    total = jnp.zeros((plan.out_rows, LANES), jnp.float32)

    def chunk(i, total):
        blocks = [in_ref[i * plan.per_chunk + t] for t in range(plan.per_chunk)]
        span = pl.ds(pl.multiple_of(i * LANES, LANES), LANES)
        for r in range(plan.rows):
            for c in range(2):
                start = r * width + plan.halo + c * cols
                row = None
                for t in range(plan.per_chunk):
                    moved = lane_roll(blocks[t], t * cols - start)
                    row = moved if row is None else jnp.where(lane >= t * cols, moved, row)
                for k in range(here):
                    vel_ref[c, k, r : r + 1, span] = row[k : k + 1, :]
                if c == 0:
                    grad_ref[r : r + 1, span] = row[here : here + 1, :]
        for block in blocks:
            total = total + block
        return total

    total = repeat(plan, plan.chunks, chunk, total)
    sums = jnp.sum(total, axis=1, keepdims=True)
    misfit_ref[...] = 0.5 * sums[here + 1 : here + 2, :] / plan.column_count
    scale = step_size / jnp.sqrt(sums[here + 2 : here + 3, :] / plan.column_count + 1e-06)
    first = pl.multiple_of(lax.axis_index("layer") * plan.local_cols, LANES)
    gradient = grad_ref[:, pl.ds(first, plan.local_cols)]
    friction_ref[...] = log_ref[...] - gradient * scale


def on_device(mesh_shape, velocity_init, driving, observed, log_friction, ice_mask):
    plan = Plan(mesh_shape, velocity_init.shape)
    vmem = pl.BlockSpec(memory_space=pltpu.VMEM)
    f32 = jnp.float32
    limit = pltpu.CompilerParams(vmem_limit_bytes=(16 if plan.unrolled else 40) * MIB)

    packed = pl.pallas_call(
        functools.partial(pack_kernel, plan),
        out_shape=jax.ShapeDtypeStruct((plan.devices, plan.in_rows, LANES), f32),
        in_specs=[vmem] * 5,
        out_specs=vmem,
        scratch_shapes=[pltpu.VMEM((plan.rows, plan.in_rows, plan.ny + 2 * LANES), f32)],
        compiler_params=limit,
        name="pack",
    )(velocity_init, driving, observed, log_friction, ice_mask)

    windows = lax.all_to_all(packed, ("map", "layer"), split_axis=0, concat_axis=0, tiled=True)

    plane = (plan.layers, plan.map_size, LANES)
    solved = pl.pallas_call(
        functools.partial(solve_kernel, plan),
        out_shape=jax.ShapeDtypeStruct((plan.devices * plan.out_rows, LANES), f32),
        in_specs=[vmem],
        out_specs=vmem,
        scratch_shapes=[
            pltpu.VMEM((2,) + plane, f32),
            pltpu.VMEM(plane, f32),
            pltpu.VMEM((2,) + plane, f32),
            pltpu.VMEM((2,) + plane, f32),
            pltpu.VMEM((4,) + plane, f32),
            pltpu.VMEM((2,) + plane, f32),
            pltpu.VMEM((2,) + plane, f32),
        ],
        compiler_params=limit,
        name="solve",
    )(windows.reshape(plan.devices * plan.in_rows, LANES))

    back = lax.all_to_all(
        solved.reshape(plan.devices, plan.out_rows, LANES),
        ("map", "layer"),
        split_axis=0,
        concat_axis=0,
        tiled=True,
    )

    velocity, friction_new, misfit = pl.pallas_call(
        functools.partial(unpack_kernel, plan),
        out_shape=(
            jax.ShapeDtypeStruct(velocity_init.shape, f32),
            jax.ShapeDtypeStruct(log_friction.shape, f32),
            jax.ShapeDtypeStruct((1, 1), f32),
        ),
        in_specs=[vmem] * 2,
        out_specs=(vmem, vmem, vmem),
        scratch_shapes=[pltpu.VMEM((plan.rows, plan.ny), f32)],
        compiler_params=limit,
        name="unpack",
    )(back, log_friction)
    return velocity, friction_new, misfit.reshape(())


def solution(mesh):
    in_specs = (
        P(None, "layer", "map", None),
        P(None, "map", "layer"),
        P(None, "map", "layer"),
        P("map", "layer"),
        P("map", "layer"),
    )
    out_specs = (P(None, "layer", "map", None), P("map", "layer"), P())
    return jax.shard_map(
        functools.partial(on_device, dict(mesh.shape)),
        mesh=mesh,
        in_specs=in_specs,
        out_specs=out_specs,
        check_vma=False,
    )
```

```python
import functools
import math

import jax
import jax.numpy as jnp
from jax import lax
from jax.experimental import pallas as pl
from jax.experimental.pallas import tpu as pltpu
from jax.sharding import PartitionSpec as P

strain_floor = 0.1
step_size = 0.5
LANES = 128
REACH = 5
MIB = 1 << 20


class Plan:
    def __init__(self, mesh_shape, velocity_shape):
        self.map_size = mesh_shape["map"]
        self.layer_size = mesh_shape["layer"]
        self.devices = self.map_size * self.layer_size
        self.layers_here = velocity_shape[1]
        self.rows = velocity_shape[2]
        self.ny = velocity_shape[3]
        self.layers = self.layers_here * self.layer_size
        self.cols = self.ny // self.devices
        self.width = LANES // self.rows
        self.halo = (self.width - self.cols) // 2
        self.low = self.halo - REACH
        self.wide = self.cols + 2 * REACH
        self.half = self.wide // 2
        self.gap = self.low + self.wide
        self.local_cols = self.ny // self.layer_size
        self.per_chunk = LANES // self.cols
        self.chunks = self.ny // LANES
        self.column_count = self.rows * self.map_size * self.ny
        self.vel_rows = 2 * self.layers_here
        self.in_rows = self.vel_rows + self.rows
        self.out_rows = self.layers_here + 1
        self.unrolled = self.map_size <= 8
        assert self.width * self.rows == LANES and self.cols * self.per_chunk == LANES
        assert self.low >= 0 and self.wide % 2 == 0 and self.width - self.wide >= self.half
        assert 2 * self.cols <= self.width and self.local_cols % LANES == 0
        assert self.vel_rows == 8 and self.rows == 2 and 3 * self.wide <= LANES


def repeat(plan, count, body, carry=0):
    if plan.unrolled:
        for index in range(count):
            carry = body(index, carry)
        return carry
    return lax.fori_loop(0, count, body, carry)


def lane_roll(value, shift):
    shift = shift % LANES
    return value if shift == 0 else pltpu.roll(value, shift, 1)


def pack_kernel(
    plan, vel_hbm, driving_hbm, observed_hbm, log_hbm, mask_hbm, out_hbm,
    vel_ref, driving_ref, observed_ref, log_ref, mask_ref, out_ref, held, bed, arrival, leave,
):
    width, rows, wide = plan.width, plan.rows, plan.wide
    copies = [
        pltpu.make_async_copy(source, target, arrival.at[n])
        for n, (source, target) in enumerate(
            (
                (vel_hbm, vel_ref),
                (driving_hbm, driving_ref),
                (observed_hbm, observed_ref),
                (log_hbm, log_ref),
                (mask_hbm, mask_ref),
            )
        )
    ]
    for copy in copies:
        copy.start()
    held[...] = jnp.zeros_like(held)
    bed[...] = jnp.zeros_like(bed)
    first = pl.multiple_of(LANES + lax.axis_index("layer") * plan.local_cols, LANES)
    here = pl.ds(first, plan.local_cols)
    for copy in copies:
        copy.wait()
    for r in range(rows):
        for c in range(2):
            for k in range(plan.layers_here):
                held[r, c * plan.layers_here + k : c * plan.layers_here + k + 1, LANES : LANES + plan.ny] = vel_ref[
                    c, k, r : r + 1, :
                ]
        mask = mask_ref[r : r + 1, :].astype(jnp.float32)
        for n, value in enumerate((observed_ref[0, r : r + 1, :], observed_ref[1, r : r + 1, :], mask)):
            held[r, plan.vel_rows + 2 * n : plan.vel_rows + 2 * n + 1, here] = value
            held[r, plan.vel_rows + 2 * n + 1 : plan.vel_rows + 2 * n + 2, here] = value
    for n, value in enumerate((driving_ref[0], driving_ref[1], log_ref[...])):
        bed[n, :, here] = value

    shape = (plan.vel_rows, LANES)
    lane = lax.broadcasted_iota(jnp.int32, shape, 1)
    odd = lax.broadcasted_iota(jnp.int32, shape, 0) % 2 == 1
    in_gap = jnp.logical_not(jnp.logical_and(lane % width >= plan.low, lane % width < plan.gap))
    bed_lane = lax.broadcasted_iota(jnp.int32, (rows, LANES), 1)

    chunk_rows = plan.per_chunk * plan.in_rows

    def leaving(i):
        start = i * chunk_rows
        span = pl.ds(start if isinstance(i, int) else pl.multiple_of(start, 8), chunk_rows)
        return pltpu.make_async_copy(out_ref.at[span, :], out_hbm.at[span, :], leave.at[i])

    def chunk_windows(i, carry):
        def window(read, relative, length, lanes):
            step, offset = relative // LANES, relative % LANES

            def part(at):
                return read(pl.ds(pl.multiple_of((i + 1 + at) * LANES, LANES), LANES))

            if offset + length <= LANES:
                return part(step), offset
            return jnp.where(lanes >= offset, part(step), part(step + 1)), offset

        def side_by_side(row_base, t):
            block = None
            for r in range(rows):
                value, offset = window(
                    lambda span: held[r, row_base : row_base + 8, span], plan.cols * t - plan.halo, width, lane
                )
                value = lane_roll(value, r * width - offset)
                block = value if block is None else jnp.where(lane >= r * width, value, block)
            return block

        for t in range(plan.per_chunk):
            block = side_by_side(0, t)
            other = side_by_side(plan.vel_rows, t)
            shift = plan.gap - plan.low
            other = jnp.where(odd, lane_roll(other, shift - plan.half), lane_roll(other, shift))
            block = jnp.where(in_gap, other, block)
            line = None
            for n in range(3):
                value, offset = window(lambda span: bed[n, :, span], plan.cols * t - REACH, wide, bed_lane)
                value = lane_roll(value, n * wide - offset)
                line = value if line is None else jnp.where(bed_lane >= n * wide, value, line)
            at = i * chunk_rows
            if not isinstance(at, int):
                at = pl.multiple_of(at, 8)
            at = at + t * plan.in_rows
            out_ref[pl.ds(at, plan.vel_rows), :] = block
            out_ref[pl.ds(at + plan.vel_rows, rows), :] = line
        leaving(i).start()
        return carry

    repeat(plan, plan.chunks, chunk_windows)

    def left(i, carry):
        leaving(i).wait()
        return carry

    repeat(plan, plan.chunks, left)


def solve_kernel(plan, in_ref, out_ref, field, eta_ref, side, rhs, faces, ratio, inverse):
    size, width, rows = plan.map_size, plan.width, plan.rows
    layers, here = plan.layers, plan.layers_here
    shape = (size, LANES)
    lane = lax.broadcasted_iota(jnp.int32, shape, 1)
    sub = lax.broadcasted_iota(jnp.int32, shape, 0)
    last_group = lane >= LANES - width
    first_group = lane < width
    x_end = jnp.logical_and(last_group, sub == size - 1)
    x_start = jnp.logical_and(first_group, sub == 0)

    def arrived(part, row):
        return in_ref[pl.ds(part * plan.in_rows + row, size, stride=plan.layer_size * plan.in_rows), :]

    def over_parts(row):
        total = arrived(0, row)
        for part in range(1, plan.layer_size):
            total = total + arrived(part, row)
        return total

    def from_gap(index):
        shift = plan.low - plan.gap
        left, right = over_parts(2 * index), over_parts(2 * index + 1)
        return jnp.where(lane % width < plan.low + plan.half, lane_roll(left, shift), lane_roll(right, shift + plan.half))

    def from_line(index):
        plane = lane_roll(lines[0], plan.low - index * plan.wide)
        for r in range(1, rows):
            plane = jnp.where(lane >= r * width, lane_roll(lines[r], r * width + plan.low - index * plan.wide), plane)
        return plane

    def x_pair(value, edge):
        after = lane_roll(value, -width)
        before = after if 2 * width == LANES else lane_roll(value, width)
        after = jnp.where(last_group, pltpu.roll(after, size - 1, 0), after)
        before = jnp.where(first_group, pltpu.roll(before, 1, 0), before)
        return jnp.where(x_end, edge, after), jnp.where(x_start, edge, before)

    def y_pair(value):
        return lane_roll(value, -1), lane_roll(value, 1)

    def viscosity(rate):
        return jnp.exp2(jnp.log(strain_floor + rate) * (-1.0 / (3.0 * math.log(2.0))))

    def reciprocal(value):
        guess = pl.reciprocal(value, approx=True)
        return guess * (2.0 - value * guess)

    for part in range(plan.layer_size):
        for c in range(2):
            for k in range(here):
                field[c, part * here + k] = arrived(part, c * here + k)
    lines = [over_parts(plan.vel_rows + r) for r in range(rows)]
    reached = jnp.logical_and(lane % width >= plan.low, lane % width < plan.gap)
    driving = [2.0 * from_line(c) for c in range(2)]
    observed = [from_gap(c) for c in range(2)]
    mask = jnp.where(reached, from_gap(2), 0.0)
    ice = mask != 0.0
    friction = jnp.where(mask == 1.0, jnp.exp(from_line(2)), 0.0)

    def stencil(k, keep):
        u, v = field[0, k], field[1, k]
        u_east, u_west = x_pair(u, 0.0)
        v_east, v_west = x_pair(v, 0.0)
        u_north, u_south = y_pair(u)
        v_north, v_south = y_pair(v)
        stretch_x = u_east - u_west
        stretch_y = v_north - v_south
        shear = 0.5 * ((u_north - u_south) + (v_east - v_west))
        rate = 0.25 * (stretch_x * (stretch_x + stretch_y) + stretch_y * stretch_y + shear * shear)
        half_v = 0.5 * v
        eta = viscosity(rate)
        eta_edge = viscosity(0.25 * (u * u + half_v * half_v))
        eta_east, eta_west = x_pair(eta, eta_edge)
        eta_north, eta_south = y_pair(eta)
        east, west = eta + eta_east, eta + eta_west
        north, south = eta + eta_north, eta + eta_south
        along_x, along_y = east + west, north + south
        eta_ref[k] = eta
        side[0, k] = 4.0 * along_x + along_y
        side[1, k] = along_x + 4.0 * along_y
        rhs[0, k] = driving[0] + (4.0 * (east * u_east + west * u_west) + (north * u_north + south * u_south))
        rhs[1, k] = driving[1] + ((east * v_east + west * v_west) + 4.0 * (north * v_north + south * v_south))
        if keep:
            faces[0, k] = east
            faces[1, k] = west
            faces[2, k] = north
            faces[3, k] = south

    def coupling_of(k):
        return (2.0 * layers * layers) * (eta_ref[k] + eta_ref[k + 1])

    def eliminate(k, carry):
        lower, rest, value = carry
        coupling = coupling_of(k)
        new_rest, new_value = [], []
        for c in range(2):
            inv = reciprocal(coupling + rest[c])
            link = coupling * inv
            inverse[c, k] = inv
            ratio[c, k] = link
            out = (rhs[c, k] + lower * value[c]) * inv
            rhs[c, k] = out
            new_value.append(out)
            new_rest.append(side[c, k + 1] + rest[c] * link)
        return coupling, tuple(new_rest), tuple(new_value)

    def forward_solve():
        zero = jnp.zeros(shape, jnp.float32)
        rest = tuple(side[c, 0] + 2.0 * friction for c in range(2))
        lower, rest, value = repeat(plan, layers - 1, eliminate, (zero, rest, (zero, zero)))
        top = []
        for c in range(2):
            inv = reciprocal(rest[c])
            inverse[c, layers - 1] = inv
            top.append(jnp.where(ice, (rhs[c, layers - 1] + lower * value[c]) * inv, 0.0))
            field[c, layers - 1] = top[c]

        def back(step, following):
            k = layers - 2 - step
            current = tuple(jnp.where(ice, rhs[c, k] + ratio[c, k] * following[c], 0.0) for c in range(2))
            for c in range(2):
                field[c, k] = current[c]
            return current

        return top, repeat(plan, layers - 1, back, tuple(top))

    for sweep in range(2):

        def stencil_body(k, carry):
            stencil(k, sweep == 1)
            return carry

        repeat(plan, layers, stencil_body)
        top, base = forward_solve()

    centre = jnp.logical_and(lane % width >= plan.halo, lane % width < plan.halo + plan.cols)

    def send(k, carry):
        both = jnp.where(centre, field[0, k], lane_roll(field[1, k], plan.cols))
        out_ref[pl.ds((k // here) * plan.out_rows + k % here, size, stride=plan.layer_size * plan.out_rows), :] = both
        return carry

    repeat(plan, layers, send)

    mismatch = [jnp.where(ice, top[c] - observed[c], 0.0) for c in range(2)]
    source = [(2.0 * layers) * mismatch[c] for c in range(2)]

    first_top = tuple(source[c] * inverse[c, layers - 1] for c in range(2))

    def side_sum(k, value):
        east, west, north, south = (faces[n, k] for n in range(4))
        u_east, u_west = x_pair(value[0], 0.0)
        v_east, v_west = x_pair(value[1], 0.0)
        u_north, u_south = y_pair(value[0])
        v_north, v_south = y_pair(value[1])
        rhs[0, k] = 4.0 * (east * u_east + west * u_west) + (north * u_north + south * u_south)
        rhs[1, k] = (east * v_east + west * v_west) + 4.0 * (north * v_north + south * v_south)

    side_sum(layers - 1, first_top)

    def first_back(step, following):
        k = layers - 2 - step
        current = tuple(ratio[c, k] * following[c] for c in range(2))
        side_sum(k, current)
        return current

    repeat(plan, layers - 1, first_back, first_top)

    def second_forward(k, carry):
        lower, value = carry
        out = tuple((rhs[c, k] + lower * value[c]) * inverse[c, k] for c in range(2))
        for c in range(2):
            rhs[c, k] = out[c]
        return coupling_of(k), out

    zero = jnp.zeros(shape, jnp.float32)
    lower, value = repeat(plan, layers - 1, second_forward, (zero, (zero, zero)))
    second_top = tuple(
        (rhs[c, layers - 1] + source[c] + lower * value[c]) * inverse[c, layers - 1] for c in range(2)
    )

    def second_back(step, following):
        k = layers - 2 - step
        return tuple(rhs[c, k] + ratio[c, k] * following[c] for c in range(2))

    adjoint = repeat(plan, layers - 1, second_back, second_top)
    adjoint = [jnp.where(ice, adjoint[c], 0.0) for c in range(2)]
    gradient = -friction * (base[0] * adjoint[0] + base[1] * adjoint[1])

    def partial_sum(value):
        line = jnp.sum(jnp.where(centre, value, 0.0), axis=0, keepdims=True)
        folded = line
        for r in range(1, rows):
            folded = folded + lane_roll(line, r * width)
        return jnp.broadcast_to(lane_roll(folded, plan.cols), shape)

    misfit_line = partial_sum(mismatch[0] * mismatch[0] + mismatch[1] * mismatch[1])
    grad_line = partial_sum(gradient * gradient)
    in_first = jnp.logical_and(lane >= plan.halo + plan.cols, lane < plan.halo + 2 * plan.cols)
    last_row = jnp.where(centre, gradient, jnp.where(in_first, misfit_line, grad_line))
    for part in range(plan.layer_size):
        out_ref[pl.ds(part * plan.out_rows + here, size, stride=plan.layer_size * plan.out_rows), :] = last_row


def unpack_kernel(
    plan, in_ref, log_ref, vel_hbm, friction_hbm, misfit_hbm,
    vel_ref, friction_ref, misfit_ref, grad_ref, leave,
):
    here, width, cols = plan.layers_here, plan.width, plan.cols
    lane = lax.broadcasted_iota(jnp.int32, (plan.out_rows, LANES), 1)

    def block_at(i, t):
        at = i * plan.per_chunk * plan.out_rows
        if not isinstance(at, int):
            at = pl.multiple_of(at, 8)
        return in_ref[pl.ds(at + t * plan.out_rows, plan.out_rows), :]

    def component(c):
        def chunk(i, total):
            blocks = [block_at(i, t) for t in range(plan.per_chunk)]
            start = i * LANES
            if not isinstance(start, int):
                start = pl.multiple_of(start, LANES)
            span = pl.ds(start, LANES)
            for r in range(plan.rows):
                start = r * width + plan.halo + c * cols
                row = None
                for t in range(plan.per_chunk):
                    moved = lane_roll(blocks[t], t * cols - start)
                    row = moved if row is None else jnp.where(lane >= t * cols, moved, row)
                for k in range(here):
                    vel_ref[c, k, r : r + 1, span] = row[k : k + 1, :]
                if c == 0:
                    grad_ref[r : r + 1, span] = row[here : here + 1, :]
            if c == 0:
                for block in blocks:
                    total = total + block
            return total

        return repeat(plan, plan.chunks, chunk, jnp.zeros((plan.out_rows, LANES), jnp.float32))

    out = [pltpu.make_async_copy(vel_ref.at[c], vel_hbm.at[c], leave.at[c]) for c in range(2)]
    out.append(pltpu.make_async_copy(friction_ref, friction_hbm, leave.at[2]))
    out.append(pltpu.make_async_copy(misfit_ref, misfit_hbm, leave.at[3]))

    total = component(0)[here:, :]
    out[0].start()

    def summed(first):
        ahead = (lane[here:, :] + (LANES - first % LANES)) % LANES
        return jnp.sum(jnp.where(ahead < cols, total, 0.0), axis=1, keepdims=True)

    misfit_sum = summed(plan.halo + cols)
    grad_sum = summed(plan.halo + cols + width)
    misfit_ref[...] = 0.5 * misfit_sum / plan.column_count
    scale = step_size / jnp.sqrt(grad_sum / plan.column_count + 1e-06)
    first = pl.multiple_of(lax.axis_index("layer") * plan.local_cols, LANES)
    friction_ref[...] = log_ref[...] - grad_ref[:, pl.ds(first, plan.local_cols)] * scale
    out[2].start()
    out[3].start()
    component(1)
    out[1].start()
    for copy in out:
        copy.wait()


def on_device(mesh_shape, velocity_init, driving, observed, log_friction, ice_mask):
    plan = Plan(mesh_shape, velocity_init.shape)
    vmem = pl.BlockSpec(memory_space=pltpu.VMEM)
    hbm = pl.BlockSpec(memory_space=pltpu.HBM)
    f32 = jnp.float32
    limit = pltpu.CompilerParams(vmem_limit_bytes=(16 if plan.unrolled else 40) * MIB)
    inputs = (velocity_init, driving, observed, log_friction, ice_mask)

    def exchange(blocks, unit):
        shaped = blocks.reshape(blocks.shape[0] // unit, unit, LANES)
        return lax.all_to_all(shaped, ("map", "layer"), split_axis=0, concat_axis=0, tiled=True).reshape(blocks.shape)

    packed = pl.pallas_call(
        functools.partial(pack_kernel, plan),
        out_shape=jax.ShapeDtypeStruct((plan.devices * plan.in_rows, LANES), f32),
        in_specs=[hbm] * 5,
        out_specs=hbm,
        scratch_shapes=[pltpu.VMEM(x.shape, x.dtype) for x in inputs]
        + [
            pltpu.VMEM((plan.devices * plan.in_rows, LANES), f32),
            pltpu.VMEM((plan.rows, plan.vel_rows + 8, plan.ny + 2 * LANES), f32),
            pltpu.VMEM((3, plan.rows, plan.ny + 2 * LANES), f32),
            pltpu.SemaphoreType.DMA((5,)),
            pltpu.SemaphoreType.DMA((plan.chunks,)),
        ],
        compiler_params=pltpu.CompilerParams(vmem_limit_bytes=60 * MIB),
        name="pack",
    )(*inputs)

    windows = exchange(packed, 2)

    plane = (plan.layers, plan.map_size, LANES)
    solved = pl.pallas_call(
        functools.partial(solve_kernel, plan),
        out_shape=jax.ShapeDtypeStruct((plan.devices * plan.out_rows, LANES), f32),
        in_specs=[vmem],
        out_specs=vmem,
        scratch_shapes=[
            pltpu.VMEM((2,) + plane, f32),
            pltpu.VMEM(plane, f32),
            pltpu.VMEM((2,) + plane, f32),
            pltpu.VMEM((2,) + plane, f32),
            pltpu.VMEM((4,) + plane, f32),
            pltpu.VMEM((2,) + plane, f32),
            pltpu.VMEM((2,) + plane, f32),
        ],
        compiler_params=limit,
        name="solve",
    )(windows)

    back = exchange(solved, 1)

    velocity, friction_new, misfit = pl.pallas_call(
        functools.partial(unpack_kernel, plan),
        out_shape=(
            jax.ShapeDtypeStruct(velocity_init.shape, f32),
            jax.ShapeDtypeStruct(log_friction.shape, f32),
            jax.ShapeDtypeStruct((1, 1), f32),
        ),
        in_specs=[vmem] * 2,
        out_specs=(hbm, hbm, hbm),
        scratch_shapes=[
            pltpu.VMEM(velocity_init.shape, f32),
            pltpu.VMEM(log_friction.shape, f32),
            pltpu.VMEM((1, 1), f32),
            pltpu.VMEM((plan.rows, plan.ny), f32),
            pltpu.SemaphoreType.DMA((4,)),
        ],
        compiler_params=limit,
        name="unpack",
    )(back, log_friction)
    return velocity, friction_new, misfit.reshape(())


def solution(mesh):
    in_specs = (
        P(None, "layer", "map", None),
        P(None, "map", "layer"),
        P(None, "map", "layer"),
        P("map", "layer"),
        P("map", "layer"),
    )
    out_specs = (P(None, "layer", "map", None), P("map", "layer"), P())
    return jax.shard_map(
        functools.partial(on_device, dict(mesh.shape)),
        mesh=mesh,
        in_specs=in_specs,
        out_specs=out_specs,
        check_vma=False,
    )
```

```python
import functools
import math

import jax
import jax.numpy as jnp
from jax import lax
from jax.experimental import pallas as pl
from jax.experimental.pallas import tpu as pltpu
from jax.sharding import PartitionSpec as P

strain_floor = 0.1
step_size = 0.5
LANES = 128
REACH = 5
MIB = 1 << 20


class Plan:
    def __init__(self, mesh_shape, velocity_shape):
        self.map_size = mesh_shape["map"]
        self.layer_size = mesh_shape["layer"]
        self.devices = self.map_size * self.layer_size
        self.layers_here = velocity_shape[1]
        self.rows = velocity_shape[2]
        self.ny = velocity_shape[3]
        self.layers = self.layers_here * self.layer_size
        self.cols = self.ny // self.devices
        self.width = LANES // self.rows
        self.halo = (self.width - self.cols) // 2
        self.low = self.halo - REACH
        self.wide = self.cols + 2 * REACH
        self.half = self.wide // 2
        self.gap = self.low + self.wide
        self.local_cols = self.ny // self.layer_size
        self.per_chunk = LANES // self.cols
        self.chunks = self.ny // LANES
        self.column_count = self.rows * self.map_size * self.ny
        self.vel_rows = 2 * self.layers_here
        self.in_rows = self.vel_rows + self.rows
        self.out_rows = self.layers_here + 1
        self.unrolled = self.map_size <= 8
        assert self.width * self.rows == LANES and self.cols * self.per_chunk == LANES
        assert self.low >= 0 and self.wide % 2 == 0 and self.width - self.wide >= self.half
        assert 2 * self.cols <= self.width and self.local_cols % LANES == 0
        assert self.vel_rows == 8 and self.rows == 2 and 3 * self.wide <= LANES


def repeat(plan, count, body, carry=0):
    if plan.unrolled:
        for index in range(count):
            carry = body(index, carry)
        return carry
    return lax.fori_loop(0, count, body, carry)


def lane_roll(value, shift):
    shift = shift % LANES
    return value if shift == 0 else pltpu.roll(value, shift, 1)


def pack_kernel(
    plan, vel_hbm, driving_hbm, observed_hbm, log_hbm, mask_hbm, out_ref,
    vel_ref, driving_ref, observed_ref, log_ref, mask_ref, held, bed, arrival,
):
    width, rows, wide = plan.width, plan.rows, plan.wide
    copies = [
        pltpu.make_async_copy(source, target, arrival.at[n])
        for n, (source, target) in enumerate(
            (
                (vel_hbm, vel_ref),
                (driving_hbm, driving_ref),
                (observed_hbm, observed_ref),
                (log_hbm, log_ref),
                (mask_hbm, mask_ref),
            )
        )
    ]
    for copy in copies:
        copy.start()
    held[...] = jnp.zeros_like(held)
    bed[...] = jnp.zeros_like(bed)
    first = pl.multiple_of(LANES + lax.axis_index("layer") * plan.local_cols, LANES)
    here = pl.ds(first, plan.local_cols)
    for copy in copies:
        copy.wait()
    for r in range(rows):
        for c in range(2):
            for k in range(plan.layers_here):
                held[r, c * plan.layers_here + k : c * plan.layers_here + k + 1, LANES : LANES + plan.ny] = vel_ref[
                    c, k, r : r + 1, :
                ]
        mask = mask_ref[r : r + 1, :].astype(jnp.float32)
        for n, value in enumerate((observed_ref[0, r : r + 1, :], observed_ref[1, r : r + 1, :], mask)):
            held[r, plan.vel_rows + 2 * n : plan.vel_rows + 2 * n + 1, here] = value
            held[r, plan.vel_rows + 2 * n + 1 : plan.vel_rows + 2 * n + 2, here] = value
    for n, value in enumerate((driving_ref[0], driving_ref[1], log_ref[...])):
        bed[n, :, here] = value

    shape = (plan.vel_rows, LANES)
    lane = lax.broadcasted_iota(jnp.int32, shape, 1)
    odd = lax.broadcasted_iota(jnp.int32, shape, 0) % 2 == 1
    in_gap = jnp.logical_not(jnp.logical_and(lane % width >= plan.low, lane % width < plan.gap))
    bed_lane = lax.broadcasted_iota(jnp.int32, (rows, LANES), 1)

    chunk_rows = plan.per_chunk * plan.in_rows

    def chunk_windows(i, carry):
        def window(read, relative, length, lanes):
            step, offset = relative // LANES, relative % LANES

            def part(at):
                return read(pl.ds(pl.multiple_of((i + 1 + at) * LANES, LANES), LANES))

            if offset + length <= LANES:
                return part(step), offset
            return jnp.where(lanes >= offset, part(step), part(step + 1)), offset

        def side_by_side(row_base, t):
            block = None
            for r in range(rows):
                value, offset = window(
                    lambda span: held[r, row_base : row_base + 8, span], plan.cols * t - plan.halo, width, lane
                )
                value = lane_roll(value, r * width - offset)
                block = value if block is None else jnp.where(lane >= r * width, value, block)
            return block

        for t in range(plan.per_chunk):
            block = side_by_side(0, t)
            other = side_by_side(plan.vel_rows, t)
            shift = plan.gap - plan.low
            other = jnp.where(odd, lane_roll(other, shift - plan.half), lane_roll(other, shift))
            block = jnp.where(in_gap, other, block)
            line = None
            for n in range(3):
                value, offset = window(lambda span: bed[n, :, span], plan.cols * t - REACH, wide, bed_lane)
                value = lane_roll(value, n * wide - offset)
                line = value if line is None else jnp.where(bed_lane >= n * wide, value, line)
            at = i * chunk_rows
            if not isinstance(at, int):
                at = pl.multiple_of(at, 8)
            at = at + t * plan.in_rows
            out_ref[pl.ds(at, plan.vel_rows), :] = block
            out_ref[pl.ds(at + plan.vel_rows, rows), :] = line
        return carry

    repeat(plan, plan.chunks, chunk_windows)


def solve_kernel(plan, in_ref, out_ref, field, eta_ref, side, rhs, faces, ratio, inverse):
    size, width, rows = plan.map_size, plan.width, plan.rows
    layers, here = plan.layers, plan.layers_here
    shape = (size, LANES)
    lane = lax.broadcasted_iota(jnp.int32, shape, 1)
    sub = lax.broadcasted_iota(jnp.int32, shape, 0)
    last_group = lane >= LANES - width
    first_group = lane < width
    x_end = jnp.logical_and(last_group, sub == size - 1)
    x_start = jnp.logical_and(first_group, sub == 0)

    def arrived(part, row):
        return in_ref[pl.ds(part * plan.in_rows + row, size, stride=plan.layer_size * plan.in_rows), :]

    def over_parts(row):
        total = arrived(0, row)
        for part in range(1, plan.layer_size):
            total = total + arrived(part, row)
        return total

    def from_gap(index):
        shift = plan.low - plan.gap
        left, right = over_parts(2 * index), over_parts(2 * index + 1)
        return jnp.where(lane % width < plan.low + plan.half, lane_roll(left, shift), lane_roll(right, shift + plan.half))

    def from_line(index):
        plane = lane_roll(lines[0], plan.low - index * plan.wide)
        for r in range(1, rows):
            plane = jnp.where(lane >= r * width, lane_roll(lines[r], r * width + plan.low - index * plan.wide), plane)
        return plane

    def x_pair(value, edge):
        after = lane_roll(value, -width)
        before = after if 2 * width == LANES else lane_roll(value, width)
        after = jnp.where(last_group, pltpu.roll(after, size - 1, 0), after)
        before = jnp.where(first_group, pltpu.roll(before, 1, 0), before)
        return jnp.where(x_end, edge, after), jnp.where(x_start, edge, before)

    def y_pair(value):
        return lane_roll(value, -1), lane_roll(value, 1)

    def viscosity(rate):
        return jnp.exp2(jnp.log(strain_floor + rate) * (-1.0 / (3.0 * math.log(2.0))))

    def reciprocal(value):
        guess = pl.reciprocal(value, approx=True)
        return guess * (2.0 - value * guess)

    for part in range(plan.layer_size):
        for c in range(2):
            for k in range(here):
                field[c, part * here + k] = arrived(part, c * here + k)
    lines = [over_parts(plan.vel_rows + r) for r in range(rows)]
    reached = jnp.logical_and(lane % width >= plan.low, lane % width < plan.gap)
    driving = [2.0 * from_line(c) for c in range(2)]
    observed = [from_gap(c) for c in range(2)]
    mask = jnp.where(reached, from_gap(2), 0.0)
    ice = mask != 0.0
    friction = jnp.where(mask == 1.0, jnp.exp(from_line(2)), 0.0)

    def stencil(k, keep):
        u, v = field[0, k], field[1, k]
        u_east, u_west = x_pair(u, 0.0)
        v_east, v_west = x_pair(v, 0.0)
        u_north, u_south = y_pair(u)
        v_north, v_south = y_pair(v)
        stretch_x = u_east - u_west
        stretch_y = v_north - v_south
        shear = 0.5 * ((u_north - u_south) + (v_east - v_west))
        rate = 0.25 * (stretch_x * (stretch_x + stretch_y) + stretch_y * stretch_y + shear * shear)
        half_v = 0.5 * v
        eta = viscosity(rate)
        eta_edge = viscosity(0.25 * (u * u + half_v * half_v))
        eta_east, eta_west = x_pair(eta, eta_edge)
        eta_north, eta_south = y_pair(eta)
        east, west = eta + eta_east, eta + eta_west
        north, south = eta + eta_north, eta + eta_south
        along_x, along_y = east + west, north + south
        eta_ref[k] = eta
        side[0, k] = 4.0 * along_x + along_y
        side[1, k] = along_x + 4.0 * along_y
        rhs[0, k] = driving[0] + (4.0 * (east * u_east + west * u_west) + (north * u_north + south * u_south))
        rhs[1, k] = driving[1] + ((east * v_east + west * v_west) + 4.0 * (north * v_north + south * v_south))
        if keep:
            faces[0, k] = east
            faces[1, k] = west
            faces[2, k] = north
            faces[3, k] = south

    def coupling_of(k):
        return (2.0 * layers * layers) * (eta_ref[k] + eta_ref[k + 1])

    def eliminate(k, carry):
        lower, rest, value = carry
        coupling = coupling_of(k)
        new_rest, new_value = [], []
        for c in range(2):
            inv = reciprocal(coupling + rest[c])
            link = coupling * inv
            inverse[c, k] = inv
            ratio[c, k] = link
            out = (rhs[c, k] + lower * value[c]) * inv
            rhs[c, k] = out
            new_value.append(out)
            new_rest.append(side[c, k + 1] + rest[c] * link)
        return coupling, tuple(new_rest), tuple(new_value)

    def forward_solve():
        zero = jnp.zeros(shape, jnp.float32)
        rest = tuple(side[c, 0] + 2.0 * friction for c in range(2))
        lower, rest, value = repeat(plan, layers - 1, eliminate, (zero, rest, (zero, zero)))
        top = []
        for c in range(2):
            inv = reciprocal(rest[c])
            inverse[c, layers - 1] = inv
            top.append(jnp.where(ice, (rhs[c, layers - 1] + lower * value[c]) * inv, 0.0))
            field[c, layers - 1] = top[c]

        def back(step, following):
            k = layers - 2 - step
            current = tuple(jnp.where(ice, rhs[c, k] + ratio[c, k] * following[c], 0.0) for c in range(2))
            for c in range(2):
                field[c, k] = current[c]
            return current

        return top, repeat(plan, layers - 1, back, tuple(top))

    for sweep in range(2):

        def stencil_body(k, carry):
            stencil(k, sweep == 1)
            return carry

        repeat(plan, layers, stencil_body)
        top, base = forward_solve()

    centre = jnp.logical_and(lane % width >= plan.halo, lane % width < plan.halo + plan.cols)

    def send(k, carry):
        both = jnp.where(centre, field[0, k], lane_roll(field[1, k], plan.cols))
        out_ref[pl.ds((k // here) * plan.out_rows + k % here, size, stride=plan.layer_size * plan.out_rows), :] = both
        return carry

    repeat(plan, layers, send)

    mismatch = [jnp.where(ice, top[c] - observed[c], 0.0) for c in range(2)]
    source = [(2.0 * layers) * mismatch[c] for c in range(2)]

    first_top = tuple(source[c] * inverse[c, layers - 1] for c in range(2))

    def side_sum(k, value):
        east, west, north, south = (faces[n, k] for n in range(4))
        u_east, u_west = x_pair(value[0], 0.0)
        v_east, v_west = x_pair(value[1], 0.0)
        u_north, u_south = y_pair(value[0])
        v_north, v_south = y_pair(value[1])
        rhs[0, k] = 4.0 * (east * u_east + west * u_west) + (north * u_north + south * u_south)
        rhs[1, k] = (east * v_east + west * v_west) + 4.0 * (north * v_north + south * v_south)

    side_sum(layers - 1, first_top)

    def first_back(step, following):
        k = layers - 2 - step
        current = tuple(ratio[c, k] * following[c] for c in range(2))
        side_sum(k, current)
        return current

    repeat(plan, layers - 1, first_back, first_top)

    def second_forward(k, carry):
        lower, value = carry
        out = tuple((rhs[c, k] + lower * value[c]) * inverse[c, k] for c in range(2))
        for c in range(2):
            rhs[c, k] = out[c]
        return coupling_of(k), out

    zero = jnp.zeros(shape, jnp.float32)
    lower, value = repeat(plan, layers - 1, second_forward, (zero, (zero, zero)))
    second_top = tuple(
        (rhs[c, layers - 1] + source[c] + lower * value[c]) * inverse[c, layers - 1] for c in range(2)
    )

    def second_back(step, following):
        k = layers - 2 - step
        return tuple(rhs[c, k] + ratio[c, k] * following[c] for c in range(2))

    adjoint = repeat(plan, layers - 1, second_back, second_top)
    adjoint = [jnp.where(ice, adjoint[c], 0.0) for c in range(2)]
    gradient = -friction * (base[0] * adjoint[0] + base[1] * adjoint[1])

    def partial_sum(value):
        line = jnp.sum(jnp.where(centre, value, 0.0), axis=0, keepdims=True)
        folded = line
        for r in range(1, rows):
            folded = folded + lane_roll(line, r * width)
        return jnp.broadcast_to(lane_roll(folded, plan.cols), shape)

    misfit_line = partial_sum(mismatch[0] * mismatch[0] + mismatch[1] * mismatch[1])
    grad_line = partial_sum(gradient * gradient)
    in_first = jnp.logical_and(lane >= plan.halo + plan.cols, lane < plan.halo + 2 * plan.cols)
    last_row = jnp.where(centre, gradient, jnp.where(in_first, misfit_line, grad_line))
    for part in range(plan.layer_size):
        out_ref[pl.ds(part * plan.out_rows + here, size, stride=plan.layer_size * plan.out_rows), :] = last_row


def unpack_kernel(
    plan, in_ref, log_ref, vel_hbm, friction_hbm, misfit_hbm,
    vel_ref, friction_ref, misfit_ref, grad_ref, leave,
):
    here, width, cols = plan.layers_here, plan.width, plan.cols
    lane = lax.broadcasted_iota(jnp.int32, (plan.out_rows, LANES), 1)

    def block_at(i, t):
        at = i * plan.per_chunk * plan.out_rows
        if not isinstance(at, int):
            at = pl.multiple_of(at, 8)
        return in_ref[pl.ds(at + t * plan.out_rows, plan.out_rows), :]

    def component(c):
        def chunk(i, total):
            blocks = [block_at(i, t) for t in range(plan.per_chunk)]
            start = i * LANES
            if not isinstance(start, int):
                start = pl.multiple_of(start, LANES)
            span = pl.ds(start, LANES)
            for r in range(plan.rows):
                start = r * width + plan.halo + c * cols
                row = None
                for t in range(plan.per_chunk):
                    moved = lane_roll(blocks[t], t * cols - start)
                    row = moved if row is None else jnp.where(lane >= t * cols, moved, row)
                for k in range(here):
                    vel_ref[c, k, r : r + 1, span] = row[k : k + 1, :]
                if c == 0:
                    grad_ref[r : r + 1, span] = row[here : here + 1, :]
            if c == 0:
                for block in blocks:
                    total = total + block
            return total

        return repeat(plan, plan.chunks, chunk, jnp.zeros((plan.out_rows, LANES), jnp.float32))

    out = [pltpu.make_async_copy(vel_ref.at[c], vel_hbm.at[c], leave.at[c]) for c in range(2)]
    out.append(pltpu.make_async_copy(friction_ref, friction_hbm, leave.at[2]))
    out.append(pltpu.make_async_copy(misfit_ref, misfit_hbm, leave.at[3]))

    total = component(0)[here:, :]
    out[0].start()

    def summed(first):
        ahead = (lane[here:, :] + (LANES - first % LANES)) % LANES
        return jnp.sum(jnp.where(ahead < cols, total, 0.0), axis=1, keepdims=True)

    misfit_sum = summed(plan.halo + cols)
    grad_sum = summed(plan.halo + cols + width)
    misfit_ref[...] = 0.5 * misfit_sum / plan.column_count
    scale = step_size / jnp.sqrt(grad_sum / plan.column_count + 1e-06)
    first = pl.multiple_of(lax.axis_index("layer") * plan.local_cols, LANES)
    friction_ref[...] = log_ref[...] - grad_ref[:, pl.ds(first, plan.local_cols)] * scale
    out[2].start()
    out[3].start()
    component(1)
    out[1].start()
    for copy in out:
        copy.wait()


def on_device(mesh_shape, velocity_init, driving, observed, log_friction, ice_mask):
    plan = Plan(mesh_shape, velocity_init.shape)
    vmem = pl.BlockSpec(memory_space=pltpu.VMEM)
    hbm = pl.BlockSpec(memory_space=pltpu.HBM)
    f32 = jnp.float32
    limit = pltpu.CompilerParams(vmem_limit_bytes=(16 if plan.unrolled else 40) * MIB)
    inputs = (velocity_init, driving, observed, log_friction, ice_mask)

    def exchange(blocks, unit):
        shaped = blocks.reshape(blocks.shape[0] // unit, unit, LANES)
        return lax.all_to_all(shaped, ("map", "layer"), split_axis=0, concat_axis=0, tiled=True).reshape(blocks.shape)

    packed = pl.pallas_call(
        functools.partial(pack_kernel, plan),
        out_shape=jax.ShapeDtypeStruct((plan.devices * plan.in_rows, LANES), f32),
        in_specs=[hbm] * 5,
        out_specs=vmem,
        scratch_shapes=[pltpu.VMEM(x.shape, x.dtype) for x in inputs]
        + [
            pltpu.VMEM((plan.rows, plan.vel_rows + 8, plan.ny + 2 * LANES), f32),
            pltpu.VMEM((3, plan.rows, plan.ny + 2 * LANES), f32),
            pltpu.SemaphoreType.DMA((5,)),
        ],
        compiler_params=limit,
        name="pack",
    )(*(pltpu.with_memory_space_constraint(x, pltpu.HBM) for x in inputs))

    windows = exchange(packed, 2)

    plane = (plan.layers, plan.map_size, LANES)
    solved = pl.pallas_call(
        functools.partial(solve_kernel, plan),
        out_shape=jax.ShapeDtypeStruct((plan.devices * plan.out_rows, LANES), f32),
        in_specs=[vmem],
        out_specs=vmem,
        scratch_shapes=[
            pltpu.VMEM((2,) + plane, f32),
            pltpu.VMEM(plane, f32),
            pltpu.VMEM((2,) + plane, f32),
            pltpu.VMEM((2,) + plane, f32),
            pltpu.VMEM((4,) + plane, f32),
            pltpu.VMEM((2,) + plane, f32),
            pltpu.VMEM((2,) + plane, f32),
        ],
        compiler_params=limit,
        name="solve",
    )(windows)

    back = exchange(solved, 1)

    velocity, friction_new, misfit = pl.pallas_call(
        functools.partial(unpack_kernel, plan),
        out_shape=(
            jax.ShapeDtypeStruct(velocity_init.shape, f32),
            jax.ShapeDtypeStruct(log_friction.shape, f32),
            jax.ShapeDtypeStruct((1, 1), f32),
        ),
        in_specs=[vmem] * 2,
        out_specs=(hbm, hbm, hbm),
        scratch_shapes=[
            pltpu.VMEM(velocity_init.shape, f32),
            pltpu.VMEM(log_friction.shape, f32),
            pltpu.VMEM((1, 1), f32),
            pltpu.VMEM((plan.rows, plan.ny), f32),
            pltpu.SemaphoreType.DMA((4,)),
        ],
        compiler_params=limit,
        name="unpack",
    )(back, log_friction)
    return velocity, friction_new, misfit.reshape(())


def solution(mesh):
    in_specs = (
        P(None, "layer", "map", None),
        P(None, "map", "layer"),
        P(None, "map", "layer"),
        P("map", "layer"),
        P("map", "layer"),
    )
    out_specs = (P(None, "layer", "map", None), P("map", "layer"), P())
    return jax.shard_map(
        functools.partial(on_device, dict(mesh.shape)),
        mesh=mesh,
        in_specs=in_specs,
        out_specs=out_specs,
        check_vma=False,
    )
```

```python
import functools
import math

import jax
import jax.numpy as jnp
from jax import lax
from jax.experimental import pallas as pl
from jax.experimental.pallas import tpu as pltpu
from jax.sharding import PartitionSpec as P

strain_floor = 0.1
step_size = 0.5
LANES = 128
REACH = 5
MIB = 1 << 20


class Plan:
    def __init__(self, mesh_shape, velocity_shape):
        self.map_size = mesh_shape["map"]
        self.layer_size = mesh_shape["layer"]
        self.devices = self.map_size * self.layer_size
        self.layers_here = velocity_shape[1]
        self.rows = velocity_shape[2]
        self.ny = velocity_shape[3]
        self.layers = self.layers_here * self.layer_size
        self.cols = self.ny // self.devices
        self.width = LANES // self.rows
        self.halo = (self.width - self.cols) // 2
        self.low = self.halo - REACH
        self.wide = self.cols + 2 * REACH
        self.half = self.wide // 2
        self.gap = self.low + self.wide
        self.local_cols = self.ny // self.layer_size
        self.per_chunk = LANES // self.cols
        self.chunks = self.ny // LANES
        self.column_count = self.rows * self.map_size * self.ny
        self.vel_rows = 2 * self.layers_here
        self.in_rows = self.vel_rows + self.rows
        self.out_rows = self.layers_here + 1
        self.unrolled = self.map_size <= 8
        assert self.width * self.rows == LANES and self.cols * self.per_chunk == LANES
        assert self.low >= 0 and self.wide % 2 == 0 and self.width - self.wide >= self.half
        assert 2 * self.cols <= self.width and self.local_cols % LANES == 0
        assert self.vel_rows == 8 and self.rows == 2 and 3 * self.wide <= LANES


def repeat(plan, count, body, carry=0):
    if plan.unrolled:
        for index in range(count):
            carry = body(index, carry)
        return carry
    return lax.fori_loop(0, count, body, carry)


def lane_roll(value, shift):
    shift = shift % LANES
    return value if shift == 0 else pltpu.roll(value, shift, 1)


def pack_kernel(
    plan, vel_hbm, driving_hbm, observed_hbm, log_hbm, mask_hbm, out_ref,
    vel_ref, driving_ref, observed_ref, log_ref, mask_ref, held, bed, arrival,
):
    width, rows, wide = plan.width, plan.rows, plan.wide
    copies = [
        pltpu.make_async_copy(source, target, arrival.at[n])
        for n, (source, target) in enumerate(
            (
                (vel_hbm, vel_ref),
                (driving_hbm, driving_ref),
                (observed_hbm, observed_ref),
                (log_hbm, log_ref),
                (mask_hbm, mask_ref),
            )
        )
    ]
    for copy in copies:
        copy.start()
    held[...] = jnp.zeros_like(held)
    bed[...] = jnp.zeros_like(bed)
    first = pl.multiple_of(LANES + lax.axis_index("layer") * plan.local_cols, LANES)
    here = pl.ds(first, plan.local_cols)
    for copy in copies:
        copy.wait()
    for r in range(rows):
        for c in range(2):
            for k in range(plan.layers_here):
                held[r, c * plan.layers_here + k : c * plan.layers_here + k + 1, LANES : LANES + plan.ny] = vel_ref[
                    c, k, r : r + 1, :
                ]
        mask = mask_ref[r : r + 1, :].astype(jnp.float32)
        for n, value in enumerate((observed_ref[0, r : r + 1, :], observed_ref[1, r : r + 1, :], mask)):
            held[r, plan.vel_rows + 2 * n : plan.vel_rows + 2 * n + 1, here] = value
            held[r, plan.vel_rows + 2 * n + 1 : plan.vel_rows + 2 * n + 2, here] = value
    for n, value in enumerate((driving_ref[0], driving_ref[1], log_ref[...])):
        bed[n, :, here] = value

    shape = (plan.vel_rows, LANES)
    lane = lax.broadcasted_iota(jnp.int32, shape, 1)
    odd = lax.broadcasted_iota(jnp.int32, shape, 0) % 2 == 1
    in_gap = jnp.logical_not(jnp.logical_and(lane % width >= plan.low, lane % width < plan.gap))
    bed_lane = lax.broadcasted_iota(jnp.int32, (rows, LANES), 1)

    chunk_rows = plan.per_chunk * plan.in_rows

    def chunk_windows(i, carry):
        def window(read, relative, length, lanes):
            step, offset = relative // LANES, relative % LANES

            def part(at):
                return read(pl.ds(pl.multiple_of((i + 1 + at) * LANES, LANES), LANES))

            if offset + length <= LANES:
                return part(step), offset
            return jnp.where(lanes >= offset, part(step), part(step + 1)), offset

        def side_by_side(row_base, t):
            block = None
            for r in range(rows):
                value, offset = window(
                    lambda span: held[r, row_base : row_base + 8, span], plan.cols * t - plan.halo, width, lane
                )
                value = lane_roll(value, r * width - offset)
                block = value if block is None else jnp.where(lane >= r * width, value, block)
            return block

        for t in range(plan.per_chunk):
            block = side_by_side(0, t)
            other = side_by_side(plan.vel_rows, t)
            shift = plan.gap - plan.low
            other = jnp.where(odd, lane_roll(other, shift - plan.half), lane_roll(other, shift))
            block = jnp.where(in_gap, other, block)
            line = None
            for n in range(3):
                value, offset = window(lambda span: bed[n, :, span], plan.cols * t - REACH, wide, bed_lane)
                value = lane_roll(value, n * wide - offset)
                line = value if line is None else jnp.where(bed_lane >= n * wide, value, line)
            at = pl.multiple_of(i * chunk_rows, 8) + t * plan.in_rows
            out_ref[pl.ds(at, plan.vel_rows), :] = block
            out_ref[pl.ds(at + plan.vel_rows, rows), :] = line
        return carry

    lax.fori_loop(0, plan.chunks, chunk_windows, 0)


def solve_kernel(plan, in_ref, out_ref, field, eta_ref, side, rhs, faces, ratio, inverse):
    size, width, rows = plan.map_size, plan.width, plan.rows
    layers, here = plan.layers, plan.layers_here
    shape = (size, LANES)
    lane = lax.broadcasted_iota(jnp.int32, shape, 1)
    sub = lax.broadcasted_iota(jnp.int32, shape, 0)
    last_group = lane >= LANES - width
    first_group = lane < width
    x_end = jnp.logical_and(last_group, sub == size - 1)
    x_start = jnp.logical_and(first_group, sub == 0)

    def arrived(part, row):
        return in_ref[pl.ds(part * plan.in_rows + row, size, stride=plan.layer_size * plan.in_rows), :]

    def over_parts(row):
        total = arrived(0, row)
        for part in range(1, plan.layer_size):
            total = total + arrived(part, row)
        return total

    def from_gap(index):
        shift = plan.low - plan.gap
        left, right = over_parts(2 * index), over_parts(2 * index + 1)
        return jnp.where(lane % width < plan.low + plan.half, lane_roll(left, shift), lane_roll(right, shift + plan.half))

    def from_line(index):
        plane = lane_roll(lines[0], plan.low - index * plan.wide)
        for r in range(1, rows):
            plane = jnp.where(lane >= r * width, lane_roll(lines[r], r * width + plan.low - index * plan.wide), plane)
        return plane

    def x_pair(value, edge):
        after = lane_roll(value, -width)
        before = after if 2 * width == LANES else lane_roll(value, width)
        after = jnp.where(last_group, pltpu.roll(after, size - 1, 0), after)
        before = jnp.where(first_group, pltpu.roll(before, 1, 0), before)
        return jnp.where(x_end, edge, after), jnp.where(x_start, edge, before)

    def y_pair(value):
        return lane_roll(value, -1), lane_roll(value, 1)

    def viscosity(rate):
        return jnp.exp2(jnp.log(strain_floor + rate) * (-1.0 / (3.0 * math.log(2.0))))

    def reciprocal(value):
        guess = pl.reciprocal(value, approx=True)
        return guess * (2.0 - value * guess)

    for part in range(plan.layer_size):
        for c in range(2):
            for k in range(here):
                field[c, part * here + k] = arrived(part, c * here + k)
    lines = [over_parts(plan.vel_rows + r) for r in range(rows)]
    reached = jnp.logical_and(lane % width >= plan.low, lane % width < plan.gap)
    driving = [2.0 * from_line(c) for c in range(2)]
    observed = [from_gap(c) for c in range(2)]
    mask = jnp.where(reached, from_gap(2), 0.0)
    ice = mask != 0.0
    friction = jnp.where(mask == 1.0, jnp.exp(from_line(2)), 0.0)

    def stencil(k, keep):
        u, v = field[0, k], field[1, k]
        u_east, u_west = x_pair(u, 0.0)
        v_east, v_west = x_pair(v, 0.0)
        u_north, u_south = y_pair(u)
        v_north, v_south = y_pair(v)
        stretch_x = u_east - u_west
        stretch_y = v_north - v_south
        shear = 0.5 * ((u_north - u_south) + (v_east - v_west))
        rate = 0.25 * (stretch_x * (stretch_x + stretch_y) + stretch_y * stretch_y + shear * shear)
        half_v = 0.5 * v
        eta = viscosity(rate)
        eta_edge = viscosity(0.25 * (u * u + half_v * half_v))
        eta_east, eta_west = x_pair(eta, eta_edge)
        eta_north, eta_south = y_pair(eta)
        east, west = eta + eta_east, eta + eta_west
        north, south = eta + eta_north, eta + eta_south
        along_x, along_y = east + west, north + south
        eta_ref[k] = eta
        side[0, k] = 4.0 * along_x + along_y
        side[1, k] = along_x + 4.0 * along_y
        rhs[0, k] = driving[0] + (4.0 * (east * u_east + west * u_west) + (north * u_north + south * u_south))
        rhs[1, k] = driving[1] + ((east * v_east + west * v_west) + 4.0 * (north * v_north + south * v_south))
        if keep:
            faces[0, k] = east
            faces[1, k] = west
            faces[2, k] = north
            faces[3, k] = south

    def coupling_of(k):
        return (2.0 * layers * layers) * (eta_ref[k] + eta_ref[k + 1])

    def eliminate(k, carry):
        lower, rest, value = carry
        coupling = coupling_of(k)
        new_rest, new_value = [], []
        for c in range(2):
            inv = reciprocal(coupling + rest[c])
            link = coupling * inv
            inverse[c, k] = inv
            ratio[c, k] = link
            out = (rhs[c, k] + lower * value[c]) * inv
            rhs[c, k] = out
            new_value.append(out)
            new_rest.append(side[c, k + 1] + rest[c] * link)
        return coupling, tuple(new_rest), tuple(new_value)

    def forward_solve():
        zero = jnp.zeros(shape, jnp.float32)
        rest = tuple(side[c, 0] + 2.0 * friction for c in range(2))
        lower, rest, value = repeat(plan, layers - 1, eliminate, (zero, rest, (zero, zero)))
        top = []
        for c in range(2):
            inv = reciprocal(rest[c])
            inverse[c, layers - 1] = inv
            top.append(jnp.where(ice, (rhs[c, layers - 1] + lower * value[c]) * inv, 0.0))
            field[c, layers - 1] = top[c]

        def back(step, following):
            k = layers - 2 - step
            current = tuple(jnp.where(ice, rhs[c, k] + ratio[c, k] * following[c], 0.0) for c in range(2))
            for c in range(2):
                field[c, k] = current[c]
            return current

        return top, repeat(plan, layers - 1, back, tuple(top))

    for sweep in range(2):

        def stencil_body(k, carry):
            stencil(k, sweep == 1)
            return carry

        repeat(plan, layers, stencil_body)
        top, base = forward_solve()

    centre = jnp.logical_and(lane % width >= plan.halo, lane % width < plan.halo + plan.cols)

    def send(k, carry):
        both = jnp.where(centre, field[0, k], lane_roll(field[1, k], plan.cols))
        out_ref[pl.ds((k // here) * plan.out_rows + k % here, size, stride=plan.layer_size * plan.out_rows), :] = both
        return carry

    repeat(plan, layers, send)

    mismatch = [jnp.where(ice, top[c] - observed[c], 0.0) for c in range(2)]
    source = [(2.0 * layers) * mismatch[c] for c in range(2)]

    first_top = tuple(source[c] * inverse[c, layers - 1] for c in range(2))

    def side_sum(k, value):
        east, west, north, south = (faces[n, k] for n in range(4))
        u_east, u_west = x_pair(value[0], 0.0)
        v_east, v_west = x_pair(value[1], 0.0)
        u_north, u_south = y_pair(value[0])
        v_north, v_south = y_pair(value[1])
        rhs[0, k] = 4.0 * (east * u_east + west * u_west) + (north * u_north + south * u_south)
        rhs[1, k] = (east * v_east + west * v_west) + 4.0 * (north * v_north + south * v_south)

    side_sum(layers - 1, first_top)

    def first_back(step, following):
        k = layers - 2 - step
        current = tuple(ratio[c, k] * following[c] for c in range(2))
        side_sum(k, current)
        return current

    repeat(plan, layers - 1, first_back, first_top)

    def second_forward(k, carry):
        lower, value = carry
        out = tuple((rhs[c, k] + lower * value[c]) * inverse[c, k] for c in range(2))
        for c in range(2):
            rhs[c, k] = out[c]
        return coupling_of(k), out

    zero = jnp.zeros(shape, jnp.float32)
    lower, value = repeat(plan, layers - 1, second_forward, (zero, (zero, zero)))
    second_top = tuple(
        (rhs[c, layers - 1] + source[c] + lower * value[c]) * inverse[c, layers - 1] for c in range(2)
    )

    def second_back(step, following):
        k = layers - 2 - step
        return tuple(rhs[c, k] + ratio[c, k] * following[c] for c in range(2))

    adjoint = repeat(plan, layers - 1, second_back, second_top)
    adjoint = [jnp.where(ice, adjoint[c], 0.0) for c in range(2)]
    gradient = -friction * (base[0] * adjoint[0] + base[1] * adjoint[1])

    def partial_sum(value):
        line = jnp.sum(jnp.where(centre, value, 0.0), axis=0, keepdims=True)
        folded = line
        for r in range(1, rows):
            folded = folded + lane_roll(line, r * width)
        return jnp.broadcast_to(lane_roll(folded, plan.cols), shape)

    misfit_line = partial_sum(mismatch[0] * mismatch[0] + mismatch[1] * mismatch[1])
    grad_line = partial_sum(gradient * gradient)
    in_first = jnp.logical_and(lane >= plan.halo + plan.cols, lane < plan.halo + 2 * plan.cols)
    last_row = jnp.where(centre, gradient, jnp.where(in_first, misfit_line, grad_line))
    for part in range(plan.layer_size):
        out_ref[pl.ds(part * plan.out_rows + here, size, stride=plan.layer_size * plan.out_rows), :] = last_row


def unpack_kernel(
    plan, in_ref, log_ref, vel_hbm, friction_hbm, misfit_hbm,
    vel_ref, friction_ref, misfit_ref, grad_ref, leave,
):
    here, width, cols = plan.layers_here, plan.width, plan.cols
    lane = lax.broadcasted_iota(jnp.int32, (plan.out_rows, LANES), 1)

    def block_at(i, t):
        at = i * plan.per_chunk * plan.out_rows
        if not isinstance(at, int):
            at = pl.multiple_of(at, 8)
        return in_ref[pl.ds(at + t * plan.out_rows, plan.out_rows), :]

    def component(c):
        def chunk(i, total):
            blocks = [block_at(i, t) for t in range(plan.per_chunk)]
            start = i * LANES
            if not isinstance(start, int):
                start = pl.multiple_of(start, LANES)
            span = pl.ds(start, LANES)
            for r in range(plan.rows):
                start = r * width + plan.halo + c * cols
                row = None
                for t in range(plan.per_chunk):
                    moved = lane_roll(blocks[t], t * cols - start)
                    row = moved if row is None else jnp.where(lane >= t * cols, moved, row)
                for k in range(here):
                    vel_ref[c, k, r : r + 1, span] = row[k : k + 1, :]
                if c == 0:
                    grad_ref[r : r + 1, span] = row[here : here + 1, :]
            if c == 0:
                for block in blocks:
                    total = total + block
            return total

        return repeat(plan, plan.chunks, chunk, jnp.zeros((plan.out_rows, LANES), jnp.float32))

    out = [pltpu.make_async_copy(vel_ref.at[c], vel_hbm.at[c], leave.at[c]) for c in range(2)]
    out.append(pltpu.make_async_copy(friction_ref, friction_hbm, leave.at[2]))
    out.append(pltpu.make_async_copy(misfit_ref, misfit_hbm, leave.at[3]))

    total = component(0)[here:, :]
    out[0].start()

    def summed(first):
        ahead = (lane[here:, :] + (LANES - first % LANES)) % LANES
        return jnp.sum(jnp.where(ahead < cols, total, 0.0), axis=1, keepdims=True)

    misfit_sum = summed(plan.halo + cols)
    grad_sum = summed(plan.halo + cols + width)
    misfit_ref[...] = 0.5 * misfit_sum / plan.column_count
    scale = step_size / jnp.sqrt(grad_sum / plan.column_count + 1e-06)
    first = pl.multiple_of(lax.axis_index("layer") * plan.local_cols, LANES)
    friction_ref[...] = log_ref[...] - grad_ref[:, pl.ds(first, plan.local_cols)] * scale
    out[2].start()
    out[3].start()
    component(1)
    out[1].start()
    for copy in out:
        copy.wait()


def on_device(mesh_shape, velocity_init, driving, observed, log_friction, ice_mask):
    plan = Plan(mesh_shape, velocity_init.shape)
    vmem = pl.BlockSpec(memory_space=pltpu.VMEM)
    hbm = pl.BlockSpec(memory_space=pltpu.HBM)
    f32 = jnp.float32
    limit = pltpu.CompilerParams(vmem_limit_bytes=(16 if plan.unrolled else 40) * MIB)
    inputs = (velocity_init, driving, observed, log_friction, ice_mask)

    def exchange(blocks, unit):
        shaped = blocks.reshape(blocks.shape[0] // unit, unit, LANES)
        return lax.all_to_all(shaped, ("map", "layer"), split_axis=0, concat_axis=0, tiled=True).reshape(blocks.shape)

    packed = pl.pallas_call(
        functools.partial(pack_kernel, plan),
        out_shape=jax.ShapeDtypeStruct((plan.devices * plan.in_rows, LANES), f32),
        in_specs=[hbm] * 5,
        out_specs=vmem,
        scratch_shapes=[pltpu.VMEM(x.shape, x.dtype) for x in inputs]
        + [
            pltpu.VMEM((plan.rows, plan.vel_rows + 8, plan.ny + 2 * LANES), f32),
            pltpu.VMEM((3, plan.rows, plan.ny + 2 * LANES), f32),
            pltpu.SemaphoreType.DMA((5,)),
        ],
        compiler_params=limit,
        name="pack",
    )(*(pltpu.with_memory_space_constraint(x, pltpu.HBM) for x in inputs))

    windows = exchange(packed, 2)

    plane = (plan.layers, plan.map_size, LANES)
    solved = pl.pallas_call(
        functools.partial(solve_kernel, plan),
        out_shape=jax.ShapeDtypeStruct((plan.devices * plan.out_rows, LANES), f32),
        in_specs=[vmem],
        out_specs=vmem,
        scratch_shapes=[
            pltpu.VMEM((2,) + plane, f32),
            pltpu.VMEM(plane, f32),
            pltpu.VMEM((2,) + plane, f32),
            pltpu.VMEM((2,) + plane, f32),
            pltpu.VMEM((4,) + plane, f32),
            pltpu.VMEM((2,) + plane, f32),
            pltpu.VMEM((2,) + plane, f32),
        ],
        compiler_params=limit,
        name="solve",
    )(windows)

    back = exchange(solved, 1)

    velocity, friction_new, misfit = pl.pallas_call(
        functools.partial(unpack_kernel, plan),
        out_shape=(
            jax.ShapeDtypeStruct(velocity_init.shape, f32),
            jax.ShapeDtypeStruct(log_friction.shape, f32),
            jax.ShapeDtypeStruct((1, 1), f32),
        ),
        in_specs=[vmem] * 2,
        out_specs=(hbm, hbm, hbm),
        scratch_shapes=[
            pltpu.VMEM(velocity_init.shape, f32),
            pltpu.VMEM(log_friction.shape, f32),
            pltpu.VMEM((1, 1), f32),
            pltpu.VMEM((plan.rows, plan.ny), f32),
            pltpu.SemaphoreType.DMA((4,)),
        ],
        compiler_params=limit,
        name="unpack",
    )(back, log_friction)
    return velocity, friction_new, misfit.reshape(())


def solution(mesh):
    in_specs = (
        P(None, "layer", "map", None),
        P(None, "map", "layer"),
        P(None, "map", "layer"),
        P("map", "layer"),
        P("map", "layer"),
    )
    out_specs = (P(None, "layer", "map", None), P("map", "layer"), P())
    return jax.shard_map(
        functools.partial(on_device, dict(mesh.shape)),
        mesh=mesh,
        in_specs=in_specs,
        out_specs=out_specs,
        check_vma=False,
    )
```

```python
import functools
import math

import jax
import jax.numpy as jnp
from jax import lax
from jax.experimental import pallas as pl
from jax.experimental.pallas import tpu as pltpu
from jax.sharding import PartitionSpec as P

strain_floor = 0.1
step_size = 0.5
LANES = 128
REACH = 5
MIB = 1 << 20


class Plan:
    def __init__(self, mesh_shape, velocity_shape):
        self.map_size = mesh_shape["map"]
        self.layer_size = mesh_shape["layer"]
        self.devices = self.map_size * self.layer_size
        self.layers_here = velocity_shape[1]
        self.rows = velocity_shape[2]
        self.ny = velocity_shape[3]
        self.layers = self.layers_here * self.layer_size
        self.cols = self.ny // self.devices
        self.width = LANES // self.rows
        self.halo = (self.width - self.cols) // 2
        self.low = self.halo - REACH
        self.wide = self.cols + 2 * REACH
        self.half = self.wide // 2
        self.gap = self.low + self.wide
        self.local_cols = self.ny // self.layer_size
        self.per_chunk = LANES // self.cols
        self.chunks = self.ny // LANES
        self.column_count = self.rows * self.map_size * self.ny
        self.vel_rows = 2 * self.layers_here
        self.in_rows = self.vel_rows + self.rows
        self.out_rows = self.layers_here + 1
        self.unrolled = self.map_size <= 8
        assert self.width * self.rows == LANES and self.cols * self.per_chunk == LANES
        assert self.low >= 0 and self.wide % 2 == 0 and self.width - self.wide >= self.half
        assert 2 * self.cols <= self.width and self.local_cols % LANES == 0
        assert self.vel_rows == 8 and self.rows == 2 and 3 * self.wide <= LANES


def repeat(plan, count, body, carry=0):
    if plan.unrolled:
        for index in range(count):
            carry = body(index, carry)
        return carry
    return lax.fori_loop(0, count, body, carry)


def lane_roll(value, shift):
    shift = shift % LANES
    return value if shift == 0 else pltpu.roll(value, shift, 1)


def pack_kernel(
    plan, vel_hbm, driving_hbm, observed_hbm, log_hbm, mask_hbm, out_ref,
    vel_ref, driving_ref, observed_ref, log_ref, mask_ref, arrival,
):
    width, rows, wide, half = plan.width, plan.rows, plan.wide, plan.half
    pairs = (
        (vel_hbm, vel_ref),
        (driving_hbm, driving_ref),
        (observed_hbm, observed_ref),
        (log_hbm, log_ref),
        (mask_hbm, mask_ref),
    )
    copies = [pltpu.make_async_copy(pair[0], pair[1], arrival.at[n]) for n, pair in enumerate(pairs)]
    for copy in copies:
        copy.start()
    shape = (plan.vel_rows, LANES)
    lane = lax.broadcasted_iota(jnp.int32, shape, 1)
    sub = lax.broadcasted_iota(jnp.int32, shape, 0)
    in_gap = jnp.logical_not(jnp.logical_and(lane % width >= plan.low, lane % width < plan.gap))
    no_line = jnp.zeros((rows, LANES), jnp.float32)

    def slide(part, start, length, place):
        step, offset = start // LANES, start % LANES
        value = part(step)
        if offset + length > LANES:
            after = part(step + 1)
            value = jnp.where(lax.broadcasted_iota(jnp.int32, value.shape, 1) >= offset, value, after)
        return lane_roll(value, place - offset)

    copies[0].wait()

    def chunk_windows(i, carry):
        def velocity(r):
            def part(step):
                chunk = i + step
                if isinstance(chunk, int) and not 0 <= chunk < plan.chunks:
                    return jnp.zeros(shape, jnp.float32)
                at = chunk if isinstance(chunk, int) else jnp.clip(chunk, 0, plan.chunks - 1)
                value = vel_ref[pl.ds(at * rows + r, plan.vel_rows, stride=plan.chunks * rows), :]
                if isinstance(chunk, int):
                    return value
                return jnp.where(jnp.logical_and(chunk >= 0, chunk < plan.chunks), value, 0.0)

            return part

        for t in range(plan.per_chunk):
            block = None
            for r in range(rows):
                value = slide(velocity(r), plan.cols * t - plan.halo, width, r * width)
                block = value if block is None else jnp.where(lane >= r * width, value, block)
            at = i * plan.per_chunk * plan.in_rows
            if not isinstance(at, int):
                at = pl.multiple_of(at, 8)
            at = at + t * plan.in_rows
            out_ref[pl.ds(at, plan.vel_rows), :] = jnp.where(in_gap, 0.0, block)
            out_ref[pl.ds(at + plan.vel_rows, rows), :] = no_line
        return carry

    repeat(plan, plan.chunks, chunk_windows)
    for copy in copies[1:]:
        copy.wait()

    place = lax.axis_index("layer")
    local_chunks = plan.local_cols // LANES

    def line_part(ref, row):
        def part(step):
            if not 0 <= step < local_chunks:
                return no_line
            return ref[row + step * rows : row + (step + 1) * rows, :]

        return part

    def gap_part(r):
        def part(step):
            if not 0 <= step < local_chunks:
                return jnp.zeros(shape, jnp.float32)
            at = step * rows + r
            skip = local_chunks * rows
            first = jnp.broadcast_to(observed_ref[at : at + 1, :], shape)
            second = jnp.broadcast_to(observed_ref[skip + at : skip + at + 1, :], shape)
            third = jnp.broadcast_to(mask_ref[at : at + 1, :], shape).astype(jnp.float32)
            return jnp.where(sub < 2, first, jnp.where(sub < 4, second, third))

        return part

    gap_parts = [[gap_part(r)(step) for step in range(-1, local_chunks + 1)] for r in range(rows)]
    own = plan.local_cols // plan.cols
    spill = -(-REACH // plan.cols)

    def column_block(q):
        start = q * plan.cols - REACH
        line = None
        for n, part in enumerate(
            (line_part(driving_ref, 0), line_part(driving_ref, local_chunks * rows), line_part(log_ref, 0))
        ):
            value = slide(part, start, wide, n * wide)
            lanes = lax.broadcasted_iota(jnp.int32, value.shape, 1)
            line = value if line is None else jnp.where(lanes >= n * wide, value, line)
        block = None
        for r in range(rows):
            halves = [
                slide(lambda step: gap_parts[r][step + 1], start + h * half, half, (r * width + plan.gap) % LANES)
                for h in range(2)
            ]
            value = jnp.where(sub % 2 == 0, halves[0], halves[1])
            ahead = (lane + (LANES - plan.gap)) % LANES
            block = value if block is None else jnp.where(ahead >= r * width, value, block)
        at = pl.multiple_of(place * (own * plan.in_rows), 8) + q * plan.in_rows
        here = pl.ds(at, plan.vel_rows)
        out_ref[here, :] = jnp.where(in_gap, block, out_ref[here, :])
        out_ref[pl.ds(at + plan.vel_rows, rows), :] = line

    for q in range(own):
        column_block(q)

    @pl.when(place > 0)
    def _():
        for q in range(-spill, 0):
            column_block(q)

    @pl.when(place < plan.layer_size - 1)
    def _():
        for q in range(own, own + spill):
            column_block(q)


def solve_kernel(plan, in_ref, out_ref, field, eta_ref, side, rhs, faces, ratio, inverse):
    size, width, rows = plan.map_size, plan.width, plan.rows
    layers, here = plan.layers, plan.layers_here
    shape = (size, LANES)
    lane = lax.broadcasted_iota(jnp.int32, shape, 1)
    sub = lax.broadcasted_iota(jnp.int32, shape, 0)
    last_group = lane >= LANES - width
    first_group = lane < width
    x_end = jnp.logical_and(last_group, sub == size - 1)
    x_start = jnp.logical_and(first_group, sub == 0)

    def arrived(part, row):
        return in_ref[pl.ds(part * plan.in_rows + row, size, stride=plan.layer_size * plan.in_rows), :]

    def over_parts(row):
        total = arrived(0, row)
        for part in range(1, plan.layer_size):
            total = total + arrived(part, row)
        return total

    def from_gap(index):
        shift = plan.low - plan.gap
        left, right = over_parts(2 * index), over_parts(2 * index + 1)
        return jnp.where(lane % width < plan.low + plan.half, lane_roll(left, shift), lane_roll(right, shift + plan.half))

    def from_line(index):
        plane = lane_roll(lines[0], plan.low - index * plan.wide)
        for r in range(1, rows):
            plane = jnp.where(lane >= r * width, lane_roll(lines[r], r * width + plan.low - index * plan.wide), plane)
        return plane

    def x_pair(value, edge):
        after = lane_roll(value, -width)
        before = after if 2 * width == LANES else lane_roll(value, width)
        after = jnp.where(last_group, pltpu.roll(after, size - 1, 0), after)
        before = jnp.where(first_group, pltpu.roll(before, 1, 0), before)
        return jnp.where(x_end, edge, after), jnp.where(x_start, edge, before)

    def y_pair(value):
        return lane_roll(value, -1), lane_roll(value, 1)

    def viscosity(rate):
        return jnp.exp2(jnp.log(strain_floor + rate) * (-1.0 / (3.0 * math.log(2.0))))

    def reciprocal(value):
        guess = pl.reciprocal(value, approx=True)
        return guess * (2.0 - value * guess)

    for part in range(plan.layer_size):
        for c in range(2):
            for k in range(here):
                field[c, part * here + k] = arrived(part, c * here + k)
    lines = [over_parts(plan.vel_rows + r) for r in range(rows)]
    reached = jnp.logical_and(lane % width >= plan.low, lane % width < plan.gap)
    driving = [2.0 * from_line(c) for c in range(2)]
    observed = [from_gap(c) for c in range(2)]
    mask = jnp.where(reached, from_gap(2), 0.0)
    ice = mask != 0.0
    friction = jnp.where(mask == 1.0, jnp.exp(from_line(2)), 0.0)

    def stencil(k, keep):
        u, v = field[0, k], field[1, k]
        u_east, u_west = x_pair(u, 0.0)
        v_east, v_west = x_pair(v, 0.0)
        u_north, u_south = y_pair(u)
        v_north, v_south = y_pair(v)
        stretch_x = u_east - u_west
        stretch_y = v_north - v_south
        shear = 0.5 * ((u_north - u_south) + (v_east - v_west))
        rate = 0.25 * (stretch_x * (stretch_x + stretch_y) + stretch_y * stretch_y + shear * shear)
        half_v = 0.5 * v
        eta = viscosity(rate)
        eta_edge = viscosity(0.25 * (u * u + half_v * half_v))
        eta_east, eta_west = x_pair(eta, eta_edge)
        eta_north, eta_south = y_pair(eta)
        east, west = eta + eta_east, eta + eta_west
        north, south = eta + eta_north, eta + eta_south
        along_x, along_y = east + west, north + south
        eta_ref[k] = eta
        side[0, k] = 4.0 * along_x + along_y
        side[1, k] = along_x + 4.0 * along_y
        rhs[0, k] = driving[0] + (4.0 * (east * u_east + west * u_west) + (north * u_north + south * u_south))
        rhs[1, k] = driving[1] + ((east * v_east + west * v_west) + 4.0 * (north * v_north + south * v_south))
        if keep:
            faces[0, k] = east
            faces[1, k] = west
            faces[2, k] = north
            faces[3, k] = south

    def coupling_of(k):
        return (2.0 * layers * layers) * (eta_ref[k] + eta_ref[k + 1])

    def eliminate(k, carry):
        lower, rest, value = carry
        coupling = coupling_of(k)
        new_rest, new_value = [], []
        for c in range(2):
            inv = reciprocal(coupling + rest[c])
            link = coupling * inv
            inverse[c, k] = inv
            ratio[c, k] = link
            out = (rhs[c, k] + lower * value[c]) * inv
            rhs[c, k] = out
            new_value.append(out)
            new_rest.append(side[c, k + 1] + rest[c] * link)
        return coupling, tuple(new_rest), tuple(new_value)

    def forward_solve():
        zero = jnp.zeros(shape, jnp.float32)
        rest = tuple(side[c, 0] + 2.0 * friction for c in range(2))
        lower, rest, value = repeat(plan, layers - 1, eliminate, (zero, rest, (zero, zero)))
        top = []
        for c in range(2):
            inv = reciprocal(rest[c])
            inverse[c, layers - 1] = inv
            top.append(jnp.where(ice, (rhs[c, layers - 1] + lower * value[c]) * inv, 0.0))
            field[c, layers - 1] = top[c]

        def back(step, following):
            k = layers - 2 - step
            current = tuple(jnp.where(ice, rhs[c, k] + ratio[c, k] * following[c], 0.0) for c in range(2))
            for c in range(2):
                field[c, k] = current[c]
            return current

        return top, repeat(plan, layers - 1, back, tuple(top))

    for sweep in range(2):

        def stencil_body(k, carry):
            stencil(k, sweep == 1)
            return carry

        repeat(plan, layers, stencil_body)
        top, base = forward_solve()

    centre = jnp.logical_and(lane % width >= plan.halo, lane % width < plan.halo + plan.cols)

    def send(k, carry):
        both = jnp.where(centre, field[0, k], lane_roll(field[1, k], plan.cols))
        out_ref[pl.ds((k // here) * plan.out_rows + k % here, size, stride=plan.layer_size * plan.out_rows), :] = both
        return carry

    repeat(plan, layers, send)

    mismatch = [jnp.where(ice, top[c] - observed[c], 0.0) for c in range(2)]
    source = [(2.0 * layers) * mismatch[c] for c in range(2)]

    first_top = tuple(source[c] * inverse[c, layers - 1] for c in range(2))

    def side_sum(k, value):
        east, west, north, south = (faces[n, k] for n in range(4))
        u_east, u_west = x_pair(value[0], 0.0)
        v_east, v_west = x_pair(value[1], 0.0)
        u_north, u_south = y_pair(value[0])
        v_north, v_south = y_pair(value[1])
        rhs[0, k] = 4.0 * (east * u_east + west * u_west) + (north * u_north + south * u_south)
        rhs[1, k] = (east * v_east + west * v_west) + 4.0 * (north * v_north + south * v_south)

    side_sum(layers - 1, first_top)

    def first_back(step, following):
        k = layers - 2 - step
        current = tuple(ratio[c, k] * following[c] for c in range(2))
        side_sum(k, current)
        return current

    repeat(plan, layers - 1, first_back, first_top)

    def second_forward(k, carry):
        lower, value = carry
        out = tuple((rhs[c, k] + lower * value[c]) * inverse[c, k] for c in range(2))
        for c in range(2):
            rhs[c, k] = out[c]
        return coupling_of(k), out

    zero = jnp.zeros(shape, jnp.float32)
    lower, value = repeat(plan, layers - 1, second_forward, (zero, (zero, zero)))
    second_top = tuple(
        (rhs[c, layers - 1] + source[c] + lower * value[c]) * inverse[c, layers - 1] for c in range(2)
    )

    def second_back(step, following):
        k = layers - 2 - step
        return tuple(rhs[c, k] + ratio[c, k] * following[c] for c in range(2))

    adjoint = repeat(plan, layers - 1, second_back, second_top)
    adjoint = [jnp.where(ice, adjoint[c], 0.0) for c in range(2)]
    gradient = -friction * (base[0] * adjoint[0] + base[1] * adjoint[1])

    def partial_sum(value):
        line = jnp.sum(jnp.where(centre, value, 0.0), axis=0, keepdims=True)
        folded = line
        for r in range(1, rows):
            folded = folded + lane_roll(line, r * width)
        return jnp.broadcast_to(lane_roll(folded, plan.cols), shape)

    misfit_line = partial_sum(mismatch[0] * mismatch[0] + mismatch[1] * mismatch[1])
    grad_line = partial_sum(gradient * gradient)
    in_first = jnp.logical_and(lane >= plan.halo + plan.cols, lane < plan.halo + 2 * plan.cols)
    last_row = jnp.where(centre, gradient, jnp.where(in_first, misfit_line, grad_line))
    for part in range(plan.layer_size):
        out_ref[pl.ds(part * plan.out_rows + here, size, stride=plan.layer_size * plan.out_rows), :] = last_row


def unpack_kernel(
    plan, in_ref, log_ref, vel_hbm, friction_hbm, misfit_hbm,
    vel_ref, friction_ref, misfit_ref, grad_ref, leave,
):
    here, width, cols, rows = plan.layers_here, plan.width, plan.cols, plan.rows
    local_chunks = plan.local_cols // LANES

    total = jnp.sum(
        in_ref[pl.ds(here, plan.devices, stride=plan.out_rows), :].astype(jnp.float32), axis=0, keepdims=True
    )
    line_lane = lax.broadcasted_iota(jnp.int32, (1, LANES), 1)

    def summed(first):
        ahead = (line_lane + (LANES - first % LANES)) % LANES
        return jnp.sum(jnp.where(ahead < cols, total, 0.0), axis=1, keepdims=True)

    misfit_sum = summed(plan.halo + cols)
    grad_sum = summed(plan.halo + cols + width)
    misfit_ref[...] = 0.5 * misfit_sum / plan.column_count
    scale = step_size / jnp.sqrt(grad_sum / plan.column_count + 1e-06)

    lane = lax.broadcasted_iota(jnp.int32, (plan.out_rows, LANES), 1)
    starts = [(r, c, r * width + plan.halo + c * cols) for r in range(rows) for c in range(2)]

    def chunk(i, carry):
        at = i * plan.per_chunk * plan.out_rows
        if not isinstance(at, int):
            at = pl.multiple_of(at, 8)
        turned = [
            lane_roll(in_ref[pl.ds(at + t * plan.out_rows, plan.out_rows), :], t * cols)
            for t in range(plan.per_chunk)
        ]
        for r, c, start in starts:
            ahead = (lane + (LANES - start % LANES)) % LANES
            row = turned[0]
            for t in range(1, plan.per_chunk):
                row = jnp.where(ahead >= t * cols, turned[t], row)
            row = lane_roll(row, -start)
            vel_ref[pl.ds(c * here * plan.chunks * rows + i * rows + r, here, stride=plan.chunks * rows), :] = row[:here]
            if c == 0:
                owner, step = i // local_chunks, i % local_chunks
                grad_ref[owner, pl.ds(step * rows + r, 1), :] = row[here : here + 1]
        return carry

    repeat(plan, plan.chunks, chunk)
    out = [
        pltpu.make_async_copy(vel_ref, vel_hbm, leave.at[0]),
        pltpu.make_async_copy(friction_ref, friction_hbm, leave.at[1]),
        pltpu.make_async_copy(misfit_ref, misfit_hbm, leave.at[2]),
    ]
    out[0].start()
    friction_ref[...] = log_ref[...] - grad_ref[lax.axis_index("layer")] * scale
    out[1].start()
    out[2].start()
    for copy in out:
        copy.wait()


def as_lines(x):
    chunked = x.reshape(x.shape[:-1] + (x.shape[-1] // LANES, LANES))
    return jnp.swapaxes(chunked, -3, -2).reshape(-1, LANES)


def from_lines(lines, shape):
    chunked = lines.reshape(shape[:-2] + (shape[-1] // LANES, shape[-2], LANES))
    return jnp.swapaxes(chunked, -3, -2).reshape(shape)


def on_device(mesh_shape, velocity_init, driving, observed, log_friction, ice_mask):
    plan = Plan(mesh_shape, velocity_init.shape)
    vmem = pl.BlockSpec(memory_space=pltpu.VMEM)
    hbm = pl.BlockSpec(memory_space=pltpu.HBM)
    f32 = jnp.float32
    limit = pltpu.CompilerParams(vmem_limit_bytes=(16 if plan.unrolled else 40) * MIB)
    inputs = [as_lines(x) for x in (velocity_init, driving, observed, log_friction, ice_mask)]

    def exchange(blocks, unit):
        shaped = blocks.reshape(blocks.shape[0] // unit, unit, LANES)
        return lax.all_to_all(shaped, ("map", "layer"), split_axis=0, concat_axis=0, tiled=True).reshape(blocks.shape)

    packed = pl.pallas_call(
        functools.partial(pack_kernel, plan),
        out_shape=jax.ShapeDtypeStruct((plan.devices * plan.in_rows, LANES), f32),
        in_specs=[hbm] * 5,
        out_specs=vmem,
        scratch_shapes=[pltpu.VMEM(x.shape, x.dtype) for x in inputs]
        + [
            pltpu.SemaphoreType.DMA((5,)),
        ],
        compiler_params=limit,
        name="pack",
    )(*(pltpu.with_memory_space_constraint(x, pltpu.HBM) for x in inputs))

    windows = exchange(packed, 2)

    plane = (plan.layers, plan.map_size, LANES)
    solved = pl.pallas_call(
        functools.partial(solve_kernel, plan),
        out_shape=jax.ShapeDtypeStruct((plan.devices * plan.out_rows, LANES), f32),
        in_specs=[vmem],
        out_specs=vmem,
        scratch_shapes=[
            pltpu.VMEM((2,) + plane, f32),
            pltpu.VMEM(plane, f32),
            pltpu.VMEM((2,) + plane, f32),
            pltpu.VMEM((2,) + plane, f32),
            pltpu.VMEM((4,) + plane, f32),
            pltpu.VMEM((2,) + plane, f32),
            pltpu.VMEM((2,) + plane, f32),
        ],
        compiler_params=limit,
        name="solve",
    )(windows)

    back = exchange(solved, 1)

    vel_lines, log_lines = inputs[0], inputs[3]
    velocity, friction_new, misfit = pl.pallas_call(
        functools.partial(unpack_kernel, plan),
        out_shape=(
            jax.ShapeDtypeStruct(vel_lines.shape, f32),
            jax.ShapeDtypeStruct(log_lines.shape, f32),
            jax.ShapeDtypeStruct((1, 1), f32),
        ),
        in_specs=[vmem] * 2,
        out_specs=(hbm, hbm, hbm),
        scratch_shapes=[
            pltpu.VMEM(vel_lines.shape, f32),
            pltpu.VMEM(log_lines.shape, f32),
            pltpu.VMEM((1, 1), f32),
            pltpu.VMEM((plan.layer_size,) + log_lines.shape, f32),
            pltpu.SemaphoreType.DMA((3,)),
        ],
        compiler_params=limit,
        name="unpack",
    )(back, log_lines)
    return (
        from_lines(velocity, velocity_init.shape),
        from_lines(friction_new, log_friction.shape),
        misfit.reshape(()),
    )


def solution(mesh):
    in_specs = (
        P(None, "layer", "map", None),
        P(None, "map", "layer"),
        P(None, "map", "layer"),
        P("map", "layer"),
        P("map", "layer"),
    )
    out_specs = (P(None, "layer", "map", None), P("map", "layer"), P())
    return jax.shard_map(
        functools.partial(on_device, dict(mesh.shape)),
        mesh=mesh,
        in_specs=in_specs,
        out_specs=out_specs,
        check_vma=False,
    )
```

```python
import functools
import math

import jax
import jax.numpy as jnp
from jax import lax
from jax.experimental import pallas as pl
from jax.experimental.pallas import tpu as pltpu
from jax.sharding import PartitionSpec as P

strain_floor = 0.1
step_size = 0.5
LANES = 128
REACH = 5
MIB = 1 << 20


class Plan:
    def __init__(self, mesh_shape, velocity_shape):
        self.map_size = mesh_shape["map"]
        self.layer_size = mesh_shape["layer"]
        self.devices = self.map_size * self.layer_size
        self.layers_here = velocity_shape[1]
        self.rows = velocity_shape[2]
        self.ny = velocity_shape[3]
        self.layers = self.layers_here * self.layer_size
        self.cols = self.ny // self.devices
        self.width = LANES // self.rows
        self.halo = (self.width - self.cols) // 2
        self.low = self.halo - REACH
        self.wide = self.cols + 2 * REACH
        self.half = self.wide // 2
        self.gap = self.low + self.wide
        self.local_cols = self.ny // self.layer_size
        self.per_chunk = LANES // self.cols
        self.chunks = self.ny // LANES
        self.column_count = self.rows * self.map_size * self.ny
        self.vel_rows = 2 * self.layers_here
        self.in_rows = self.vel_rows + self.rows
        self.out_rows = self.layers_here + 1
        self.unrolled = self.map_size <= 8
        assert self.width * self.rows == LANES and self.cols * self.per_chunk == LANES
        assert self.low >= 0 and self.wide % 2 == 0 and self.width - self.wide >= self.half
        assert 2 * self.cols <= self.width and self.local_cols % LANES == 0
        assert self.vel_rows == 8 and self.rows == 2 and 3 * self.wide <= LANES


def repeat(plan, count, body, carry=0):
    if plan.unrolled:
        for index in range(count):
            carry = body(index, carry)
        return carry
    return lax.fori_loop(0, count, body, carry)


def lane_roll(value, shift):
    shift = shift % LANES
    return value if shift == 0 else pltpu.roll(value, shift, 1)


def pack_kernel(
    plan, vel_hbm, driving_hbm, observed_hbm, log_hbm, mask_hbm, out_ref,
    vel_ref, driving_ref, observed_ref, log_ref, mask_ref, arrival,
):
    width, rows, wide, half = plan.width, plan.rows, plan.wide, plan.half
    pairs = (
        (vel_hbm, vel_ref),
        (driving_hbm, driving_ref),
        (observed_hbm, observed_ref),
        (log_hbm, log_ref),
        (mask_hbm, mask_ref),
    )
    copies = [pltpu.make_async_copy(pair[0], pair[1], arrival.at[n]) for n, pair in enumerate(pairs)]
    for copy in copies:
        copy.start()
    shape = (plan.vel_rows, LANES)
    lane = lax.broadcasted_iota(jnp.int32, shape, 1)
    sub = lax.broadcasted_iota(jnp.int32, shape, 0)
    in_gap = jnp.logical_not(jnp.logical_and(lane % width >= plan.low, lane % width < plan.gap))
    no_line = jnp.zeros((rows, LANES), jnp.float32)

    def slide(part, start, length, place):
        step, offset = start // LANES, start % LANES
        value = part(step)
        if offset + length > LANES:
            after = part(step + 1)
            value = jnp.where(lax.broadcasted_iota(jnp.int32, value.shape, 1) >= offset, value, after)
        return lane_roll(value, place - offset)

    copies[0].wait()

    def chunk_windows(i, carry):
        def velocity(r):
            def part(step):
                chunk = i + step
                if isinstance(chunk, int) and not 0 <= chunk < plan.chunks:
                    return jnp.zeros(shape, jnp.float32)
                at = chunk if isinstance(chunk, int) else jnp.clip(chunk, 0, plan.chunks - 1)
                value = vel_ref[pl.ds(at * rows + r, plan.vel_rows, stride=plan.chunks * rows), :]
                if isinstance(chunk, int):
                    return value
                return jnp.where(jnp.logical_and(chunk >= 0, chunk < plan.chunks), value, 0.0)

            return part

        for t in range(plan.per_chunk):
            block = None
            for r in range(rows):
                value = slide(velocity(r), plan.cols * t - plan.halo, width, r * width)
                block = value if block is None else jnp.where(lane >= r * width, value, block)
            at = i * plan.per_chunk * plan.in_rows
            if not isinstance(at, int):
                at = pl.multiple_of(at, 8)
            at = at + t * plan.in_rows
            out_ref[pl.ds(at, plan.vel_rows), :] = jnp.where(in_gap, 0.0, block)
            out_ref[pl.ds(at + plan.vel_rows, rows), :] = no_line
        return carry

    repeat(plan, plan.chunks, chunk_windows)
    for copy in copies[1:]:
        copy.wait()

    place = lax.axis_index("layer")
    local_chunks = plan.local_cols // LANES

    def line_part(ref, row):
        def part(step):
            if not 0 <= step < local_chunks:
                return no_line
            return ref[row + step * rows : row + (step + 1) * rows, :]

        return part

    def gap_part(r):
        def part(step):
            if not 0 <= step < local_chunks:
                return jnp.zeros(shape, jnp.float32)
            at = step * rows + r
            skip = local_chunks * rows
            first = jnp.broadcast_to(observed_ref[at : at + 1, :], shape)
            second = jnp.broadcast_to(observed_ref[skip + at : skip + at + 1, :], shape)
            third = jnp.broadcast_to(mask_ref[at : at + 1, :], shape).astype(jnp.float32)
            return jnp.where(sub < 2, first, jnp.where(sub < 4, second, third))

        return part

    gap_parts = [[gap_part(r)(step) for step in range(-1, local_chunks + 1)] for r in range(rows)]
    own = plan.local_cols // plan.cols
    spill = -(-REACH // plan.cols)

    def column_block(q):
        start = q * plan.cols - REACH
        line = None
        for n, part in enumerate(
            (line_part(driving_ref, 0), line_part(driving_ref, local_chunks * rows), line_part(log_ref, 0))
        ):
            value = slide(part, start, wide, n * wide)
            lanes = lax.broadcasted_iota(jnp.int32, value.shape, 1)
            line = value if line is None else jnp.where(lanes >= n * wide, value, line)
        block = None
        for r in range(rows):
            halves = [
                slide(lambda step: gap_parts[r][step + 1], start + h * half, half, (r * width + plan.gap) % LANES)
                for h in range(2)
            ]
            value = jnp.where(sub % 2 == 0, halves[0], halves[1])
            ahead = (lane + (LANES - plan.gap)) % LANES
            block = value if block is None else jnp.where(ahead >= r * width, value, block)
        at = pl.multiple_of(place * (own * plan.in_rows), 8) + q * plan.in_rows
        here = pl.ds(at, plan.vel_rows)
        out_ref[here, :] = jnp.where(in_gap, block, out_ref[here, :])
        out_ref[pl.ds(at + plan.vel_rows, rows), :] = line

    for q in range(own):
        column_block(q)

    @pl.when(place > 0)
    def _():
        for q in range(-spill, 0):
            column_block(q)

    @pl.when(place < plan.layer_size - 1)
    def _():
        for q in range(own, own + spill):
            column_block(q)


def solve_kernel(plan, in_ref, out_ref, field, eta_ref, side, rhs, faces, ratio, inverse):
    size, width, rows = plan.map_size, plan.width, plan.rows
    layers, here = plan.layers, plan.layers_here
    shape = (size, LANES)
    lane = lax.broadcasted_iota(jnp.int32, shape, 1)
    sub = lax.broadcasted_iota(jnp.int32, shape, 0)
    last_group = lane >= LANES - width
    first_group = lane < width
    x_end = jnp.logical_and(last_group, sub == size - 1)
    x_start = jnp.logical_and(first_group, sub == 0)

    def arrived(part, row):
        return in_ref[pl.ds(part * plan.in_rows + row, size, stride=plan.layer_size * plan.in_rows), :]

    def over_parts(row):
        total = arrived(0, row)
        for part in range(1, plan.layer_size):
            total = total + arrived(part, row)
        return total

    def from_gap(index):
        shift = plan.low - plan.gap
        left, right = over_parts(2 * index), over_parts(2 * index + 1)
        return jnp.where(lane % width < plan.low + plan.half, lane_roll(left, shift), lane_roll(right, shift + plan.half))

    def from_line(index):
        plane = lane_roll(lines[0], plan.low - index * plan.wide)
        for r in range(1, rows):
            plane = jnp.where(lane >= r * width, lane_roll(lines[r], r * width + plan.low - index * plan.wide), plane)
        return plane

    def x_pair(value, edge):
        after = lane_roll(value, -width)
        before = after if 2 * width == LANES else lane_roll(value, width)
        after = jnp.where(last_group, pltpu.roll(after, size - 1, 0), after)
        before = jnp.where(first_group, pltpu.roll(before, 1, 0), before)
        return jnp.where(x_end, edge, after), jnp.where(x_start, edge, before)

    def y_pair(value):
        return lane_roll(value, -1), lane_roll(value, 1)

    def viscosity(rate):
        return jnp.exp2(jnp.log(strain_floor + rate) * (-1.0 / (3.0 * math.log(2.0))))

    for part in range(plan.layer_size):
        for c in range(2):
            for k in range(here):
                field[c, part * here + k] = arrived(part, c * here + k)
    lines = [over_parts(plan.vel_rows + r) for r in range(rows)]
    reached = jnp.logical_and(lane % width >= plan.low, lane % width < plan.gap)
    driving = [2.0 * from_line(c) for c in range(2)]
    observed = [from_gap(c) for c in range(2)]
    mask = jnp.where(reached, from_gap(2), 0.0)
    ice = mask != 0.0
    friction = jnp.where(mask == 1.0, jnp.exp(from_line(2)), 0.0)

    def stencil(k, keep):
        u, v = field[0, k], field[1, k]
        u_east, u_west = x_pair(u, 0.0)
        v_east, v_west = x_pair(v, 0.0)
        u_north, u_south = y_pair(u)
        v_north, v_south = y_pair(v)
        stretch_x = u_east - u_west
        stretch_y = v_north - v_south
        shear = 0.5 * ((u_north - u_south) + (v_east - v_west))
        rate = 0.25 * (stretch_x * (stretch_x + stretch_y) + stretch_y * stretch_y + shear * shear)
        half_v = 0.5 * v
        eta = viscosity(rate)
        eta_edge = viscosity(0.25 * (u * u + half_v * half_v))
        eta_east, eta_west = x_pair(eta, eta_edge)
        eta_north, eta_south = y_pair(eta)
        east, west = eta + eta_east, eta + eta_west
        north, south = eta + eta_north, eta + eta_south
        along_x, along_y = east + west, north + south
        eta_ref[k] = eta
        side[0, k] = 4.0 * along_x + along_y
        side[1, k] = along_x + 4.0 * along_y
        rhs[0, k] = driving[0] + (4.0 * (east * u_east + west * u_west) + (north * u_north + south * u_south))
        rhs[1, k] = driving[1] + ((east * v_east + west * v_west) + 4.0 * (north * v_north + south * v_south))
        if keep:
            faces[0, k] = east
            faces[1, k] = west
            faces[2, k] = north
            faces[3, k] = south

    def coupling_of(k):
        return (2.0 * layers * layers) * (eta_ref[k] + eta_ref[k + 1])

    middle = layers // 2
    zero = jnp.zeros(shape, jnp.float32)

    def eliminate(k, coupling, carry):
        before, passed, value = carry
        new_passed, new_value = [], []
        for c in range(2):
            rest = side[c, k] + passed[c]
            pivot = coupling + rest
            guess = pl.reciprocal(pivot, approx=True)
            correct = 2.0 - pivot * guess
            new_passed.append((coupling * rest * guess) * correct)
            inv = guess * correct
            inverse[c, k] = inv
            ratio[c, k] = coupling * inv
            out = (rhs[c, k] + before * value[c]) * inv
            rhs[c, k] = out
            new_value.append(out)
        return coupling, tuple(new_passed), tuple(new_value)

    def lower_step(k, carry):
        return eliminate(k, coupling_of(k), carry)

    def upper_step(k, carry):
        return eliminate(k, coupling_of(k - 1), carry)

    def fronts(step, carry):
        lower, upper = carry
        return lower_step(step, lower), upper_step(layers - 1 - step, upper)

    def spread(first, body):
        def outward(step, carry):
            below, above = carry
            return body(middle - 1 - step, below), body(middle + 1 + step, above)

        below, above = repeat(plan, layers - 1 - middle, outward, (first, first))
        for k in range(2 * middle - layers, -1, -1):
            below = body(k, below)
        return below, above

    def sweep(keep):
        def stencil_body(k, carry):
            stencil(k, keep)
            return carry

        bed = tuple(2.0 * friction for _ in range(2))
        lower, upper = (zero, bed, (zero, zero)), (zero, (zero, zero), (zero, zero))
        if plan.unrolled:
            stencil(0, keep)
            stencil(layers - 1, keep)
            for step in range(layers - 1 - middle):
                stencil(step + 1, keep)
                if layers - 2 - step > step + 1:
                    stencil(layers - 2 - step, keep)
                lower, upper = fronts(step, (lower, upper))
        else:
            repeat(plan, layers, stencil_body)
            lower, upper = repeat(plan, layers - 1 - middle, fronts, (lower, upper))
        for k in range(layers - 1 - middle, middle):
            lower = lower_step(k, lower)
        centre_value = []
        for c in range(2):
            pivot = side[c, middle] + lower[1][c] + upper[1][c]
            guess = pl.reciprocal(pivot, approx=True)
            inv = guess * (2.0 - pivot * guess)
            inverse[c, middle] = inv
            total = rhs[c, middle] + (lower[0] * lower[2][c] + upper[0] * upper[2][c])
            centre_value.append(jnp.where(ice, total * inv, 0.0))
            field[c, middle] = centre_value[c]

        def solved(k, nearer):
            current = tuple(jnp.where(ice, rhs[c, k] + ratio[c, k] * nearer[c], 0.0) for c in range(2))
            for c in range(2):
                field[c, k] = current[c]
            return current

        return spread(tuple(centre_value), solved)

    sweep(False)
    base, top = sweep(True)

    centre = jnp.logical_and(lane % width >= plan.halo, lane % width < plan.halo + plan.cols)

    def send(k, carry):
        both = jnp.where(centre, field[0, k], lane_roll(field[1, k], plan.cols))
        out_ref[pl.ds((k // here) * plan.out_rows + k % here, size, stride=plan.layer_size * plan.out_rows), :] = both
        return carry

    repeat(plan, layers, send)

    mismatch = [jnp.where(ice, top[c] - observed[c], 0.0) for c in range(2)]
    source = [(2.0 * layers) * mismatch[c] for c in range(2)]

    def side_sum(k, value):
        east, west, north, south = (faces[n, k] for n in range(4))
        u_east, u_west = x_pair(value[0], 0.0)
        v_east, v_west = x_pair(value[1], 0.0)
        u_north, u_south = y_pair(value[0])
        v_north, v_south = y_pair(value[1])
        first = 4.0 * (east * u_east + west * u_west) + (north * u_north + south * u_south)
        second = (east * v_east + west * v_west) + 4.0 * (north * v_north + south * v_south)
        return first, second

    carried = tuple(source[c] * inverse[c, layers - 1] for c in range(2))
    for c in range(2):
        rhs[c, layers - 1] = carried[c]

    def first_inward(step, carried):
        k = layers - 2 - step
        out = tuple(coupling_of(k) * carried[c] * inverse[c, k] for c in range(2))
        for c in range(2):
            rhs[c, k] = out[c]
        return out

    carried = repeat(plan, layers - 2 - middle, first_inward, carried)
    first_middle = tuple(coupling_of(middle) * carried[c] * inverse[c, middle] for c in range(2))

    def first_outward(step, carry):
        below, above = carry
        low, high = middle - 1 - step, middle + 1 + step
        below = tuple(ratio[c, low] * below[c] for c in range(2))
        above = tuple(rhs[c, high] + ratio[c, high] * above[c] for c in range(2))
        for k, value in ((low, below), (high, above)):
            total = side_sum(k, value)
            for c in range(2):
                rhs[c, k] = total[c] * inverse[c, k]
        return below, above

    middle_sum = side_sum(middle, first_middle)
    below, above = repeat(plan, layers - 1 - middle, first_outward, (first_middle, first_middle))
    for k in range(2 * middle - layers, -1, -1):
        below = tuple(ratio[c, k] * below[c] for c in range(2))
        total = side_sum(k, below)
        for c in range(2):
            rhs[c, k] = total[c] * inverse[c, k]
    for c in range(2):
        rhs[c, layers - 1] = rhs[c, layers - 1] + source[c] * inverse[c, layers - 1]

    def second_inward(step, carry):
        below, above = carry
        low, high = step + 1, layers - 2 - step
        below = tuple(rhs[c, low] + (coupling_of(low - 1) * inverse[c, low]) * below[c] for c in range(2))
        above = tuple(rhs[c, high] + (coupling_of(high) * inverse[c, high]) * above[c] for c in range(2))
        for c in range(2):
            rhs[c, low] = below[c]
        return below, above

    below, above = repeat(
        plan,
        layers - 2 - middle,
        second_inward,
        (tuple(rhs[c, 0] for c in range(2)), tuple(rhs[c, layers - 1] for c in range(2))),
    )
    for k in range(layers - 1 - middle, middle):
        below = tuple(rhs[c, k] + (coupling_of(k - 1) * inverse[c, k]) * below[c] for c in range(2))
        for c in range(2):
            rhs[c, k] = below[c]
    adjoint = tuple(
        (middle_sum[c] + (coupling_of(middle - 1) * below[c] + coupling_of(middle) * above[c])) * inverse[c, middle]
        for c in range(2)
    )

    def second_outward(step, nearer):
        k = middle - 1 - step
        return tuple(rhs[c, k] + ratio[c, k] * nearer[c] for c in range(2))

    adjoint = repeat(plan, middle, second_outward, adjoint)
    adjoint = [jnp.where(ice, adjoint[c], 0.0) for c in range(2)]
    gradient = -friction * (base[0] * adjoint[0] + base[1] * adjoint[1])

    def partial_sum(value):
        line = jnp.sum(jnp.where(centre, value, 0.0), axis=0, keepdims=True)
        folded = line
        for r in range(1, rows):
            folded = folded + lane_roll(line, r * width)
        return jnp.broadcast_to(lane_roll(folded, plan.cols), shape)

    misfit_line = partial_sum(mismatch[0] * mismatch[0] + mismatch[1] * mismatch[1])
    grad_line = partial_sum(gradient * gradient)
    in_first = jnp.logical_and(lane >= plan.halo + plan.cols, lane < plan.halo + 2 * plan.cols)
    last_row = jnp.where(centre, gradient, jnp.where(in_first, misfit_line, grad_line))
    for part in range(plan.layer_size):
        out_ref[pl.ds(part * plan.out_rows + here, size, stride=plan.layer_size * plan.out_rows), :] = last_row


def unpack_kernel(
    plan, in_ref, log_ref, vel_hbm, friction_hbm, misfit_hbm,
    vel_ref, friction_ref, misfit_ref, grad_ref, leave,
):
    here, width, cols, rows = plan.layers_here, plan.width, plan.cols, plan.rows
    local_chunks = plan.local_cols // LANES

    total = jnp.sum(
        in_ref[pl.ds(here, plan.devices, stride=plan.out_rows), :], axis=0, keepdims=True
    )
    line_lane = lax.broadcasted_iota(jnp.int32, (1, LANES), 1)

    def summed(first):
        ahead = (line_lane + (LANES - first % LANES)) % LANES
        return jnp.sum(jnp.where(ahead < cols, total, 0.0), axis=1, keepdims=True)

    misfit_sum = summed(plan.halo + cols)
    grad_sum = summed(plan.halo + cols + width)
    misfit_ref[...] = 0.5 * misfit_sum / plan.column_count
    scale = step_size / jnp.sqrt(grad_sum / plan.column_count + 1e-06)

    lane = lax.broadcasted_iota(jnp.int32, (plan.out_rows, LANES), 1)
    def chunk(c, i):
        at = i * plan.per_chunk * plan.out_rows
        if not isinstance(at, int):
            at = pl.multiple_of(at, 8)
        turned = [
            lane_roll(in_ref[pl.ds(at + t * plan.out_rows, plan.out_rows), :], t * cols)
            for t in range(plan.per_chunk)
        ]
        for r in range(rows):
            start = r * width + plan.halo + c * cols
            ahead = (lane + (LANES - start % LANES)) % LANES
            row = turned[0]
            for t in range(1, plan.per_chunk):
                row = jnp.where(ahead >= t * cols, turned[t], row)
            row = lane_roll(row, -start)
            vel_ref[c, pl.ds(i * rows + r, here, stride=plan.chunks * rows), :] = row[:here]
            if c == 0:
                owner, step = i // local_chunks, i % local_chunks
                grad_ref[owner, pl.ds(step * rows + r, 1), :] = row[here : here + 1]

    out = [pltpu.make_async_copy(vel_ref.at[c], vel_hbm.at[c], leave.at[c]) for c in range(2)]
    out.append(pltpu.make_async_copy(friction_ref, friction_hbm, leave.at[2]))
    out.append(pltpu.make_async_copy(misfit_ref, misfit_hbm, leave.at[3]))
    out[3].start()
    for c in range(2):

        def chunk_body(i, carry):
            chunk(c, i)
            return carry

        repeat(plan, plan.chunks, chunk_body)
        out[c].start()
        if c == 0:
            friction_ref[...] = log_ref[...] - grad_ref[lax.axis_index("layer")] * scale
            out[2].start()
    for copy in out:
        copy.wait()


def as_lines(x):
    chunked = x.reshape(x.shape[:-1] + (x.shape[-1] // LANES, LANES))
    return jnp.swapaxes(chunked, -3, -2).reshape(-1, LANES)


def from_lines(lines, shape):
    chunked = lines.reshape(shape[:-2] + (shape[-1] // LANES, shape[-2], LANES))
    return jnp.swapaxes(chunked, -3, -2).reshape(shape)


def on_device(mesh_shape, velocity_init, driving, observed, log_friction, ice_mask):
    plan = Plan(mesh_shape, velocity_init.shape)
    vmem = pl.BlockSpec(memory_space=pltpu.VMEM)
    hbm = pl.BlockSpec(memory_space=pltpu.HBM)
    f32 = jnp.float32
    limit = pltpu.CompilerParams(vmem_limit_bytes=(16 if plan.unrolled else 40) * MIB)
    inputs = [as_lines(x) for x in (velocity_init, driving, observed, log_friction, ice_mask)]

    def exchange(blocks, unit):
        shaped = blocks.reshape(blocks.shape[0] // unit, unit, LANES)
        return lax.all_to_all(shaped, ("map", "layer"), split_axis=0, concat_axis=0, tiled=True).reshape(blocks.shape)

    packed = pl.pallas_call(
        functools.partial(pack_kernel, plan),
        out_shape=jax.ShapeDtypeStruct((plan.devices * plan.in_rows, LANES), f32),
        in_specs=[hbm] * 5,
        out_specs=vmem,
        scratch_shapes=[pltpu.VMEM(x.shape, x.dtype) for x in inputs]
        + [
            pltpu.SemaphoreType.DMA((5,)),
        ],
        compiler_params=limit,
        name="pack",
    )(*(pltpu.with_memory_space_constraint(x, pltpu.HBM) for x in inputs))

    windows = exchange(packed, 2)

    plane = (plan.layers, plan.map_size, LANES)
    solved = pl.pallas_call(
        functools.partial(solve_kernel, plan),
        out_shape=jax.ShapeDtypeStruct((plan.devices * plan.out_rows, LANES), f32),
        in_specs=[vmem],
        out_specs=vmem,
        scratch_shapes=[
            pltpu.VMEM((2,) + plane, f32),
            pltpu.VMEM(plane, f32),
            pltpu.VMEM((2,) + plane, f32),
            pltpu.VMEM((2,) + plane, f32),
            pltpu.VMEM((4,) + plane, f32),
            pltpu.VMEM((2,) + plane, f32),
            pltpu.VMEM((2,) + plane, f32),
        ],
        compiler_params=limit,
        name="solve",
    )(windows)

    back = exchange(solved, 1)

    vel_lines, log_lines = inputs[0].reshape(2, -1, LANES), inputs[3]
    velocity, friction_new, misfit = pl.pallas_call(
        functools.partial(unpack_kernel, plan),
        out_shape=(
            jax.ShapeDtypeStruct(vel_lines.shape, f32),
            jax.ShapeDtypeStruct(log_lines.shape, f32),
            jax.ShapeDtypeStruct((1, 1), f32),
        ),
        in_specs=[vmem] * 2,
        out_specs=(hbm, hbm, hbm),
        scratch_shapes=[
            pltpu.VMEM(vel_lines.shape, f32),
            pltpu.VMEM(log_lines.shape, f32),
            pltpu.VMEM((1, 1), f32),
            pltpu.VMEM((plan.layer_size,) + log_lines.shape, f32),
            pltpu.SemaphoreType.DMA((4,)),
        ],
        compiler_params=limit,
        name="unpack",
    )(back, log_lines)
    return (
        from_lines(velocity, velocity_init.shape),
        from_lines(friction_new, log_friction.shape),
        misfit.reshape(()),
    )


def solution(mesh):
    in_specs = (
        P(None, "layer", "map", None),
        P(None, "map", "layer"),
        P(None, "map", "layer"),
        P("map", "layer"),
        P("map", "layer"),
    )
    out_specs = (P(None, "layer", "map", None), P("map", "layer"), P())
    return jax.shard_map(
        functools.partial(on_device, dict(mesh.shape)),
        mesh=mesh,
        in_specs=in_specs,
        out_specs=out_specs,
        check_vma=False,
    )
```

```python
import functools
import math

import jax
import jax.numpy as jnp
from jax import lax
from jax.experimental import pallas as pl
from jax.experimental.pallas import tpu as pltpu
from jax.sharding import PartitionSpec as P

strain_floor = 0.1
step_size = 0.5
LANES = 128
REACH = 5
MIB = 1 << 20
VELOCITY_COPIES = 4


class Plan:
    def __init__(self, mesh_shape, velocity_shape):
        self.map_size = mesh_shape["map"]
        self.layer_size = mesh_shape["layer"]
        self.devices = self.map_size * self.layer_size
        self.layers_here = velocity_shape[1]
        self.rows = velocity_shape[2]
        self.ny = velocity_shape[3]
        self.layers = self.layers_here * self.layer_size
        self.cols = self.ny // self.devices
        self.width = LANES // self.rows
        self.halo = (self.width - self.cols) // 2
        self.low = self.halo - REACH
        self.wide = self.cols + 2 * REACH
        self.half = self.wide // 2
        self.gap = self.low + self.wide
        self.local_cols = self.ny // self.layer_size
        self.per_chunk = LANES // self.cols
        self.chunks = self.ny // LANES
        self.column_count = self.rows * self.map_size * self.ny
        self.vel_rows = 2 * self.layers_here
        self.in_rows = self.vel_rows + self.rows
        self.out_rows = self.layers_here + 1
        self.unrolled = self.map_size <= 8
        assert self.width * self.rows == LANES and self.cols * self.per_chunk == LANES
        assert self.low >= 0 and self.wide % 2 == 0 and self.width - self.wide >= self.half
        assert 2 * self.cols <= self.width and self.local_cols % LANES == 0
        assert self.vel_rows == 8 and self.rows == 2 and 3 * self.wide <= LANES


def repeat(plan, count, body, carry=0):
    if plan.unrolled:
        for index in range(count):
            carry = body(index, carry)
        return carry
    return lax.fori_loop(0, count, body, carry)


def lane_roll(value, shift):
    shift = shift % LANES
    return value if shift == 0 else pltpu.roll(value, shift, 1)


def pack_kernel(
    plan, vel_hbm, driving_hbm, observed_hbm, log_hbm, mask_hbm, out_ref,
    vel_ref, driving_ref, observed_ref, log_ref, mask_ref, arrival,
):
    width, rows, wide, half = plan.width, plan.rows, plan.wide, plan.half
    piece = vel_ref.shape[0] // VELOCITY_COPIES
    spans = [pl.ds(n * piece, piece) for n in range(VELOCITY_COPIES)]
    pairs = [(vel_hbm.at[span, :], vel_ref.at[span, :]) for span in spans] + [
        (driving_hbm, driving_ref),
        (observed_hbm, observed_ref),
        (log_hbm, log_ref),
        (mask_hbm, mask_ref),
    ]
    copies = [pltpu.make_async_copy(pair[0], pair[1], arrival.at[n]) for n, pair in enumerate(pairs)]
    for copy in copies:
        copy.start()
    shape = (plan.vel_rows, LANES)
    lane = lax.broadcasted_iota(jnp.int32, shape, 1)
    sub = lax.broadcasted_iota(jnp.int32, shape, 0)
    in_gap = jnp.logical_not(jnp.logical_and(lane % width >= plan.low, lane % width < plan.gap))
    no_line = jnp.zeros((rows, LANES), jnp.float32)

    def slide(part, start, length, place):
        step, offset = start // LANES, start % LANES
        value = part(step)
        if offset + length > LANES:
            after = part(step + 1)
            value = jnp.where(lax.broadcasted_iota(jnp.int32, value.shape, 1) >= offset, value, after)
        return lane_roll(value, place - offset)

    for copy in copies[:VELOCITY_COPIES]:
        copy.wait()

    def chunk_windows(i, carry):
        def velocity(r):
            def part(step):
                chunk = i + step
                if isinstance(chunk, int) and not 0 <= chunk < plan.chunks:
                    return jnp.zeros(shape, jnp.float32)
                at = chunk if isinstance(chunk, int) else jnp.clip(chunk, 0, plan.chunks - 1)
                value = vel_ref[pl.ds(at * rows + r, plan.vel_rows, stride=plan.chunks * rows), :]
                if isinstance(chunk, int):
                    return value
                return jnp.where(jnp.logical_and(chunk >= 0, chunk < plan.chunks), value, 0.0)

            return part

        for t in range(plan.per_chunk):
            block = None
            for r in range(rows):
                value = slide(velocity(r), plan.cols * t - plan.halo, width, r * width)
                block = value if block is None else jnp.where(lane >= r * width, value, block)
            at = i * plan.per_chunk * plan.in_rows
            if not isinstance(at, int):
                at = pl.multiple_of(at, 8)
            at = at + t * plan.in_rows
            out_ref[pl.ds(at, plan.vel_rows), :] = jnp.where(in_gap, 0.0, block)
            out_ref[pl.ds(at + plan.vel_rows, rows), :] = no_line
        return carry

    repeat(plan, plan.chunks, chunk_windows)
    for copy in copies[VELOCITY_COPIES:]:
        copy.wait()

    place = lax.axis_index("layer")
    local_chunks = plan.local_cols // LANES

    def line_part(ref, row):
        def part(step):
            if not 0 <= step < local_chunks:
                return no_line
            return ref[row + step * rows : row + (step + 1) * rows, :]

        return part

    def gap_part(r):
        def part(step):
            if not 0 <= step < local_chunks:
                return jnp.zeros(shape, jnp.float32)
            at = step * rows + r
            skip = local_chunks * rows
            first = jnp.broadcast_to(observed_ref[at : at + 1, :], shape)
            second = jnp.broadcast_to(observed_ref[skip + at : skip + at + 1, :], shape)
            third = jnp.broadcast_to(mask_ref[at : at + 1, :], shape).astype(jnp.float32)
            return jnp.where(sub < 2, first, jnp.where(sub < 4, second, third))

        return part

    gap_parts = [[gap_part(r)(step) for step in range(-1, local_chunks + 1)] for r in range(rows)]
    own = plan.local_cols // plan.cols
    spill = -(-REACH // plan.cols)

    def column_block(q):
        start = q * plan.cols - REACH
        line = None
        for n, part in enumerate(
            (line_part(driving_ref, 0), line_part(driving_ref, local_chunks * rows), line_part(log_ref, 0))
        ):
            value = slide(part, start, wide, n * wide)
            lanes = lax.broadcasted_iota(jnp.int32, value.shape, 1)
            line = value if line is None else jnp.where(lanes >= n * wide, value, line)
        block = None
        for r in range(rows):
            halves = [
                slide(lambda step: gap_parts[r][step + 1], start + h * half, half, (r * width + plan.gap) % LANES)
                for h in range(2)
            ]
            value = jnp.where(sub % 2 == 0, halves[0], halves[1])
            ahead = (lane + (LANES - plan.gap)) % LANES
            block = value if block is None else jnp.where(ahead >= r * width, value, block)
        at = pl.multiple_of(place * (own * plan.in_rows), 8) + q * plan.in_rows
        here = pl.ds(at, plan.vel_rows)
        out_ref[here, :] = jnp.where(in_gap, block, out_ref[here, :])
        out_ref[pl.ds(at + plan.vel_rows, rows), :] = line

    for q in range(own):
        column_block(q)

    @pl.when(place > 0)
    def _():
        for q in range(-spill, 0):
            column_block(q)

    @pl.when(place < plan.layer_size - 1)
    def _():
        for q in range(own, own + spill):
            column_block(q)


def solve_kernel(plan, in_ref, out_ref, field, eta_ref, side, rhs, faces, ratio, inverse):
    size, width, rows = plan.map_size, plan.width, plan.rows
    layers, here = plan.layers, plan.layers_here
    shape = (size, LANES)
    lane = lax.broadcasted_iota(jnp.int32, shape, 1)
    sub = lax.broadcasted_iota(jnp.int32, shape, 0)
    last_group = lane >= LANES - width
    first_group = lane < width
    x_end = jnp.logical_and(last_group, sub == size - 1)
    x_start = jnp.logical_and(first_group, sub == 0)

    def arrived(part, row):
        return in_ref[pl.ds(part * plan.in_rows + row, size, stride=plan.layer_size * plan.in_rows), :]

    def over_parts(row):
        total = arrived(0, row)
        for part in range(1, plan.layer_size):
            total = total + arrived(part, row)
        return total

    def from_gap(index):
        shift = plan.low - plan.gap
        left, right = over_parts(2 * index), over_parts(2 * index + 1)
        return jnp.where(lane % width < plan.low + plan.half, lane_roll(left, shift), lane_roll(right, shift + plan.half))

    def from_line(index):
        plane = lane_roll(lines[0], plan.low - index * plan.wide)
        for r in range(1, rows):
            plane = jnp.where(lane >= r * width, lane_roll(lines[r], r * width + plan.low - index * plan.wide), plane)
        return plane

    def x_pair(value, edge):
        after = lane_roll(value, -width)
        before = after if 2 * width == LANES else lane_roll(value, width)
        after = jnp.where(last_group, pltpu.roll(after, size - 1, 0), after)
        before = jnp.where(first_group, pltpu.roll(before, 1, 0), before)
        return jnp.where(x_end, edge, after), jnp.where(x_start, edge, before)

    def y_pair(value):
        return lane_roll(value, -1), lane_roll(value, 1)

    def viscosity(rate):
        return jnp.exp2(jnp.log(strain_floor + rate) * (-1.0 / (3.0 * math.log(2.0))))

    for part in range(plan.layer_size):
        for c in range(2):
            for k in range(here):
                field[c, part * here + k] = arrived(part, c * here + k)
    lines = [over_parts(plan.vel_rows + r) for r in range(rows)]
    reached = jnp.logical_and(lane % width >= plan.low, lane % width < plan.gap)
    driving = [2.0 * from_line(c) for c in range(2)]
    observed = [from_gap(c) for c in range(2)]
    mask = jnp.where(reached, from_gap(2), 0.0)
    ice = mask != 0.0
    friction = jnp.where(mask == 1.0, jnp.exp(from_line(2)), 0.0)

    def stencil(k, keep):
        u, v = field[0, k], field[1, k]
        u_east, u_west = x_pair(u, 0.0)
        v_east, v_west = x_pair(v, 0.0)
        u_north, u_south = y_pair(u)
        v_north, v_south = y_pair(v)
        stretch_x = u_east - u_west
        stretch_y = v_north - v_south
        shear = 0.5 * ((u_north - u_south) + (v_east - v_west))
        rate = 0.25 * (stretch_x * (stretch_x + stretch_y) + stretch_y * stretch_y + shear * shear)
        half_v = 0.5 * v
        eta = viscosity(rate)
        eta_edge = viscosity(0.25 * (u * u + half_v * half_v))
        eta_east, eta_west = x_pair(eta, eta_edge)
        eta_north, eta_south = y_pair(eta)
        east, west = eta + eta_east, eta + eta_west
        north, south = eta + eta_north, eta + eta_south
        along_x, along_y = east + west, north + south
        eta_ref[k] = eta
        side[0, k] = 4.0 * along_x + along_y
        side[1, k] = along_x + 4.0 * along_y
        rhs[0, k] = driving[0] + (4.0 * (east * u_east + west * u_west) + (north * u_north + south * u_south))
        rhs[1, k] = driving[1] + ((east * v_east + west * v_west) + 4.0 * (north * v_north + south * v_south))
        if keep:
            faces[0, k] = east
            faces[1, k] = west
            faces[2, k] = north
            faces[3, k] = south

    def coupling_of(k):
        return (2.0 * layers * layers) * (eta_ref[k] + eta_ref[k + 1])

    middle = layers // 2
    zero = jnp.zeros(shape, jnp.float32)

    def eliminate(k, coupling, carry):
        before, passed, value = carry
        new_passed, new_value = [], []
        for c in range(2):
            rest = side[c, k] + passed[c]
            pivot = coupling + rest
            guess = pl.reciprocal(pivot, approx=True)
            correct = 2.0 - pivot * guess
            new_passed.append((coupling * rest * guess) * correct)
            inv = guess * correct
            inverse[c, k] = inv
            ratio[c, k] = coupling * inv
            out = (rhs[c, k] + before * value[c]) * inv
            rhs[c, k] = out
            new_value.append(out)
        return coupling, tuple(new_passed), tuple(new_value)

    def lower_step(k, carry):
        return eliminate(k, coupling_of(k), carry)

    def upper_step(k, carry):
        return eliminate(k, coupling_of(k - 1), carry)

    def fronts(step, carry):
        lower, upper = carry
        return lower_step(step, lower), upper_step(layers - 1 - step, upper)

    def spread(first, body):
        def outward(step, carry):
            below, above = carry
            return body(middle - 1 - step, below), body(middle + 1 + step, above)

        below, above = repeat(plan, layers - 1 - middle, outward, (first, first))
        for k in range(2 * middle - layers, -1, -1):
            below = body(k, below)
        return below, above

    def sweep(keep):
        def stencil_body(k, carry):
            stencil(k, keep)
            return carry

        bed = tuple(2.0 * friction for _ in range(2))
        lower, upper = (zero, bed, (zero, zero)), (zero, (zero, zero), (zero, zero))
        if plan.unrolled:
            stencil(0, keep)
            stencil(layers - 1, keep)
            for step in range(layers - 1 - middle):
                stencil(step + 1, keep)
                if layers - 2 - step > step + 1:
                    stencil(layers - 2 - step, keep)
                lower, upper = fronts(step, (lower, upper))
        else:
            repeat(plan, layers, stencil_body)
            lower, upper = repeat(plan, layers - 1 - middle, fronts, (lower, upper))
        for k in range(layers - 1 - middle, middle):
            lower = lower_step(k, lower)
        centre_value = []
        for c in range(2):
            pivot = side[c, middle] + lower[1][c] + upper[1][c]
            guess = pl.reciprocal(pivot, approx=True)
            inv = guess * (2.0 - pivot * guess)
            inverse[c, middle] = inv
            total = rhs[c, middle] + (lower[0] * lower[2][c] + upper[0] * upper[2][c])
            centre_value.append(jnp.where(ice, total * inv, 0.0))
            field[c, middle] = centre_value[c]

        def solved(k, nearer):
            current = tuple(jnp.where(ice, rhs[c, k] + ratio[c, k] * nearer[c], 0.0) for c in range(2))
            for c in range(2):
                field[c, k] = current[c]
            return current

        return spread(tuple(centre_value), solved)

    sweep(False)
    base, top = sweep(True)

    centre = jnp.logical_and(lane % width >= plan.halo, lane % width < plan.halo + plan.cols)

    def send(k, carry):
        both = jnp.where(centre, field[0, k], lane_roll(field[1, k], plan.cols))
        out_ref[pl.ds((k // here) * plan.out_rows + k % here, size, stride=plan.layer_size * plan.out_rows), :] = both
        return carry

    repeat(plan, layers, send)

    mismatch = [jnp.where(ice, top[c] - observed[c], 0.0) for c in range(2)]
    source = [(2.0 * layers) * mismatch[c] for c in range(2)]

    def side_sum(k, value):
        east, west, north, south = (faces[n, k] for n in range(4))
        u_east, u_west = x_pair(value[0], 0.0)
        v_east, v_west = x_pair(value[1], 0.0)
        u_north, u_south = y_pair(value[0])
        v_north, v_south = y_pair(value[1])
        first = 4.0 * (east * u_east + west * u_west) + (north * u_north + south * u_south)
        second = (east * v_east + west * v_west) + 4.0 * (north * v_north + south * v_south)
        return first, second

    carried = tuple(source[c] * inverse[c, layers - 1] for c in range(2))
    for c in range(2):
        rhs[c, layers - 1] = carried[c]

    def first_inward(step, carried):
        k = layers - 2 - step
        out = tuple(coupling_of(k) * carried[c] * inverse[c, k] for c in range(2))
        for c in range(2):
            rhs[c, k] = out[c]
        return out

    carried = repeat(plan, layers - 2 - middle, first_inward, carried)
    first_middle = tuple(coupling_of(middle) * carried[c] * inverse[c, middle] for c in range(2))

    def first_outward(step, carry):
        below, above = carry
        low, high = middle - 1 - step, middle + 1 + step
        below = tuple(ratio[c, low] * below[c] for c in range(2))
        above = tuple(rhs[c, high] + ratio[c, high] * above[c] for c in range(2))
        for k, value in ((low, below), (high, above)):
            total = side_sum(k, value)
            for c in range(2):
                rhs[c, k] = total[c] * inverse[c, k]
        return below, above

    middle_sum = side_sum(middle, first_middle)
    below, above = repeat(plan, layers - 1 - middle, first_outward, (first_middle, first_middle))
    for k in range(2 * middle - layers, -1, -1):
        below = tuple(ratio[c, k] * below[c] for c in range(2))
        total = side_sum(k, below)
        for c in range(2):
            rhs[c, k] = total[c] * inverse[c, k]
    for c in range(2):
        rhs[c, layers - 1] = rhs[c, layers - 1] + source[c] * inverse[c, layers - 1]

    def second_inward(step, carry):
        below, above = carry
        low, high = step + 1, layers - 2 - step
        below = tuple(rhs[c, low] + (coupling_of(low - 1) * inverse[c, low]) * below[c] for c in range(2))
        above = tuple(rhs[c, high] + (coupling_of(high) * inverse[c, high]) * above[c] for c in range(2))
        for c in range(2):
            rhs[c, low] = below[c]
        return below, above

    below, above = repeat(
        plan,
        layers - 2 - middle,
        second_inward,
        (tuple(rhs[c, 0] for c in range(2)), tuple(rhs[c, layers - 1] for c in range(2))),
    )
    for k in range(layers - 1 - middle, middle):
        below = tuple(rhs[c, k] + (coupling_of(k - 1) * inverse[c, k]) * below[c] for c in range(2))
        for c in range(2):
            rhs[c, k] = below[c]
    adjoint = tuple(
        (middle_sum[c] + (coupling_of(middle - 1) * below[c] + coupling_of(middle) * above[c])) * inverse[c, middle]
        for c in range(2)
    )

    def second_outward(step, nearer):
        k = middle - 1 - step
        return tuple(rhs[c, k] + ratio[c, k] * nearer[c] for c in range(2))

    adjoint = repeat(plan, middle, second_outward, adjoint)
    adjoint = [jnp.where(ice, adjoint[c], 0.0) for c in range(2)]
    gradient = -friction * (base[0] * adjoint[0] + base[1] * adjoint[1])

    def partial_sum(value):
        line = jnp.sum(jnp.where(centre, value, 0.0), axis=0, keepdims=True)
        folded = line
        for r in range(1, rows):
            folded = folded + lane_roll(line, r * width)
        return jnp.broadcast_to(lane_roll(folded, plan.cols), shape)

    misfit_line = partial_sum(mismatch[0] * mismatch[0] + mismatch[1] * mismatch[1])
    grad_line = partial_sum(gradient * gradient)
    in_first = jnp.logical_and(lane >= plan.halo + plan.cols, lane < plan.halo + 2 * plan.cols)
    last_row = jnp.where(centre, gradient, jnp.where(in_first, misfit_line, grad_line))
    for part in range(plan.layer_size):
        out_ref[pl.ds(part * plan.out_rows + here, size, stride=plan.layer_size * plan.out_rows), :] = last_row


def unpack_kernel(
    plan, in_ref, log_ref, vel_hbm, friction_hbm, misfit_hbm,
    vel_ref, friction_ref, misfit_ref, grad_ref, leave,
):
    here, width, cols, rows = plan.layers_here, plan.width, plan.cols, plan.rows
    local_chunks = plan.local_cols // LANES

    total = jnp.sum(
        in_ref[pl.ds(here, plan.devices, stride=plan.out_rows), :], axis=0, keepdims=True
    )
    line_lane = lax.broadcasted_iota(jnp.int32, (1, LANES), 1)

    def summed(first):
        ahead = (line_lane + (LANES - first % LANES)) % LANES
        return jnp.sum(jnp.where(ahead < cols, total, 0.0), axis=1, keepdims=True)

    misfit_sum = summed(plan.halo + cols)
    grad_sum = summed(plan.halo + cols + width)
    scale = step_size / jnp.sqrt(grad_sum / plan.column_count + 1e-06)

    lane = lax.broadcasted_iota(jnp.int32, (plan.out_rows, LANES), 1)
    def chunk(c, i):
        at = i * plan.per_chunk * plan.out_rows
        if not isinstance(at, int):
            at = pl.multiple_of(at, 8)
        turned = [
            lane_roll(in_ref[pl.ds(at + t * plan.out_rows, plan.out_rows), :], t * cols)
            for t in range(plan.per_chunk)
        ]
        for r in range(rows):
            start = r * width + plan.halo + c * cols
            ahead = (lane + (LANES - start % LANES)) % LANES
            row = turned[0]
            for t in range(1, plan.per_chunk):
                row = jnp.where(ahead >= t * cols, turned[t], row)
            row = lane_roll(row, -start)
            vel_ref[c, pl.ds(i * rows + r, here, stride=plan.chunks * rows), :] = row[:here]
            if c == 0:
                owner, step = i // local_chunks, i % local_chunks
                grad_ref[owner, pl.ds(step * rows + r, 1), :] = row[here : here + 1]

    out = [pltpu.make_async_copy(vel_ref.at[c], vel_hbm.at[c], leave.at[c]) for c in range(2)]
    out.append(pltpu.make_async_copy(friction_ref, friction_hbm, leave.at[2]))
    out.append(pltpu.make_async_copy(misfit_ref, misfit_hbm, leave.at[3]))
    for c in range(2):

        def chunk_body(i, carry):
            chunk(c, i)
            return carry

        repeat(plan, plan.chunks, chunk_body)
        out[c].start()
    friction_ref[...] = log_ref[...] - grad_ref[lax.axis_index("layer")] * scale
    out[2].start()
    misfit_ref[...] = 0.5 * misfit_sum / plan.column_count
    out[3].start()
    for copy in out:
        copy.wait()


def as_lines(x):
    chunked = x.reshape(x.shape[:-1] + (x.shape[-1] // LANES, LANES))
    return jnp.swapaxes(chunked, -3, -2).reshape(-1, LANES)


def from_lines(lines, shape):
    chunked = lines.reshape(shape[:-2] + (shape[-1] // LANES, shape[-2], LANES))
    return jnp.swapaxes(chunked, -3, -2).reshape(shape)


def on_device(mesh_shape, velocity_init, driving, observed, log_friction, ice_mask):
    plan = Plan(mesh_shape, velocity_init.shape)
    vmem = pl.BlockSpec(memory_space=pltpu.VMEM)
    hbm = pl.BlockSpec(memory_space=pltpu.HBM)
    f32 = jnp.float32
    limit = pltpu.CompilerParams(vmem_limit_bytes=(16 if plan.unrolled else 40) * MIB)
    inputs = [as_lines(x) for x in (velocity_init, driving, observed, log_friction, ice_mask)]

    def exchange(blocks, unit):
        shaped = blocks.reshape(blocks.shape[0] // unit, unit, LANES)
        return lax.all_to_all(shaped, ("map", "layer"), split_axis=0, concat_axis=0, tiled=True).reshape(blocks.shape)

    packed = pl.pallas_call(
        functools.partial(pack_kernel, plan),
        out_shape=jax.ShapeDtypeStruct((plan.devices * plan.in_rows, LANES), f32),
        in_specs=[hbm] * 5,
        out_specs=vmem,
        scratch_shapes=[pltpu.VMEM(x.shape, x.dtype) for x in inputs]
        + [
            pltpu.SemaphoreType.DMA((VELOCITY_COPIES + 4,)),
        ],
        compiler_params=limit,
        name="pack",
    )(*(pltpu.with_memory_space_constraint(x, pltpu.HBM) for x in inputs))

    windows = exchange(packed, 2)

    plane = (plan.layers, plan.map_size, LANES)
    solved = pl.pallas_call(
        functools.partial(solve_kernel, plan),
        out_shape=jax.ShapeDtypeStruct((plan.devices * plan.out_rows, LANES), f32),
        in_specs=[vmem],
        out_specs=vmem,
        scratch_shapes=[
            pltpu.VMEM((2,) + plane, f32),
            pltpu.VMEM(plane, f32),
            pltpu.VMEM((2,) + plane, f32),
            pltpu.VMEM((2,) + plane, f32),
            pltpu.VMEM((4,) + plane, f32),
            pltpu.VMEM((2,) + plane, f32),
            pltpu.VMEM((2,) + plane, f32),
        ],
        compiler_params=limit,
        name="solve",
    )(windows)

    back = exchange(solved, 1)

    vel_lines, log_lines = inputs[0].reshape(2, -1, LANES), inputs[3]
    velocity, friction_new, misfit = pl.pallas_call(
        functools.partial(unpack_kernel, plan),
        out_shape=(
            jax.ShapeDtypeStruct(vel_lines.shape, f32),
            jax.ShapeDtypeStruct(log_lines.shape, f32),
            jax.ShapeDtypeStruct((1, 1), f32),
        ),
        in_specs=[vmem] * 2,
        out_specs=(hbm, hbm, hbm),
        scratch_shapes=[
            pltpu.VMEM(vel_lines.shape, f32),
            pltpu.VMEM(log_lines.shape, f32),
            pltpu.VMEM((1, 1), f32),
            pltpu.VMEM((plan.layer_size,) + log_lines.shape, f32),
            pltpu.SemaphoreType.DMA((4,)),
        ],
        compiler_params=limit,
        name="unpack",
    )(back, log_lines)
    return (
        from_lines(velocity, velocity_init.shape),
        from_lines(friction_new, log_friction.shape),
        misfit.reshape(()),
    )


def solution(mesh):
    in_specs = (
        P(None, "layer", "map", None),
        P(None, "map", "layer"),
        P(None, "map", "layer"),
        P("map", "layer"),
        P("map", "layer"),
    )
    out_specs = (P(None, "layer", "map", None), P("map", "layer"), P())
    return jax.shard_map(
        functools.partial(on_device, dict(mesh.shape)),
        mesh=mesh,
        in_specs=in_specs,
        out_specs=out_specs,
        check_vma=False,
    )
```

```python
import functools
import math

import jax
import jax.numpy as jnp
from jax import lax
from jax.experimental import pallas as pl
from jax.experimental.pallas import tpu as pltpu
from jax.sharding import PartitionSpec as P

strain_floor = 0.1
step_size = 0.5
LANES = 128
REACH = 5
MIB = 1 << 20
VELOCITY_COPIES = 4


class Plan:
    def __init__(self, mesh_shape, velocity_shape):
        self.map_size = mesh_shape["map"]
        self.layer_size = mesh_shape["layer"]
        self.devices = self.map_size * self.layer_size
        self.layers_here = velocity_shape[1]
        self.rows = velocity_shape[2]
        self.ny = velocity_shape[3]
        self.layers = self.layers_here * self.layer_size
        self.cols = self.ny // self.devices
        self.width = LANES // self.rows
        self.halo = (self.width - self.cols) // 2
        self.low = self.halo - REACH
        self.wide = self.cols + 2 * REACH
        self.half = self.wide // 2
        self.gap = self.low + self.wide
        self.local_cols = self.ny // self.layer_size
        self.per_chunk = LANES // self.cols
        self.chunks = self.ny // LANES
        self.column_count = self.rows * self.map_size * self.ny
        self.vel_rows = 2 * self.layers_here
        self.in_rows = self.vel_rows + self.rows
        self.out_rows = self.layers_here + 1
        self.unrolled = self.map_size <= 8
        assert self.width * self.rows == LANES and self.cols * self.per_chunk == LANES
        assert self.low >= 0 and self.wide % 2 == 0 and self.width - self.wide >= self.half
        assert 2 * self.cols <= self.width and self.local_cols % LANES == 0
        assert self.vel_rows == 8 and self.rows == 2 and 3 * self.wide <= LANES


def repeat(plan, count, body, carry=0):
    if plan.unrolled:
        for index in range(count):
            carry = body(index, carry)
        return carry
    return lax.fori_loop(0, count, body, carry)


def lane_roll(value, shift):
    shift = shift % LANES
    return value if shift == 0 else pltpu.roll(value, shift, 1)


def pack_kernel(
    plan, vel_hbm, driving_hbm, observed_hbm, log_hbm, mask_hbm, out_ref,
    vel_ref, driving_ref, observed_ref, log_ref, mask_ref, arrival,
):
    width, rows, wide, half = plan.width, plan.rows, plan.wide, plan.half
    piece = vel_ref.shape[0] // VELOCITY_COPIES
    spans = [pl.ds(n * piece, piece) for n in range(VELOCITY_COPIES)]
    pairs = [(vel_hbm.at[span, :], vel_ref.at[span, :]) for span in spans] + [
        (driving_hbm, driving_ref),
        (observed_hbm, observed_ref),
        (log_hbm, log_ref),
        (mask_hbm, mask_ref),
    ]
    copies = [pltpu.make_async_copy(pair[0], pair[1], arrival.at[n]) for n, pair in enumerate(pairs)]
    for copy in copies:
        copy.start()
    shape = (plan.vel_rows, LANES)
    lane = lax.broadcasted_iota(jnp.int32, shape, 1)
    sub = lax.broadcasted_iota(jnp.int32, shape, 0)
    in_gap = jnp.logical_not(jnp.logical_and(lane % width >= plan.low, lane % width < plan.gap))
    no_line = jnp.zeros((rows, LANES), jnp.float32)

    def slide(part, start, length, place):
        step, offset = start // LANES, start % LANES
        value = part(step)
        if offset + length > LANES:
            after = part(step + 1)
            value = jnp.where(lax.broadcasted_iota(jnp.int32, value.shape, 1) >= offset, value, after)
        return lane_roll(value, place - offset)

    for copy in copies[:VELOCITY_COPIES]:
        copy.wait()

    def chunk_windows(i, carry):
        def velocity(r):
            def part(step):
                chunk = i + step
                if isinstance(chunk, int) and not 0 <= chunk < plan.chunks:
                    return jnp.zeros(shape, jnp.float32)
                at = chunk if isinstance(chunk, int) else jnp.clip(chunk, 0, plan.chunks - 1)
                value = vel_ref[pl.ds(at * rows + r, plan.vel_rows, stride=plan.chunks * rows), :]
                if isinstance(chunk, int):
                    return value
                return jnp.where(jnp.logical_and(chunk >= 0, chunk < plan.chunks), value, 0.0)

            return part

        for t in range(plan.per_chunk):
            block = None
            for r in range(rows):
                value = slide(velocity(r), plan.cols * t - plan.halo, width, r * width)
                block = value if block is None else jnp.where(lane >= r * width, value, block)
            at = i * plan.per_chunk * plan.in_rows
            if not isinstance(at, int):
                at = pl.multiple_of(at, 8)
            at = at + t * plan.in_rows
            out_ref[pl.ds(at, plan.vel_rows), :] = jnp.where(in_gap, 0.0, block)
            out_ref[pl.ds(at + plan.vel_rows, rows), :] = no_line
        return carry

    repeat(plan, plan.chunks, chunk_windows)
    for copy in copies[VELOCITY_COPIES:]:
        copy.wait()

    place = lax.axis_index("layer")
    local_chunks = plan.local_cols // LANES

    def line_part(ref, row):
        def part(step):
            if not 0 <= step < local_chunks:
                return no_line
            return ref[row + step * rows : row + (step + 1) * rows, :]

        return part

    def gap_part(r):
        def part(step):
            if not 0 <= step < local_chunks:
                return jnp.zeros(shape, jnp.float32)
            at = step * rows + r
            skip = local_chunks * rows
            first = jnp.broadcast_to(observed_ref[at : at + 1, :], shape)
            second = jnp.broadcast_to(observed_ref[skip + at : skip + at + 1, :], shape)
            third = jnp.broadcast_to(mask_ref[at : at + 1, :], shape).astype(jnp.float32)
            return jnp.where(sub < 2, first, jnp.where(sub < 4, second, third))

        return part

    gap_parts = [[gap_part(r)(step) for step in range(-1, local_chunks + 1)] for r in range(rows)]
    own = plan.local_cols // plan.cols
    spill = -(-REACH // plan.cols)

    def column_block(q):
        start = q * plan.cols - REACH
        line = None
        for n, part in enumerate(
            (line_part(driving_ref, 0), line_part(driving_ref, local_chunks * rows), line_part(log_ref, 0))
        ):
            value = slide(part, start, wide, n * wide)
            lanes = lax.broadcasted_iota(jnp.int32, value.shape, 1)
            line = value if line is None else jnp.where(lanes >= n * wide, value, line)
        block = None
        for r in range(rows):
            halves = [
                slide(lambda step: gap_parts[r][step + 1], start + h * half, half, (r * width + plan.gap) % LANES)
                for h in range(2)
            ]
            value = jnp.where(sub % 2 == 0, halves[0], halves[1])
            ahead = (lane + (LANES - plan.gap)) % LANES
            block = value if block is None else jnp.where(ahead >= r * width, value, block)
        at = pl.multiple_of(place * (own * plan.in_rows), 8) + q * plan.in_rows
        here = pl.ds(at, plan.vel_rows)
        out_ref[here, :] = jnp.where(in_gap, block, out_ref[here, :])
        out_ref[pl.ds(at + plan.vel_rows, rows), :] = line

    for q in range(own):
        column_block(q)

    @pl.when(place > 0)
    def _():
        for q in range(-spill, 0):
            column_block(q)

    @pl.when(place < plan.layer_size - 1)
    def _():
        for q in range(own, own + spill):
            column_block(q)


def solve_kernel(plan, in_ref, out_ref, field, eta_ref, side, rhs, faces, ratio, inverse):
    size, width, rows = plan.map_size, plan.width, plan.rows
    layers, here = plan.layers, plan.layers_here
    shape = (size, LANES)
    lane = lax.broadcasted_iota(jnp.int32, shape, 1)
    sub = lax.broadcasted_iota(jnp.int32, shape, 0)
    last_group = lane >= LANES - width
    first_group = lane < width
    x_end = jnp.logical_and(last_group, sub == size - 1)
    x_start = jnp.logical_and(first_group, sub == 0)

    def arrived(part, row):
        return in_ref[pl.ds(part * plan.in_rows + row, size, stride=plan.layer_size * plan.in_rows), :]

    def over_parts(row):
        total = arrived(0, row)
        for part in range(1, plan.layer_size):
            total = total + arrived(part, row)
        return total

    def from_gap(index):
        shift = plan.low - plan.gap
        left, right = over_parts(2 * index), over_parts(2 * index + 1)
        return jnp.where(lane % width < plan.low + plan.half, lane_roll(left, shift), lane_roll(right, shift + plan.half))

    def from_line(index):
        plane = lane_roll(lines[0], plan.low - index * plan.wide)
        for r in range(1, rows):
            plane = jnp.where(lane >= r * width, lane_roll(lines[r], r * width + plan.low - index * plan.wide), plane)
        return plane

    def x_pair(value, edge):
        after = lane_roll(value, -width)
        before = after if 2 * width == LANES else lane_roll(value, width)
        after = jnp.where(last_group, pltpu.roll(after, size - 1, 0), after)
        before = jnp.where(first_group, pltpu.roll(before, 1, 0), before)
        return jnp.where(x_end, edge, after), jnp.where(x_start, edge, before)

    def y_pair(value):
        return lane_roll(value, -1), lane_roll(value, 1)

    def viscosity(rate):
        return jnp.exp2(jnp.log(strain_floor + rate) * (-1.0 / (3.0 * math.log(2.0))))

    for part in range(plan.layer_size):
        for c in range(2):
            for k in range(here):
                field[c, part * here + k] = arrived(part, c * here + k)
    lines = [over_parts(plan.vel_rows + r) for r in range(rows)]
    reached = jnp.logical_and(lane % width >= plan.low, lane % width < plan.gap)
    driving = [2.0 * from_line(c) for c in range(2)]
    observed = [from_gap(c) for c in range(2)]
    mask = jnp.where(reached, from_gap(2), 0.0)
    ice = mask != 0.0
    friction = jnp.where(mask == 1.0, jnp.exp(from_line(2)), 0.0)

    def stencil(k, keep):
        u, v = field[0, k], field[1, k]
        u_east, u_west = x_pair(u, 0.0)
        v_east, v_west = x_pair(v, 0.0)
        u_north, u_south = y_pair(u)
        v_north, v_south = y_pair(v)
        stretch_x = u_east - u_west
        stretch_y = v_north - v_south
        shear = 0.5 * ((u_north - u_south) + (v_east - v_west))
        rate = 0.25 * (stretch_x * (stretch_x + stretch_y) + stretch_y * stretch_y + shear * shear)
        half_v = 0.5 * v
        eta = viscosity(rate)
        eta_edge = viscosity(0.25 * (u * u + half_v * half_v))
        eta_east, eta_west = x_pair(eta, eta_edge)
        eta_north, eta_south = y_pair(eta)
        east, west = eta + eta_east, eta + eta_west
        north, south = eta + eta_north, eta + eta_south
        along_x, along_y = east + west, north + south
        eta_ref[k] = eta
        side[0, k] = 4.0 * along_x + along_y
        side[1, k] = along_x + 4.0 * along_y
        rhs[0, k] = driving[0] + (4.0 * (east * u_east + west * u_west) + (north * u_north + south * u_south))
        rhs[1, k] = driving[1] + ((east * v_east + west * v_west) + 4.0 * (north * v_north + south * v_south))
        if keep:
            faces[0, k] = east
            faces[1, k] = west
            faces[2, k] = north
            faces[3, k] = south

    def coupling_of(k):
        return (2.0 * layers * layers) * (eta_ref[k] + eta_ref[k + 1])

    middle = layers // 2
    zero = jnp.zeros(shape, jnp.float32)

    def eliminate(k, coupling, carry):
        before, passed, value = carry
        new_passed, new_value = [], []
        for c in range(2):
            rest = side[c, k] + passed[c]
            pivot = coupling + rest
            guess = pl.reciprocal(pivot, approx=True)
            correct = 2.0 - pivot * guess
            new_passed.append((coupling * rest * guess) * correct)
            inv = guess * correct
            inverse[c, k] = inv
            ratio[c, k] = coupling * inv
            out = (rhs[c, k] + before * value[c]) * inv
            rhs[c, k] = out
            new_value.append(out)
        return coupling, tuple(new_passed), tuple(new_value)

    def lower_step(k, carry):
        return eliminate(k, coupling_of(k), carry)

    def upper_step(k, carry):
        return eliminate(k, coupling_of(k - 1), carry)

    def fronts(step, carry):
        lower, upper = carry
        return lower_step(step, lower), upper_step(layers - 1 - step, upper)

    def spread(first, body):
        def outward(step, carry):
            below, above = carry
            return body(middle - 1 - step, below), body(middle + 1 + step, above)

        below, above = repeat(plan, layers - 1 - middle, outward, (first, first))
        for k in range(2 * middle - layers, -1, -1):
            below = body(k, below)
        return below, above

    def sweep(keep):
        def stencil_body(k, carry):
            stencil(k, keep)
            return carry

        bed = tuple(2.0 * friction for _ in range(2))
        lower, upper = (zero, bed, (zero, zero)), (zero, (zero, zero), (zero, zero))
        if plan.unrolled:
            stencil(0, keep)
            stencil(layers - 1, keep)
            for step in range(layers - 1 - middle):
                stencil(step + 1, keep)
                if layers - 2 - step > step + 1:
                    stencil(layers - 2 - step, keep)
                lower, upper = fronts(step, (lower, upper))
        else:
            repeat(plan, layers, stencil_body)
            lower, upper = repeat(plan, layers - 1 - middle, fronts, (lower, upper))
        for k in range(layers - 1 - middle, middle):
            lower = lower_step(k, lower)
        centre_value = []
        for c in range(2):
            pivot = side[c, middle] + lower[1][c] + upper[1][c]
            guess = pl.reciprocal(pivot, approx=True)
            inv = guess * (2.0 - pivot * guess)
            inverse[c, middle] = inv
            total = rhs[c, middle] + (lower[0] * lower[2][c] + upper[0] * upper[2][c])
            centre_value.append(jnp.where(ice, total * inv, 0.0))
            field[c, middle] = centre_value[c]

        def solved(k, nearer):
            current = tuple(jnp.where(ice, rhs[c, k] + ratio[c, k] * nearer[c], 0.0) for c in range(2))
            for c in range(2):
                field[c, k] = current[c]
            return current

        return spread(tuple(centre_value), solved)

    sweep(False)
    base, top = sweep(True)

    centre = jnp.logical_and(lane % width >= plan.halo, lane % width < plan.halo + plan.cols)

    def send(k, carry):
        both = jnp.where(centre, field[0, k], lane_roll(field[1, k], plan.cols))
        out_ref[pl.ds((k // here) * plan.out_rows + k % here, size, stride=plan.layer_size * plan.out_rows), :] = both
        return carry

    repeat(plan, layers, send)

    mismatch = [jnp.where(ice, top[c] - observed[c], 0.0) for c in range(2)]
    source = [(2.0 * layers) * mismatch[c] for c in range(2)]

    def side_sum(k, value):
        east, west, north, south = (faces[n, k] for n in range(4))
        u_east, u_west = x_pair(value[0], 0.0)
        v_east, v_west = x_pair(value[1], 0.0)
        u_north, u_south = y_pair(value[0])
        v_north, v_south = y_pair(value[1])
        first = 4.0 * (east * u_east + west * u_west) + (north * u_north + south * u_south)
        second = (east * v_east + west * v_west) + 4.0 * (north * v_north + south * v_south)
        return first, second

    carried = tuple(source[c] * inverse[c, layers - 1] for c in range(2))
    for c in range(2):
        rhs[c, layers - 1] = carried[c]

    def first_inward(step, carried):
        k = layers - 2 - step
        out = tuple(coupling_of(k) * carried[c] * inverse[c, k] for c in range(2))
        for c in range(2):
            rhs[c, k] = out[c]
        return out

    carried = repeat(plan, layers - 2 - middle, first_inward, carried)
    first_middle = tuple(coupling_of(middle) * carried[c] * inverse[c, middle] for c in range(2))

    def first_outward(step, carry):
        below, above = carry
        low, high = middle - 1 - step, middle + 1 + step
        below = tuple(ratio[c, low] * below[c] for c in range(2))
        above = tuple(rhs[c, high] + ratio[c, high] * above[c] for c in range(2))
        for k, value in ((low, below), (high, above)):
            total = side_sum(k, value)
            for c in range(2):
                rhs[c, k] = total[c] * inverse[c, k]
        return below, above

    middle_sum = side_sum(middle, first_middle)
    below, above = repeat(plan, layers - 1 - middle, first_outward, (first_middle, first_middle))
    for k in range(2 * middle - layers, -1, -1):
        below = tuple(ratio[c, k] * below[c] for c in range(2))
        total = side_sum(k, below)
        for c in range(2):
            rhs[c, k] = total[c] * inverse[c, k]
    for c in range(2):
        rhs[c, layers - 1] = rhs[c, layers - 1] + source[c] * inverse[c, layers - 1]

    def second_inward(step, carry):
        below, above = carry
        low, high = step + 1, layers - 2 - step
        below = tuple(rhs[c, low] + (coupling_of(low - 1) * inverse[c, low]) * below[c] for c in range(2))
        above = tuple(rhs[c, high] + (coupling_of(high) * inverse[c, high]) * above[c] for c in range(2))
        for c in range(2):
            rhs[c, low] = below[c]
        return below, above

    below, above = repeat(
        plan,
        layers - 2 - middle,
        second_inward,
        (tuple(rhs[c, 0] for c in range(2)), tuple(rhs[c, layers - 1] for c in range(2))),
    )
    for k in range(layers - 1 - middle, middle):
        below = tuple(rhs[c, k] + (coupling_of(k - 1) * inverse[c, k]) * below[c] for c in range(2))
        for c in range(2):
            rhs[c, k] = below[c]
    adjoint = tuple(
        (middle_sum[c] + (coupling_of(middle - 1) * below[c] + coupling_of(middle) * above[c])) * inverse[c, middle]
        for c in range(2)
    )

    def second_outward(step, nearer):
        k = middle - 1 - step
        return tuple(rhs[c, k] + ratio[c, k] * nearer[c] for c in range(2))

    adjoint = repeat(plan, middle, second_outward, adjoint)
    adjoint = [jnp.where(ice, adjoint[c], 0.0) for c in range(2)]
    product = base[0] * adjoint[0] + base[1] * adjoint[1]
    gradient = -friction * product

    def partial_sum(value):
        line = jnp.sum(jnp.where(centre, value, 0.0), axis=0, keepdims=True)
        folded = line
        for r in range(1, rows):
            folded = folded + lane_roll(line, r * width)
        return jnp.broadcast_to(lane_roll(folded, plan.cols), shape)

    misfit_line = partial_sum(mismatch[0] * mismatch[0] + mismatch[1] * mismatch[1])
    grad_line = partial_sum(gradient * gradient)
    in_first = jnp.logical_and(lane >= plan.halo + plan.cols, lane < plan.halo + 2 * plan.cols)
    last_row = jnp.where(centre, product, jnp.where(in_first, misfit_line, grad_line))
    for part in range(plan.layer_size):
        out_ref[pl.ds(part * plan.out_rows + here, size, stride=plan.layer_size * plan.out_rows), :] = last_row


def unpack_kernel(
    plan, in_ref, log_ref, bed_ref, vel_hbm, friction_hbm, misfit_hbm,
    vel_ref, friction_ref, misfit_ref, grad_ref, leave,
):
    here, width, cols, rows = plan.layers_here, plan.width, plan.cols, plan.rows
    local_chunks = plan.local_cols // LANES

    total = jnp.sum(
        in_ref[pl.ds(here, plan.devices, stride=plan.out_rows), :], axis=0, keepdims=True
    )
    line_lane = lax.broadcasted_iota(jnp.int32, (1, LANES), 1)

    def summed(first):
        ahead = (line_lane + (LANES - first % LANES)) % LANES
        return jnp.sum(jnp.where(ahead < cols, total, 0.0), axis=1, keepdims=True)

    misfit_sum = summed(plan.halo + cols)
    grad_sum = summed(plan.halo + cols + width)
    scale = step_size / jnp.sqrt(grad_sum / plan.column_count + 1e-06)

    lane = lax.broadcasted_iota(jnp.int32, (plan.out_rows, LANES), 1)
    def chunk(c, i):
        at = i * plan.per_chunk * plan.out_rows
        if not isinstance(at, int):
            at = pl.multiple_of(at, 8)
        turned = [
            lane_roll(in_ref[pl.ds(at + t * plan.out_rows, plan.out_rows), :], t * cols)
            for t in range(plan.per_chunk)
        ]
        for r in range(rows):
            start = r * width + plan.halo + c * cols
            ahead = (lane + (LANES - start % LANES)) % LANES
            row = turned[0]
            for t in range(1, plan.per_chunk):
                row = jnp.where(ahead >= t * cols, turned[t], row)
            row = lane_roll(row, -start)
            vel_ref[c, pl.ds(i * rows + r, here, stride=plan.chunks * rows), :] = row[:here]
            if c == 0:
                owner, step = i // local_chunks, i % local_chunks
                grad_ref[owner, pl.ds(step * rows + r, 1), :] = row[here : here + 1]

    out = [pltpu.make_async_copy(vel_ref.at[c], vel_hbm.at[c], leave.at[c]) for c in range(2)]
    out.append(pltpu.make_async_copy(friction_ref, friction_hbm, leave.at[2]))
    out.append(pltpu.make_async_copy(misfit_ref, misfit_hbm, leave.at[3]))
    for c in range(2):

        def chunk_body(i, carry):
            chunk(c, i)
            return carry

        repeat(plan, plan.chunks, chunk_body)
        out[c].start()
    gradient = -bed_ref[...] * grad_ref[lax.axis_index("layer")]
    friction_ref[...] = log_ref[...] - gradient * scale
    out[2].start()
    misfit_ref[...] = 0.5 * misfit_sum / plan.column_count
    out[3].start()
    for copy in out:
        copy.wait()


def as_lines(x):
    chunked = x.reshape(x.shape[:-1] + (x.shape[-1] // LANES, LANES))
    return jnp.swapaxes(chunked, -3, -2).reshape(-1, LANES)


def from_lines(lines, shape):
    chunked = lines.reshape(shape[:-2] + (shape[-1] // LANES, shape[-2], LANES))
    return jnp.swapaxes(chunked, -3, -2).reshape(shape)


def on_device(mesh_shape, velocity_init, driving, observed, log_friction, ice_mask):
    plan = Plan(mesh_shape, velocity_init.shape)
    vmem = pl.BlockSpec(memory_space=pltpu.VMEM)
    hbm = pl.BlockSpec(memory_space=pltpu.HBM)
    f32 = jnp.float32
    limit = pltpu.CompilerParams(vmem_limit_bytes=(16 if plan.unrolled else 40) * MIB)
    inputs = [as_lines(x) for x in (velocity_init, driving, observed, log_friction, ice_mask)]

    def exchange(blocks, unit):
        shaped = blocks.reshape(blocks.shape[0] // unit, unit, LANES)
        return lax.all_to_all(shaped, ("map", "layer"), split_axis=0, concat_axis=0, tiled=True).reshape(blocks.shape)

    packed = pl.pallas_call(
        functools.partial(pack_kernel, plan),
        out_shape=jax.ShapeDtypeStruct((plan.devices * plan.in_rows, LANES), f32),
        in_specs=[hbm] * 5,
        out_specs=vmem,
        scratch_shapes=[pltpu.VMEM(x.shape, x.dtype) for x in inputs]
        + [
            pltpu.SemaphoreType.DMA((VELOCITY_COPIES + 4,)),
        ],
        compiler_params=limit,
        name="pack",
    )(*(pltpu.with_memory_space_constraint(x, pltpu.HBM) for x in inputs))

    windows = exchange(packed, 2)
    bed_lines = jnp.where(inputs[4] == 1, jnp.exp(inputs[3]), 0.0)

    plane = (plan.layers, plan.map_size, LANES)
    solved = pl.pallas_call(
        functools.partial(solve_kernel, plan),
        out_shape=jax.ShapeDtypeStruct((plan.devices * plan.out_rows, LANES), f32),
        in_specs=[vmem],
        out_specs=vmem,
        scratch_shapes=[
            pltpu.VMEM((2,) + plane, f32),
            pltpu.VMEM(plane, f32),
            pltpu.VMEM((2,) + plane, f32),
            pltpu.VMEM((2,) + plane, f32),
            pltpu.VMEM((4,) + plane, f32),
            pltpu.VMEM((2,) + plane, f32),
            pltpu.VMEM((2,) + plane, f32),
        ],
        compiler_params=limit,
        name="solve",
    )(windows)

    back = exchange(solved, 1)

    vel_lines, log_lines = inputs[0].reshape(2, -1, LANES), inputs[3]
    velocity, friction_new, misfit = pl.pallas_call(
        functools.partial(unpack_kernel, plan),
        out_shape=(
            jax.ShapeDtypeStruct(vel_lines.shape, f32),
            jax.ShapeDtypeStruct(log_lines.shape, f32),
            jax.ShapeDtypeStruct((1, 1), f32),
        ),
        in_specs=[vmem] * 3,
        out_specs=(hbm, hbm, hbm),
        scratch_shapes=[
            pltpu.VMEM(vel_lines.shape, f32),
            pltpu.VMEM(log_lines.shape, f32),
            pltpu.VMEM((1, 1), f32),
            pltpu.VMEM((plan.layer_size,) + log_lines.shape, f32),
            pltpu.SemaphoreType.DMA((4,)),
        ],
        compiler_params=limit,
        name="unpack",
    )(back, log_lines, bed_lines)
    return (
        from_lines(velocity, velocity_init.shape),
        from_lines(friction_new, log_friction.shape),
        misfit.reshape(()),
    )


def solution(mesh):
    in_specs = (
        P(None, "layer", "map", None),
        P(None, "map", "layer"),
        P(None, "map", "layer"),
        P("map", "layer"),
        P("map", "layer"),
    )
    out_specs = (P(None, "layer", "map", None), P("map", "layer"), P())
    return jax.shard_map(
        functools.partial(on_device, dict(mesh.shape)),
        mesh=mesh,
        in_specs=in_specs,
        out_specs=out_specs,
        check_vma=False,
    )
```

```python
import functools
import math

import jax
import jax.numpy as jnp
from jax import lax
from jax.experimental import pallas as pl
from jax.experimental.pallas import tpu as pltpu
from jax.sharding import PartitionSpec as P

strain_floor = 0.1
step_size = 0.5
LANES = 128
REACH = 5
MIB = 1 << 20
VELOCITY_COPIES = 4


class Plan:
    def __init__(self, mesh_shape, velocity_shape):
        self.map_size = mesh_shape["map"]
        self.layer_size = mesh_shape["layer"]
        self.devices = self.map_size * self.layer_size
        self.layers_here = velocity_shape[1]
        self.rows = velocity_shape[2]
        self.ny = velocity_shape[3]
        self.layers = self.layers_here * self.layer_size
        self.cols = self.ny // self.devices
        self.width = LANES // self.rows
        self.halo = (self.width - self.cols) // 2
        self.low = self.halo - REACH
        self.wide = self.cols + 2 * REACH
        self.half = self.wide // 2
        self.gap = self.low + self.wide
        self.local_cols = self.ny // self.layer_size
        self.per_chunk = LANES // self.cols
        self.chunks = self.ny // LANES
        self.column_count = self.rows * self.map_size * self.ny
        self.vel_rows = 2 * self.layers_here
        self.in_rows = self.vel_rows + self.rows
        self.out_rows = self.layers_here + 1
        self.unrolled = self.map_size <= 8
        assert self.width * self.rows == LANES and self.cols * self.per_chunk == LANES
        assert self.low >= 0 and self.wide % 2 == 0 and self.width - self.wide >= self.half
        assert 2 * self.cols <= self.width and self.local_cols % LANES == 0
        assert self.vel_rows == 8 and self.rows == 2 and 3 * self.wide <= LANES


def repeat(plan, count, body, carry=0):
    if plan.unrolled:
        for index in range(count):
            carry = body(index, carry)
        return carry
    return lax.fori_loop(0, count, body, carry)


def lane_roll(value, shift):
    shift = shift % LANES
    return value if shift == 0 else pltpu.roll(value, shift, 1)


def pack_kernel(
    plan, vel_hbm, driving_hbm, observed_hbm, log_hbm, mask_hbm, out_ref,
    vel_ref, driving_ref, observed_ref, log_ref, mask_ref, arrival,
):
    width, rows, wide, half = plan.width, plan.rows, plan.wide, plan.half
    piece = vel_ref.shape[0] // VELOCITY_COPIES
    spans = [pl.ds(n * piece, piece) for n in range(VELOCITY_COPIES)]
    pairs = [(vel_hbm.at[span, :], vel_ref.at[span, :]) for span in spans] + [
        (driving_hbm, driving_ref),
        (observed_hbm, observed_ref),
        (log_hbm, log_ref),
        (mask_hbm, mask_ref),
    ]
    copies = [pltpu.make_async_copy(pair[0], pair[1], arrival.at[n]) for n, pair in enumerate(pairs)]
    for copy in copies:
        copy.start()
    shape = (plan.vel_rows, LANES)
    lane = lax.broadcasted_iota(jnp.int32, shape, 1)
    sub = lax.broadcasted_iota(jnp.int32, shape, 0)
    in_gap = jnp.logical_not(jnp.logical_and(lane % width >= plan.low, lane % width < plan.gap))
    no_line = jnp.zeros((rows, LANES), jnp.float32)

    def slide(part, start, length, place):
        step, offset = start // LANES, start % LANES
        value = part(step)
        if offset + length > LANES:
            after = part(step + 1)
            value = jnp.where(lax.broadcasted_iota(jnp.int32, value.shape, 1) >= offset, value, after)
        return lane_roll(value, place - offset)

    for copy in copies[:VELOCITY_COPIES]:
        copy.wait()

    def chunk_windows(i, carry):
        def velocity(r):
            def part(step):
                chunk = i + step
                if isinstance(chunk, int) and not 0 <= chunk < plan.chunks:
                    return jnp.zeros(shape, jnp.float32)
                at = chunk if isinstance(chunk, int) else jnp.clip(chunk, 0, plan.chunks - 1)
                value = vel_ref[pl.ds(at * rows + r, plan.vel_rows, stride=plan.chunks * rows), :]
                if isinstance(chunk, int):
                    return value
                return jnp.where(jnp.logical_and(chunk >= 0, chunk < plan.chunks), value, 0.0)

            return part

        for t in range(plan.per_chunk):
            block = None
            for r in range(rows):
                value = slide(velocity(r), plan.cols * t - plan.halo, width, r * width)
                block = value if block is None else jnp.where(lane >= r * width, value, block)
            at = i * plan.per_chunk * plan.in_rows
            if not isinstance(at, int):
                at = pl.multiple_of(at, 8)
            at = at + t * plan.in_rows
            out_ref[pl.ds(at, plan.vel_rows), :] = jnp.where(in_gap, 0.0, block)
            out_ref[pl.ds(at + plan.vel_rows, rows), :] = no_line
        return carry

    repeat(plan, plan.chunks, chunk_windows)
    for copy in copies[VELOCITY_COPIES:]:
        copy.wait()

    place = lax.axis_index("layer")
    local_chunks = plan.local_cols // LANES

    def line_part(ref, row):
        def part(step):
            if not 0 <= step < local_chunks:
                return no_line
            return ref[row + step * rows : row + (step + 1) * rows, :]

        return part

    def gap_part(r):
        def part(step):
            if not 0 <= step < local_chunks:
                return jnp.zeros(shape, jnp.float32)
            at = step * rows + r
            skip = local_chunks * rows
            first = jnp.broadcast_to(observed_ref[at : at + 1, :], shape)
            second = jnp.broadcast_to(observed_ref[skip + at : skip + at + 1, :], shape)
            third = jnp.broadcast_to(mask_ref[at : at + 1, :], shape).astype(jnp.float32)
            return jnp.where(sub < 2, first, jnp.where(sub < 4, second, third))

        return part

    gap_parts = [[gap_part(r)(step) for step in range(-1, local_chunks + 1)] for r in range(rows)]
    own = plan.local_cols // plan.cols
    spill = -(-REACH // plan.cols)

    def column_block(q):
        start = q * plan.cols - REACH
        line = None
        for n, part in enumerate(
            (line_part(driving_ref, 0), line_part(driving_ref, local_chunks * rows), line_part(log_ref, 0))
        ):
            value = slide(part, start, wide, n * wide)
            lanes = lax.broadcasted_iota(jnp.int32, value.shape, 1)
            line = value if line is None else jnp.where(lanes >= n * wide, value, line)
        block = None
        for r in range(rows):
            halves = [
                slide(lambda step: gap_parts[r][step + 1], start + h * half, half, (r * width + plan.gap) % LANES)
                for h in range(2)
            ]
            value = jnp.where(sub % 2 == 0, halves[0], halves[1])
            ahead = (lane + (LANES - plan.gap)) % LANES
            block = value if block is None else jnp.where(ahead >= r * width, value, block)
        at = pl.multiple_of(place * (own * plan.in_rows), 8) + q * plan.in_rows
        here = pl.ds(at, plan.vel_rows)
        out_ref[here, :] = jnp.where(in_gap, block, out_ref[here, :])
        out_ref[pl.ds(at + plan.vel_rows, rows), :] = line

    for q in range(own):
        column_block(q)

    @pl.when(place > 0)
    def _():
        for q in range(-spill, 0):
            column_block(q)

    @pl.when(place < plan.layer_size - 1)
    def _():
        for q in range(own, own + spill):
            column_block(q)


def solve_kernel(plan, in_ref, out_ref, field, eta_ref, side, rhs, faces, ratio, inverse):
    size, width, rows = plan.map_size, plan.width, plan.rows
    layers, here = plan.layers, plan.layers_here
    shape = (size, LANES)
    lane = lax.broadcasted_iota(jnp.int32, shape, 1)
    sub = lax.broadcasted_iota(jnp.int32, shape, 0)
    last_group = lane >= LANES - width
    first_group = lane < width
    x_end = jnp.logical_and(last_group, sub == size - 1)
    x_start = jnp.logical_and(first_group, sub == 0)

    def arrived(part, row):
        return in_ref[pl.ds(part * size * plan.in_rows + row, size, stride=plan.in_rows), :]

    def over_parts(row):
        total = arrived(0, row)
        for part in range(1, plan.layer_size):
            total = total + arrived(part, row)
        return total

    def from_gap(index):
        shift = plan.low - plan.gap
        left, right = over_parts(2 * index), over_parts(2 * index + 1)
        return jnp.where(lane % width < plan.low + plan.half, lane_roll(left, shift), lane_roll(right, shift + plan.half))

    def from_line(index):
        plane = lane_roll(lines[0], plan.low - index * plan.wide)
        for r in range(1, rows):
            plane = jnp.where(lane >= r * width, lane_roll(lines[r], r * width + plan.low - index * plan.wide), plane)
        return plane

    def x_pair(value, edge):
        after = lane_roll(value, -width)
        before = after if 2 * width == LANES else lane_roll(value, width)
        after = jnp.where(last_group, pltpu.roll(after, size - 1, 0), after)
        before = jnp.where(first_group, pltpu.roll(before, 1, 0), before)
        return jnp.where(x_end, edge, after), jnp.where(x_start, edge, before)

    def y_pair(value):
        return lane_roll(value, -1), lane_roll(value, 1)

    def viscosity(rate):
        return jnp.exp2(jnp.log(strain_floor + rate) * (-1.0 / (3.0 * math.log(2.0))))

    for part in range(plan.layer_size):
        for c in range(2):
            for k in range(here):
                field[c, part * here + k] = arrived(part, c * here + k)
    lines = [over_parts(plan.vel_rows + r) for r in range(rows)]
    reached = jnp.logical_and(lane % width >= plan.low, lane % width < plan.gap)
    driving = [2.0 * from_line(c) for c in range(2)]
    observed = [from_gap(c) for c in range(2)]
    mask = jnp.where(reached, from_gap(2), 0.0)
    ice = mask != 0.0
    friction = jnp.where(mask == 1.0, jnp.exp(from_line(2)), 0.0)

    def stencil(k, keep):
        u, v = field[0, k], field[1, k]
        u_east, u_west = x_pair(u, 0.0)
        v_east, v_west = x_pair(v, 0.0)
        u_north, u_south = y_pair(u)
        v_north, v_south = y_pair(v)
        stretch_x = u_east - u_west
        stretch_y = v_north - v_south
        shear = 0.5 * ((u_north - u_south) + (v_east - v_west))
        rate = 0.25 * (stretch_x * (stretch_x + stretch_y) + stretch_y * stretch_y + shear * shear)
        half_v = 0.5 * v
        eta = viscosity(rate)
        eta_edge = viscosity(0.25 * (u * u + half_v * half_v))
        eta_east, eta_west = x_pair(eta, eta_edge)
        eta_north, eta_south = y_pair(eta)
        east, west = eta + eta_east, eta + eta_west
        north, south = eta + eta_north, eta + eta_south
        along_x, along_y = east + west, north + south
        eta_ref[k] = eta
        side[0, k] = 4.0 * along_x + along_y
        side[1, k] = along_x + 4.0 * along_y
        rhs[0, k] = driving[0] + (4.0 * (east * u_east + west * u_west) + (north * u_north + south * u_south))
        rhs[1, k] = driving[1] + ((east * v_east + west * v_west) + 4.0 * (north * v_north + south * v_south))
        if keep:
            faces[0, k] = east
            faces[1, k] = west
            faces[2, k] = north
            faces[3, k] = south

    def coupling_of(k):
        return (2.0 * layers * layers) * (eta_ref[k] + eta_ref[k + 1])

    middle = layers // 2
    zero = jnp.zeros(shape, jnp.float32)

    def eliminate(k, coupling, carry):
        before, passed, value = carry
        new_passed, new_value = [], []
        for c in range(2):
            rest = side[c, k] + passed[c]
            pivot = coupling + rest
            guess = pl.reciprocal(pivot, approx=True)
            correct = 2.0 - pivot * guess
            new_passed.append((coupling * rest * guess) * correct)
            inv = guess * correct
            inverse[c, k] = inv
            ratio[c, k] = coupling * inv
            out = (rhs[c, k] + before * value[c]) * inv
            rhs[c, k] = out
            new_value.append(out)
        return coupling, tuple(new_passed), tuple(new_value)

    def lower_step(k, carry):
        return eliminate(k, coupling_of(k), carry)

    def upper_step(k, carry):
        return eliminate(k, coupling_of(k - 1), carry)

    def fronts(step, carry):
        lower, upper = carry
        return lower_step(step, lower), upper_step(layers - 1 - step, upper)

    def spread(first, body):
        def outward(step, carry):
            below, above = carry
            return body(middle - 1 - step, below), body(middle + 1 + step, above)

        below, above = repeat(plan, layers - 1 - middle, outward, (first, first))
        for k in range(2 * middle - layers, -1, -1):
            below = body(k, below)
        return below, above

    def sweep(keep):
        def stencil_body(k, carry):
            stencil(k, keep)
            return carry

        bed = tuple(2.0 * friction for _ in range(2))
        lower, upper = (zero, bed, (zero, zero)), (zero, (zero, zero), (zero, zero))
        if plan.unrolled:
            stencil(0, keep)
            stencil(layers - 1, keep)
            for step in range(layers - 1 - middle):
                stencil(step + 1, keep)
                if layers - 2 - step > step + 1:
                    stencil(layers - 2 - step, keep)
                lower, upper = fronts(step, (lower, upper))
        else:
            repeat(plan, layers, stencil_body)
            lower, upper = repeat(plan, layers - 1 - middle, fronts, (lower, upper))
        for k in range(layers - 1 - middle, middle):
            lower = lower_step(k, lower)
        centre_value = []
        for c in range(2):
            pivot = side[c, middle] + lower[1][c] + upper[1][c]
            guess = pl.reciprocal(pivot, approx=True)
            inv = guess * (2.0 - pivot * guess)
            inverse[c, middle] = inv
            total = rhs[c, middle] + (lower[0] * lower[2][c] + upper[0] * upper[2][c])
            centre_value.append(jnp.where(ice, total * inv, 0.0))
            field[c, middle] = centre_value[c]

        def solved(k, nearer):
            current = tuple(jnp.where(ice, rhs[c, k] + ratio[c, k] * nearer[c], 0.0) for c in range(2))
            for c in range(2):
                field[c, k] = current[c]
            return current

        return spread(tuple(centre_value), solved)

    sweep(False)
    base, top = sweep(True)

    centre = jnp.logical_and(lane % width >= plan.halo, lane % width < plan.halo + plan.cols)

    def send(k, carry):
        both = jnp.where(centre, field[0, k], lane_roll(field[1, k], plan.cols))
        out_ref[pl.ds((k // here) * size * plan.out_rows + k % here, size, stride=plan.out_rows), :] = both
        return carry

    repeat(plan, layers, send)

    mismatch = [jnp.where(ice, top[c] - observed[c], 0.0) for c in range(2)]
    source = [(2.0 * layers) * mismatch[c] for c in range(2)]

    def side_sum(k, value):
        east, west, north, south = (faces[n, k] for n in range(4))
        u_east, u_west = x_pair(value[0], 0.0)
        v_east, v_west = x_pair(value[1], 0.0)
        u_north, u_south = y_pair(value[0])
        v_north, v_south = y_pair(value[1])
        first = 4.0 * (east * u_east + west * u_west) + (north * u_north + south * u_south)
        second = (east * v_east + west * v_west) + 4.0 * (north * v_north + south * v_south)
        return first, second

    carried = tuple(source[c] * inverse[c, layers - 1] for c in range(2))
    for c in range(2):
        rhs[c, layers - 1] = carried[c]

    def first_inward(step, carried):
        k = layers - 2 - step
        out = tuple(coupling_of(k) * carried[c] * inverse[c, k] for c in range(2))
        for c in range(2):
            rhs[c, k] = out[c]
        return out

    carried = repeat(plan, layers - 2 - middle, first_inward, carried)
    first_middle = tuple(coupling_of(middle) * carried[c] * inverse[c, middle] for c in range(2))

    def first_outward(step, carry):
        below, above = carry
        low, high = middle - 1 - step, middle + 1 + step
        below = tuple(ratio[c, low] * below[c] for c in range(2))
        above = tuple(rhs[c, high] + ratio[c, high] * above[c] for c in range(2))
        for k, value in ((low, below), (high, above)):
            total = side_sum(k, value)
            for c in range(2):
                rhs[c, k] = total[c] * inverse[c, k]
        return below, above

    middle_sum = side_sum(middle, first_middle)
    below, above = repeat(plan, layers - 1 - middle, first_outward, (first_middle, first_middle))
    for k in range(2 * middle - layers, -1, -1):
        below = tuple(ratio[c, k] * below[c] for c in range(2))
        total = side_sum(k, below)
        for c in range(2):
            rhs[c, k] = total[c] * inverse[c, k]
    for c in range(2):
        rhs[c, layers - 1] = rhs[c, layers - 1] + source[c] * inverse[c, layers - 1]

    def second_inward(step, carry):
        below, above = carry
        low, high = step + 1, layers - 2 - step
        below = tuple(rhs[c, low] + (coupling_of(low - 1) * inverse[c, low]) * below[c] for c in range(2))
        above = tuple(rhs[c, high] + (coupling_of(high) * inverse[c, high]) * above[c] for c in range(2))
        for c in range(2):
            rhs[c, low] = below[c]
        return below, above

    below, above = repeat(
        plan,
        layers - 2 - middle,
        second_inward,
        (tuple(rhs[c, 0] for c in range(2)), tuple(rhs[c, layers - 1] for c in range(2))),
    )
    for k in range(layers - 1 - middle, middle):
        below = tuple(rhs[c, k] + (coupling_of(k - 1) * inverse[c, k]) * below[c] for c in range(2))
        for c in range(2):
            rhs[c, k] = below[c]
    adjoint = tuple(
        (middle_sum[c] + (coupling_of(middle - 1) * below[c] + coupling_of(middle) * above[c])) * inverse[c, middle]
        for c in range(2)
    )

    def second_outward(step, nearer):
        k = middle - 1 - step
        return tuple(rhs[c, k] + ratio[c, k] * nearer[c] for c in range(2))

    adjoint = repeat(plan, middle, second_outward, adjoint)
    adjoint = [jnp.where(ice, adjoint[c], 0.0) for c in range(2)]
    gradient = -friction * (base[0] * adjoint[0] + base[1] * adjoint[1])

    def partial_sum(value):
        line = jnp.sum(jnp.where(centre, value, 0.0), axis=0, keepdims=True)
        folded = line
        for r in range(1, rows):
            folded = folded + lane_roll(line, r * width)
        return jnp.broadcast_to(lane_roll(folded, plan.cols), shape)

    misfit_line = partial_sum(mismatch[0] * mismatch[0] + mismatch[1] * mismatch[1])
    grad_line = partial_sum(gradient * gradient)
    in_first = jnp.logical_and(lane >= plan.halo + plan.cols, lane < plan.halo + 2 * plan.cols)
    last_row = jnp.where(centre, gradient, jnp.where(in_first, misfit_line, grad_line))
    for part in range(plan.layer_size):
        out_ref[pl.ds(part * size * plan.out_rows + here, size, stride=plan.out_rows), :] = last_row


def unpack_kernel(
    plan, in_ref, log_ref, vel_hbm, friction_hbm, misfit_hbm,
    vel_ref, friction_ref, misfit_ref, grad_ref, leave,
):
    here, width, cols, rows = plan.layers_here, plan.width, plan.cols, plan.rows
    local_chunks = plan.local_cols // LANES

    total = jnp.sum(
        in_ref[pl.ds(here, plan.devices, stride=plan.out_rows), :], axis=0, keepdims=True
    )
    line_lane = lax.broadcasted_iota(jnp.int32, (1, LANES), 1)

    def summed(first):
        ahead = (line_lane + (LANES - first % LANES)) % LANES
        return jnp.sum(jnp.where(ahead < cols, total, 0.0), axis=1, keepdims=True)

    misfit_sum = summed(plan.halo + cols)
    grad_sum = summed(plan.halo + cols + width)
    scale = step_size / jnp.sqrt(grad_sum / plan.column_count + 1e-06)

    lane = lax.broadcasted_iota(jnp.int32, (plan.out_rows, LANES), 1)
    def chunk(c, i):
        at = i * plan.per_chunk * plan.out_rows
        if not isinstance(at, int):
            at = pl.multiple_of(at, 8)
        turned = [
            lane_roll(in_ref[pl.ds(at + t * plan.out_rows, plan.out_rows), :], t * cols)
            for t in range(plan.per_chunk)
        ]
        for r in range(rows):
            start = r * width + plan.halo + c * cols
            ahead = (lane + (LANES - start % LANES)) % LANES
            row = turned[0]
            for t in range(1, plan.per_chunk):
                row = jnp.where(ahead >= t * cols, turned[t], row)
            row = lane_roll(row, -start)
            vel_ref[c, pl.ds(i * rows + r, here, stride=plan.chunks * rows), :] = row[:here]
            if c == 0:
                owner, step = i // local_chunks, i % local_chunks
                grad_ref[owner, pl.ds(step * rows + r, 1), :] = row[here : here + 1]

    out = [pltpu.make_async_copy(vel_ref.at[c], vel_hbm.at[c], leave.at[c]) for c in range(2)]
    out.append(pltpu.make_async_copy(friction_ref, friction_hbm, leave.at[2]))
    out.append(pltpu.make_async_copy(misfit_ref, misfit_hbm, leave.at[3]))
    for c in range(2):

        def chunk_body(i, carry):
            chunk(c, i)
            return carry

        repeat(plan, plan.chunks, chunk_body)
        out[c].start()
    friction_ref[...] = log_ref[...] - grad_ref[lax.axis_index("layer")] * scale
    out[2].start()
    misfit_ref[...] = 0.5 * misfit_sum / plan.column_count
    out[3].start()
    for copy in out:
        copy.wait()


def as_lines(x):
    chunked = x.reshape(x.shape[:-1] + (x.shape[-1] // LANES, LANES))
    return jnp.swapaxes(chunked, -3, -2).reshape(-1, LANES)


def from_lines(lines, shape):
    chunked = lines.reshape(shape[:-2] + (shape[-1] // LANES, shape[-2], LANES))
    return jnp.swapaxes(chunked, -3, -2).reshape(shape)


def on_device(mesh_shape, velocity_init, driving, observed, log_friction, ice_mask):
    plan = Plan(mesh_shape, velocity_init.shape)
    vmem = pl.BlockSpec(memory_space=pltpu.VMEM)
    hbm = pl.BlockSpec(memory_space=pltpu.HBM)
    f32 = jnp.float32
    limit = pltpu.CompilerParams(vmem_limit_bytes=(16 if plan.unrolled else 40) * MIB)
    inputs = [as_lines(x) for x in (velocity_init, driving, observed, log_friction, ice_mask)]

    def exchange(blocks, unit):
        shaped = blocks.reshape(blocks.shape[0] // unit, unit, LANES)
        return lax.all_to_all(shaped, ("layer", "map"), split_axis=0, concat_axis=0, tiled=True).reshape(blocks.shape)

    packed = pl.pallas_call(
        functools.partial(pack_kernel, plan),
        out_shape=jax.ShapeDtypeStruct((plan.devices * plan.in_rows, LANES), f32),
        in_specs=[hbm] * 5,
        out_specs=vmem,
        scratch_shapes=[pltpu.VMEM(x.shape, x.dtype) for x in inputs]
        + [
            pltpu.SemaphoreType.DMA((VELOCITY_COPIES + 4,)),
        ],
        compiler_params=limit,
        name="pack",
    )(*(pltpu.with_memory_space_constraint(x, pltpu.HBM) for x in inputs))

    windows = exchange(packed, 2)

    plane = (plan.layers, plan.map_size, LANES)
    solved = pl.pallas_call(
        functools.partial(solve_kernel, plan),
        out_shape=jax.ShapeDtypeStruct((plan.devices * plan.out_rows, LANES), f32),
        in_specs=[vmem],
        out_specs=vmem,
        scratch_shapes=[
            pltpu.VMEM((2,) + plane, f32),
            pltpu.VMEM(plane, f32),
            pltpu.VMEM((2,) + plane, f32),
            pltpu.VMEM((2,) + plane, f32),
            pltpu.VMEM((4,) + plane, f32),
            pltpu.VMEM((2,) + plane, f32),
            pltpu.VMEM((2,) + plane, f32),
        ],
        compiler_params=limit,
        name="solve",
    )(windows)

    back = exchange(solved, 1)

    vel_lines, log_lines = inputs[0].reshape(2, -1, LANES), inputs[3]
    velocity, friction_new, misfit = pl.pallas_call(
        functools.partial(unpack_kernel, plan),
        out_shape=(
            jax.ShapeDtypeStruct(vel_lines.shape, f32),
            jax.ShapeDtypeStruct(log_lines.shape, f32),
            jax.ShapeDtypeStruct((1, 1), f32),
        ),
        in_specs=[vmem] * 2,
        out_specs=(hbm, hbm, hbm),
        scratch_shapes=[
            pltpu.VMEM(vel_lines.shape, f32),
            pltpu.VMEM(log_lines.shape, f32),
            pltpu.VMEM((1, 1), f32),
            pltpu.VMEM((plan.layer_size,) + log_lines.shape, f32),
            pltpu.SemaphoreType.DMA((4,)),
        ],
        compiler_params=limit,
        name="unpack",
    )(back, log_lines)
    return (
        from_lines(velocity, velocity_init.shape),
        from_lines(friction_new, log_friction.shape),
        misfit.reshape(()),
    )


def solution(mesh):
    in_specs = (
        P(None, "layer", "map", None),
        P(None, "map", "layer"),
        P(None, "map", "layer"),
        P("map", "layer"),
        P("map", "layer"),
    )
    out_specs = (P(None, "layer", "map", None), P("map", "layer"), P())
    return jax.shard_map(
        functools.partial(on_device, dict(mesh.shape)),
        mesh=mesh,
        in_specs=in_specs,
        out_specs=out_specs,
        check_vma=False,
    )
```

```python
import functools
import math

import jax
import jax.numpy as jnp
from jax import lax
from jax.experimental import pallas as pl
from jax.experimental.pallas import tpu as pltpu
from jax.sharding import PartitionSpec as P

strain_floor = 0.1
step_size = 0.5
LANES = 128
REACH = 5
BED_REACH = 3
MIB = 1 << 20
VELOCITY_COPIES = 4


class Plan:
    def __init__(self, mesh_shape, velocity_shape):
        self.map_size = mesh_shape["map"]
        self.layer_size = mesh_shape["layer"]
        self.devices = self.map_size * self.layer_size
        self.layers_here = velocity_shape[1]
        self.rows = velocity_shape[2]
        self.ny = velocity_shape[3]
        self.layers = self.layers_here * self.layer_size
        self.cols = self.ny // self.devices
        self.width = LANES // self.rows
        self.halo = (self.width - self.cols) // 2
        self.low = self.halo - REACH
        self.wide = self.cols + 2 * REACH
        self.half = self.wide // 2
        self.gap = self.low + self.wide
        self.local_cols = self.ny // self.layer_size
        self.per_chunk = LANES // self.cols
        self.chunks = self.ny // LANES
        self.column_count = self.rows * self.map_size * self.ny
        self.vel_rows = 2 * self.layers_here
        self.in_rows = self.vel_rows + 1
        self.left_at = self.gap
        self.right_at = self.gap + self.cols // 2 + 1
        self.out_rows = self.layers_here + 1
        self.unrolled = self.map_size <= 8
        assert self.width * self.rows == LANES and self.cols * self.per_chunk == LANES
        assert self.low >= 0 and self.wide % 2 == 0 and self.width - self.wide >= self.half
        assert 2 * self.cols <= self.width and self.local_cols % LANES == 0
        assert self.vel_rows == 8 and self.rows == 2 and 4 * self.cols <= LANES


def repeat(plan, count, body, carry=0):
    if plan.unrolled:
        for index in range(count):
            carry = body(index, carry)
        return carry
    return lax.fori_loop(0, count, body, carry)


def lane_roll(value, shift):
    shift = shift % LANES
    return value if shift == 0 else pltpu.roll(value, shift, 1)


def pack_kernel(
    plan, vel_hbm, driving_hbm, observed_hbm, log_hbm, mask_hbm, out_ref,
    vel_ref, driving_ref, observed_ref, log_ref, mask_ref, arrival,
):
    width, rows, cols, half = plan.width, plan.rows, plan.cols, plan.half
    piece = vel_ref.shape[0] // VELOCITY_COPIES
    spans = [pl.ds(n * piece, piece) for n in range(VELOCITY_COPIES)]
    pairs = [(vel_hbm.at[span, :], vel_ref.at[span, :]) for span in spans] + [
        (driving_hbm, driving_ref),
        (observed_hbm, observed_ref),
        (log_hbm, log_ref),
        (mask_hbm, mask_ref),
    ]
    copies = [pltpu.make_async_copy(pair[0], pair[1], arrival.at[n]) for n, pair in enumerate(pairs)]
    for copy in copies:
        copy.start()
    shape = (plan.vel_rows, LANES)
    lane = lax.broadcasted_iota(jnp.int32, shape, 1)
    sub = lax.broadcasted_iota(jnp.int32, shape, 0)
    in_gap = jnp.logical_not(jnp.logical_and(lane % width >= plan.low, lane % width < plan.gap))
    no_line = jnp.zeros((1, LANES), jnp.float32)

    def slide(part, start, length, place):
        step, offset = start // LANES, start % LANES
        value = part(step)
        if offset + length > LANES:
            after = part(step + 1)
            value = jnp.where(lax.broadcasted_iota(jnp.int32, value.shape, 1) >= offset, value, after)
        return lane_roll(value, place - offset)

    for copy in copies[:VELOCITY_COPIES]:
        copy.wait()

    def chunk_windows(i, carry):
        def velocity(r):
            def part(step):
                chunk = i + step
                if isinstance(chunk, int) and not 0 <= chunk < plan.chunks:
                    return jnp.zeros(shape, jnp.float32)
                at = chunk if isinstance(chunk, int) else jnp.clip(chunk, 0, plan.chunks - 1)
                value = vel_ref[pl.ds(at * rows + r, plan.vel_rows, stride=plan.chunks * rows), :]
                if isinstance(chunk, int):
                    return value
                return jnp.where(jnp.logical_and(chunk >= 0, chunk < plan.chunks), value, 0.0)

            return part

        for t in range(plan.per_chunk):
            block = None
            for r in range(rows):
                value = slide(velocity(r), plan.cols * t - plan.halo, width, r * width)
                block = value if block is None else jnp.where(lane >= r * width, value, block)
            at = i * plan.per_chunk * plan.in_rows
            if not isinstance(at, int):
                at = pl.multiple_of(at, 8)
            at = at + t * plan.in_rows
            out_ref[pl.ds(at, plan.vel_rows), :] = jnp.where(in_gap, 0.0, block)
            out_ref[pl.ds(at + plan.vel_rows, 1), :] = no_line
        return carry

    repeat(plan, plan.chunks, chunk_windows)
    for copy in copies[VELOCITY_COPIES:]:
        copy.wait()

    place = lax.axis_index("layer")
    local_chunks = plan.local_cols // LANES

    skip = local_chunks * rows
    no_block = jnp.zeros(shape, jnp.float32)

    def whole(ref, row):
        return jnp.broadcast_to(ref[row : row + 1, :], shape).astype(jnp.float32)

    def gap_part(r, step):
        at = step * rows + r
        observed = jnp.where(sub < 2, whole(observed_ref, at), whole(observed_ref, skip + at))
        return jnp.where(sub < 4, observed, jnp.where(sub < 6, whole(mask_ref, at), whole(log_ref, at)))

    def driving_part(r, step):
        at = step * rows + r
        return jnp.where(sub < 2, whole(driving_ref, at), whole(driving_ref, skip + at))

    def sequence(make):
        return [
            [no_block] + [make(r, step) for step in range(local_chunks)] + [no_block] for r in range(rows)
        ]

    gap_parts, driving_parts = sequence(gap_part), sequence(driving_part)
    own = plan.local_cols // cols
    spill = -(-REACH // cols)

    def column_block(q):
        start = q * cols
        block = None
        for r in range(rows):

            def in_gaps(step):
                return gap_parts[r][step + 1]

            def of_driving(step):
                return driving_parts[r][step + 1]

            at = r * width
            first = slide(in_gaps, start - REACH, half, (at + plan.gap) % LANES)
            second = slide(in_gaps, start - REACH + half, half, (at + plan.gap) % LANES)
            before = slide(of_driving, start - BED_REACH, BED_REACH, (at + plan.left_at) % LANES)
            after = slide(of_driving, start + cols, BED_REACH, (at + plan.right_at) % LANES)
            ahead = (lane + (LANES - plan.gap - at)) % LANES
            of_observed = sub < 4
            first = jnp.where(jnp.logical_and(of_observed, ahead < BED_REACH), before, first)
            second = jnp.where(jnp.logical_and(of_observed, ahead >= plan.right_at - plan.gap), after, second)
            value = jnp.where(sub % 2 == 0, first, second)
            ahead = (lane + (LANES - plan.gap)) % LANES
            block = value if block is None else jnp.where(ahead >= r * width, value, block)
        at = pl.multiple_of(place * (own * plan.in_rows), 8) + q * plan.in_rows
        here = pl.ds(at, plan.vel_rows)
        out_ref[here, :] = jnp.where(in_gap, block, out_ref[here, :])
        if not 0 <= q < own:
            return
        line = None
        step, offset = start // LANES, start % LANES
        for r in range(rows):
            for c in range(2):
                row = c * skip + step * rows + r
                put = (2 * r + c) * cols
                value = lane_roll(driving_ref[row : row + 1, :], put - offset)
                line = value if line is None else jnp.where(lane[:1] >= put, value, line)
        out_ref[pl.ds(at + plan.vel_rows, 1), :] = line

    for q in range(own):
        column_block(q)

    @pl.when(place > 0)
    def _():
        for q in range(-spill, 0):
            column_block(q)

    @pl.when(place < plan.layer_size - 1)
    def _():
        for q in range(own, own + spill):
            column_block(q)


def solve_kernel(plan, in_ref, out_ref, field, eta_ref, side, rhs, faces, ratio, inverse):
    size, width, rows = plan.map_size, plan.width, plan.rows
    layers, here = plan.layers, plan.layers_here
    shape = (size, LANES)
    lane = lax.broadcasted_iota(jnp.int32, shape, 1)
    sub = lax.broadcasted_iota(jnp.int32, shape, 0)
    last_group = lane >= LANES - width
    first_group = lane < width
    x_end = jnp.logical_and(last_group, sub == size - 1)
    x_start = jnp.logical_and(first_group, sub == 0)

    def arrived(part, row):
        return in_ref[pl.ds(part * size * plan.in_rows + row, size, stride=plan.in_rows), :]

    def over_parts(row):
        total = arrived(0, row)
        for part in range(1, plan.layer_size):
            total = total + arrived(part, row)
        return total

    def moved(value, source, target):
        return lane_roll(value, target - source)

    def from_gap(halves):
        left, right = (moved(value, plan.gap, plan.low + h * plan.half) for h, value in enumerate(halves))
        return jnp.where(lane % width < plan.low + plan.half, left, right)

    def from_line(c):
        plane = None
        for r in range(rows):
            value = moved(line, (2 * r + c) * plan.cols, r * width + plan.halo)
            plane = value if plane is None else jnp.where(lane >= r * width, value, plane)
        return plane

    def driving_of(c, halves):
        left = moved(halves[0], plan.left_at, plan.halo - BED_REACH)
        right = moved(halves[1], plan.right_at, plan.halo + plan.cols)
        return jnp.where(centre, from_line(c), jnp.where(lane % width < plan.halo, left, right))

    def x_pair(value, edge):
        after = lane_roll(value, -width)
        before = after if 2 * width == LANES else lane_roll(value, width)
        after = jnp.where(last_group, pltpu.roll(after, size - 1, 0), after)
        before = jnp.where(first_group, pltpu.roll(before, 1, 0), before)
        return jnp.where(x_end, edge, after), jnp.where(x_start, edge, before)

    def y_pair(value):
        return lane_roll(value, -1), lane_roll(value, 1)

    def viscosity(rate):
        return jnp.exp2(jnp.log(strain_floor + rate) * (-1.0 / (3.0 * math.log(2.0))))

    for part in range(plan.layer_size):
        for c in range(2):
            for k in range(here):
                field[c, part * here + k] = arrived(part, c * here + k)
    line = over_parts(plan.vel_rows)
    gaps = [[over_parts(2 * n), over_parts(2 * n + 1)] for n in range(4)]
    reached = jnp.logical_and(lane % width >= plan.low, lane % width < plan.gap)
    centre = jnp.logical_and(lane % width >= plan.halo, lane % width < plan.halo + plan.cols)
    driving = [2.0 * driving_of(c, gaps[c]) for c in range(2)]
    observed = [from_gap(gaps[c]) for c in range(2)]
    mask = jnp.where(reached, from_gap(gaps[2]), 0.0)
    ice = mask != 0.0
    friction = jnp.where(mask == 1.0, jnp.exp(from_gap(gaps[3])), 0.0)

    def stencil(k, keep):
        u, v = field[0, k], field[1, k]
        u_east, u_west = x_pair(u, 0.0)
        v_east, v_west = x_pair(v, 0.0)
        u_north, u_south = y_pair(u)
        v_north, v_south = y_pair(v)
        stretch_x = u_east - u_west
        stretch_y = v_north - v_south
        shear = 0.5 * ((u_north - u_south) + (v_east - v_west))
        rate = 0.25 * (stretch_x * (stretch_x + stretch_y) + stretch_y * stretch_y + shear * shear)
        half_v = 0.5 * v
        eta = viscosity(rate)
        eta_edge = viscosity(0.25 * (u * u + half_v * half_v))
        eta_east, eta_west = x_pair(eta, eta_edge)
        eta_north, eta_south = y_pair(eta)
        east, west = eta + eta_east, eta + eta_west
        north, south = eta + eta_north, eta + eta_south
        along_x, along_y = east + west, north + south
        eta_ref[k] = eta
        side[0, k] = 4.0 * along_x + along_y
        side[1, k] = along_x + 4.0 * along_y
        rhs[0, k] = driving[0] + (4.0 * (east * u_east + west * u_west) + (north * u_north + south * u_south))
        rhs[1, k] = driving[1] + ((east * v_east + west * v_west) + 4.0 * (north * v_north + south * v_south))
        if keep:
            faces[0, k] = east
            faces[1, k] = west
            faces[2, k] = north
            faces[3, k] = south

    def coupling_of(k):
        return (2.0 * layers * layers) * (eta_ref[k] + eta_ref[k + 1])

    middle = layers // 2
    zero = jnp.zeros(shape, jnp.float32)

    def eliminate(k, coupling, carry):
        before, passed, value = carry
        new_passed, new_value = [], []
        for c in range(2):
            rest = side[c, k] + passed[c]
            pivot = coupling + rest
            guess = pl.reciprocal(pivot, approx=True)
            correct = 2.0 - pivot * guess
            new_passed.append((coupling * rest * guess) * correct)
            inv = guess * correct
            inverse[c, k] = inv
            ratio[c, k] = coupling * inv
            out = (rhs[c, k] + before * value[c]) * inv
            rhs[c, k] = out
            new_value.append(out)
        return coupling, tuple(new_passed), tuple(new_value)

    def lower_step(k, carry):
        return eliminate(k, coupling_of(k), carry)

    def upper_step(k, carry):
        return eliminate(k, coupling_of(k - 1), carry)

    def fronts(step, carry):
        lower, upper = carry
        return lower_step(step, lower), upper_step(layers - 1 - step, upper)

    def spread(first, body):
        def outward(step, carry):
            below, above = carry
            return body(middle - 1 - step, below), body(middle + 1 + step, above)

        below, above = repeat(plan, layers - 1 - middle, outward, (first, first))
        for k in range(2 * middle - layers, -1, -1):
            below = body(k, below)
        return below, above

    def sweep(keep):
        def stencil_body(k, carry):
            stencil(k, keep)
            return carry

        bed = tuple(2.0 * friction for _ in range(2))
        lower, upper = (zero, bed, (zero, zero)), (zero, (zero, zero), (zero, zero))
        if plan.unrolled:
            stencil(0, keep)
            stencil(layers - 1, keep)
            for step in range(layers - 1 - middle):
                stencil(step + 1, keep)
                if layers - 2 - step > step + 1:
                    stencil(layers - 2 - step, keep)
                lower, upper = fronts(step, (lower, upper))
        else:
            repeat(plan, layers, stencil_body)
            lower, upper = repeat(plan, layers - 1 - middle, fronts, (lower, upper))
        for k in range(layers - 1 - middle, middle):
            lower = lower_step(k, lower)
        centre_value = []
        for c in range(2):
            pivot = side[c, middle] + lower[1][c] + upper[1][c]
            guess = pl.reciprocal(pivot, approx=True)
            inv = guess * (2.0 - pivot * guess)
            inverse[c, middle] = inv
            total = rhs[c, middle] + (lower[0] * lower[2][c] + upper[0] * upper[2][c])
            centre_value.append(jnp.where(ice, total * inv, 0.0))
            field[c, middle] = centre_value[c]

        def solved(k, nearer):
            current = tuple(jnp.where(ice, rhs[c, k] + ratio[c, k] * nearer[c], 0.0) for c in range(2))
            for c in range(2):
                field[c, k] = current[c]
            return current

        return spread(tuple(centre_value), solved)

    sweep(False)
    base, top = sweep(True)

    def send(k, carry):
        both = jnp.where(centre, field[0, k], lane_roll(field[1, k], plan.cols))
        out_ref[pl.ds((k // here) * size * plan.out_rows + k % here, size, stride=plan.out_rows), :] = both
        return carry

    repeat(plan, layers, send)

    mismatch = [jnp.where(ice, top[c] - observed[c], 0.0) for c in range(2)]
    source = [(2.0 * layers) * mismatch[c] for c in range(2)]

    def side_sum(k, value):
        east, west, north, south = (faces[n, k] for n in range(4))
        u_east, u_west = x_pair(value[0], 0.0)
        v_east, v_west = x_pair(value[1], 0.0)
        u_north, u_south = y_pair(value[0])
        v_north, v_south = y_pair(value[1])
        first = 4.0 * (east * u_east + west * u_west) + (north * u_north + south * u_south)
        second = (east * v_east + west * v_west) + 4.0 * (north * v_north + south * v_south)
        return first, second

    carried = tuple(source[c] * inverse[c, layers - 1] for c in range(2))
    for c in range(2):
        rhs[c, layers - 1] = carried[c]

    def first_inward(step, carried):
        k = layers - 2 - step
        out = tuple(coupling_of(k) * carried[c] * inverse[c, k] for c in range(2))
        for c in range(2):
            rhs[c, k] = out[c]
        return out

    carried = repeat(plan, layers - 2 - middle, first_inward, carried)
    first_middle = tuple(coupling_of(middle) * carried[c] * inverse[c, middle] for c in range(2))

    def first_outward(step, carry):
        below, above = carry
        low, high = middle - 1 - step, middle + 1 + step
        below = tuple(ratio[c, low] * below[c] for c in range(2))
        above = tuple(rhs[c, high] + ratio[c, high] * above[c] for c in range(2))
        for k, value in ((low, below), (high, above)):
            total = side_sum(k, value)
            for c in range(2):
                rhs[c, k] = total[c] * inverse[c, k]
        return below, above

    middle_sum = side_sum(middle, first_middle)
    below, above = repeat(plan, layers - 1 - middle, first_outward, (first_middle, first_middle))
    for k in range(2 * middle - layers, -1, -1):
        below = tuple(ratio[c, k] * below[c] for c in range(2))
        total = side_sum(k, below)
        for c in range(2):
            rhs[c, k] = total[c] * inverse[c, k]
    for c in range(2):
        rhs[c, layers - 1] = rhs[c, layers - 1] + source[c] * inverse[c, layers - 1]

    def second_inward(step, carry):
        below, above = carry
        low, high = step + 1, layers - 2 - step
        below = tuple(rhs[c, low] + (coupling_of(low - 1) * inverse[c, low]) * below[c] for c in range(2))
        above = tuple(rhs[c, high] + (coupling_of(high) * inverse[c, high]) * above[c] for c in range(2))
        for c in range(2):
            rhs[c, low] = below[c]
        return below, above

    below, above = repeat(
        plan,
        layers - 2 - middle,
        second_inward,
        (tuple(rhs[c, 0] for c in range(2)), tuple(rhs[c, layers - 1] for c in range(2))),
    )
    for k in range(layers - 1 - middle, middle):
        below = tuple(rhs[c, k] + (coupling_of(k - 1) * inverse[c, k]) * below[c] for c in range(2))
        for c in range(2):
            rhs[c, k] = below[c]
    adjoint = tuple(
        (middle_sum[c] + (coupling_of(middle - 1) * below[c] + coupling_of(middle) * above[c])) * inverse[c, middle]
        for c in range(2)
    )

    def second_outward(step, nearer):
        k = middle - 1 - step
        return tuple(rhs[c, k] + ratio[c, k] * nearer[c] for c in range(2))

    adjoint = repeat(plan, middle, second_outward, adjoint)
    adjoint = [jnp.where(ice, adjoint[c], 0.0) for c in range(2)]
    gradient = -friction * (base[0] * adjoint[0] + base[1] * adjoint[1])

    def partial_sum(value):
        line = jnp.sum(jnp.where(centre, value, 0.0), axis=0, keepdims=True)
        folded = line
        for r in range(1, rows):
            folded = folded + lane_roll(line, r * width)
        return jnp.broadcast_to(lane_roll(folded, plan.cols), shape)

    misfit_line = partial_sum(mismatch[0] * mismatch[0] + mismatch[1] * mismatch[1])
    grad_line = partial_sum(gradient * gradient)
    in_first = jnp.logical_and(lane >= plan.halo + plan.cols, lane < plan.halo + 2 * plan.cols)
    last_row = jnp.where(centre, gradient, jnp.where(in_first, misfit_line, grad_line))
    for part in range(plan.layer_size):
        out_ref[pl.ds(part * size * plan.out_rows + here, size, stride=plan.out_rows), :] = last_row


def unpack_kernel(
    plan, in_ref, log_ref, vel_hbm, friction_hbm, misfit_hbm,
    vel_ref, friction_ref, misfit_ref, grad_ref, leave,
):
    here, width, cols, rows = plan.layers_here, plan.width, plan.cols, plan.rows
    local_chunks = plan.local_cols // LANES

    total = jnp.sum(
        in_ref[pl.ds(here, plan.devices, stride=plan.out_rows), :], axis=0, keepdims=True
    )
    line_lane = lax.broadcasted_iota(jnp.int32, (1, LANES), 1)

    def summed(first):
        ahead = (line_lane + (LANES - first % LANES)) % LANES
        return jnp.sum(jnp.where(ahead < cols, total, 0.0), axis=1, keepdims=True)

    misfit_sum = summed(plan.halo + cols)
    grad_sum = summed(plan.halo + cols + width)
    scale = step_size / jnp.sqrt(grad_sum / plan.column_count + 1e-06)

    lane = lax.broadcasted_iota(jnp.int32, (plan.out_rows, LANES), 1)
    def chunk(c, i):
        at = i * plan.per_chunk * plan.out_rows
        if not isinstance(at, int):
            at = pl.multiple_of(at, 8)
        turned = [
            lane_roll(in_ref[pl.ds(at + t * plan.out_rows, plan.out_rows), :], t * cols)
            for t in range(plan.per_chunk)
        ]
        for r in range(rows):
            start = r * width + plan.halo + c * cols
            ahead = (lane + (LANES - start % LANES)) % LANES
            row = turned[0]
            for t in range(1, plan.per_chunk):
                row = jnp.where(ahead >= t * cols, turned[t], row)
            row = lane_roll(row, -start)
            vel_ref[c, pl.ds(i * rows + r, here, stride=plan.chunks * rows), :] = row[:here]
            if c == 0:
                owner, step = i // local_chunks, i % local_chunks
                grad_ref[owner, pl.ds(step * rows + r, 1), :] = row[here : here + 1]

    out = [pltpu.make_async_copy(vel_ref.at[c], vel_hbm.at[c], leave.at[c]) for c in range(2)]
    out.append(pltpu.make_async_copy(friction_ref, friction_hbm, leave.at[2]))
    out.append(pltpu.make_async_copy(misfit_ref, misfit_hbm, leave.at[3]))
    for c in range(2):

        def chunk_body(i, carry):
            chunk(c, i)
            return carry

        repeat(plan, plan.chunks, chunk_body)
        out[c].start()
    friction_ref[...] = log_ref[...] - grad_ref[lax.axis_index("layer")] * scale
    out[2].start()
    misfit_ref[...] = 0.5 * misfit_sum / plan.column_count
    out[3].start()
    for copy in out:
        copy.wait()


def as_lines(x):
    chunked = x.reshape(x.shape[:-1] + (x.shape[-1] // LANES, LANES))
    return jnp.swapaxes(chunked, -3, -2).reshape(-1, LANES)


def from_lines(lines, shape):
    chunked = lines.reshape(shape[:-2] + (shape[-1] // LANES, shape[-2], LANES))
    return jnp.swapaxes(chunked, -3, -2).reshape(shape)


def on_device(mesh_shape, velocity_init, driving, observed, log_friction, ice_mask):
    plan = Plan(mesh_shape, velocity_init.shape)
    vmem = pl.BlockSpec(memory_space=pltpu.VMEM)
    hbm = pl.BlockSpec(memory_space=pltpu.HBM)
    f32 = jnp.float32
    limit = pltpu.CompilerParams(vmem_limit_bytes=(16 if plan.unrolled else 40) * MIB)
    inputs = [as_lines(x) for x in (velocity_init, driving, observed, log_friction, ice_mask)]

    def exchange(blocks):
        shaped = blocks.reshape(blocks.shape[0], 1, LANES)
        return lax.all_to_all(shaped, ("layer", "map"), split_axis=0, concat_axis=0, tiled=True).reshape(blocks.shape)

    packed = pl.pallas_call(
        functools.partial(pack_kernel, plan),
        out_shape=jax.ShapeDtypeStruct((plan.devices * plan.in_rows, LANES), f32),
        in_specs=[hbm] * 5,
        out_specs=vmem,
        scratch_shapes=[pltpu.VMEM(x.shape, x.dtype) for x in inputs]
        + [
            pltpu.SemaphoreType.DMA((VELOCITY_COPIES + 4,)),
        ],
        compiler_params=limit,
        name="pack",
    )(*(pltpu.with_memory_space_constraint(x, pltpu.HBM) for x in inputs))

    windows = exchange(packed)

    plane = (plan.layers, plan.map_size, LANES)
    solved = pl.pallas_call(
        functools.partial(solve_kernel, plan),
        out_shape=jax.ShapeDtypeStruct((plan.devices * plan.out_rows, LANES), f32),
        in_specs=[vmem],
        out_specs=vmem,
        scratch_shapes=[
            pltpu.VMEM((2,) + plane, f32),
            pltpu.VMEM(plane, f32),
            pltpu.VMEM((2,) + plane, f32),
            pltpu.VMEM((2,) + plane, f32),
            pltpu.VMEM((4,) + plane, f32),
            pltpu.VMEM((2,) + plane, f32),
            pltpu.VMEM((2,) + plane, f32),
        ],
        compiler_params=limit,
        name="solve",
    )(windows)

    back = exchange(solved)

    vel_lines, log_lines = inputs[0].reshape(2, -1, LANES), inputs[3]
    velocity, friction_new, misfit = pl.pallas_call(
        functools.partial(unpack_kernel, plan),
        out_shape=(
            jax.ShapeDtypeStruct(vel_lines.shape, f32),
            jax.ShapeDtypeStruct(log_lines.shape, f32),
            jax.ShapeDtypeStruct((1, 1), f32),
        ),
        in_specs=[vmem] * 2,
        out_specs=(hbm, hbm, hbm),
        scratch_shapes=[
            pltpu.VMEM(vel_lines.shape, f32),
            pltpu.VMEM(log_lines.shape, f32),
            pltpu.VMEM((1, 1), f32),
            pltpu.VMEM((plan.layer_size,) + log_lines.shape, f32),
            pltpu.SemaphoreType.DMA((4,)),
        ],
        compiler_params=limit,
        name="unpack",
    )(back, log_lines)
    return (
        from_lines(velocity, velocity_init.shape),
        from_lines(friction_new, log_friction.shape),
        misfit.reshape(()),
    )


def solution(mesh):
    in_specs = (
        P(None, "layer", "map", None),
        P(None, "map", "layer"),
        P(None, "map", "layer"),
        P("map", "layer"),
        P("map", "layer"),
    )
    out_specs = (P(None, "layer", "map", None), P("map", "layer"), P())
    return jax.shard_map(
        functools.partial(on_device, dict(mesh.shape)),
        mesh=mesh,
        in_specs=in_specs,
        out_specs=out_specs,
        check_vma=False,
    )
```

```python
import functools
import math

import jax
import jax.numpy as jnp
from jax import lax
from jax.experimental import pallas as pl
from jax.experimental.pallas import tpu as pltpu
from jax.sharding import PartitionSpec as P

strain_floor = 0.1
step_size = 0.5
LANES = 128
REACH = 5
BED_REACH = 3
MIB = 1 << 20
VELOCITY_COPIES = 4


class Plan:
    def __init__(self, mesh_shape, velocity_shape):
        self.map_size = mesh_shape["map"]
        self.layer_size = mesh_shape["layer"]
        self.devices = self.map_size * self.layer_size
        self.layers_here = velocity_shape[1]
        self.rows = velocity_shape[2]
        self.ny = velocity_shape[3]
        self.layers = self.layers_here * self.layer_size
        self.cols = self.ny // self.devices
        self.width = LANES // self.rows
        self.halo = (self.width - self.cols) // 2
        self.low = self.halo - REACH
        self.wide = self.cols + 2 * REACH
        self.half = self.wide // 2
        self.gap = self.low + self.wide
        self.local_cols = self.ny // self.layer_size
        self.per_chunk = LANES // self.cols
        self.chunks = self.ny // LANES
        self.column_count = self.rows * self.map_size * self.ny
        self.vel_rows = 2 * self.layers_here
        self.in_rows = self.vel_rows + 1
        self.left_at = self.gap
        self.right_at = self.gap + self.cols // 2 + 1
        self.out_rows = self.layers_here + 1
        self.unrolled = self.map_size <= 8
        assert self.width * self.rows == LANES and self.cols * self.per_chunk == LANES
        assert self.low >= 0 and self.wide % 2 == 0 and self.width - self.wide >= self.half
        assert 2 * self.cols <= self.width and self.local_cols % LANES == 0
        assert self.vel_rows == 8 and self.rows == 2 and 4 * self.cols <= LANES


def repeat(plan, count, body, carry=0):
    if plan.unrolled:
        for index in range(count):
            carry = body(index, carry)
        return carry
    return lax.fori_loop(0, count, body, carry)


def lane_roll(value, shift):
    shift = shift % LANES
    return value if shift == 0 else pltpu.roll(value, shift, 1)


def pack_kernel(
    plan, vel_hbm, driving_hbm, observed_hbm, log_hbm, mask_hbm, out_ref,
    vel_ref, driving_ref, observed_ref, log_ref, mask_ref, arrival,
):
    width, rows, cols, half = plan.width, plan.rows, plan.cols, plan.half
    piece = vel_ref.shape[0] // VELOCITY_COPIES
    spans = [pl.ds(n * piece, piece) for n in range(VELOCITY_COPIES)]
    pairs = [(vel_hbm.at[span, :], vel_ref.at[span, :]) for span in spans] + [
        (driving_hbm, driving_ref),
        (observed_hbm, observed_ref),
        (log_hbm, log_ref),
        (mask_hbm, mask_ref),
    ]
    copies = [pltpu.make_async_copy(pair[0], pair[1], arrival.at[n]) for n, pair in enumerate(pairs)]
    for copy in copies:
        copy.start()
    shape = (plan.vel_rows, LANES)
    lane = lax.broadcasted_iota(jnp.int32, shape, 1)
    sub = lax.broadcasted_iota(jnp.int32, shape, 0)
    in_gap = jnp.logical_not(jnp.logical_and(lane % width >= plan.low, lane % width < plan.gap))
    no_line = jnp.zeros((1, LANES), jnp.float32)

    def slide(part, start, length, place):
        step, offset = start // LANES, start % LANES
        value = part(step)
        if offset + length > LANES:
            after = part(step + 1)
            value = jnp.where(lax.broadcasted_iota(jnp.int32, value.shape, 1) >= offset, value, after)
        return lane_roll(value, place - offset)

    for copy in copies[:VELOCITY_COPIES]:
        copy.wait()

    def chunk_windows(i, carry):
        def velocity(r):
            def part(step):
                chunk = i + step
                if isinstance(chunk, int) and not 0 <= chunk < plan.chunks:
                    return jnp.zeros(shape, jnp.float32)
                at = chunk if isinstance(chunk, int) else jnp.clip(chunk, 0, plan.chunks - 1)
                value = vel_ref[pl.ds(at * rows + r, plan.vel_rows, stride=plan.chunks * rows), :]
                if isinstance(chunk, int):
                    return value
                return jnp.where(jnp.logical_and(chunk >= 0, chunk < plan.chunks), value, 0.0)

            return part

        for t in range(plan.per_chunk):
            block = None
            for r in range(rows):
                value = slide(velocity(r), plan.cols * t - plan.halo, width, r * width)
                block = value if block is None else jnp.where(lane >= r * width, value, block)
            at = (plan.chunks - 1 - i) * plan.per_chunk * plan.in_rows
            if not isinstance(at, int):
                at = pl.multiple_of(at, 8)
            at = at + (plan.per_chunk - 1 - t) * plan.in_rows
            out_ref[pl.ds(at, plan.vel_rows), :] = jnp.where(in_gap, 0.0, block)
            out_ref[pl.ds(at + plan.vel_rows, 1), :] = no_line
        return carry

    repeat(plan, plan.chunks, chunk_windows)
    for copy in copies[VELOCITY_COPIES:]:
        copy.wait()

    place = lax.axis_index("layer")
    local_chunks = plan.local_cols // LANES

    skip = local_chunks * rows
    no_block = jnp.zeros(shape, jnp.float32)

    def whole(ref, row):
        return jnp.broadcast_to(ref[row : row + 1, :], shape).astype(jnp.float32)

    def gap_part(r, step):
        at = step * rows + r
        observed = jnp.where(sub < 2, whole(observed_ref, at), whole(observed_ref, skip + at))
        return jnp.where(sub < 4, observed, jnp.where(sub < 6, whole(mask_ref, at), whole(log_ref, at)))

    def driving_part(r, step):
        at = step * rows + r
        return jnp.where(sub < 2, whole(driving_ref, at), whole(driving_ref, skip + at))

    def sequence(make):
        return [
            [no_block] + [make(r, step) for step in range(local_chunks)] + [no_block] for r in range(rows)
        ]

    gap_parts, driving_parts = sequence(gap_part), sequence(driving_part)
    own = plan.local_cols // cols
    spill = -(-REACH // cols)

    def column_block(q):
        start = q * cols
        block = None
        for r in range(rows):

            def in_gaps(step):
                return gap_parts[r][step + 1]

            def of_driving(step):
                return driving_parts[r][step + 1]

            at = r * width
            first = slide(in_gaps, start - REACH, half, (at + plan.gap) % LANES)
            second = slide(in_gaps, start - REACH + half, half, (at + plan.gap) % LANES)
            before = slide(of_driving, start - BED_REACH, BED_REACH, (at + plan.left_at) % LANES)
            after = slide(of_driving, start + cols, BED_REACH, (at + plan.right_at) % LANES)
            ahead = (lane + (LANES - plan.gap - at)) % LANES
            of_observed = sub < 4
            first = jnp.where(jnp.logical_and(of_observed, ahead < BED_REACH), before, first)
            second = jnp.where(jnp.logical_and(of_observed, ahead >= plan.right_at - plan.gap), after, second)
            value = jnp.where(sub % 2 == 0, first, second)
            ahead = (lane + (LANES - plan.gap)) % LANES
            block = value if block is None else jnp.where(ahead >= r * width, value, block)
        at = pl.multiple_of((plan.layer_size - 1 - place) * (own * plan.in_rows), 8) + (own - 1 - q) * plan.in_rows
        here = pl.ds(at, plan.vel_rows)
        out_ref[here, :] = jnp.where(in_gap, block, out_ref[here, :])
        if not 0 <= q < own:
            return
        line = None
        step, offset = start // LANES, start % LANES
        for r in range(rows):
            for c in range(2):
                row = c * skip + step * rows + r
                put = (2 * r + c) * cols
                value = lane_roll(driving_ref[row : row + 1, :], put - offset)
                line = value if line is None else jnp.where(lane[:1] >= put, value, line)
        out_ref[pl.ds(at + plan.vel_rows, 1), :] = line

    for q in range(own):
        column_block(q)

    @pl.when(place > 0)
    def _():
        for q in range(-spill, 0):
            column_block(q)

    @pl.when(place < plan.layer_size - 1)
    def _():
        for q in range(own, own + spill):
            column_block(q)


def solve_kernel(plan, in_ref, out_ref, field, eta_ref, side, rhs, faces, ratio, inverse):
    size, width, rows = plan.map_size, plan.width, plan.rows
    layers, here = plan.layers, plan.layers_here
    shape = (size, LANES)
    lane = lax.broadcasted_iota(jnp.int32, shape, 1)
    sub = lax.broadcasted_iota(jnp.int32, shape, 0)
    last_group = lane >= LANES - width
    first_group = lane < width
    x_end = jnp.logical_and(last_group, sub == 0)
    x_start = jnp.logical_and(first_group, sub == size - 1)

    def block_row(part, rows_of_block, row):
        first = (plan.layer_size - 1 - part) * size * rows_of_block
        return pl.ds(first + row, size, stride=rows_of_block)

    def arrived(part, row):
        return in_ref[block_row(part, plan.in_rows, row), :]

    def over_parts(row):
        total = arrived(0, row)
        for part in range(1, plan.layer_size):
            total = total + arrived(part, row)
        return total

    def moved(value, source, target):
        return lane_roll(value, target - source)

    def from_gap(halves):
        left, right = (moved(value, plan.gap, plan.low + h * plan.half) for h, value in enumerate(halves))
        return jnp.where(lane % width < plan.low + plan.half, left, right)

    def from_line(c):
        plane = None
        for r in range(rows):
            value = moved(line, (2 * r + c) * plan.cols, r * width + plan.halo)
            plane = value if plane is None else jnp.where(lane >= r * width, value, plane)
        return plane

    def driving_of(c, halves):
        left = moved(halves[0], plan.left_at, plan.halo - BED_REACH)
        right = moved(halves[1], plan.right_at, plan.halo + plan.cols)
        return jnp.where(centre, from_line(c), jnp.where(lane % width < plan.halo, left, right))

    def x_pair(value, edge):
        after = lane_roll(value, -width)
        before = after if 2 * width == LANES else lane_roll(value, width)
        after = jnp.where(last_group, pltpu.roll(after, 1, 0), after)
        before = jnp.where(first_group, pltpu.roll(before, size - 1, 0), before)
        return jnp.where(x_end, edge, after), jnp.where(x_start, edge, before)

    def y_pair(value):
        return lane_roll(value, -1), lane_roll(value, 1)

    def viscosity(rate):
        return jnp.exp2(jnp.log(strain_floor + rate) * (-1.0 / (3.0 * math.log(2.0))))

    for part in range(plan.layer_size):
        for c in range(2):
            for k in range(here):
                field[c, part * here + k] = arrived(part, c * here + k)
    line = over_parts(plan.vel_rows)
    gaps = [[over_parts(2 * n), over_parts(2 * n + 1)] for n in range(4)]
    reached = jnp.logical_and(lane % width >= plan.low, lane % width < plan.gap)
    centre = jnp.logical_and(lane % width >= plan.halo, lane % width < plan.halo + plan.cols)
    driving = [2.0 * driving_of(c, gaps[c]) for c in range(2)]
    observed = [from_gap(gaps[c]) for c in range(2)]
    mask = jnp.where(reached, from_gap(gaps[2]), 0.0)
    ice = mask != 0.0
    friction = jnp.where(mask == 1.0, jnp.exp(from_gap(gaps[3])), 0.0)

    def stencil(k, keep):
        u, v = field[0, k], field[1, k]
        u_east, u_west = x_pair(u, 0.0)
        v_east, v_west = x_pair(v, 0.0)
        u_north, u_south = y_pair(u)
        v_north, v_south = y_pair(v)
        stretch_x = u_east - u_west
        stretch_y = v_north - v_south
        shear = 0.5 * ((u_north - u_south) + (v_east - v_west))
        rate = 0.25 * (stretch_x * (stretch_x + stretch_y) + stretch_y * stretch_y + shear * shear)
        half_v = 0.5 * v
        eta = viscosity(rate)
        eta_edge = viscosity(0.25 * (u * u + half_v * half_v))
        eta_east, eta_west = x_pair(eta, eta_edge)
        eta_north, eta_south = y_pair(eta)
        east, west = eta + eta_east, eta + eta_west
        north, south = eta + eta_north, eta + eta_south
        along_x, along_y = east + west, north + south
        eta_ref[k] = eta
        side[0, k] = 4.0 * along_x + along_y
        side[1, k] = along_x + 4.0 * along_y
        rhs[0, k] = driving[0] + (4.0 * (east * u_east + west * u_west) + (north * u_north + south * u_south))
        rhs[1, k] = driving[1] + ((east * v_east + west * v_west) + 4.0 * (north * v_north + south * v_south))
        if keep:
            faces[0, k] = east
            faces[1, k] = west
            faces[2, k] = north
            faces[3, k] = south

    def coupling_of(k):
        return (2.0 * layers * layers) * (eta_ref[k] + eta_ref[k + 1])

    middle = layers // 2
    zero = jnp.zeros(shape, jnp.float32)

    def eliminate(k, coupling, carry):
        before, passed, value = carry
        new_passed, new_value = [], []
        for c in range(2):
            rest = side[c, k] + passed[c]
            pivot = coupling + rest
            guess = pl.reciprocal(pivot, approx=True)
            correct = 2.0 - pivot * guess
            new_passed.append((coupling * rest * guess) * correct)
            inv = guess * correct
            inverse[c, k] = inv
            ratio[c, k] = coupling * inv
            out = (rhs[c, k] + before * value[c]) * inv
            rhs[c, k] = out
            new_value.append(out)
        return coupling, tuple(new_passed), tuple(new_value)

    def lower_step(k, carry):
        return eliminate(k, coupling_of(k), carry)

    def upper_step(k, carry):
        return eliminate(k, coupling_of(k - 1), carry)

    def fronts(step, carry):
        lower, upper = carry
        return lower_step(step, lower), upper_step(layers - 1 - step, upper)

    def spread(first, body):
        def outward(step, carry):
            below, above = carry
            return body(middle - 1 - step, below), body(middle + 1 + step, above)

        below, above = repeat(plan, layers - 1 - middle, outward, (first, first))
        for k in range(2 * middle - layers, -1, -1):
            below = body(k, below)
        return below, above

    def sweep(keep):
        def stencil_body(k, carry):
            stencil(k, keep)
            return carry

        bed = tuple(2.0 * friction for _ in range(2))
        lower, upper = (zero, bed, (zero, zero)), (zero, (zero, zero), (zero, zero))
        if plan.unrolled:
            stencil(0, keep)
            stencil(layers - 1, keep)
            for step in range(layers - 1 - middle):
                stencil(step + 1, keep)
                if layers - 2 - step > step + 1:
                    stencil(layers - 2 - step, keep)
                lower, upper = fronts(step, (lower, upper))
        else:
            repeat(plan, layers, stencil_body)
            lower, upper = repeat(plan, layers - 1 - middle, fronts, (lower, upper))
        for k in range(layers - 1 - middle, middle):
            lower = lower_step(k, lower)
        centre_value = []
        for c in range(2):
            pivot = side[c, middle] + lower[1][c] + upper[1][c]
            guess = pl.reciprocal(pivot, approx=True)
            inv = guess * (2.0 - pivot * guess)
            inverse[c, middle] = inv
            total = rhs[c, middle] + (lower[0] * lower[2][c] + upper[0] * upper[2][c])
            centre_value.append(jnp.where(ice, total * inv, 0.0))
            field[c, middle] = centre_value[c]

        def solved(k, nearer):
            current = tuple(jnp.where(ice, rhs[c, k] + ratio[c, k] * nearer[c], 0.0) for c in range(2))
            for c in range(2):
                field[c, k] = current[c]
            return current

        return spread(tuple(centre_value), solved)

    sweep(False)
    base, top = sweep(True)

    def send(k, carry):
        both = jnp.where(centre, field[0, k], lane_roll(field[1, k], plan.cols))
        out_ref[block_row(k // here, plan.out_rows, k % here), :] = both
        return carry

    repeat(plan, layers, send)

    mismatch = [jnp.where(ice, top[c] - observed[c], 0.0) for c in range(2)]
    source = [(2.0 * layers) * mismatch[c] for c in range(2)]

    def side_sum(k, value):
        east, west, north, south = (faces[n, k] for n in range(4))
        u_east, u_west = x_pair(value[0], 0.0)
        v_east, v_west = x_pair(value[1], 0.0)
        u_north, u_south = y_pair(value[0])
        v_north, v_south = y_pair(value[1])
        first = 4.0 * (east * u_east + west * u_west) + (north * u_north + south * u_south)
        second = (east * v_east + west * v_west) + 4.0 * (north * v_north + south * v_south)
        return first, second

    carried = tuple(source[c] * inverse[c, layers - 1] for c in range(2))
    for c in range(2):
        rhs[c, layers - 1] = carried[c]

    def first_inward(step, carried):
        k = layers - 2 - step
        out = tuple(coupling_of(k) * carried[c] * inverse[c, k] for c in range(2))
        for c in range(2):
            rhs[c, k] = out[c]
        return out

    carried = repeat(plan, layers - 2 - middle, first_inward, carried)
    first_middle = tuple(coupling_of(middle) * carried[c] * inverse[c, middle] for c in range(2))

    def first_outward(step, carry):
        below, above = carry
        low, high = middle - 1 - step, middle + 1 + step
        below = tuple(ratio[c, low] * below[c] for c in range(2))
        above = tuple(rhs[c, high] + ratio[c, high] * above[c] for c in range(2))
        for k, value in ((low, below), (high, above)):
            total = side_sum(k, value)
            for c in range(2):
                rhs[c, k] = total[c] * inverse[c, k]
        return below, above

    middle_sum = side_sum(middle, first_middle)
    below, above = repeat(plan, layers - 1 - middle, first_outward, (first_middle, first_middle))
    for k in range(2 * middle - layers, -1, -1):
        below = tuple(ratio[c, k] * below[c] for c in range(2))
        total = side_sum(k, below)
        for c in range(2):
            rhs[c, k] = total[c] * inverse[c, k]
    for c in range(2):
        rhs[c, layers - 1] = rhs[c, layers - 1] + source[c] * inverse[c, layers - 1]

    def second_inward(step, carry):
        below, above = carry
        low, high = step + 1, layers - 2 - step
        below = tuple(rhs[c, low] + (coupling_of(low - 1) * inverse[c, low]) * below[c] for c in range(2))
        above = tuple(rhs[c, high] + (coupling_of(high) * inverse[c, high]) * above[c] for c in range(2))
        for c in range(2):
            rhs[c, low] = below[c]
        return below, above

    below, above = repeat(
        plan,
        layers - 2 - middle,
        second_inward,
        (tuple(rhs[c, 0] for c in range(2)), tuple(rhs[c, layers - 1] for c in range(2))),
    )
    for k in range(layers - 1 - middle, middle):
        below = tuple(rhs[c, k] + (coupling_of(k - 1) * inverse[c, k]) * below[c] for c in range(2))
        for c in range(2):
            rhs[c, k] = below[c]
    adjoint = tuple(
        (middle_sum[c] + (coupling_of(middle - 1) * below[c] + coupling_of(middle) * above[c])) * inverse[c, middle]
        for c in range(2)
    )

    def second_outward(step, nearer):
        k = middle - 1 - step
        return tuple(rhs[c, k] + ratio[c, k] * nearer[c] for c in range(2))

    adjoint = repeat(plan, middle, second_outward, adjoint)
    adjoint = [jnp.where(ice, adjoint[c], 0.0) for c in range(2)]
    gradient = -friction * (base[0] * adjoint[0] + base[1] * adjoint[1])

    def partial_sum(value):
        line = jnp.sum(jnp.where(centre, value, 0.0), axis=0, keepdims=True)
        folded = line
        for r in range(1, rows):
            folded = folded + lane_roll(line, r * width)
        return jnp.broadcast_to(lane_roll(folded, plan.cols), shape)

    misfit_line = partial_sum(mismatch[0] * mismatch[0] + mismatch[1] * mismatch[1])
    grad_line = partial_sum(gradient * gradient)
    in_first = jnp.logical_and(lane >= plan.halo + plan.cols, lane < plan.halo + 2 * plan.cols)
    last_row = jnp.where(centre, gradient, jnp.where(in_first, misfit_line, grad_line))
    for part in range(plan.layer_size):
        out_ref[block_row(part, plan.out_rows, here), :] = last_row


def unpack_kernel(
    plan, in_ref, log_ref, vel_hbm, friction_hbm, misfit_hbm,
    vel_ref, friction_ref, misfit_ref, grad_ref, leave,
):
    here, width, cols, rows = plan.layers_here, plan.width, plan.cols, plan.rows
    local_chunks = plan.local_cols // LANES

    total = jnp.sum(
        in_ref[pl.ds(here, plan.devices, stride=plan.out_rows), :], axis=0, keepdims=True
    )
    line_lane = lax.broadcasted_iota(jnp.int32, (1, LANES), 1)

    def summed(first):
        ahead = (line_lane + (LANES - first % LANES)) % LANES
        return jnp.sum(jnp.where(ahead < cols, total, 0.0), axis=1, keepdims=True)

    misfit_sum = summed(plan.halo + cols)
    grad_sum = summed(plan.halo + cols + width)
    scale = step_size / jnp.sqrt(grad_sum / plan.column_count + 1e-06)

    lane = lax.broadcasted_iota(jnp.int32, (plan.out_rows, LANES), 1)
    def chunk(c, i):
        at = (plan.chunks - 1 - i) * plan.per_chunk * plan.out_rows
        if not isinstance(at, int):
            at = pl.multiple_of(at, 8)
        turned = [
            lane_roll(in_ref[pl.ds(at + (plan.per_chunk - 1 - t) * plan.out_rows, plan.out_rows), :], t * cols)
            for t in range(plan.per_chunk)
        ]
        for r in range(rows):
            start = r * width + plan.halo + c * cols
            ahead = (lane + (LANES - start % LANES)) % LANES
            row = turned[0]
            for t in range(1, plan.per_chunk):
                row = jnp.where(ahead >= t * cols, turned[t], row)
            row = lane_roll(row, -start)
            vel_ref[c, pl.ds(i * rows + r, here, stride=plan.chunks * rows), :] = row[:here]
            if c == 0:
                owner, step = i // local_chunks, i % local_chunks
                grad_ref[owner, pl.ds(step * rows + r, 1), :] = row[here : here + 1]

    out = [pltpu.make_async_copy(vel_ref.at[c], vel_hbm.at[c], leave.at[c]) for c in range(2)]
    out.append(pltpu.make_async_copy(friction_ref, friction_hbm, leave.at[2]))
    out.append(pltpu.make_async_copy(misfit_ref, misfit_hbm, leave.at[3]))
    for c in range(2):

        def chunk_body(i, carry):
            chunk(c, i)
            return carry

        repeat(plan, plan.chunks, chunk_body)
        out[c].start()
    friction_ref[...] = log_ref[...] - grad_ref[lax.axis_index("layer")] * scale
    out[2].start()
    misfit_ref[...] = 0.5 * misfit_sum / plan.column_count
    out[3].start()
    for copy in out:
        copy.wait()


def as_lines(x):
    chunked = x.reshape(x.shape[:-1] + (x.shape[-1] // LANES, LANES))
    return jnp.swapaxes(chunked, -3, -2).reshape(-1, LANES)


def from_lines(lines, shape):
    chunked = lines.reshape(shape[:-2] + (shape[-1] // LANES, shape[-2], LANES))
    return jnp.swapaxes(chunked, -3, -2).reshape(shape)


def on_device(mesh_shape, velocity_init, driving, observed, log_friction, ice_mask):
    plan = Plan(mesh_shape, velocity_init.shape)
    vmem = pl.BlockSpec(memory_space=pltpu.VMEM)
    hbm = pl.BlockSpec(memory_space=pltpu.HBM)
    f32 = jnp.float32
    limit = pltpu.CompilerParams(vmem_limit_bytes=(16 if plan.unrolled else 40) * MIB)
    inputs = [as_lines(x) for x in (velocity_init, driving, observed, log_friction, ice_mask)]

    def exchange(blocks):
        shaped = blocks.reshape(blocks.shape[0], 1, LANES)
        ranks = [
            m * plan.layer_size + part
            for part in reversed(range(plan.layer_size))
            for m in reversed(range(plan.map_size))
        ]
        return lax.all_to_all(
            shaped, ("map", "layer"), split_axis=0, concat_axis=0, tiled=True, axis_index_groups=[ranks]
        ).reshape(blocks.shape)

    packed = pl.pallas_call(
        functools.partial(pack_kernel, plan),
        out_shape=jax.ShapeDtypeStruct((plan.devices * plan.in_rows, LANES), f32),
        in_specs=[hbm] * 5,
        out_specs=vmem,
        scratch_shapes=[pltpu.VMEM(x.shape, x.dtype) for x in inputs]
        + [
            pltpu.SemaphoreType.DMA((VELOCITY_COPIES + 4,)),
        ],
        compiler_params=limit,
        name="pack",
    )(*(pltpu.with_memory_space_constraint(x, pltpu.HBM) for x in inputs))

    windows = exchange(packed)

    plane = (plan.layers, plan.map_size, LANES)
    solved = pl.pallas_call(
        functools.partial(solve_kernel, plan),
        out_shape=jax.ShapeDtypeStruct((plan.devices * plan.out_rows, LANES), f32),
        in_specs=[vmem],
        out_specs=vmem,
        scratch_shapes=[
            pltpu.VMEM((2,) + plane, f32),
            pltpu.VMEM(plane, f32),
            pltpu.VMEM((2,) + plane, f32),
            pltpu.VMEM((2,) + plane, f32),
            pltpu.VMEM((4,) + plane, f32),
            pltpu.VMEM((2,) + plane, f32),
            pltpu.VMEM((2,) + plane, f32),
        ],
        compiler_params=limit,
        name="solve",
    )(windows)

    back = exchange(solved)

    vel_lines, log_lines = inputs[0].reshape(2, -1, LANES), inputs[3]
    velocity, friction_new, misfit = pl.pallas_call(
        functools.partial(unpack_kernel, plan),
        out_shape=(
            jax.ShapeDtypeStruct(vel_lines.shape, f32),
            jax.ShapeDtypeStruct(log_lines.shape, f32),
            jax.ShapeDtypeStruct((1, 1), f32),
        ),
        in_specs=[vmem] * 2,
        out_specs=(hbm, hbm, hbm),
        scratch_shapes=[
            pltpu.VMEM(vel_lines.shape, f32),
            pltpu.VMEM(log_lines.shape, f32),
            pltpu.VMEM((1, 1), f32),
            pltpu.VMEM((plan.layer_size,) + log_lines.shape, f32),
            pltpu.SemaphoreType.DMA((4,)),
        ],
        compiler_params=limit,
        name="unpack",
    )(back, log_lines)
    return (
        from_lines(velocity, velocity_init.shape),
        from_lines(friction_new, log_friction.shape),
        misfit.reshape(()),
    )


def solution(mesh):
    in_specs = (
        P(None, "layer", "map", None),
        P(None, "map", "layer"),
        P(None, "map", "layer"),
        P("map", "layer"),
        P("map", "layer"),
    )
    out_specs = (P(None, "layer", "map", None), P("map", "layer"), P())
    return jax.shard_map(
        functools.partial(on_device, dict(mesh.shape)),
        mesh=mesh,
        in_specs=in_specs,
        out_specs=out_specs,
        check_vma=False,
    )
```

```python
import functools
import math

import jax
import jax.numpy as jnp
from jax import lax
from jax.experimental import pallas as pl
from jax.experimental.pallas import tpu as pltpu
from jax.sharding import PartitionSpec as P

strain_floor = 0.1
step_size = 0.5
LANES = 128
REACH = 5
BED_REACH = 3
PAD = 8
MIB = 1 << 20
VELOCITY_COPIES = 4


class Plan:
    def __init__(self, mesh_shape, velocity_shape):
        self.map_size = mesh_shape["map"]
        self.layer_size = mesh_shape["layer"]
        self.devices = self.map_size * self.layer_size
        self.layers_here = velocity_shape[1]
        self.rows = velocity_shape[2]
        self.ny = velocity_shape[3]
        self.layers = self.layers_here * self.layer_size
        self.cols = self.ny // self.devices
        self.width = LANES // self.rows
        self.halo = (self.width - self.cols) // 2
        self.low = self.halo - REACH
        self.wide = self.cols + 2 * REACH
        self.half = self.wide // 2
        self.gap = self.low + self.wide
        self.local_cols = self.ny // self.layer_size
        self.per_chunk = LANES // self.cols
        self.chunks = self.ny // LANES
        self.column_count = self.rows * self.map_size * self.ny
        self.vel_rows = 2 * self.layers_here
        self.in_rows = self.vel_rows + 1
        self.left_at = self.gap
        self.right_at = self.gap + self.cols // 2 + 1
        self.out_rows = self.layers_here + 1
        self.unrolled = self.map_size <= 8
        assert self.width * self.rows == LANES and self.cols * self.per_chunk == LANES
        assert self.low >= 0 and self.wide % 2 == 0 and self.width - self.wide >= self.half
        assert 2 * self.cols <= self.width and self.local_cols % LANES == 0
        assert self.vel_rows == 8 and self.rows == 2 and 4 * self.cols <= LANES and self.map_size % 8 == 0


def repeat(plan, count, body, carry=0):
    if plan.unrolled:
        for index in range(count):
            carry = body(index, carry)
        return carry
    return lax.fori_loop(0, count, body, carry)


def lane_roll(value, shift):
    shift = shift % LANES
    return value if shift == 0 else pltpu.roll(value, shift, 1)


def pack_kernel(
    plan, vel_hbm, driving_hbm, observed_hbm, log_hbm, mask_hbm, out_ref,
    vel_ref, driving_ref, observed_ref, log_ref, mask_ref, arrival,
):
    width, rows, cols, half = plan.width, plan.rows, plan.cols, plan.half
    piece = vel_ref.shape[0] // VELOCITY_COPIES
    spans = [pl.ds(n * piece, piece) for n in range(VELOCITY_COPIES)]
    pairs = [(vel_hbm.at[span, :], vel_ref.at[span, :]) for span in spans] + [
        (driving_hbm, driving_ref),
        (observed_hbm, observed_ref),
        (log_hbm, log_ref),
        (mask_hbm, mask_ref),
    ]
    copies = [pltpu.make_async_copy(pair[0], pair[1], arrival.at[n]) for n, pair in enumerate(pairs)]
    for copy in copies:
        copy.start()
    shape = (plan.vel_rows, LANES)
    lane = lax.broadcasted_iota(jnp.int32, shape, 1)
    sub = lax.broadcasted_iota(jnp.int32, shape, 0)
    in_gap = jnp.logical_not(jnp.logical_and(lane % width >= plan.low, lane % width < plan.gap))
    no_line = jnp.zeros((1, LANES), jnp.float32)

    def slide(part, start, length, place):
        step, offset = start // LANES, start % LANES
        value = part(step)
        if offset + length > LANES:
            after = part(step + 1)
            value = jnp.where(lax.broadcasted_iota(jnp.int32, value.shape, 1) >= offset, value, after)
        return lane_roll(value, place - offset)

    for copy in copies[:VELOCITY_COPIES]:
        copy.wait()

    def chunk_windows(i, carry):
        def velocity(r):
            def part(step):
                chunk = i + step
                if isinstance(chunk, int) and not 0 <= chunk < plan.chunks:
                    return jnp.zeros(shape, jnp.float32)
                at = chunk if isinstance(chunk, int) else jnp.clip(chunk, 0, plan.chunks - 1)
                value = vel_ref[pl.ds(at * rows + r, plan.vel_rows, stride=plan.chunks * rows), :]
                if isinstance(chunk, int):
                    return value
                return jnp.where(jnp.logical_and(chunk >= 0, chunk < plan.chunks), value, 0.0)

            return part

        for t in range(plan.per_chunk):
            block = None
            for r in range(rows):
                value = slide(velocity(r), plan.cols * t - plan.halo, width, r * width)
                block = value if block is None else jnp.where(lane >= r * width, value, block)
            at = (plan.chunks - 1 - i) * plan.per_chunk * plan.in_rows
            if not isinstance(at, int):
                at = pl.multiple_of(at, 8)
            at = at + (plan.per_chunk - 1 - t) * plan.in_rows
            out_ref[pl.ds(at, plan.vel_rows), :] = jnp.where(in_gap, 0.0, block)
            out_ref[pl.ds(at + plan.vel_rows, 1), :] = no_line
        return carry

    repeat(plan, plan.chunks, chunk_windows)
    for copy in copies[VELOCITY_COPIES:]:
        copy.wait()

    place = lax.axis_index("layer")
    local_chunks = plan.local_cols // LANES

    skip = local_chunks * rows
    no_block = jnp.zeros(shape, jnp.float32)

    def whole(ref, row):
        return jnp.broadcast_to(ref[row : row + 1, :], shape).astype(jnp.float32)

    def gap_part(r, step):
        at = step * rows + r
        observed = jnp.where(sub < 2, whole(observed_ref, at), whole(observed_ref, skip + at))
        return jnp.where(sub < 4, observed, jnp.where(sub < 6, whole(mask_ref, at), whole(log_ref, at)))

    def driving_part(r, step):
        at = step * rows + r
        return jnp.where(sub < 2, whole(driving_ref, at), whole(driving_ref, skip + at))

    def sequence(make):
        return [
            [no_block] + [make(r, step) for step in range(local_chunks)] + [no_block] for r in range(rows)
        ]

    gap_parts, driving_parts = sequence(gap_part), sequence(driving_part)
    own = plan.local_cols // cols
    spill = -(-REACH // cols)

    def column_block(q):
        start = q * cols
        block = None
        for r in range(rows):

            def in_gaps(step):
                return gap_parts[r][step + 1]

            def of_driving(step):
                return driving_parts[r][step + 1]

            at = r * width
            first = slide(in_gaps, start - REACH, half, (at + plan.gap) % LANES)
            second = slide(in_gaps, start - REACH + half, half, (at + plan.gap) % LANES)
            before = slide(of_driving, start - BED_REACH, BED_REACH, (at + plan.left_at) % LANES)
            after = slide(of_driving, start + cols, BED_REACH, (at + plan.right_at) % LANES)
            ahead = (lane + (LANES - plan.gap - at)) % LANES
            of_observed = sub < 4
            first = jnp.where(jnp.logical_and(of_observed, ahead < BED_REACH), before, first)
            second = jnp.where(jnp.logical_and(of_observed, ahead >= plan.right_at - plan.gap), after, second)
            value = jnp.where(sub % 2 == 0, first, second)
            ahead = (lane + (LANES - plan.gap)) % LANES
            block = value if block is None else jnp.where(ahead >= r * width, value, block)
        at = pl.multiple_of((plan.layer_size - 1 - place) * (own * plan.in_rows), 8) + (own - 1 - q) * plan.in_rows
        here = pl.ds(at, plan.vel_rows)
        out_ref[here, :] = jnp.where(in_gap, block, out_ref[here, :])
        if not 0 <= q < own:
            return
        line = None
        step, offset = start // LANES, start % LANES
        for r in range(rows):
            for c in range(2):
                row = c * skip + step * rows + r
                put = (2 * r + c) * cols
                value = lane_roll(driving_ref[row : row + 1, :], put - offset)
                line = value if line is None else jnp.where(lane[:1] >= put, value, line)
        out_ref[pl.ds(at + plan.vel_rows, 1), :] = line

    for q in range(own):
        column_block(q)

    @pl.when(place > 0)
    def _():
        for q in range(-spill, 0):
            column_block(q)

    @pl.when(place < plan.layer_size - 1)
    def _():
        for q in range(own, own + spill):
            column_block(q)


def solve_kernel(plan, in_ref, out_ref, field, eta_ref, side, rhs, faces, ratio, inverse, swapped, eta_swapped):
    size, width, rows = plan.map_size, plan.width, plan.rows
    layers, here = plan.layers, plan.layers_here
    shape = (size, LANES)
    lane = lax.broadcasted_iota(jnp.int32, shape, 1)
    last_group = lane >= LANES - width
    first_group = lane < width
    def block_row(part, rows_of_block, row):
        first = (plan.layer_size - 1 - part) * size * rows_of_block
        return pl.ds(first + row, size, stride=rows_of_block)

    def arrived(part, row):
        return in_ref[block_row(part, plan.in_rows, row), :]

    def over_parts(row):
        total = arrived(0, row)
        for part in range(1, plan.layer_size):
            total = total + arrived(part, row)
        return total

    def moved(value, source, target):
        return lane_roll(value, target - source)

    def from_gap(halves):
        left, right = (moved(value, plan.gap, plan.low + h * plan.half) for h, value in enumerate(halves))
        return jnp.where(lane % width < plan.low + plan.half, left, right)

    def from_line(c):
        plane = None
        for r in range(rows):
            value = moved(line, (2 * r + c) * plan.cols, r * width + plan.halo)
            plane = value if plane is None else jnp.where(lane >= r * width, value, plane)
        return plane

    def driving_of(c, halves):
        left = moved(halves[0], plan.left_at, plan.halo - BED_REACH)
        right = moved(halves[1], plan.right_at, plan.halo + plan.cols)
        return jnp.where(centre, from_line(c), jnp.where(lane % width < plan.halo, left, right))

    body = pl.ds(PAD, size)

    def x_pair(ref, index):
        same = ref[index + (body,)]
        after = jnp.where(last_group, ref[index + (pl.ds(PAD - 1, size),)], same)
        before = jnp.where(first_group, ref[index + (pl.ds(PAD + 1, size),)], same)
        return after, before

    def swap_in(c, k, value):
        swapped[c, k, body] = lane_roll(value, width)

    edge = jnp.zeros((2, layers, PAD, LANES), jnp.float32)
    swapped[:, :, pl.ds(0, PAD)] = edge
    swapped[:, :, pl.ds(PAD + size, PAD)] = edge

    def y_pair(value):
        return lane_roll(value, -1), lane_roll(value, 1)

    def viscosity(rate):
        return jnp.exp2(jnp.log(strain_floor + rate) * (-1.0 / (3.0 * math.log(2.0))))

    for part in range(plan.layer_size):
        for c in range(2):
            for k in range(here):
                value = arrived(part, c * here + k)
                field[c, part * here + k] = value
                swap_in(c, part * here + k, value)
    line = over_parts(plan.vel_rows)
    gaps = [[over_parts(2 * n), over_parts(2 * n + 1)] for n in range(4)]
    reached = jnp.logical_and(lane % width >= plan.low, lane % width < plan.gap)
    centre = jnp.logical_and(lane % width >= plan.halo, lane % width < plan.halo + plan.cols)
    driving = [2.0 * driving_of(c, gaps[c]) for c in range(2)]
    observed = [from_gap(gaps[c]) for c in range(2)]
    mask = jnp.where(reached, from_gap(gaps[2]), 0.0)
    ice = mask != 0.0
    friction = jnp.where(mask == 1.0, jnp.exp(from_gap(gaps[3])), 0.0)

    def stencil(k, keep):
        u, v = field[0, k], field[1, k]
        u_east, u_west = x_pair(swapped, (0, k))
        v_east, v_west = x_pair(swapped, (1, k))
        u_north, u_south = y_pair(u)
        v_north, v_south = y_pair(v)
        stretch_x = u_east - u_west
        stretch_y = v_north - v_south
        shear = 0.5 * ((u_north - u_south) + (v_east - v_west))
        rate = 0.25 * (stretch_x * (stretch_x + stretch_y) + stretch_y * stretch_y + shear * shear)
        half_v = 0.5 * v
        eta = viscosity(rate)
        eta_edge = viscosity(0.25 * (u * u + half_v * half_v))
        eta_swapped[k, body] = lane_roll(eta, width)
        eta_swapped[k, pl.ds(PAD - 1, 1)] = eta_edge[:1]
        eta_swapped[k, pl.ds(PAD + size, 1)] = eta_edge[size - 1 :]
        eta_east, eta_west = x_pair(eta_swapped, (k,))
        eta_north, eta_south = y_pair(eta)
        east, west = eta + eta_east, eta + eta_west
        north, south = eta + eta_north, eta + eta_south
        along_x, along_y = east + west, north + south
        eta_ref[k] = eta
        side[0, k] = 4.0 * along_x + along_y
        side[1, k] = along_x + 4.0 * along_y
        rhs[0, k] = driving[0] + (4.0 * (east * u_east + west * u_west) + (north * u_north + south * u_south))
        rhs[1, k] = driving[1] + ((east * v_east + west * v_west) + 4.0 * (north * v_north + south * v_south))
        if keep:
            faces[0, k] = east
            faces[1, k] = west
            faces[2, k] = north
            faces[3, k] = south

    def coupling_of(k):
        return (2.0 * layers * layers) * (eta_ref[k] + eta_ref[k + 1])

    middle = layers // 2
    zero = jnp.zeros(shape, jnp.float32)

    def eliminate(k, coupling, carry):
        before, passed, value = carry
        new_passed, new_value = [], []
        for c in range(2):
            rest = side[c, k] + passed[c]
            pivot = coupling + rest
            guess = pl.reciprocal(pivot, approx=True)
            correct = 2.0 - pivot * guess
            new_passed.append((coupling * rest * guess) * correct)
            inv = guess * correct
            inverse[c, k] = inv
            ratio[c, k] = coupling * inv
            out = (rhs[c, k] + before * value[c]) * inv
            rhs[c, k] = out
            new_value.append(out)
        return coupling, tuple(new_passed), tuple(new_value)

    def lower_step(k, carry):
        return eliminate(k, coupling_of(k), carry)

    def upper_step(k, carry):
        return eliminate(k, coupling_of(k - 1), carry)

    def fronts(step, carry):
        lower, upper = carry
        return lower_step(step, lower), upper_step(layers - 1 - step, upper)

    def spread(first, body):
        def outward(step, carry):
            below, above = carry
            return body(middle - 1 - step, below), body(middle + 1 + step, above)

        below, above = repeat(plan, layers - 1 - middle, outward, (first, first))
        for k in range(2 * middle - layers, -1, -1):
            below = body(k, below)
        return below, above

    def sweep(keep):
        def stencil_body(k, carry):
            stencil(k, keep)
            return carry

        bed = tuple(2.0 * friction for _ in range(2))
        lower, upper = (zero, bed, (zero, zero)), (zero, (zero, zero), (zero, zero))
        if plan.unrolled:
            stencil(0, keep)
            stencil(layers - 1, keep)
            for step in range(layers - 1 - middle):
                stencil(step + 1, keep)
                if layers - 2 - step > step + 1:
                    stencil(layers - 2 - step, keep)
                lower, upper = fronts(step, (lower, upper))
        else:
            repeat(plan, layers, stencil_body)
            lower, upper = repeat(plan, layers - 1 - middle, fronts, (lower, upper))
        for k in range(layers - 1 - middle, middle):
            lower = lower_step(k, lower)
        centre_value = []
        for c in range(2):
            pivot = side[c, middle] + lower[1][c] + upper[1][c]
            guess = pl.reciprocal(pivot, approx=True)
            inv = guess * (2.0 - pivot * guess)
            inverse[c, middle] = inv
            total = rhs[c, middle] + (lower[0] * lower[2][c] + upper[0] * upper[2][c])
            centre_value.append(jnp.where(ice, total * inv, 0.0))
            field[c, middle] = centre_value[c]
            swap_in(c, middle, centre_value[c])

        def solved(k, nearer):
            current = tuple(jnp.where(ice, rhs[c, k] + ratio[c, k] * nearer[c], 0.0) for c in range(2))
            for c in range(2):
                field[c, k] = current[c]
                swap_in(c, k, current[c])
            return current

        return spread(tuple(centre_value), solved)

    sweep(False)
    base, top = sweep(True)

    def send(k, carry):
        both = jnp.where(centre, field[0, k], lane_roll(field[1, k], plan.cols))
        out_ref[block_row(k // here, plan.out_rows, k % here), :] = both
        return carry

    repeat(plan, layers, send)

    mismatch = [jnp.where(ice, top[c] - observed[c], 0.0) for c in range(2)]
    source = [(2.0 * layers) * mismatch[c] for c in range(2)]

    def side_sum(k, value):
        east, west, north, south = (faces[n, k] for n in range(4))
        for c in range(2):
            swap_in(c, k, value[c])
        u_east, u_west = x_pair(swapped, (0, k))
        v_east, v_west = x_pair(swapped, (1, k))
        u_north, u_south = y_pair(value[0])
        v_north, v_south = y_pair(value[1])
        first = 4.0 * (east * u_east + west * u_west) + (north * u_north + south * u_south)
        second = (east * v_east + west * v_west) + 4.0 * (north * v_north + south * v_south)
        return first, second

    carried = tuple(source[c] * inverse[c, layers - 1] for c in range(2))
    for c in range(2):
        rhs[c, layers - 1] = carried[c]

    def first_inward(step, carried):
        k = layers - 2 - step
        out = tuple(coupling_of(k) * carried[c] * inverse[c, k] for c in range(2))
        for c in range(2):
            rhs[c, k] = out[c]
        return out

    carried = repeat(plan, layers - 2 - middle, first_inward, carried)
    first_middle = tuple(coupling_of(middle) * carried[c] * inverse[c, middle] for c in range(2))

    def first_outward(step, carry):
        below, above = carry
        low, high = middle - 1 - step, middle + 1 + step
        below = tuple(ratio[c, low] * below[c] for c in range(2))
        above = tuple(rhs[c, high] + ratio[c, high] * above[c] for c in range(2))
        for k, value in ((low, below), (high, above)):
            total = side_sum(k, value)
            for c in range(2):
                rhs[c, k] = total[c] * inverse[c, k]
        return below, above

    middle_sum = side_sum(middle, first_middle)
    below, above = repeat(plan, layers - 1 - middle, first_outward, (first_middle, first_middle))
    for k in range(2 * middle - layers, -1, -1):
        below = tuple(ratio[c, k] * below[c] for c in range(2))
        total = side_sum(k, below)
        for c in range(2):
            rhs[c, k] = total[c] * inverse[c, k]
    for c in range(2):
        rhs[c, layers - 1] = rhs[c, layers - 1] + source[c] * inverse[c, layers - 1]

    def second_inward(step, carry):
        below, above = carry
        low, high = step + 1, layers - 2 - step
        below = tuple(rhs[c, low] + (coupling_of(low - 1) * inverse[c, low]) * below[c] for c in range(2))
        above = tuple(rhs[c, high] + (coupling_of(high) * inverse[c, high]) * above[c] for c in range(2))
        for c in range(2):
            rhs[c, low] = below[c]
        return below, above

    below, above = repeat(
        plan,
        layers - 2 - middle,
        second_inward,
        (tuple(rhs[c, 0] for c in range(2)), tuple(rhs[c, layers - 1] for c in range(2))),
    )
    for k in range(layers - 1 - middle, middle):
        below = tuple(rhs[c, k] + (coupling_of(k - 1) * inverse[c, k]) * below[c] for c in range(2))
        for c in range(2):
            rhs[c, k] = below[c]
    adjoint = tuple(
        (middle_sum[c] + (coupling_of(middle - 1) * below[c] + coupling_of(middle) * above[c])) * inverse[c, middle]
        for c in range(2)
    )

    def second_outward(step, nearer):
        k = middle - 1 - step
        return tuple(rhs[c, k] + ratio[c, k] * nearer[c] for c in range(2))

    adjoint = repeat(plan, middle, second_outward, adjoint)
    adjoint = [jnp.where(ice, adjoint[c], 0.0) for c in range(2)]
    gradient = -friction * (base[0] * adjoint[0] + base[1] * adjoint[1])

    def partial_sum(value):
        line = jnp.sum(jnp.where(centre, value, 0.0), axis=0, keepdims=True)
        folded = line
        for r in range(1, rows):
            folded = folded + lane_roll(line, r * width)
        return jnp.broadcast_to(lane_roll(folded, plan.cols), shape)

    misfit_line = partial_sum(mismatch[0] * mismatch[0] + mismatch[1] * mismatch[1])
    grad_line = partial_sum(gradient * gradient)
    in_first = jnp.logical_and(lane >= plan.halo + plan.cols, lane < plan.halo + 2 * plan.cols)
    last_row = jnp.where(centre, gradient, jnp.where(in_first, misfit_line, grad_line))
    for part in range(plan.layer_size):
        out_ref[block_row(part, plan.out_rows, here), :] = last_row


def unpack_kernel(
    plan, in_ref, log_ref, vel_hbm, friction_hbm, misfit_hbm,
    vel_ref, friction_ref, misfit_ref, grad_ref, leave,
):
    here, width, cols, rows = plan.layers_here, plan.width, plan.cols, plan.rows
    local_chunks = plan.local_cols // LANES

    total = jnp.sum(
        in_ref[pl.ds(here, plan.devices, stride=plan.out_rows), :], axis=0, keepdims=True
    )
    line_lane = lax.broadcasted_iota(jnp.int32, (1, LANES), 1)

    def summed(first):
        ahead = (line_lane + (LANES - first % LANES)) % LANES
        return jnp.sum(jnp.where(ahead < cols, total, 0.0), axis=1, keepdims=True)

    misfit_sum = summed(plan.halo + cols)
    grad_sum = summed(plan.halo + cols + width)
    scale = step_size / jnp.sqrt(grad_sum / plan.column_count + 1e-06)

    lane = lax.broadcasted_iota(jnp.int32, (plan.out_rows, LANES), 1)
    def chunk(c, i):
        at = (plan.chunks - 1 - i) * plan.per_chunk * plan.out_rows
        if not isinstance(at, int):
            at = pl.multiple_of(at, 8)
        turned = [
            lane_roll(in_ref[pl.ds(at + (plan.per_chunk - 1 - t) * plan.out_rows, plan.out_rows), :], t * cols)
            for t in range(plan.per_chunk)
        ]
        for r in range(rows):
            start = r * width + plan.halo + c * cols
            ahead = (lane + (LANES - start % LANES)) % LANES
            row = turned[0]
            for t in range(1, plan.per_chunk):
                row = jnp.where(ahead >= t * cols, turned[t], row)
            row = lane_roll(row, -start)
            vel_ref[c, pl.ds(i * rows + r, here, stride=plan.chunks * rows), :] = row[:here]
            if c == 0:
                owner, step = i // local_chunks, i % local_chunks
                grad_ref[owner, pl.ds(step * rows + r, 1), :] = row[here : here + 1]

    out = [pltpu.make_async_copy(vel_ref.at[c], vel_hbm.at[c], leave.at[c]) for c in range(2)]
    out.append(pltpu.make_async_copy(friction_ref, friction_hbm, leave.at[2]))
    out.append(pltpu.make_async_copy(misfit_ref, misfit_hbm, leave.at[3]))
    for c in range(2):

        def chunk_body(i, carry):
            chunk(c, i)
            return carry

        repeat(plan, plan.chunks, chunk_body)
        out[c].start()
    friction_ref[...] = log_ref[...] - grad_ref[lax.axis_index("layer")] * scale
    out[2].start()
    misfit_ref[...] = 0.5 * misfit_sum / plan.column_count
    out[3].start()
    for copy in out:
        copy.wait()


def as_lines(x):
    chunked = x.reshape(x.shape[:-1] + (x.shape[-1] // LANES, LANES))
    return jnp.swapaxes(chunked, -3, -2).reshape(-1, LANES)


def from_lines(lines, shape):
    chunked = lines.reshape(shape[:-2] + (shape[-1] // LANES, shape[-2], LANES))
    return jnp.swapaxes(chunked, -3, -2).reshape(shape)


def on_device(mesh_shape, velocity_init, driving, observed, log_friction, ice_mask):
    plan = Plan(mesh_shape, velocity_init.shape)
    vmem = pl.BlockSpec(memory_space=pltpu.VMEM)
    hbm = pl.BlockSpec(memory_space=pltpu.HBM)
    f32 = jnp.float32
    limit = pltpu.CompilerParams(vmem_limit_bytes=(16 if plan.unrolled else 40) * MIB)
    inputs = [as_lines(x) for x in (velocity_init, driving, observed, log_friction, ice_mask)]

    def exchange(blocks):
        shaped = blocks.reshape(blocks.shape[0], 1, LANES)
        ranks = [
            m * plan.layer_size + part
            for part in reversed(range(plan.layer_size))
            for m in reversed(range(plan.map_size))
        ]
        return lax.all_to_all(
            shaped, ("map", "layer"), split_axis=0, concat_axis=0, tiled=True, axis_index_groups=[ranks]
        ).reshape(blocks.shape)

    packed = pl.pallas_call(
        functools.partial(pack_kernel, plan),
        out_shape=jax.ShapeDtypeStruct((plan.devices * plan.in_rows, LANES), f32),
        in_specs=[hbm] * 5,
        out_specs=vmem,
        scratch_shapes=[pltpu.VMEM(x.shape, x.dtype) for x in inputs]
        + [
            pltpu.SemaphoreType.DMA((VELOCITY_COPIES + 4,)),
        ],
        compiler_params=limit,
        name="pack",
    )(*(pltpu.with_memory_space_constraint(x, pltpu.HBM) for x in inputs))

    windows = exchange(packed)

    plane = (plan.layers, plan.map_size, LANES)
    solved = pl.pallas_call(
        functools.partial(solve_kernel, plan),
        out_shape=jax.ShapeDtypeStruct((plan.devices * plan.out_rows, LANES), f32),
        in_specs=[vmem],
        out_specs=vmem,
        scratch_shapes=[
            pltpu.VMEM((2,) + plane, f32),
            pltpu.VMEM(plane, f32),
            pltpu.VMEM((2,) + plane, f32),
            pltpu.VMEM((2,) + plane, f32),
            pltpu.VMEM((4,) + plane, f32),
            pltpu.VMEM((2,) + plane, f32),
            pltpu.VMEM((2,) + plane, f32),
            pltpu.VMEM((2, plan.layers, plan.map_size + 2 * PAD, LANES), f32),
            pltpu.VMEM((plan.layers, plan.map_size + 2 * PAD, LANES), f32),
        ],
        compiler_params=limit,
        name="solve",
    )(windows)

    back = exchange(solved)

    vel_lines, log_lines = inputs[0].reshape(2, -1, LANES), inputs[3]
    velocity, friction_new, misfit = pl.pallas_call(
        functools.partial(unpack_kernel, plan),
        out_shape=(
            jax.ShapeDtypeStruct(vel_lines.shape, f32),
            jax.ShapeDtypeStruct(log_lines.shape, f32),
            jax.ShapeDtypeStruct((1, 1), f32),
        ),
        in_specs=[vmem] * 2,
        out_specs=(hbm, hbm, hbm),
        scratch_shapes=[
            pltpu.VMEM(vel_lines.shape, f32),
            pltpu.VMEM(log_lines.shape, f32),
            pltpu.VMEM((1, 1), f32),
            pltpu.VMEM((plan.layer_size,) + log_lines.shape, f32),
            pltpu.SemaphoreType.DMA((4,)),
        ],
        compiler_params=limit,
        name="unpack",
    )(back, log_lines)
    return (
        from_lines(velocity, velocity_init.shape),
        from_lines(friction_new, log_friction.shape),
        misfit.reshape(()),
    )


def solution(mesh):
    in_specs = (
        P(None, "layer", "map", None),
        P(None, "map", "layer"),
        P(None, "map", "layer"),
        P("map", "layer"),
        P("map", "layer"),
    )
    out_specs = (P(None, "layer", "map", None), P("map", "layer"), P())
    return jax.shard_map(
        functools.partial(on_device, dict(mesh.shape)),
        mesh=mesh,
        in_specs=in_specs,
        out_specs=out_specs,
        check_vma=False,
    )
```

```python
import functools
import math

import jax
import jax.numpy as jnp
from jax import lax
from jax.experimental import pallas as pl
from jax.experimental.pallas import tpu as pltpu
from jax.sharding import PartitionSpec as P

strain_floor = 0.1
step_size = 0.5
LANES = 128
REACH = 5
BED_REACH = 3
MIB = 1 << 20
VELOCITY_COPIES = 4


class Plan:
    def __init__(self, mesh_shape, velocity_shape):
        self.map_size = mesh_shape["map"]
        self.layer_size = mesh_shape["layer"]
        self.devices = self.map_size * self.layer_size
        self.layers_here = velocity_shape[1]
        self.rows = velocity_shape[2]
        self.ny = velocity_shape[3]
        self.layers = self.layers_here * self.layer_size
        self.cols = self.ny // self.devices
        self.width = LANES // self.rows
        self.halo = (self.width - self.cols) // 2
        self.low = self.halo - REACH
        self.wide = self.cols + 2 * REACH
        self.half = self.wide // 2
        self.gap = self.low + self.wide
        self.local_cols = self.ny // self.layer_size
        self.per_chunk = LANES // self.cols
        self.chunks = self.ny // LANES
        self.column_count = self.rows * self.map_size * self.ny
        self.vel_rows = 2 * self.layers_here
        self.in_rows = self.vel_rows + 1
        self.left_at = self.gap
        self.right_at = self.gap + self.cols // 2 + 1
        self.out_rows = self.layers_here + 1
        self.unrolled = self.map_size <= 8
        assert self.width * self.rows == LANES and self.cols * self.per_chunk == LANES
        assert self.low >= 0 and self.wide % 2 == 0 and self.width - self.wide >= self.half
        assert 2 * self.cols <= self.width and self.local_cols % LANES == 0
        assert self.vel_rows == 8 and self.rows == 2 and 4 * self.cols <= LANES


def repeat(plan, count, body, carry=0):
    if plan.unrolled:
        for index in range(count):
            carry = body(index, carry)
        return carry
    return lax.fori_loop(0, count, body, carry)


def lane_roll(value, shift):
    shift = shift % LANES
    return value if shift == 0 else pltpu.roll(value, shift, 1)


def pack_kernel(
    plan, vel_hbm, driving_hbm, observed_hbm, log_hbm, mask_hbm, out_ref,
    vel_ref, driving_ref, observed_ref, log_ref, mask_ref, arrival,
):
    width, rows, cols, half = plan.width, plan.rows, plan.cols, plan.half
    piece = vel_ref.shape[0] // VELOCITY_COPIES
    spans = [pl.ds(n * piece, piece) for n in range(VELOCITY_COPIES)]
    pairs = [(vel_hbm.at[span, :], vel_ref.at[span, :]) for span in spans] + [
        (driving_hbm, driving_ref),
        (observed_hbm, observed_ref),
        (log_hbm, log_ref),
        (mask_hbm, mask_ref),
    ]
    copies = [pltpu.make_async_copy(pair[0], pair[1], arrival.at[n]) for n, pair in enumerate(pairs)]
    for copy in copies:
        copy.start()
    shape = (plan.vel_rows, LANES)
    lane = lax.broadcasted_iota(jnp.int32, shape, 1)
    sub = lax.broadcasted_iota(jnp.int32, shape, 0)
    in_gap = jnp.logical_not(jnp.logical_and(lane % width >= plan.low, lane % width < plan.gap))
    no_line = jnp.zeros((1, LANES), jnp.float32)

    def slide(part, start, length, place):
        step, offset = start // LANES, start % LANES
        value = part(step)
        if offset + length > LANES:
            after = part(step + 1)
            value = jnp.where(lax.broadcasted_iota(jnp.int32, value.shape, 1) >= offset, value, after)
        return lane_roll(value, place - offset)

    for copy in copies[:VELOCITY_COPIES]:
        copy.wait()

    def chunk_windows(i, carry):
        def velocity(r):
            def part(step):
                chunk = i + step
                if isinstance(chunk, int) and not 0 <= chunk < plan.chunks:
                    return jnp.zeros(shape, jnp.float32)
                at = chunk if isinstance(chunk, int) else jnp.clip(chunk, 0, plan.chunks - 1)
                value = vel_ref[pl.ds(at * rows + r, plan.vel_rows, stride=plan.chunks * rows), :]
                if isinstance(chunk, int):
                    return value
                return jnp.where(jnp.logical_and(chunk >= 0, chunk < plan.chunks), value, 0.0)

            return part

        for t in range(plan.per_chunk):
            block = None
            for r in range(rows):
                value = slide(velocity(r), plan.cols * t - plan.halo, width, r * width)
                block = value if block is None else jnp.where(lane >= r * width, value, block)
            at = (plan.chunks - 1 - i) * plan.per_chunk * plan.in_rows
            if not isinstance(at, int):
                at = pl.multiple_of(at, 8)
            at = at + (plan.per_chunk - 1 - t) * plan.in_rows
            out_ref[pl.ds(at, plan.vel_rows), :] = jnp.where(in_gap, 0.0, block)
            out_ref[pl.ds(at + plan.vel_rows, 1), :] = no_line
        return carry

    repeat(plan, plan.chunks, chunk_windows)
    for copy in copies[VELOCITY_COPIES:]:
        copy.wait()

    place = lax.axis_index("layer")
    local_chunks = plan.local_cols // LANES

    skip = local_chunks * rows
    no_block = jnp.zeros(shape, jnp.float32)

    def whole(ref, row):
        return jnp.broadcast_to(ref[row : row + 1, :], shape).astype(jnp.float32)

    def gap_part(r, step):
        at = step * rows + r
        observed = jnp.where(sub < 2, whole(observed_ref, at), whole(observed_ref, skip + at))
        return jnp.where(sub < 4, observed, jnp.where(sub < 6, whole(mask_ref, at), whole(log_ref, at)))

    def driving_part(r, step):
        at = step * rows + r
        return jnp.where(sub < 2, whole(driving_ref, at), whole(driving_ref, skip + at))

    def sequence(make):
        return [
            [no_block] + [make(r, step) for step in range(local_chunks)] + [no_block] for r in range(rows)
        ]

    gap_parts, driving_parts = sequence(gap_part), sequence(driving_part)
    own = plan.local_cols // cols
    spill = -(-REACH // cols)

    def column_block(q):
        start = q * cols
        block = None
        for r in range(rows):

            def in_gaps(step):
                return gap_parts[r][step + 1]

            def of_driving(step):
                return driving_parts[r][step + 1]

            at = r * width
            first = slide(in_gaps, start - REACH, half, (at + plan.gap) % LANES)
            second = slide(in_gaps, start - REACH + half, half, (at + plan.gap) % LANES)
            before = slide(of_driving, start - BED_REACH, BED_REACH, (at + plan.left_at) % LANES)
            after = slide(of_driving, start + cols, BED_REACH, (at + plan.right_at) % LANES)
            ahead = (lane + (LANES - plan.gap - at)) % LANES
            of_observed = sub < 4
            first = jnp.where(jnp.logical_and(of_observed, ahead < BED_REACH), before, first)
            second = jnp.where(jnp.logical_and(of_observed, ahead >= plan.right_at - plan.gap), after, second)
            value = jnp.where(sub % 2 == 0, first, second)
            ahead = (lane + (LANES - plan.gap)) % LANES
            block = value if block is None else jnp.where(ahead >= r * width, value, block)
        at = pl.multiple_of((plan.layer_size - 1 - place) * (own * plan.in_rows), 8) + (own - 1 - q) * plan.in_rows
        here = pl.ds(at, plan.vel_rows)
        out_ref[here, :] = jnp.where(in_gap, block, out_ref[here, :])
        if not 0 <= q < own:
            return
        line = None
        step, offset = start // LANES, start % LANES
        for r in range(rows):
            for c in range(2):
                row = c * skip + step * rows + r
                put = (2 * r + c) * cols
                value = lane_roll(driving_ref[row : row + 1, :], put - offset)
                line = value if line is None else jnp.where(lane[:1] >= put, value, line)
        out_ref[pl.ds(at + plan.vel_rows, 1), :] = line

    for q in range(own):
        column_block(q)

    @pl.when(place > 0)
    def _():
        for q in range(-spill, 0):
            column_block(q)

    @pl.when(place < plan.layer_size - 1)
    def _():
        for q in range(own, own + spill):
            column_block(q)


def solve_kernel(plan, in_ref, out_ref, field, eta_ref, side, rhs, faces, ratio, inverse):
    size, width, rows = plan.map_size, plan.width, plan.rows
    layers, here = plan.layers, plan.layers_here
    shape = (size, LANES)
    lane = lax.broadcasted_iota(jnp.int32, shape, 1)
    sub = lax.broadcasted_iota(jnp.int32, shape, 0)
    last_group = lane >= LANES - width
    first_group = lane < width
    x_end = jnp.logical_and(last_group, sub == 0)
    x_start = jnp.logical_and(first_group, sub == size - 1)

    def block_row(part, rows_of_block, row):
        first = (plan.layer_size - 1 - part) * size * rows_of_block
        return pl.ds(first + row, size, stride=rows_of_block)

    def arrived(part, row):
        return in_ref[block_row(part, plan.in_rows, row), :]

    def over_parts(row):
        total = arrived(0, row)
        for part in range(1, plan.layer_size):
            total = total + arrived(part, row)
        return total

    def moved(value, source, target):
        return lane_roll(value, target - source)

    def from_gap(halves):
        left, right = (moved(value, plan.gap, plan.low + h * plan.half) for h, value in enumerate(halves))
        return jnp.where(lane % width < plan.low + plan.half, left, right)

    def from_line(c):
        plane = None
        for r in range(rows):
            value = moved(line, (2 * r + c) * plan.cols, r * width + plan.halo)
            plane = value if plane is None else jnp.where(lane >= r * width, value, plane)
        return plane

    def driving_of(c, halves):
        left = moved(halves[0], plan.left_at, plan.halo - BED_REACH)
        right = moved(halves[1], plan.right_at, plan.halo + plan.cols)
        return jnp.where(centre, from_line(c), jnp.where(lane % width < plan.halo, left, right))

    def x_pair(value, edge):
        after = lane_roll(value, -width)
        before = after if 2 * width == LANES else lane_roll(value, width)
        after = jnp.where(last_group, pltpu.roll(after, 1, 0), after)
        before = jnp.where(first_group, pltpu.roll(before, size - 1, 0), before)
        return jnp.where(x_end, edge, after), jnp.where(x_start, edge, before)

    def y_pair(value):
        return lane_roll(value, -1), lane_roll(value, 1)

    def viscosity(rate):
        return jnp.exp2(jnp.log(strain_floor + rate) * (-1.0 / (3.0 * math.log(2.0))))

    for part in range(plan.layer_size):
        for c in range(2):
            for k in range(here):
                field[c, part * here + k] = arrived(part, c * here + k)
    line = over_parts(plan.vel_rows)
    gaps = [[over_parts(2 * n), over_parts(2 * n + 1)] for n in range(4)]
    reached = jnp.logical_and(lane % width >= plan.low, lane % width < plan.gap)
    centre = jnp.logical_and(lane % width >= plan.halo, lane % width < plan.halo + plan.cols)
    driving = [2.0 * driving_of(c, gaps[c]) for c in range(2)]
    observed = [from_gap(gaps[c]) for c in range(2)]
    mask = jnp.where(reached, from_gap(gaps[2]), 0.0)
    ice = mask != 0.0
    friction = jnp.where(mask == 1.0, jnp.exp(from_gap(gaps[3])), 0.0)

    def stencil(k):
        u, v = field[0, k], field[1, k]
        u_east, u_west = x_pair(u, 0.0)
        v_east, v_west = x_pair(v, 0.0)
        u_north, u_south = y_pair(u)
        v_north, v_south = y_pair(v)
        stretch_x = u_east - u_west
        stretch_y = v_north - v_south
        shear = 0.5 * ((u_north - u_south) + (v_east - v_west))
        rate = 0.25 * (stretch_x * (stretch_x + stretch_y) + stretch_y * stretch_y + shear * shear)
        half_v = 0.5 * v
        eta = viscosity(rate)
        eta_edge = viscosity(0.25 * (u * u + half_v * half_v))
        eta_east, eta_west = x_pair(eta, eta_edge)
        eta_north, eta_south = y_pair(eta)
        east, west = eta + eta_east, eta + eta_west
        north, south = eta + eta_north, eta + eta_south
        along_x, along_y = east + west, north + south
        eta_ref[k] = eta
        side[0, k] = 4.0 * along_x + along_y
        side[1, k] = along_x + 4.0 * along_y
        rhs[0, k] = driving[0] + (4.0 * (east * u_east + west * u_west) + (north * u_north + south * u_south))
        rhs[1, k] = driving[1] + ((east * v_east + west * v_west) + 4.0 * (north * v_north + south * v_south))
        faces[0, k] = east
        faces[1, k] = west
        faces[2, k] = north
        faces[3, k] = south

    def coupling_of(k):
        return (2.0 * layers * layers) * (eta_ref[k] + eta_ref[k + 1])

    middle = layers // 2
    zero = jnp.zeros(shape, jnp.float32)

    def eliminate(k, coupling, carry):
        before, passed, value = carry
        new_passed, new_value = [], []
        for c in range(2):
            rest = side[c, k] + passed[c]
            pivot = coupling + rest
            guess = pl.reciprocal(pivot, approx=True)
            correct = 2.0 - pivot * guess
            new_passed.append((coupling * rest * guess) * correct)
            inv = guess * correct
            inverse[c, k] = inv
            ratio[c, k] = coupling * inv
            out = (rhs[c, k] + before * value[c]) * inv
            rhs[c, k] = out
            new_value.append(out)
        return coupling, tuple(new_passed), tuple(new_value)

    def lower_step(k, carry):
        return eliminate(k, coupling_of(k), carry)

    def upper_step(k, carry):
        return eliminate(k, coupling_of(k - 1), carry)

    def fronts(step, carry):
        lower, upper = carry
        return lower_step(step, lower), upper_step(layers - 1 - step, upper)

    def spread(first, body):
        def outward(step, carry):
            below, above = carry
            return body(middle - 1 - step, below), body(middle + 1 + step, above)

        below, above = repeat(plan, layers - 1 - middle, outward, (first, first))
        for k in range(2 * middle - layers, -1, -1):
            below = body(k, below)
        return below, above

    def sweep():
        def stencil_body(k, carry):
            stencil(k)
            return carry

        bed = tuple(2.0 * friction for _ in range(2))
        lower, upper = (zero, bed, (zero, zero)), (zero, (zero, zero), (zero, zero))
        if plan.unrolled:
            stencil(0)
            stencil(layers - 1)
            for step in range(layers - 1 - middle):
                stencil(step + 1)
                if layers - 2 - step > step + 1:
                    stencil(layers - 2 - step)
                lower, upper = fronts(step, (lower, upper))
        else:
            repeat(plan, layers, stencil_body)
            lower, upper = repeat(plan, layers - 1 - middle, fronts, (lower, upper))
        for k in range(layers - 1 - middle, middle):
            lower = lower_step(k, lower)
        centre_value = []
        for c in range(2):
            pivot = side[c, middle] + lower[1][c] + upper[1][c]
            guess = pl.reciprocal(pivot, approx=True)
            inv = guess * (2.0 - pivot * guess)
            inverse[c, middle] = inv
            total = rhs[c, middle] + (lower[0] * lower[2][c] + upper[0] * upper[2][c])
            centre_value.append(jnp.where(ice, total * inv, 0.0))
            field[c, middle] = centre_value[c]

        def solved(k, nearer):
            current = tuple(jnp.where(ice, rhs[c, k] + ratio[c, k] * nearer[c], 0.0) for c in range(2))
            for c in range(2):
                field[c, k] = current[c]
            return current

        return spread(tuple(centre_value), solved)

    nothing = (zero, zero)
    base, top = lax.fori_loop(0, 2, lambda _, carry: sweep(), (nothing, nothing))

    def send(k, carry):
        both = jnp.where(centre, field[0, k], lane_roll(field[1, k], plan.cols))
        out_ref[block_row(k // here, plan.out_rows, k % here), :] = both
        return carry

    repeat(plan, layers, send)

    mismatch = [jnp.where(ice, top[c] - observed[c], 0.0) for c in range(2)]
    source = [(2.0 * layers) * mismatch[c] for c in range(2)]

    def side_sum(k, value):
        east, west, north, south = (faces[n, k] for n in range(4))
        u_east, u_west = x_pair(value[0], 0.0)
        v_east, v_west = x_pair(value[1], 0.0)
        u_north, u_south = y_pair(value[0])
        v_north, v_south = y_pair(value[1])
        first = 4.0 * (east * u_east + west * u_west) + (north * u_north + south * u_south)
        second = (east * v_east + west * v_west) + 4.0 * (north * v_north + south * v_south)
        return first, second

    carried = tuple(source[c] * inverse[c, layers - 1] for c in range(2))
    for c in range(2):
        rhs[c, layers - 1] = carried[c]

    def first_inward(step, carried):
        k = layers - 2 - step
        out = tuple(coupling_of(k) * carried[c] * inverse[c, k] for c in range(2))
        for c in range(2):
            rhs[c, k] = out[c]
        return out

    carried = repeat(plan, layers - 2 - middle, first_inward, carried)
    first_middle = tuple(coupling_of(middle) * carried[c] * inverse[c, middle] for c in range(2))

    def first_outward(step, carry):
        below, above = carry
        low, high = middle - 1 - step, middle + 1 + step
        below = tuple(ratio[c, low] * below[c] for c in range(2))
        above = tuple(rhs[c, high] + ratio[c, high] * above[c] for c in range(2))
        for k, value in ((low, below), (high, above)):
            total = side_sum(k, value)
            for c in range(2):
                rhs[c, k] = total[c] * inverse[c, k]
        return below, above

    middle_sum = side_sum(middle, first_middle)
    below, above = repeat(plan, layers - 1 - middle, first_outward, (first_middle, first_middle))
    for k in range(2 * middle - layers, -1, -1):
        below = tuple(ratio[c, k] * below[c] for c in range(2))
        total = side_sum(k, below)
        for c in range(2):
            rhs[c, k] = total[c] * inverse[c, k]
    for c in range(2):
        rhs[c, layers - 1] = rhs[c, layers - 1] + source[c] * inverse[c, layers - 1]

    def second_inward(step, carry):
        below, above = carry
        low, high = step + 1, layers - 2 - step
        below = tuple(rhs[c, low] + (coupling_of(low - 1) * inverse[c, low]) * below[c] for c in range(2))
        above = tuple(rhs[c, high] + (coupling_of(high) * inverse[c, high]) * above[c] for c in range(2))
        for c in range(2):
            rhs[c, low] = below[c]
        return below, above

    below, above = repeat(
        plan,
        layers - 2 - middle,
        second_inward,
        (tuple(rhs[c, 0] for c in range(2)), tuple(rhs[c, layers - 1] for c in range(2))),
    )
    for k in range(layers - 1 - middle, middle):
        below = tuple(rhs[c, k] + (coupling_of(k - 1) * inverse[c, k]) * below[c] for c in range(2))
        for c in range(2):
            rhs[c, k] = below[c]
    adjoint = tuple(
        (middle_sum[c] + (coupling_of(middle - 1) * below[c] + coupling_of(middle) * above[c])) * inverse[c, middle]
        for c in range(2)
    )

    def second_outward(step, nearer):
        k = middle - 1 - step
        return tuple(rhs[c, k] + ratio[c, k] * nearer[c] for c in range(2))

    adjoint = repeat(plan, middle, second_outward, adjoint)
    adjoint = [jnp.where(ice, adjoint[c], 0.0) for c in range(2)]
    gradient = -friction * (base[0] * adjoint[0] + base[1] * adjoint[1])

    def partial_sum(value):
        line = jnp.sum(jnp.where(centre, value, 0.0), axis=0, keepdims=True)
        folded = line
        for r in range(1, rows):
            folded = folded + lane_roll(line, r * width)
        return jnp.broadcast_to(lane_roll(folded, plan.cols), shape)

    misfit_line = partial_sum(mismatch[0] * mismatch[0] + mismatch[1] * mismatch[1])
    grad_line = partial_sum(gradient * gradient)
    in_first = jnp.logical_and(lane >= plan.halo + plan.cols, lane < plan.halo + 2 * plan.cols)
    last_row = jnp.where(centre, gradient, jnp.where(in_first, misfit_line, grad_line))
    for part in range(plan.layer_size):
        out_ref[block_row(part, plan.out_rows, here), :] = last_row


def unpack_kernel(
    plan, in_ref, log_ref, vel_hbm, friction_hbm, misfit_hbm,
    vel_ref, friction_ref, misfit_ref, grad_ref, leave,
):
    here, width, cols, rows = plan.layers_here, plan.width, plan.cols, plan.rows
    local_chunks = plan.local_cols // LANES

    total = jnp.sum(
        in_ref[pl.ds(here, plan.devices, stride=plan.out_rows), :], axis=0, keepdims=True
    )
    line_lane = lax.broadcasted_iota(jnp.int32, (1, LANES), 1)

    def summed(first):
        ahead = (line_lane + (LANES - first % LANES)) % LANES
        return jnp.sum(jnp.where(ahead < cols, total, 0.0), axis=1, keepdims=True)

    misfit_sum = summed(plan.halo + cols)
    grad_sum = summed(plan.halo + cols + width)
    scale = step_size / jnp.sqrt(grad_sum / plan.column_count + 1e-06)

    lane = lax.broadcasted_iota(jnp.int32, (plan.out_rows, LANES), 1)
    def chunk(c, i):
        at = (plan.chunks - 1 - i) * plan.per_chunk * plan.out_rows
        if not isinstance(at, int):
            at = pl.multiple_of(at, 8)
        turned = [
            lane_roll(in_ref[pl.ds(at + (plan.per_chunk - 1 - t) * plan.out_rows, plan.out_rows), :], t * cols)
            for t in range(plan.per_chunk)
        ]
        for r in range(rows):
            start = r * width + plan.halo + c * cols
            ahead = (lane + (LANES - start % LANES)) % LANES
            row = turned[0]
            for t in range(1, plan.per_chunk):
                row = jnp.where(ahead >= t * cols, turned[t], row)
            row = lane_roll(row, -start)
            vel_ref[c, pl.ds(i * rows + r, here, stride=plan.chunks * rows), :] = row[:here]
            if c == 0:
                owner, step = i // local_chunks, i % local_chunks
                grad_ref[owner, pl.ds(step * rows + r, 1), :] = row[here : here + 1]

    out = [pltpu.make_async_copy(vel_ref.at[c], vel_hbm.at[c], leave.at[c]) for c in range(2)]
    out.append(pltpu.make_async_copy(friction_ref, friction_hbm, leave.at[2]))
    out.append(pltpu.make_async_copy(misfit_ref, misfit_hbm, leave.at[3]))
    for c in range(2):

        def chunk_body(i, carry):
            chunk(c, i)
            return carry

        repeat(plan, plan.chunks, chunk_body)
        out[c].start()
    friction_ref[...] = log_ref[...] - grad_ref[lax.axis_index("layer")] * scale
    out[2].start()
    misfit_ref[...] = 0.5 * misfit_sum / plan.column_count
    out[3].start()
    for copy in out:
        copy.wait()


def as_lines(x):
    chunked = x.reshape(x.shape[:-1] + (x.shape[-1] // LANES, LANES))
    return jnp.swapaxes(chunked, -3, -2).reshape(-1, LANES)


def from_lines(lines, shape):
    chunked = lines.reshape(shape[:-2] + (shape[-1] // LANES, shape[-2], LANES))
    return jnp.swapaxes(chunked, -3, -2).reshape(shape)


def on_device(mesh_shape, velocity_init, driving, observed, log_friction, ice_mask):
    plan = Plan(mesh_shape, velocity_init.shape)
    vmem = pl.BlockSpec(memory_space=pltpu.VMEM)
    hbm = pl.BlockSpec(memory_space=pltpu.HBM)
    f32 = jnp.float32
    limit = pltpu.CompilerParams(vmem_limit_bytes=(16 if plan.unrolled else 40) * MIB)
    inputs = [as_lines(x) for x in (velocity_init, driving, observed, log_friction, ice_mask)]

    def exchange(blocks):
        shaped = blocks.reshape(blocks.shape[0], 1, LANES)
        ranks = [
            m * plan.layer_size + part
            for part in reversed(range(plan.layer_size))
            for m in reversed(range(plan.map_size))
        ]
        return lax.all_to_all(
            shaped, ("map", "layer"), split_axis=0, concat_axis=0, tiled=True, axis_index_groups=[ranks]
        ).reshape(blocks.shape)

    packed = pl.pallas_call(
        functools.partial(pack_kernel, plan),
        out_shape=jax.ShapeDtypeStruct((plan.devices * plan.in_rows, LANES), f32),
        in_specs=[hbm] * 5,
        out_specs=vmem,
        scratch_shapes=[pltpu.VMEM(x.shape, x.dtype) for x in inputs]
        + [
            pltpu.SemaphoreType.DMA((VELOCITY_COPIES + 4,)),
        ],
        compiler_params=limit,
        name="pack",
    )(*(pltpu.with_memory_space_constraint(x, pltpu.HBM) for x in inputs))

    windows = exchange(packed)

    plane = (plan.layers, plan.map_size, LANES)
    solved = pl.pallas_call(
        functools.partial(solve_kernel, plan),
        out_shape=jax.ShapeDtypeStruct((plan.devices * plan.out_rows, LANES), f32),
        in_specs=[vmem],
        out_specs=vmem,
        scratch_shapes=[
            pltpu.VMEM((2,) + plane, f32),
            pltpu.VMEM(plane, f32),
            pltpu.VMEM((2,) + plane, f32),
            pltpu.VMEM((2,) + plane, f32),
            pltpu.VMEM((4,) + plane, f32),
            pltpu.VMEM((2,) + plane, f32),
            pltpu.VMEM((2,) + plane, f32),
        ],
        compiler_params=limit,
        name="solve",
    )(windows)

    back = exchange(solved)

    vel_lines, log_lines = inputs[0].reshape(2, -1, LANES), inputs[3]
    velocity, friction_new, misfit = pl.pallas_call(
        functools.partial(unpack_kernel, plan),
        out_shape=(
            jax.ShapeDtypeStruct(vel_lines.shape, f32),
            jax.ShapeDtypeStruct(log_lines.shape, f32),
            jax.ShapeDtypeStruct((1, 1), f32),
        ),
        in_specs=[vmem] * 2,
        out_specs=(hbm, hbm, hbm),
        scratch_shapes=[
            pltpu.VMEM(vel_lines.shape, f32),
            pltpu.VMEM(log_lines.shape, f32),
            pltpu.VMEM((1, 1), f32),
            pltpu.VMEM((plan.layer_size,) + log_lines.shape, f32),
            pltpu.SemaphoreType.DMA((4,)),
        ],
        compiler_params=limit,
        name="unpack",
    )(back, log_lines)
    return (
        from_lines(velocity, velocity_init.shape),
        from_lines(friction_new, log_friction.shape),
        misfit.reshape(()),
    )


def solution(mesh):
    in_specs = (
        P(None, "layer", "map", None),
        P(None, "map", "layer"),
        P(None, "map", "layer"),
        P("map", "layer"),
        P("map", "layer"),
    )
    out_specs = (P(None, "layer", "map", None), P("map", "layer"), P())
    return jax.shard_map(
        functools.partial(on_device, dict(mesh.shape)),
        mesh=mesh,
        in_specs=in_specs,
        out_specs=out_specs,
        check_vma=False,
    )
```

```python
import functools
import math

import jax
import jax.numpy as jnp
from jax import lax
from jax.experimental import pallas as pl
from jax.experimental.pallas import tpu as pltpu
from jax.sharding import PartitionSpec as P

strain_floor = 0.1
step_size = 0.5
LANES = 128
REACH = 5
BED_REACH = 3
PAD = 8
MIB = 1 << 20
VELOCITY_COPIES = 4


class Plan:
    def __init__(self, mesh_shape, velocity_shape):
        self.map_size = mesh_shape["map"]
        self.layer_size = mesh_shape["layer"]
        self.devices = self.map_size * self.layer_size
        self.layers_here = velocity_shape[1]
        self.rows = velocity_shape[2]
        self.ny = velocity_shape[3]
        self.layers = self.layers_here * self.layer_size
        self.cols = self.ny // self.devices
        self.width = LANES // self.rows
        self.halo = (self.width - self.cols) // 2
        self.low = self.halo - REACH
        self.wide = self.cols + 2 * REACH
        self.half = self.wide // 2
        self.gap = self.low + self.wide
        self.local_cols = self.ny // self.layer_size
        self.per_chunk = LANES // self.cols
        self.chunks = self.ny // LANES
        self.column_count = self.rows * self.map_size * self.ny
        self.vel_rows = 2 * self.layers_here
        self.in_rows = self.vel_rows + 1
        self.left_at = self.gap
        self.right_at = self.gap + self.cols // 2 + 1
        self.out_rows = self.layers_here + 1
        self.unrolled = self.map_size <= 8
        assert self.width * self.rows == LANES and self.cols * self.per_chunk == LANES
        assert self.low >= 0 and self.wide % 2 == 0 and self.width - self.wide >= self.half
        assert 2 * self.cols <= self.width and self.local_cols % LANES == 0
        assert self.vel_rows == 8 and self.rows == 2 and 4 * self.cols <= LANES and self.map_size % 8 == 0


def repeat(plan, count, body, carry=0):
    if plan.unrolled:
        for index in range(count):
            carry = body(index, carry)
        return carry
    return lax.fori_loop(0, count, body, carry)


def lane_roll(value, shift):
    shift = shift % LANES
    return value if shift == 0 else pltpu.roll(value, shift, 1)


def pack_kernel(
    plan, vel_hbm, driving_hbm, observed_hbm, log_hbm, mask_hbm, out_ref,
    vel_ref, driving_ref, observed_ref, log_ref, mask_ref, arrival,
):
    width, rows, cols, half = plan.width, plan.rows, plan.cols, plan.half
    piece = vel_ref.shape[0] // VELOCITY_COPIES
    spans = [pl.ds(n * piece, piece) for n in range(VELOCITY_COPIES)]
    pairs = [(vel_hbm.at[span, :], vel_ref.at[span, :]) for span in spans] + [
        (driving_hbm, driving_ref),
        (observed_hbm, observed_ref),
        (log_hbm, log_ref),
        (mask_hbm, mask_ref),
    ]
    copies = [pltpu.make_async_copy(pair[0], pair[1], arrival.at[n]) for n, pair in enumerate(pairs)]
    for copy in copies:
        copy.start()
    shape = (plan.vel_rows, LANES)
    lane = lax.broadcasted_iota(jnp.int32, shape, 1)
    sub = lax.broadcasted_iota(jnp.int32, shape, 0)
    in_gap = jnp.logical_not(jnp.logical_and(lane % width >= plan.low, lane % width < plan.gap))
    no_line = jnp.zeros((1, LANES), jnp.float32)

    def slide(part, start, length, place):
        step, offset = start // LANES, start % LANES
        value = part(step)
        if offset + length > LANES:
            after = part(step + 1)
            value = jnp.where(lax.broadcasted_iota(jnp.int32, value.shape, 1) >= offset, value, after)
        return lane_roll(value, place - offset)

    for copy in copies[:VELOCITY_COPIES]:
        copy.wait()

    def chunk_windows(i, carry):
        def velocity(r):
            def part(step):
                chunk = i + step
                if isinstance(chunk, int) and not 0 <= chunk < plan.chunks:
                    return jnp.zeros(shape, jnp.float32)
                at = chunk if isinstance(chunk, int) else jnp.clip(chunk, 0, plan.chunks - 1)
                value = vel_ref[pl.ds(at * rows + r, plan.vel_rows, stride=plan.chunks * rows), :]
                if isinstance(chunk, int):
                    return value
                return jnp.where(jnp.logical_and(chunk >= 0, chunk < plan.chunks), value, 0.0)

            return part

        for t in range(plan.per_chunk):
            block = None
            for r in range(rows):
                value = slide(velocity(r), plan.cols * t - plan.halo, width, r * width)
                block = value if block is None else jnp.where(lane >= r * width, value, block)
            at = (plan.chunks - 1 - i) * plan.per_chunk * plan.in_rows
            if not isinstance(at, int):
                at = pl.multiple_of(at, 8)
            at = at + (plan.per_chunk - 1 - t) * plan.in_rows
            out_ref[pl.ds(at, plan.vel_rows), :] = jnp.where(in_gap, 0.0, block)
            out_ref[pl.ds(at + plan.vel_rows, 1), :] = no_line
        return carry

    repeat(plan, plan.chunks, chunk_windows)
    for copy in copies[VELOCITY_COPIES:]:
        copy.wait()

    place = lax.axis_index("layer")
    local_chunks = plan.local_cols // LANES

    skip = local_chunks * rows
    no_block = jnp.zeros(shape, jnp.float32)

    def whole(ref, row):
        return jnp.broadcast_to(ref[row : row + 1, :], shape).astype(jnp.float32)

    def gap_part(r, step):
        at = step * rows + r
        observed = jnp.where(sub < 2, whole(observed_ref, at), whole(observed_ref, skip + at))
        return jnp.where(sub < 4, observed, jnp.where(sub < 6, whole(mask_ref, at), whole(log_ref, at)))

    def driving_part(r, step):
        at = step * rows + r
        return jnp.where(sub < 2, whole(driving_ref, at), whole(driving_ref, skip + at))

    def sequence(make):
        return [
            [no_block] + [make(r, step) for step in range(local_chunks)] + [no_block] for r in range(rows)
        ]

    gap_parts, driving_parts = sequence(gap_part), sequence(driving_part)
    own = plan.local_cols // cols
    spill = -(-REACH // cols)

    def column_block(q):
        start = q * cols
        block = None
        for r in range(rows):

            def in_gaps(step):
                return gap_parts[r][step + 1]

            def of_driving(step):
                return driving_parts[r][step + 1]

            at = r * width
            first = slide(in_gaps, start - REACH, half, (at + plan.gap) % LANES)
            second = slide(in_gaps, start - REACH + half, half, (at + plan.gap) % LANES)
            before = slide(of_driving, start - BED_REACH, BED_REACH, (at + plan.left_at) % LANES)
            after = slide(of_driving, start + cols, BED_REACH, (at + plan.right_at) % LANES)
            ahead = (lane + (LANES - plan.gap - at)) % LANES
            of_observed = sub < 4
            first = jnp.where(jnp.logical_and(of_observed, ahead < BED_REACH), before, first)
            second = jnp.where(jnp.logical_and(of_observed, ahead >= plan.right_at - plan.gap), after, second)
            value = jnp.where(sub % 2 == 0, first, second)
            ahead = (lane + (LANES - plan.gap)) % LANES
            block = value if block is None else jnp.where(ahead >= r * width, value, block)
        at = pl.multiple_of((plan.layer_size - 1 - place) * (own * plan.in_rows), 8) + (own - 1 - q) * plan.in_rows
        here = pl.ds(at, plan.vel_rows)
        out_ref[here, :] = jnp.where(in_gap, block, out_ref[here, :])
        if not 0 <= q < own:
            return
        line = None
        step, offset = start // LANES, start % LANES
        for r in range(rows):
            for c in range(2):
                row = c * skip + step * rows + r
                put = (2 * r + c) * cols
                value = lane_roll(driving_ref[row : row + 1, :], put - offset)
                line = value if line is None else jnp.where(lane[:1] >= put, value, line)
        out_ref[pl.ds(at + plan.vel_rows, 1), :] = line

    for q in range(own):
        column_block(q)

    @pl.when(place > 0)
    def _():
        for q in range(-spill, 0):
            column_block(q)

    @pl.when(place < plan.layer_size - 1)
    def _():
        for q in range(own, own + spill):
            column_block(q)


def solve_kernel(plan, in_ref, out_ref, field, eta_ref, side, rhs, faces, ratio, inverse, swapped, eta_swapped):
    size, width, rows = plan.map_size, plan.width, plan.rows
    layers, here = plan.layers, plan.layers_here
    shape = (size, LANES)
    lane = lax.broadcasted_iota(jnp.int32, shape, 1)
    last_group = lane >= LANES - width
    first_group = lane < width
    def block_row(part, rows_of_block, row):
        first = (plan.layer_size - 1 - part) * size * rows_of_block
        return pl.ds(first + row, size, stride=rows_of_block)

    def arrived(part, row):
        return in_ref[block_row(part, plan.in_rows, row), :]

    def over_parts(row):
        total = arrived(0, row)
        for part in range(1, plan.layer_size):
            total = total + arrived(part, row)
        return total

    def moved(value, source, target):
        return lane_roll(value, target - source)

    def from_gap(halves):
        left, right = (moved(value, plan.gap, plan.low + h * plan.half) for h, value in enumerate(halves))
        return jnp.where(lane % width < plan.low + plan.half, left, right)

    def from_line(c):
        plane = None
        for r in range(rows):
            value = moved(line, (2 * r + c) * plan.cols, r * width + plan.halo)
            plane = value if plane is None else jnp.where(lane >= r * width, value, plane)
        return plane

    def driving_of(c, halves):
        left = moved(halves[0], plan.left_at, plan.halo - BED_REACH)
        right = moved(halves[1], plan.right_at, plan.halo + plan.cols)
        return jnp.where(centre, from_line(c), jnp.where(lane % width < plan.halo, left, right))

    body = pl.ds(PAD, size)

    def x_pair(ref, index):
        same = ref[index + (body,)]
        after = jnp.where(last_group, ref[index + (pl.ds(PAD - 1, size),)], same)
        before = jnp.where(first_group, ref[index + (pl.ds(PAD + 1, size),)], same)
        return after, before

    def swap_in(c, k, value):
        swapped[c, k, body] = lane_roll(value, width)

    edge = jnp.zeros((2, layers, PAD, LANES), jnp.float32)
    swapped[:, :, pl.ds(0, PAD)] = edge
    swapped[:, :, pl.ds(PAD + size, PAD)] = edge

    def y_pair(value):
        return lane_roll(value, -1), lane_roll(value, 1)

    def viscosity(rate):
        return jnp.exp2(jnp.log(strain_floor + rate) * (-1.0 / (3.0 * math.log(2.0))))

    for part in range(plan.layer_size):
        for c in range(2):
            for k in range(here):
                value = arrived(part, c * here + k)
                field[c, part * here + k] = value
                swap_in(c, part * here + k, value)
    line = over_parts(plan.vel_rows)
    gaps = [[over_parts(2 * n), over_parts(2 * n + 1)] for n in range(4)]
    reached = jnp.logical_and(lane % width >= plan.low, lane % width < plan.gap)
    centre = jnp.logical_and(lane % width >= plan.halo, lane % width < plan.halo + plan.cols)
    driving = [2.0 * driving_of(c, gaps[c]) for c in range(2)]
    observed = [from_gap(gaps[c]) for c in range(2)]
    mask = jnp.where(reached, from_gap(gaps[2]), 0.0)
    ice = mask != 0.0
    friction = jnp.where(mask == 1.0, jnp.exp(from_gap(gaps[3])), 0.0)

    def stencil(k, keep):
        u, v = field[0, k], field[1, k]
        u_east, u_west = x_pair(swapped, (0, k))
        v_east, v_west = x_pair(swapped, (1, k))
        u_north, u_south = y_pair(u)
        v_north, v_south = y_pair(v)
        stretch_x = u_east - u_west
        stretch_y = v_north - v_south
        shear = 0.5 * ((u_north - u_south) + (v_east - v_west))
        rate = 0.25 * (stretch_x * (stretch_x + stretch_y) + stretch_y * stretch_y + shear * shear)
        half_v = 0.5 * v
        eta = viscosity(rate)
        eta_edge = viscosity(0.25 * (u * u + half_v * half_v))
        eta_swapped[k, body] = lane_roll(eta, width)
        eta_swapped[k, pl.ds(PAD - 1, 1)] = eta_edge[:1]
        eta_swapped[k, pl.ds(PAD + size, 1)] = eta_edge[size - 1 :]
        eta_east, eta_west = x_pair(eta_swapped, (k,))
        eta_north, eta_south = y_pair(eta)
        east, west = eta + eta_east, eta + eta_west
        north, south = eta + eta_north, eta + eta_south
        along_x, along_y = east + west, north + south
        eta_ref[k] = eta
        side[0, k] = 4.0 * along_x + along_y
        side[1, k] = along_x + 4.0 * along_y
        rhs[0, k] = driving[0] + (4.0 * (east * u_east + west * u_west) + (north * u_north + south * u_south))
        rhs[1, k] = driving[1] + ((east * v_east + west * v_west) + 4.0 * (north * v_north + south * v_south))
        if keep:
            faces[0, k] = east
            faces[1, k] = west
            faces[2, k] = north
            faces[3, k] = south

    def coupling_of(k):
        return (2.0 * layers * layers) * (eta_ref[k] + eta_ref[k + 1])

    middle = layers // 2
    zero = jnp.zeros(shape, jnp.float32)

    def eliminate(k, coupling, carry):
        before, passed, value = carry
        new_passed, new_value = [], []
        for c in range(2):
            rest = side[c, k] + passed[c]
            pivot = coupling + rest
            guess = pl.reciprocal(pivot, approx=True)
            correct = 2.0 - pivot * guess
            new_passed.append((coupling * rest * guess) * correct)
            inv = guess * correct
            inverse[c, k] = inv
            ratio[c, k] = coupling * inv
            out = (rhs[c, k] + before * value[c]) * inv
            rhs[c, k] = out
            new_value.append(out)
        return coupling, tuple(new_passed), tuple(new_value)

    def lower_step(k, carry):
        return eliminate(k, coupling_of(k), carry)

    def upper_step(k, carry):
        return eliminate(k, coupling_of(k - 1), carry)

    def fronts(step, carry):
        lower, upper = carry
        return lower_step(step, lower), upper_step(layers - 1 - step, upper)

    def spread(first, body):
        def outward(step, carry):
            below, above = carry
            return body(middle - 1 - step, below), body(middle + 1 + step, above)

        below, above = repeat(plan, layers - 1 - middle, outward, (first, first))
        for k in range(2 * middle - layers, -1, -1):
            below = body(k, below)
        return below, above

    def sweep(keep):
        def stencil_body(k, carry):
            stencil(k, keep)
            return carry

        bed = tuple(2.0 * friction for _ in range(2))
        lower, upper = (zero, bed, (zero, zero)), (zero, (zero, zero), (zero, zero))
        if plan.unrolled:
            stencil(0, keep)
            stencil(layers - 1, keep)
            for step in range(layers - 1 - middle):
                stencil(step + 1, keep)
                if layers - 2 - step > step + 1:
                    stencil(layers - 2 - step, keep)
                lower, upper = fronts(step, (lower, upper))
        else:
            repeat(plan, layers, stencil_body)
            lower, upper = repeat(plan, layers - 1 - middle, fronts, (lower, upper))
        for k in range(layers - 1 - middle, middle):
            lower = lower_step(k, lower)
        centre_value = []
        for c in range(2):
            pivot = side[c, middle] + lower[1][c] + upper[1][c]
            guess = pl.reciprocal(pivot, approx=True)
            inv = guess * (2.0 - pivot * guess)
            inverse[c, middle] = inv
            total = rhs[c, middle] + (lower[0] * lower[2][c] + upper[0] * upper[2][c])
            centre_value.append(jnp.where(ice, total * inv, 0.0))
            field[c, middle] = centre_value[c]
            swap_in(c, middle, centre_value[c])

        def solved(k, nearer):
            current = tuple(jnp.where(ice, rhs[c, k] + ratio[c, k] * nearer[c], 0.0) for c in range(2))
            for c in range(2):
                field[c, k] = current[c]
                swap_in(c, k, current[c])
            return current

        return spread(tuple(centre_value), solved)

    sweep(False)
    base, top = sweep(True)

    def send(k, carry):
        both = jnp.where(centre, field[0, k], lane_roll(field[1, k], plan.cols))
        out_ref[block_row(k // here, plan.out_rows, k % here), :] = both
        return carry

    repeat(plan, layers, send)

    mismatch = [jnp.where(ice, top[c] - observed[c], 0.0) for c in range(2)]
    source = [(2.0 * layers) * mismatch[c] for c in range(2)]

    def side_sum(k, value):
        east, west, north, south = (faces[n, k] for n in range(4))
        for c in range(2):
            swap_in(c, k, value[c])
        u_east, u_west = x_pair(swapped, (0, k))
        v_east, v_west = x_pair(swapped, (1, k))
        u_north, u_south = y_pair(value[0])
        v_north, v_south = y_pair(value[1])
        first = 4.0 * (east * u_east + west * u_west) + (north * u_north + south * u_south)
        second = (east * v_east + west * v_west) + 4.0 * (north * v_north + south * v_south)
        return first, second

    carried = tuple(source[c] * inverse[c, layers - 1] for c in range(2))
    for c in range(2):
        rhs[c, layers - 1] = carried[c]

    def first_inward(step, carried):
        k = layers - 2 - step
        out = tuple(coupling_of(k) * carried[c] * inverse[c, k] for c in range(2))
        for c in range(2):
            rhs[c, k] = out[c]
        return out

    carried = repeat(plan, layers - 2 - middle, first_inward, carried)
    first_middle = tuple(coupling_of(middle) * carried[c] * inverse[c, middle] for c in range(2))

    def first_outward(step, carry):
        below, above = carry
        low, high = middle - 1 - step, middle + 1 + step
        below = tuple(ratio[c, low] * below[c] for c in range(2))
        above = tuple(rhs[c, high] + ratio[c, high] * above[c] for c in range(2))
        for k, value in ((low, below), (high, above)):
            total = side_sum(k, value)
            for c in range(2):
                rhs[c, k] = total[c] * inverse[c, k]
        return below, above

    middle_sum = side_sum(middle, first_middle)
    below, above = repeat(plan, layers - 1 - middle, first_outward, (first_middle, first_middle))
    for k in range(2 * middle - layers, -1, -1):
        below = tuple(ratio[c, k] * below[c] for c in range(2))
        total = side_sum(k, below)
        for c in range(2):
            rhs[c, k] = total[c] * inverse[c, k]
    for c in range(2):
        rhs[c, layers - 1] = rhs[c, layers - 1] + source[c] * inverse[c, layers - 1]

    def second_inward(step, carry):
        below, above = carry
        low, high = step + 1, layers - 2 - step
        below = tuple(rhs[c, low] + (coupling_of(low - 1) * inverse[c, low]) * below[c] for c in range(2))
        above = tuple(rhs[c, high] + (coupling_of(high) * inverse[c, high]) * above[c] for c in range(2))
        for c in range(2):
            rhs[c, low] = below[c]
        return below, above

    below, above = repeat(
        plan,
        layers - 2 - middle,
        second_inward,
        (tuple(rhs[c, 0] for c in range(2)), tuple(rhs[c, layers - 1] for c in range(2))),
    )
    for k in range(layers - 1 - middle, middle):
        below = tuple(rhs[c, k] + (coupling_of(k - 1) * inverse[c, k]) * below[c] for c in range(2))
        for c in range(2):
            rhs[c, k] = below[c]
    adjoint = tuple(
        (middle_sum[c] + (coupling_of(middle - 1) * below[c] + coupling_of(middle) * above[c])) * inverse[c, middle]
        for c in range(2)
    )

    def second_outward(step, nearer):
        k = middle - 1 - step
        return tuple(rhs[c, k] + ratio[c, k] * nearer[c] for c in range(2))

    adjoint = repeat(plan, middle, second_outward, adjoint)
    adjoint = [jnp.where(ice, adjoint[c], 0.0) for c in range(2)]
    gradient = -friction * (base[0] * adjoint[0] + base[1] * adjoint[1])

    def partial_sum(value):
        line = jnp.sum(jnp.where(centre, value, 0.0), axis=0, keepdims=True)
        folded = line
        for r in range(1, rows):
            folded = folded + lane_roll(line, r * width)
        return jnp.broadcast_to(lane_roll(folded, plan.cols), shape)

    misfit_line = partial_sum(mismatch[0] * mismatch[0] + mismatch[1] * mismatch[1])
    grad_line = partial_sum(gradient * gradient)
    in_first = jnp.logical_and(lane >= plan.halo + plan.cols, lane < plan.halo + 2 * plan.cols)
    last_row = jnp.where(centre, gradient, jnp.where(in_first, misfit_line, grad_line))
    for part in range(plan.layer_size):
        out_ref[block_row(part, plan.out_rows, here), :] = last_row


def unpack_kernel(
    plan, in_ref, log_ref, vel_hbm, friction_hbm, misfit_hbm,
    vel_ref, friction_ref, misfit_ref, grad_ref, leave,
):
    here, width, cols, rows = plan.layers_here, plan.width, plan.cols, plan.rows
    local_chunks = plan.local_cols // LANES

    total = jnp.sum(
        in_ref[pl.ds(here, plan.devices, stride=plan.out_rows), :], axis=0, keepdims=True
    )
    line_lane = lax.broadcasted_iota(jnp.int32, (1, LANES), 1)

    def summed(first):
        ahead = (line_lane + (LANES - first % LANES)) % LANES
        return jnp.sum(jnp.where(ahead < cols, total, 0.0), axis=1, keepdims=True)

    misfit_sum = summed(plan.halo + cols)
    grad_sum = summed(plan.halo + cols + width)
    scale = step_size * lax.rsqrt(grad_sum / plan.column_count + 1e-06)

    lane = lax.broadcasted_iota(jnp.int32, (plan.out_rows, LANES), 1)
    def chunk(c, i):
        at = (plan.chunks - 1 - i) * plan.per_chunk * plan.out_rows
        if not isinstance(at, int):
            at = pl.multiple_of(at, 8)
        turned = [
            lane_roll(in_ref[pl.ds(at + (plan.per_chunk - 1 - t) * plan.out_rows, plan.out_rows), :], t * cols)
            for t in range(plan.per_chunk)
        ]
        for r in range(rows):
            start = r * width + plan.halo + c * cols
            ahead = (lane + (LANES - start % LANES)) % LANES
            row = turned[0]
            for t in range(1, plan.per_chunk):
                row = jnp.where(ahead >= t * cols, turned[t], row)
            row = lane_roll(row, -start)
            vel_ref[c, pl.ds(i * rows + r, here, stride=plan.chunks * rows), :] = row[:here]
            if c == 0:
                owner, step = i // local_chunks, i % local_chunks
                grad_ref[owner, pl.ds(step * rows + r, 1), :] = row[here : here + 1]

    def leaving(n, source, target):
        return pltpu.make_async_copy(source, target, leave.at[n])

    lines = plan.chunks * rows
    spans = [(c, pl.ds(k * lines, lines)) for c in range(2) for k in range(here)]
    out = [leaving(n, vel_ref.at[span], vel_hbm.at[span]) for n, span in enumerate(spans)]
    small = [leaving(2 * here, friction_ref, friction_hbm), leaving(2 * here + 1, misfit_ref, misfit_hbm)]
    for c in range(2):

        def chunk_body(i, carry):
            chunk(c, i)
            return carry

        repeat(plan, plan.chunks, chunk_body)
        for copy in out[c * here : (c + 1) * here]:
            copy.start()
    friction_ref[...] = log_ref[...] - grad_ref[lax.axis_index("layer")] * scale
    small[0].start()
    misfit_ref[...] = 0.5 * misfit_sum / plan.column_count
    small[1].start()
    for copy in out + small:
        copy.wait()


def as_lines(x):
    chunked = x.reshape(x.shape[:-1] + (x.shape[-1] // LANES, LANES))
    return jnp.swapaxes(chunked, -3, -2).reshape(-1, LANES)


def from_lines(lines, shape):
    chunked = lines.reshape(shape[:-2] + (shape[-1] // LANES, shape[-2], LANES))
    return jnp.swapaxes(chunked, -3, -2).reshape(shape)


def on_device(mesh_shape, velocity_init, driving, observed, log_friction, ice_mask):
    plan = Plan(mesh_shape, velocity_init.shape)
    vmem = pl.BlockSpec(memory_space=pltpu.VMEM)
    hbm = pl.BlockSpec(memory_space=pltpu.HBM)
    f32 = jnp.float32
    limit = pltpu.CompilerParams(vmem_limit_bytes=(16 if plan.unrolled else 40) * MIB)
    inputs = [as_lines(x) for x in (velocity_init, driving, observed, log_friction, ice_mask)]

    def exchange(blocks):
        shaped = blocks.reshape(blocks.shape[0], 1, LANES)
        ranks = [
            m * plan.layer_size + part
            for part in reversed(range(plan.layer_size))
            for m in reversed(range(plan.map_size))
        ]
        return lax.all_to_all(
            shaped, ("map", "layer"), split_axis=0, concat_axis=0, tiled=True, axis_index_groups=[ranks]
        ).reshape(blocks.shape)

    packed = pl.pallas_call(
        functools.partial(pack_kernel, plan),
        out_shape=jax.ShapeDtypeStruct((plan.devices * plan.in_rows, LANES), f32),
        in_specs=[hbm] * 5,
        out_specs=vmem,
        scratch_shapes=[pltpu.VMEM(x.shape, x.dtype) for x in inputs]
        + [
            pltpu.SemaphoreType.DMA((VELOCITY_COPIES + 4,)),
        ],
        compiler_params=limit,
        name="pack",
    )(*(pltpu.with_memory_space_constraint(x, pltpu.HBM) for x in inputs))

    windows = exchange(packed)

    plane = (plan.layers, plan.map_size, LANES)
    solved = pl.pallas_call(
        functools.partial(solve_kernel, plan),
        out_shape=jax.ShapeDtypeStruct((plan.devices * plan.out_rows, LANES), f32),
        in_specs=[vmem],
        out_specs=vmem,
        scratch_shapes=[
            pltpu.VMEM((2,) + plane, f32),
            pltpu.VMEM(plane, f32),
            pltpu.VMEM((2,) + plane, f32),
            pltpu.VMEM((2,) + plane, f32),
            pltpu.VMEM((4,) + plane, f32),
            pltpu.VMEM((2,) + plane, f32),
            pltpu.VMEM((2,) + plane, f32),
            pltpu.VMEM((2, plan.layers, plan.map_size + 2 * PAD, LANES), f32),
            pltpu.VMEM((plan.layers, plan.map_size + 2 * PAD, LANES), f32),
        ],
        compiler_params=limit,
        name="solve",
    )(windows)

    back = exchange(solved)

    vel_lines, log_lines = inputs[0].reshape(2, -1, LANES), inputs[3]
    velocity, friction_new, misfit = pl.pallas_call(
        functools.partial(unpack_kernel, plan),
        out_shape=(
            jax.ShapeDtypeStruct(vel_lines.shape, f32),
            jax.ShapeDtypeStruct(log_lines.shape, f32),
            jax.ShapeDtypeStruct((1, 1), f32),
        ),
        in_specs=[vmem] * 2,
        out_specs=(hbm, hbm, hbm),
        scratch_shapes=[
            pltpu.VMEM(vel_lines.shape, f32),
            pltpu.VMEM(log_lines.shape, f32),
            pltpu.VMEM((1, 1), f32),
            pltpu.VMEM((plan.layer_size,) + log_lines.shape, f32),
            pltpu.SemaphoreType.DMA((plan.vel_rows + 2,)),
        ],
        compiler_params=limit,
        name="unpack",
    )(back, log_lines)
    return (
        from_lines(velocity, velocity_init.shape),
        from_lines(friction_new, log_friction.shape),
        misfit.reshape(()),
    )


def solution(mesh):
    in_specs = (
        P(None, "layer", "map", None),
        P(None, "map", "layer"),
        P(None, "map", "layer"),
        P("map", "layer"),
        P("map", "layer"),
    )
    out_specs = (P(None, "layer", "map", None), P("map", "layer"), P())
    return jax.shard_map(
        functools.partial(on_device, dict(mesh.shape)),
        mesh=mesh,
        in_specs=in_specs,
        out_specs=out_specs,
        check_vma=False,
    )
```

```python
import functools
import math

import jax
import jax.numpy as jnp
from jax import lax
from jax.experimental import pallas as pl
from jax.experimental.pallas import tpu as pltpu
from jax.sharding import PartitionSpec as P

strain_floor = 0.1
step_size = 0.5
LANES = 128
REACH = 5
BED_REACH = 3
PAD = 8
MIB = 1 << 20
VELOCITY_COPIES = 4


class Plan:
    def __init__(self, mesh_shape, velocity_shape):
        self.map_size = mesh_shape["map"]
        self.layer_size = mesh_shape["layer"]
        self.devices = self.map_size * self.layer_size
        self.layers_here = velocity_shape[1]
        self.rows = velocity_shape[2]
        self.ny = velocity_shape[3]
        self.layers = self.layers_here * self.layer_size
        self.cols = self.ny // self.devices
        self.width = LANES // self.rows
        self.halo = (self.width - self.cols) // 2
        self.low = self.halo - REACH
        self.wide = self.cols + 2 * REACH
        self.half = self.wide // 2
        self.gap = self.low + self.wide
        self.local_cols = self.ny // self.layer_size
        self.per_chunk = LANES // self.cols
        self.chunks = self.ny // LANES
        self.column_count = self.rows * self.map_size * self.ny
        self.vel_rows = 2 * self.layers_here
        self.in_rows = self.vel_rows + 1
        self.left_at = self.gap
        self.right_at = self.gap + self.cols // 2 + 1
        self.out_rows = self.layers_here + 1
        self.unrolled = self.map_size <= 8
        assert self.layer_size & (self.layer_size - 1) == 0
        assert self.width * self.rows == LANES and self.cols * self.per_chunk == LANES
        assert self.low >= 0 and self.wide % 2 == 0 and self.width - self.wide >= self.half
        assert 2 * self.cols <= self.width and self.local_cols % LANES == 0
        assert self.vel_rows == 8 and self.rows == 2 and 4 * self.cols <= LANES and self.map_size % 8 == 0

    def chunk_place(self, i):
        here = self.local_cols // LANES
        return group_at(i // here) * here + (here - 1 - i % here)


def group_at(layer):
    return layer ^ (layer >> 1)


def repeat(plan, count, body, carry=0):
    if plan.unrolled:
        for index in range(count):
            carry = body(index, carry)
        return carry
    return lax.fori_loop(0, count, body, carry)


def lane_roll(value, shift):
    shift = shift % LANES
    return value if shift == 0 else pltpu.roll(value, shift, 1)


def pack_kernel(
    plan, vel_hbm, driving_hbm, observed_hbm, log_hbm, mask_hbm, out_ref,
    vel_ref, driving_ref, observed_ref, log_ref, mask_ref, arrival,
):
    width, rows, cols, half = plan.width, plan.rows, plan.cols, plan.half
    piece = vel_ref.shape[0] // VELOCITY_COPIES
    spans = [pl.ds(n * piece, piece) for n in range(VELOCITY_COPIES)]
    pairs = [(vel_hbm.at[span, :], vel_ref.at[span, :]) for span in spans] + [
        (driving_hbm, driving_ref),
        (observed_hbm, observed_ref),
        (log_hbm, log_ref),
        (mask_hbm, mask_ref),
    ]
    copies = [pltpu.make_async_copy(pair[0], pair[1], arrival.at[n]) for n, pair in enumerate(pairs)]
    for copy in copies:
        copy.start()
    shape = (plan.vel_rows, LANES)
    lane = lax.broadcasted_iota(jnp.int32, shape, 1)
    sub = lax.broadcasted_iota(jnp.int32, shape, 0)
    in_gap = jnp.logical_not(jnp.logical_and(lane % width >= plan.low, lane % width < plan.gap))
    no_line = jnp.zeros((1, LANES), jnp.float32)

    def slide(part, start, length, place):
        step, offset = start // LANES, start % LANES
        value = part(step)
        if offset + length > LANES:
            after = part(step + 1)
            value = jnp.where(lax.broadcasted_iota(jnp.int32, value.shape, 1) >= offset, value, after)
        return lane_roll(value, place - offset)

    for copy in copies[:VELOCITY_COPIES]:
        copy.wait()

    def chunk_windows(i, carry):
        def velocity(r):
            def part(step):
                chunk = i + step
                if isinstance(chunk, int) and not 0 <= chunk < plan.chunks:
                    return jnp.zeros(shape, jnp.float32)
                at = chunk if isinstance(chunk, int) else jnp.clip(chunk, 0, plan.chunks - 1)
                value = vel_ref[pl.ds(at * rows + r, plan.vel_rows, stride=plan.chunks * rows), :]
                if isinstance(chunk, int):
                    return value
                return jnp.where(jnp.logical_and(chunk >= 0, chunk < plan.chunks), value, 0.0)

            return part

        for t in range(plan.per_chunk):
            block = None
            for r in range(rows):
                value = slide(velocity(r), plan.cols * t - plan.halo, width, r * width)
                block = value if block is None else jnp.where(lane >= r * width, value, block)
            at = plan.chunk_place(i) * plan.per_chunk * plan.in_rows
            if not isinstance(at, int):
                at = pl.multiple_of(at, 8)
            at = at + (plan.per_chunk - 1 - t) * plan.in_rows
            out_ref[pl.ds(at, plan.vel_rows), :] = jnp.where(in_gap, 0.0, block)
            out_ref[pl.ds(at + plan.vel_rows, 1), :] = no_line
        return carry

    repeat(plan, plan.chunks, chunk_windows)
    for copy in copies[VELOCITY_COPIES:]:
        copy.wait()

    place = lax.axis_index("layer")
    local_chunks = plan.local_cols // LANES

    skip = local_chunks * rows
    no_block = jnp.zeros(shape, jnp.float32)

    def whole(ref, row):
        return jnp.broadcast_to(ref[row : row + 1, :], shape).astype(jnp.float32)

    def gap_part(r, step):
        at = step * rows + r
        observed = jnp.where(sub < 2, whole(observed_ref, at), whole(observed_ref, skip + at))
        return jnp.where(sub < 4, observed, jnp.where(sub < 6, whole(mask_ref, at), whole(log_ref, at)))

    def driving_part(r, step):
        at = step * rows + r
        return jnp.where(sub < 2, whole(driving_ref, at), whole(driving_ref, skip + at))

    def sequence(make):
        return [
            [no_block] + [make(r, step) for step in range(local_chunks)] + [no_block] for r in range(rows)
        ]

    gap_parts, driving_parts = sequence(gap_part), sequence(driving_part)
    own = plan.local_cols // cols
    spill = -(-REACH // cols)

    def column_block(q):
        start = q * cols
        block = None
        for r in range(rows):

            def in_gaps(step):
                return gap_parts[r][step + 1]

            def of_driving(step):
                return driving_parts[r][step + 1]

            at = r * width
            first = slide(in_gaps, start - REACH, half, (at + plan.gap) % LANES)
            second = slide(in_gaps, start - REACH + half, half, (at + plan.gap) % LANES)
            before = slide(of_driving, start - BED_REACH, BED_REACH, (at + plan.left_at) % LANES)
            after = slide(of_driving, start + cols, BED_REACH, (at + plan.right_at) % LANES)
            ahead = (lane + (LANES - plan.gap - at)) % LANES
            of_observed = sub < 4
            first = jnp.where(jnp.logical_and(of_observed, ahead < BED_REACH), before, first)
            second = jnp.where(jnp.logical_and(of_observed, ahead >= plan.right_at - plan.gap), after, second)
            value = jnp.where(sub % 2 == 0, first, second)
            ahead = (lane + (LANES - plan.gap)) % LANES
            block = value if block is None else jnp.where(ahead >= r * width, value, block)
        owner = place if 0 <= q < own else place - 1 if q < 0 else place + 1
        at = pl.multiple_of(group_at(owner) * (own * plan.in_rows), 8) + (own - 1 - q % own) * plan.in_rows
        here = pl.ds(at, plan.vel_rows)
        out_ref[here, :] = jnp.where(in_gap, block, out_ref[here, :])
        if not 0 <= q < own:
            return
        line = None
        step, offset = start // LANES, start % LANES
        for r in range(rows):
            for c in range(2):
                row = c * skip + step * rows + r
                put = (2 * r + c) * cols
                value = lane_roll(driving_ref[row : row + 1, :], put - offset)
                line = value if line is None else jnp.where(lane[:1] >= put, value, line)
        out_ref[pl.ds(at + plan.vel_rows, 1), :] = line

    for q in range(own):
        column_block(q)

    @pl.when(place > 0)
    def _():
        for q in range(-spill, 0):
            column_block(q)

    @pl.when(place < plan.layer_size - 1)
    def _():
        for q in range(own, own + spill):
            column_block(q)


def solve_kernel(plan, in_ref, out_ref, field, eta_ref, side, rhs, faces, ratio, inverse, swapped, eta_swapped):
    size, width, rows = plan.map_size, plan.width, plan.rows
    layers, here = plan.layers, plan.layers_here
    shape = (size, LANES)
    lane = lax.broadcasted_iota(jnp.int32, shape, 1)
    last_group = lane >= LANES - width
    first_group = lane < width
    def block_row(part, rows_of_block, row):
        first = group_at(part) * size * rows_of_block
        return pl.ds(first + row, size, stride=rows_of_block)

    def arrived(part, row):
        return in_ref[block_row(part, plan.in_rows, row), :]

    def over_parts(row):
        total = arrived(0, row)
        for part in range(1, plan.layer_size):
            total = total + arrived(part, row)
        return total

    def moved(value, source, target):
        return lane_roll(value, target - source)

    def from_gap(halves):
        left, right = (moved(value, plan.gap, plan.low + h * plan.half) for h, value in enumerate(halves))
        return jnp.where(lane % width < plan.low + plan.half, left, right)

    def from_line(c):
        plane = None
        for r in range(rows):
            value = moved(line, (2 * r + c) * plan.cols, r * width + plan.halo)
            plane = value if plane is None else jnp.where(lane >= r * width, value, plane)
        return plane

    def driving_of(c, halves):
        left = moved(halves[0], plan.left_at, plan.halo - BED_REACH)
        right = moved(halves[1], plan.right_at, plan.halo + plan.cols)
        return jnp.where(centre, from_line(c), jnp.where(lane % width < plan.halo, left, right))

    body = pl.ds(PAD, size)

    def x_pair(ref, index):
        same = ref[index + (body,)]
        after = jnp.where(last_group, ref[index + (pl.ds(PAD - 1, size),)], same)
        before = jnp.where(first_group, ref[index + (pl.ds(PAD + 1, size),)], same)
        return after, before

    def swap_in(c, k, value):
        swapped[c, k, body] = lane_roll(value, width)

    edge = jnp.zeros((2, layers, PAD, LANES), jnp.float32)
    swapped[:, :, pl.ds(0, PAD)] = edge
    swapped[:, :, pl.ds(PAD + size, PAD)] = edge

    def y_pair(value):
        return lane_roll(value, -1), lane_roll(value, 1)

    def viscosity(rate):
        return jnp.exp2(jnp.log(strain_floor + rate) * (-1.0 / (3.0 * math.log(2.0))))

    for part in range(plan.layer_size):
        for c in range(2):
            for k in range(here):
                value = arrived(part, c * here + k)
                field[c, part * here + k] = value
                swap_in(c, part * here + k, value)
    line = over_parts(plan.vel_rows)
    gaps = [[over_parts(2 * n), over_parts(2 * n + 1)] for n in range(4)]
    reached = jnp.logical_and(lane % width >= plan.low, lane % width < plan.gap)
    centre = jnp.logical_and(lane % width >= plan.halo, lane % width < plan.halo + plan.cols)
    driving = [2.0 * driving_of(c, gaps[c]) for c in range(2)]
    observed = [from_gap(gaps[c]) for c in range(2)]
    mask = jnp.where(reached, from_gap(gaps[2]), 0.0)
    ice = mask != 0.0
    friction = jnp.where(mask == 1.0, jnp.exp(from_gap(gaps[3])), 0.0)

    def stencil(k, keep):
        u, v = field[0, k], field[1, k]
        u_east, u_west = x_pair(swapped, (0, k))
        v_east, v_west = x_pair(swapped, (1, k))
        u_north, u_south = y_pair(u)
        v_north, v_south = y_pair(v)
        stretch_x = u_east - u_west
        stretch_y = v_north - v_south
        shear = 0.5 * ((u_north - u_south) + (v_east - v_west))
        rate = 0.25 * (stretch_x * (stretch_x + stretch_y) + stretch_y * stretch_y + shear * shear)
        half_v = 0.5 * v
        eta = viscosity(rate)
        eta_edge = viscosity(0.25 * (u * u + half_v * half_v))
        eta_swapped[k, body] = lane_roll(eta, width)
        eta_swapped[k, pl.ds(PAD - 1, 1)] = eta_edge[:1]
        eta_swapped[k, pl.ds(PAD + size, 1)] = eta_edge[size - 1 :]
        eta_east, eta_west = x_pair(eta_swapped, (k,))
        eta_north, eta_south = y_pair(eta)
        east, west = eta + eta_east, eta + eta_west
        north, south = eta + eta_north, eta + eta_south
        along_x, along_y = east + west, north + south
        eta_ref[k] = eta
        side[0, k] = 4.0 * along_x + along_y
        side[1, k] = along_x + 4.0 * along_y
        rhs[0, k] = driving[0] + (4.0 * (east * u_east + west * u_west) + (north * u_north + south * u_south))
        rhs[1, k] = driving[1] + ((east * v_east + west * v_west) + 4.0 * (north * v_north + south * v_south))
        if keep:
            faces[0, k] = east
            faces[1, k] = west
            faces[2, k] = north
            faces[3, k] = south

    def coupling_of(k):
        return (2.0 * layers * layers) * (eta_ref[k] + eta_ref[k + 1])

    middle = layers // 2
    zero = jnp.zeros(shape, jnp.float32)

    def eliminate(k, coupling, carry):
        before, passed, value = carry
        new_passed, new_value = [], []
        for c in range(2):
            rest = side[c, k] + passed[c]
            pivot = coupling + rest
            guess = pl.reciprocal(pivot, approx=True)
            correct = 2.0 - pivot * guess
            new_passed.append((coupling * rest * guess) * correct)
            inv = guess * correct
            inverse[c, k] = inv
            ratio[c, k] = coupling * inv
            out = (rhs[c, k] + before * value[c]) * inv
            rhs[c, k] = out
            new_value.append(out)
        return coupling, tuple(new_passed), tuple(new_value)

    def lower_step(k, carry):
        return eliminate(k, coupling_of(k), carry)

    def upper_step(k, carry):
        return eliminate(k, coupling_of(k - 1), carry)

    def fronts(step, carry):
        lower, upper = carry
        return lower_step(step, lower), upper_step(layers - 1 - step, upper)

    def spread(first, body):
        def outward(step, carry):
            below, above = carry
            return body(middle - 1 - step, below), body(middle + 1 + step, above)

        below, above = repeat(plan, layers - 1 - middle, outward, (first, first))
        for k in range(2 * middle - layers, -1, -1):
            below = body(k, below)
        return below, above

    def sweep(keep):
        def stencil_body(k, carry):
            stencil(k, keep)
            return carry

        bed = tuple(2.0 * friction for _ in range(2))
        lower, upper = (zero, bed, (zero, zero)), (zero, (zero, zero), (zero, zero))
        if plan.unrolled:
            stencil(0, keep)
            stencil(layers - 1, keep)
            for step in range(layers - 1 - middle):
                stencil(step + 1, keep)
                if layers - 2 - step > step + 1:
                    stencil(layers - 2 - step, keep)
                lower, upper = fronts(step, (lower, upper))
        else:
            repeat(plan, layers, stencil_body)
            lower, upper = repeat(plan, layers - 1 - middle, fronts, (lower, upper))
        for k in range(layers - 1 - middle, middle):
            lower = lower_step(k, lower)
        centre_value = []
        for c in range(2):
            pivot = side[c, middle] + lower[1][c] + upper[1][c]
            guess = pl.reciprocal(pivot, approx=True)
            inv = guess * (2.0 - pivot * guess)
            inverse[c, middle] = inv
            total = rhs[c, middle] + (lower[0] * lower[2][c] + upper[0] * upper[2][c])
            centre_value.append(jnp.where(ice, total * inv, 0.0))
            field[c, middle] = centre_value[c]
            swap_in(c, middle, centre_value[c])

        def solved(k, nearer):
            current = tuple(jnp.where(ice, rhs[c, k] + ratio[c, k] * nearer[c], 0.0) for c in range(2))
            for c in range(2):
                field[c, k] = current[c]
                swap_in(c, k, current[c])
            return current

        return spread(tuple(centre_value), solved)

    sweep(False)
    base, top = sweep(True)

    def send(k, carry):
        both = jnp.where(centre, field[0, k], lane_roll(field[1, k], plan.cols))
        out_ref[block_row(k // here, plan.out_rows, k % here), :] = both
        return carry

    repeat(plan, layers, send)

    mismatch = [jnp.where(ice, top[c] - observed[c], 0.0) for c in range(2)]
    source = [(2.0 * layers) * mismatch[c] for c in range(2)]

    def side_sum(k, value):
        east, west, north, south = (faces[n, k] for n in range(4))
        for c in range(2):
            swap_in(c, k, value[c])
        u_east, u_west = x_pair(swapped, (0, k))
        v_east, v_west = x_pair(swapped, (1, k))
        u_north, u_south = y_pair(value[0])
        v_north, v_south = y_pair(value[1])
        first = 4.0 * (east * u_east + west * u_west) + (north * u_north + south * u_south)
        second = (east * v_east + west * v_west) + 4.0 * (north * v_north + south * v_south)
        return first, second

    carried = tuple(source[c] * inverse[c, layers - 1] for c in range(2))
    for c in range(2):
        rhs[c, layers - 1] = carried[c]

    def first_inward(step, carried):
        k = layers - 2 - step
        out = tuple(coupling_of(k) * carried[c] * inverse[c, k] for c in range(2))
        for c in range(2):
            rhs[c, k] = out[c]
        return out

    carried = repeat(plan, layers - 2 - middle, first_inward, carried)
    first_middle = tuple(coupling_of(middle) * carried[c] * inverse[c, middle] for c in range(2))

    def first_outward(step, carry):
        below, above = carry
        low, high = middle - 1 - step, middle + 1 + step
        below = tuple(ratio[c, low] * below[c] for c in range(2))
        above = tuple(rhs[c, high] + ratio[c, high] * above[c] for c in range(2))
        for k, value in ((low, below), (high, above)):
            total = side_sum(k, value)
            for c in range(2):
                rhs[c, k] = total[c] * inverse[c, k]
        return below, above

    middle_sum = side_sum(middle, first_middle)
    below, above = repeat(plan, layers - 1 - middle, first_outward, (first_middle, first_middle))
    for k in range(2 * middle - layers, -1, -1):
        below = tuple(ratio[c, k] * below[c] for c in range(2))
        total = side_sum(k, below)
        for c in range(2):
            rhs[c, k] = total[c] * inverse[c, k]
    for c in range(2):
        rhs[c, layers - 1] = rhs[c, layers - 1] + source[c] * inverse[c, layers - 1]

    def second_inward(step, carry):
        below, above = carry
        low, high = step + 1, layers - 2 - step
        below = tuple(rhs[c, low] + (coupling_of(low - 1) * inverse[c, low]) * below[c] for c in range(2))
        above = tuple(rhs[c, high] + (coupling_of(high) * inverse[c, high]) * above[c] for c in range(2))
        for c in range(2):
            rhs[c, low] = below[c]
        return below, above

    below, above = repeat(
        plan,
        layers - 2 - middle,
        second_inward,
        (tuple(rhs[c, 0] for c in range(2)), tuple(rhs[c, layers - 1] for c in range(2))),
    )
    for k in range(layers - 1 - middle, middle):
        below = tuple(rhs[c, k] + (coupling_of(k - 1) * inverse[c, k]) * below[c] for c in range(2))
        for c in range(2):
            rhs[c, k] = below[c]
    adjoint = tuple(
        (middle_sum[c] + (coupling_of(middle - 1) * below[c] + coupling_of(middle) * above[c])) * inverse[c, middle]
        for c in range(2)
    )

    def second_outward(step, nearer):
        k = middle - 1 - step
        return tuple(rhs[c, k] + ratio[c, k] * nearer[c] for c in range(2))

    adjoint = repeat(plan, middle, second_outward, adjoint)
    adjoint = [jnp.where(ice, adjoint[c], 0.0) for c in range(2)]
    gradient = -friction * (base[0] * adjoint[0] + base[1] * adjoint[1])

    def partial_sum(value):
        line = jnp.sum(jnp.where(centre, value, 0.0), axis=0, keepdims=True)
        folded = line
        for r in range(1, rows):
            folded = folded + lane_roll(line, r * width)
        return jnp.broadcast_to(lane_roll(folded, plan.cols), shape)

    misfit_line = partial_sum(mismatch[0] * mismatch[0] + mismatch[1] * mismatch[1])
    grad_line = partial_sum(gradient * gradient)
    in_first = jnp.logical_and(lane >= plan.halo + plan.cols, lane < plan.halo + 2 * plan.cols)
    last_row = jnp.where(centre, gradient, jnp.where(in_first, misfit_line, grad_line))
    for part in range(plan.layer_size):
        out_ref[block_row(part, plan.out_rows, here), :] = last_row


def unpack_kernel(
    plan, in_ref, log_ref, vel_hbm, friction_hbm, misfit_hbm,
    vel_ref, friction_ref, misfit_ref, grad_ref, leave,
):
    here, width, cols, rows = plan.layers_here, plan.width, plan.cols, plan.rows
    local_chunks = plan.local_cols // LANES

    total = jnp.sum(
        in_ref[pl.ds(here, plan.devices, stride=plan.out_rows), :], axis=0, keepdims=True
    )
    line_lane = lax.broadcasted_iota(jnp.int32, (1, LANES), 1)

    def summed(first):
        ahead = (line_lane + (LANES - first % LANES)) % LANES
        return jnp.sum(jnp.where(ahead < cols, total, 0.0), axis=1, keepdims=True)

    misfit_sum = summed(plan.halo + cols)
    grad_sum = summed(plan.halo + cols + width)
    scale = step_size / jnp.sqrt(grad_sum / plan.column_count + 1e-06)

    lane = lax.broadcasted_iota(jnp.int32, (plan.out_rows, LANES), 1)
    def chunk(c, i):
        at = plan.chunk_place(i) * plan.per_chunk * plan.out_rows
        if not isinstance(at, int):
            at = pl.multiple_of(at, 8)
        turned = [
            lane_roll(in_ref[pl.ds(at + (plan.per_chunk - 1 - t) * plan.out_rows, plan.out_rows), :], t * cols)
            for t in range(plan.per_chunk)
        ]
        for r in range(rows):
            start = r * width + plan.halo + c * cols
            ahead = (lane + (LANES - start % LANES)) % LANES
            row = turned[0]
            for t in range(1, plan.per_chunk):
                row = jnp.where(ahead >= t * cols, turned[t], row)
            row = lane_roll(row, -start)
            vel_ref[c, pl.ds(i * rows + r, here, stride=plan.chunks * rows), :] = row[:here]
            if c == 0:
                owner, step = i // local_chunks, i % local_chunks
                grad_ref[owner, pl.ds(step * rows + r, 1), :] = row[here : here + 1]

    out = [pltpu.make_async_copy(vel_ref.at[c], vel_hbm.at[c], leave.at[c]) for c in range(2)]
    out.append(pltpu.make_async_copy(friction_ref, friction_hbm, leave.at[2]))
    out.append(pltpu.make_async_copy(misfit_ref, misfit_hbm, leave.at[3]))
    for c in range(2):

        def chunk_body(i, carry):
            chunk(c, i)
            return carry

        repeat(plan, plan.chunks, chunk_body)
        out[c].start()
    friction_ref[...] = log_ref[...] - grad_ref[lax.axis_index("layer")] * scale
    out[2].start()
    misfit_ref[...] = 0.5 * misfit_sum / plan.column_count
    out[3].start()
    for copy in out:
        copy.wait()


def as_lines(x):
    chunked = x.reshape(x.shape[:-1] + (x.shape[-1] // LANES, LANES))
    return jnp.swapaxes(chunked, -3, -2).reshape(-1, LANES)


def from_lines(lines, shape):
    chunked = lines.reshape(shape[:-2] + (shape[-1] // LANES, shape[-2], LANES))
    return jnp.swapaxes(chunked, -3, -2).reshape(shape)


def on_device(mesh_shape, velocity_init, driving, observed, log_friction, ice_mask):
    plan = Plan(mesh_shape, velocity_init.shape)
    vmem = pl.BlockSpec(memory_space=pltpu.VMEM)
    hbm = pl.BlockSpec(memory_space=pltpu.HBM)
    f32 = jnp.float32
    limit = pltpu.CompilerParams(vmem_limit_bytes=(16 if plan.unrolled else 40) * MIB)
    inputs = [as_lines(x) for x in (velocity_init, driving, observed, log_friction, ice_mask)]

    def exchange(blocks):
        shaped = blocks.reshape(blocks.shape[0], 1, LANES)
        ranks = [
            m * plan.layer_size + part
            for part in sorted(range(plan.layer_size), key=group_at)
            for m in reversed(range(plan.map_size))
        ]
        return lax.all_to_all(
            shaped, ("map", "layer"), split_axis=0, concat_axis=0, tiled=True, axis_index_groups=[ranks]
        ).reshape(blocks.shape)

    packed = pl.pallas_call(
        functools.partial(pack_kernel, plan),
        out_shape=jax.ShapeDtypeStruct((plan.devices * plan.in_rows, LANES), f32),
        in_specs=[hbm] * 5,
        out_specs=vmem,
        scratch_shapes=[pltpu.VMEM(x.shape, x.dtype) for x in inputs]
        + [
            pltpu.SemaphoreType.DMA((VELOCITY_COPIES + 4,)),
        ],
        compiler_params=limit,
        name="pack",
    )(*(pltpu.with_memory_space_constraint(x, pltpu.HBM) for x in inputs))

    windows = exchange(packed)

    plane = (plan.layers, plan.map_size, LANES)
    solved = pl.pallas_call(
        functools.partial(solve_kernel, plan),
        out_shape=jax.ShapeDtypeStruct((plan.devices * plan.out_rows, LANES), f32),
        in_specs=[vmem],
        out_specs=vmem,
        scratch_shapes=[
            pltpu.VMEM((2,) + plane, f32),
            pltpu.VMEM(plane, f32),
            pltpu.VMEM((2,) + plane, f32),
            pltpu.VMEM((2,) + plane, f32),
            pltpu.VMEM((4,) + plane, f32),
            pltpu.VMEM((2,) + plane, f32),
            pltpu.VMEM((2,) + plane, f32),
            pltpu.VMEM((2, plan.layers, plan.map_size + 2 * PAD, LANES), f32),
            pltpu.VMEM((plan.layers, plan.map_size + 2 * PAD, LANES), f32),
        ],
        compiler_params=limit,
        name="solve",
    )(windows)

    back = exchange(solved)

    vel_lines, log_lines = inputs[0].reshape(2, -1, LANES), inputs[3]
    velocity, friction_new, misfit = pl.pallas_call(
        functools.partial(unpack_kernel, plan),
        out_shape=(
            jax.ShapeDtypeStruct(vel_lines.shape, f32),
            jax.ShapeDtypeStruct(log_lines.shape, f32),
            jax.ShapeDtypeStruct((1, 1), f32),
        ),
        in_specs=[vmem] * 2,
        out_specs=(hbm, hbm, hbm),
        scratch_shapes=[
            pltpu.VMEM(vel_lines.shape, f32),
            pltpu.VMEM(log_lines.shape, f32),
            pltpu.VMEM((1, 1), f32),
            pltpu.VMEM((plan.layer_size,) + log_lines.shape, f32),
            pltpu.SemaphoreType.DMA((4,)),
        ],
        compiler_params=limit,
        name="unpack",
    )(back, log_lines)
    return (
        from_lines(velocity, velocity_init.shape),
        from_lines(friction_new, log_friction.shape),
        misfit.reshape(()),
    )


def solution(mesh):
    in_specs = (
        P(None, "layer", "map", None),
        P(None, "map", "layer"),
        P(None, "map", "layer"),
        P("map", "layer"),
        P("map", "layer"),
    )
    out_specs = (P(None, "layer", "map", None), P("map", "layer"), P())
    return jax.shard_map(
        functools.partial(on_device, dict(mesh.shape)),
        mesh=mesh,
        in_specs=in_specs,
        out_specs=out_specs,
        check_vma=False,
    )
```

```python
import functools
import math

import jax
import jax.numpy as jnp
from jax import lax
from jax.experimental import pallas as pl
from jax.experimental.pallas import tpu as pltpu
from jax.sharding import PartitionSpec as P

strain_floor = 0.1
step_size = 0.5
LANES = 128
REACH = 5
BED_REACH = 3
PAD = 8
MIB = 1 << 20
VELOCITY_COPIES = 4


class Plan:
    def __init__(self, mesh_shape, velocity_shape):
        self.map_size = mesh_shape["map"]
        self.layer_size = mesh_shape["layer"]
        self.devices = self.map_size * self.layer_size
        self.layers_here = velocity_shape[1]
        self.rows = velocity_shape[2]
        self.ny = velocity_shape[3]
        self.layers = self.layers_here * self.layer_size
        self.cols = self.ny // self.devices
        self.width = LANES // self.rows
        self.halo = (self.width - self.cols) // 2
        self.low = self.halo - REACH
        self.wide = self.cols + 2 * REACH
        self.half = self.wide // 2
        self.gap = self.low + self.wide
        self.local_cols = self.ny // self.layer_size
        self.per_chunk = LANES // self.cols
        self.chunks = self.ny // LANES
        self.column_count = self.rows * self.map_size * self.ny
        self.vel_rows = 2 * self.layers_here
        self.in_rows = self.vel_rows + 1
        self.left_at = self.gap
        self.right_at = self.gap + self.cols // 2 + 1
        self.out_rows = self.layers_here + 1
        self.unrolled = self.map_size <= 8
        assert self.width * self.rows == LANES and self.cols * self.per_chunk == LANES
        assert self.low >= 0 and self.wide % 2 == 0 and self.width - self.wide >= self.half
        assert 2 * self.cols <= self.width and self.local_cols % LANES == 0
        assert self.vel_rows == 8 and self.rows == 2 and 4 * self.cols <= LANES and self.map_size % 8 == 0


def repeat(plan, count, body, carry=0):
    if plan.unrolled:
        for index in range(count):
            carry = body(index, carry)
        return carry
    return lax.fori_loop(0, count, body, carry)


def lane_roll(value, shift):
    shift = shift % LANES
    return value if shift == 0 else pltpu.roll(value, shift, 1)


def pack_kernel(
    plan, vel_hbm, driving_hbm, observed_hbm, log_hbm, mask_hbm, out_ref,
    vel_ref, driving_ref, observed_ref, log_ref, mask_ref, arrival,
):
    width, rows, cols, half = plan.width, plan.rows, plan.cols, plan.half
    piece = vel_ref.shape[0] // VELOCITY_COPIES
    spans = [pl.ds(n * piece, piece) for n in range(VELOCITY_COPIES)]
    pairs = [(vel_hbm.at[span, :], vel_ref.at[span, :]) for span in spans] + [
        (driving_hbm, driving_ref),
        (observed_hbm, observed_ref),
        (log_hbm, log_ref),
        (mask_hbm, mask_ref),
    ]
    copies = [pltpu.make_async_copy(pair[0], pair[1], arrival.at[n]) for n, pair in enumerate(pairs)]
    for copy in copies:
        copy.start()
    shape = (plan.vel_rows, LANES)
    lane = lax.broadcasted_iota(jnp.int32, shape, 1)
    sub = lax.broadcasted_iota(jnp.int32, shape, 0)
    in_gap = jnp.logical_not(jnp.logical_and(lane % width >= plan.low, lane % width < plan.gap))
    no_line = jnp.zeros((1, LANES), jnp.float32)

    def slide(part, start, length, place):
        step, offset = start // LANES, start % LANES
        value = part(step)
        if offset + length > LANES:
            after = part(step + 1)
            value = jnp.where(lax.broadcasted_iota(jnp.int32, value.shape, 1) >= offset, value, after)
        return lane_roll(value, place - offset)

    for copy in copies[:VELOCITY_COPIES]:
        copy.wait()

    def velocity_chunk(at, r):
        return vel_ref[pl.ds(at * rows + r, plan.vel_rows, stride=plan.chunks * rows), :]

    held = None
    if plan.unrolled:
        held = [[velocity_chunk(at, r) for at in range(plan.chunks)] for r in range(rows)]

    def chunk_windows(i, carry):
        def velocity(r):
            def part(step):
                chunk = i + step
                if held is not None:
                    return held[r][chunk] if 0 <= chunk < plan.chunks else jnp.zeros(shape, jnp.float32)
                value = velocity_chunk(jnp.clip(chunk, 0, plan.chunks - 1), r)
                return jnp.where(jnp.logical_and(chunk >= 0, chunk < plan.chunks), value, 0.0)

            return part

        for t in range(plan.per_chunk):
            block = None
            for r in range(rows):
                value = slide(velocity(r), plan.cols * t - plan.halo, width, r * width)
                block = value if block is None else jnp.where(lane >= r * width, value, block)
            at = (plan.chunks - 1 - i) * plan.per_chunk * plan.in_rows
            if not isinstance(at, int):
                at = pl.multiple_of(at, 8)
            at = at + (plan.per_chunk - 1 - t) * plan.in_rows
            out_ref[pl.ds(at, plan.vel_rows), :] = jnp.where(in_gap, 0.0, block)
            out_ref[pl.ds(at + plan.vel_rows, 1), :] = no_line
        return carry

    repeat(plan, plan.chunks, chunk_windows)
    for copy in copies[VELOCITY_COPIES:]:
        copy.wait()

    place = lax.axis_index("layer")
    local_chunks = plan.local_cols // LANES

    skip = local_chunks * rows
    no_block = jnp.zeros(shape, jnp.float32)

    def whole(ref, row):
        return jnp.broadcast_to(ref[row : row + 1, :], shape).astype(jnp.float32)

    def gap_part(r, step):
        at = step * rows + r
        observed = jnp.where(sub < 2, whole(observed_ref, at), whole(observed_ref, skip + at))
        return jnp.where(sub < 4, observed, jnp.where(sub < 6, whole(mask_ref, at), whole(log_ref, at)))

    def driving_part(r, step):
        at = step * rows + r
        return jnp.where(sub < 2, whole(driving_ref, at), whole(driving_ref, skip + at))

    def sequence(make):
        return [
            [no_block] + [make(r, step) for step in range(local_chunks)] + [no_block] for r in range(rows)
        ]

    gap_parts, driving_parts = sequence(gap_part), sequence(driving_part)
    own = plan.local_cols // cols
    spill = -(-REACH // cols)

    def column_block(q):
        start = q * cols
        block = None
        for r in range(rows):

            def in_gaps(step):
                return gap_parts[r][step + 1]

            def of_driving(step):
                return driving_parts[r][step + 1]

            at = r * width
            first = slide(in_gaps, start - REACH, half, (at + plan.gap) % LANES)
            second = slide(in_gaps, start - REACH + half, half, (at + plan.gap) % LANES)
            before = slide(of_driving, start - BED_REACH, BED_REACH, (at + plan.left_at) % LANES)
            after = slide(of_driving, start + cols, BED_REACH, (at + plan.right_at) % LANES)
            ahead = (lane + (LANES - plan.gap - at)) % LANES
            of_observed = sub < 4
            first = jnp.where(jnp.logical_and(of_observed, ahead < BED_REACH), before, first)
            second = jnp.where(jnp.logical_and(of_observed, ahead >= plan.right_at - plan.gap), after, second)
            value = jnp.where(sub % 2 == 0, first, second)
            ahead = (lane + (LANES - plan.gap)) % LANES
            block = value if block is None else jnp.where(ahead >= r * width, value, block)
        at = pl.multiple_of((plan.layer_size - 1 - place) * (own * plan.in_rows), 8) + (own - 1 - q) * plan.in_rows
        here = pl.ds(at, plan.vel_rows)
        out_ref[here, :] = jnp.where(in_gap, block, out_ref[here, :])
        if not 0 <= q < own:
            return
        line = None
        step, offset = start // LANES, start % LANES
        for r in range(rows):
            for c in range(2):
                row = c * skip + step * rows + r
                put = (2 * r + c) * cols
                value = lane_roll(driving_ref[row : row + 1, :], put - offset)
                line = value if line is None else jnp.where(lane[:1] >= put, value, line)
        out_ref[pl.ds(at + plan.vel_rows, 1), :] = line

    for q in range(own):
        column_block(q)

    @pl.when(place > 0)
    def _():
        for q in range(-spill, 0):
            column_block(q)

    @pl.when(place < plan.layer_size - 1)
    def _():
        for q in range(own, own + spill):
            column_block(q)


def solve_kernel(plan, in_ref, out_ref, field, eta_ref, side, rhs, faces, ratio, inverse, swapped, eta_swapped):
    size, width, rows = plan.map_size, plan.width, plan.rows
    layers, here = plan.layers, plan.layers_here
    shape = (size, LANES)
    lane = lax.broadcasted_iota(jnp.int32, shape, 1)
    last_group = lane >= LANES - width
    first_group = lane < width
    def block_row(part, rows_of_block, row):
        first = (plan.layer_size - 1 - part) * size * rows_of_block
        return pl.ds(first + row, size, stride=rows_of_block)

    def arrived(part, row):
        return in_ref[block_row(part, plan.in_rows, row), :]

    def over_parts(row):
        total = arrived(0, row)
        for part in range(1, plan.layer_size):
            total = total + arrived(part, row)
        return total

    def moved(value, source, target):
        return lane_roll(value, target - source)

    def from_gap(halves):
        left, right = (moved(value, plan.gap, plan.low + h * plan.half) for h, value in enumerate(halves))
        return jnp.where(lane % width < plan.low + plan.half, left, right)

    def from_line(c):
        plane = None
        for r in range(rows):
            value = moved(line, (2 * r + c) * plan.cols, r * width + plan.halo)
            plane = value if plane is None else jnp.where(lane >= r * width, value, plane)
        return plane

    def driving_of(c, halves):
        left = moved(halves[0], plan.left_at, plan.halo - BED_REACH)
        right = moved(halves[1], plan.right_at, plan.halo + plan.cols)
        return jnp.where(centre, from_line(c), jnp.where(lane % width < plan.halo, left, right))

    body = pl.ds(PAD, size)

    def x_pair(ref, index):
        same = ref[index + (body,)]
        after = jnp.where(last_group, ref[index + (pl.ds(PAD - 1, size),)], same)
        before = jnp.where(first_group, ref[index + (pl.ds(PAD + 1, size),)], same)
        return after, before

    def swap_in(c, k, value):
        swapped[c, k, body] = lane_roll(value, width)

    edge = jnp.zeros((2, layers, PAD, LANES), jnp.float32)
    swapped[:, :, pl.ds(0, PAD)] = edge
    swapped[:, :, pl.ds(PAD + size, PAD)] = edge

    def y_pair(value):
        return lane_roll(value, -1), lane_roll(value, 1)

    def viscosity(rate):
        return jnp.exp2(jnp.log(strain_floor + rate) * (-1.0 / (3.0 * math.log(2.0))))

    for part in range(plan.layer_size):
        for c in range(2):
            for k in range(here):
                value = arrived(part, c * here + k)
                field[c, part * here + k] = value
                swap_in(c, part * here + k, value)
    line = over_parts(plan.vel_rows)
    gaps = [[over_parts(2 * n), over_parts(2 * n + 1)] for n in range(4)]
    reached = jnp.logical_and(lane % width >= plan.low, lane % width < plan.gap)
    centre = jnp.logical_and(lane % width >= plan.halo, lane % width < plan.halo + plan.cols)
    driving = [2.0 * driving_of(c, gaps[c]) for c in range(2)]
    observed = [from_gap(gaps[c]) for c in range(2)]
    mask = jnp.where(reached, from_gap(gaps[2]), 0.0)
    ice = mask != 0.0
    friction = jnp.where(mask == 1.0, jnp.exp(from_gap(gaps[3])), 0.0)

    def stencil(k, keep):
        u, v = field[0, k], field[1, k]
        u_east, u_west = x_pair(swapped, (0, k))
        v_east, v_west = x_pair(swapped, (1, k))
        u_north, u_south = y_pair(u)
        v_north, v_south = y_pair(v)
        stretch_x = u_east - u_west
        stretch_y = v_north - v_south
        shear = 0.5 * ((u_north - u_south) + (v_east - v_west))
        rate = 0.25 * (stretch_x * (stretch_x + stretch_y) + stretch_y * stretch_y + shear * shear)
        half_v = 0.5 * v
        eta = viscosity(rate)
        eta_edge = viscosity(0.25 * (u * u + half_v * half_v))
        eta_swapped[k, body] = lane_roll(eta, width)
        eta_swapped[k, pl.ds(PAD - 1, 1)] = eta_edge[:1]
        eta_swapped[k, pl.ds(PAD + size, 1)] = eta_edge[size - 1 :]
        eta_east, eta_west = x_pair(eta_swapped, (k,))
        eta_north, eta_south = y_pair(eta)
        east, west = eta + eta_east, eta + eta_west
        north, south = eta + eta_north, eta + eta_south
        along_x, along_y = east + west, north + south
        eta_ref[k] = eta
        side[0, k] = 4.0 * along_x + along_y
        side[1, k] = along_x + 4.0 * along_y
        rhs[0, k] = driving[0] + (4.0 * (east * u_east + west * u_west) + (north * u_north + south * u_south))
        rhs[1, k] = driving[1] + ((east * v_east + west * v_west) + 4.0 * (north * v_north + south * v_south))
        if keep:
            faces[0, k] = east
            faces[1, k] = west
            faces[2, k] = north
            faces[3, k] = south

    def coupling_of(k):
        return (2.0 * layers * layers) * (eta_ref[k] + eta_ref[k + 1])

    middle = layers // 2
    zero = jnp.zeros(shape, jnp.float32)

    def eliminate(k, coupling, carry):
        before, passed, value = carry
        new_passed, new_value = [], []
        for c in range(2):
            rest = side[c, k] + passed[c]
            pivot = coupling + rest
            guess = pl.reciprocal(pivot, approx=True)
            correct = 2.0 - pivot * guess
            new_passed.append((coupling * rest * guess) * correct)
            inv = guess * correct
            inverse[c, k] = inv
            ratio[c, k] = coupling * inv
            out = (rhs[c, k] + before * value[c]) * inv
            rhs[c, k] = out
            new_value.append(out)
        return coupling, tuple(new_passed), tuple(new_value)

    def lower_step(k, carry):
        return eliminate(k, coupling_of(k), carry)

    def upper_step(k, carry):
        return eliminate(k, coupling_of(k - 1), carry)

    def fronts(step, carry):
        lower, upper = carry
        return lower_step(step, lower), upper_step(layers - 1 - step, upper)

    def spread(first, body):
        def outward(step, carry):
            below, above = carry
            return body(middle - 1 - step, below), body(middle + 1 + step, above)

        below, above = repeat(plan, layers - 1 - middle, outward, (first, first))
        for k in range(2 * middle - layers, -1, -1):
            below = body(k, below)
        return below, above

    def sweep(keep):
        def stencil_body(k, carry):
            stencil(k, keep)
            return carry

        bed = tuple(2.0 * friction for _ in range(2))
        lower, upper = (zero, bed, (zero, zero)), (zero, (zero, zero), (zero, zero))
        if plan.unrolled:
            stencil(0, keep)
            stencil(layers - 1, keep)
            for step in range(layers - 1 - middle):
                stencil(step + 1, keep)
                if layers - 2 - step > step + 1:
                    stencil(layers - 2 - step, keep)
                lower, upper = fronts(step, (lower, upper))
        else:
            repeat(plan, layers, stencil_body)
            lower, upper = repeat(plan, layers - 1 - middle, fronts, (lower, upper))
        for k in range(layers - 1 - middle, middle):
            lower = lower_step(k, lower)
        centre_value = []
        for c in range(2):
            pivot = side[c, middle] + lower[1][c] + upper[1][c]
            guess = pl.reciprocal(pivot, approx=True)
            inv = guess * (2.0 - pivot * guess)
            inverse[c, middle] = inv
            total = rhs[c, middle] + (lower[0] * lower[2][c] + upper[0] * upper[2][c])
            centre_value.append(jnp.where(ice, total * inv, 0.0))
            field[c, middle] = centre_value[c]
            swap_in(c, middle, centre_value[c])

        def solved(k, nearer):
            current = tuple(jnp.where(ice, rhs[c, k] + ratio[c, k] * nearer[c], 0.0) for c in range(2))
            for c in range(2):
                field[c, k] = current[c]
                swap_in(c, k, current[c])
            return current

        return spread(tuple(centre_value), solved)

    sweep(False)
    base, top = sweep(True)

    def send(k, carry):
        both = jnp.where(centre, field[0, k], lane_roll(field[1, k], plan.cols))
        out_ref[block_row(k // here, plan.out_rows, k % here), :] = both
        return carry

    repeat(plan, layers, send)

    mismatch = [jnp.where(ice, top[c] - observed[c], 0.0) for c in range(2)]
    source = [(2.0 * layers) * mismatch[c] for c in range(2)]

    def side_sum(k, value):
        east, west, north, south = (faces[n, k] for n in range(4))
        for c in range(2):
            swap_in(c, k, value[c])
        u_east, u_west = x_pair(swapped, (0, k))
        v_east, v_west = x_pair(swapped, (1, k))
        u_north, u_south = y_pair(value[0])
        v_north, v_south = y_pair(value[1])
        first = 4.0 * (east * u_east + west * u_west) + (north * u_north + south * u_south)
        second = (east * v_east + west * v_west) + 4.0 * (north * v_north + south * v_south)
        return first, second

    carried = tuple(source[c] * inverse[c, layers - 1] for c in range(2))
    for c in range(2):
        rhs[c, layers - 1] = carried[c]

    def first_inward(step, carried):
        k = layers - 2 - step
        out = tuple(coupling_of(k) * carried[c] * inverse[c, k] for c in range(2))
        for c in range(2):
            rhs[c, k] = out[c]
        return out

    carried = repeat(plan, layers - 2 - middle, first_inward, carried)
    first_middle = tuple(coupling_of(middle) * carried[c] * inverse[c, middle] for c in range(2))

    def first_outward(step, carry):
        below, above = carry
        low, high = middle - 1 - step, middle + 1 + step
        below = tuple(ratio[c, low] * below[c] for c in range(2))
        above = tuple(rhs[c, high] + ratio[c, high] * above[c] for c in range(2))
        for k, value in ((low, below), (high, above)):
            total = side_sum(k, value)
            for c in range(2):
                rhs[c, k] = total[c] * inverse[c, k]
        return below, above

    middle_sum = side_sum(middle, first_middle)
    below, above = repeat(plan, layers - 1 - middle, first_outward, (first_middle, first_middle))
    for k in range(2 * middle - layers, -1, -1):
        below = tuple(ratio[c, k] * below[c] for c in range(2))
        total = side_sum(k, below)
        for c in range(2):
            rhs[c, k] = total[c] * inverse[c, k]
    for c in range(2):
        rhs[c, layers - 1] = rhs[c, layers - 1] + source[c] * inverse[c, layers - 1]

    def second_inward(step, carry):
        below, above = carry
        low, high = step + 1, layers - 2 - step
        below = tuple(rhs[c, low] + (coupling_of(low - 1) * inverse[c, low]) * below[c] for c in range(2))
        above = tuple(rhs[c, high] + (coupling_of(high) * inverse[c, high]) * above[c] for c in range(2))
        for c in range(2):
            rhs[c, low] = below[c]
        return below, above

    below, above = repeat(
        plan,
        layers - 2 - middle,
        second_inward,
        (tuple(rhs[c, 0] for c in range(2)), tuple(rhs[c, layers - 1] for c in range(2))),
    )
    for k in range(layers - 1 - middle, middle):
        below = tuple(rhs[c, k] + (coupling_of(k - 1) * inverse[c, k]) * below[c] for c in range(2))
        for c in range(2):
            rhs[c, k] = below[c]
    adjoint = tuple(
        (middle_sum[c] + (coupling_of(middle - 1) * below[c] + coupling_of(middle) * above[c])) * inverse[c, middle]
        for c in range(2)
    )

    def second_outward(step, nearer):
        k = middle - 1 - step
        return tuple(rhs[c, k] + ratio[c, k] * nearer[c] for c in range(2))

    adjoint = repeat(plan, middle, second_outward, adjoint)
    adjoint = [jnp.where(ice, adjoint[c], 0.0) for c in range(2)]
    gradient = -friction * (base[0] * adjoint[0] + base[1] * adjoint[1])

    def partial_sum(value):
        line = jnp.sum(jnp.where(centre, value, 0.0), axis=0, keepdims=True)
        folded = line
        for r in range(1, rows):
            folded = folded + lane_roll(line, r * width)
        return jnp.broadcast_to(lane_roll(folded, plan.cols), shape)

    misfit_line = partial_sum(mismatch[0] * mismatch[0] + mismatch[1] * mismatch[1])
    grad_line = partial_sum(gradient * gradient)
    in_first = jnp.logical_and(lane >= plan.halo + plan.cols, lane < plan.halo + 2 * plan.cols)
    last_row = jnp.where(centre, gradient, jnp.where(in_first, misfit_line, grad_line))
    for part in range(plan.layer_size):
        out_ref[block_row(part, plan.out_rows, here), :] = last_row


def unpack_kernel(
    plan, in_ref, log_ref, vel_hbm, friction_hbm, misfit_hbm,
    vel_ref, friction_ref, misfit_ref, grad_ref, leave,
):
    here, width, cols, rows = plan.layers_here, plan.width, plan.cols, plan.rows
    local_chunks = plan.local_cols // LANES

    total = jnp.sum(
        in_ref[pl.ds(here, plan.devices, stride=plan.out_rows), :], axis=0, keepdims=True
    )
    line_lane = lax.broadcasted_iota(jnp.int32, (1, LANES), 1)

    def summed(first):
        ahead = (line_lane + (LANES - first % LANES)) % LANES
        return jnp.sum(jnp.where(ahead < cols, total, 0.0), axis=1, keepdims=True)

    misfit_sum = summed(plan.halo + cols)
    grad_sum = summed(plan.halo + cols + width)
    scale = step_size / jnp.sqrt(grad_sum / plan.column_count + 1e-06)

    lane = lax.broadcasted_iota(jnp.int32, (plan.out_rows, LANES), 1)
    def chunk(c, i):
        at = (plan.chunks - 1 - i) * plan.per_chunk * plan.out_rows
        if not isinstance(at, int):
            at = pl.multiple_of(at, 8)
        turned = [
            lane_roll(in_ref[pl.ds(at + (plan.per_chunk - 1 - t) * plan.out_rows, plan.out_rows), :], t * cols)
            for t in range(plan.per_chunk)
        ]
        for r in range(rows):
            start = r * width + plan.halo + c * cols
            ahead = (lane + (LANES - start % LANES)) % LANES
            row = turned[0]
            for t in range(1, plan.per_chunk):
                row = jnp.where(ahead >= t * cols, turned[t], row)
            row = lane_roll(row, -start)
            vel_ref[c, pl.ds(i * rows + r, here, stride=plan.chunks * rows), :] = row[:here]
            if c == 0:
                owner, step = i // local_chunks, i % local_chunks
                grad_ref[owner, pl.ds(step * rows + r, 1), :] = row[here : here + 1]

    out = [pltpu.make_async_copy(vel_ref.at[c], vel_hbm.at[c], leave.at[c]) for c in range(2)]
    out.append(pltpu.make_async_copy(friction_ref, friction_hbm, leave.at[2]))
    out.append(pltpu.make_async_copy(misfit_ref, misfit_hbm, leave.at[3]))
    for c in range(2):

        def chunk_body(i, carry):
            chunk(c, i)
            return carry

        repeat(plan, plan.chunks, chunk_body)
        out[c].start()
    friction_ref[...] = log_ref[...] - grad_ref[lax.axis_index("layer")] * scale
    out[2].start()
    misfit_ref[...] = 0.5 * misfit_sum / plan.column_count
    out[3].start()
    for copy in out:
        copy.wait()


def as_lines(x):
    chunked = x.reshape(x.shape[:-1] + (x.shape[-1] // LANES, LANES))
    return jnp.swapaxes(chunked, -3, -2).reshape(-1, LANES)


def from_lines(lines, shape):
    chunked = lines.reshape(shape[:-2] + (shape[-1] // LANES, shape[-2], LANES))
    return jnp.swapaxes(chunked, -3, -2).reshape(shape)


def on_device(mesh_shape, velocity_init, driving, observed, log_friction, ice_mask):
    plan = Plan(mesh_shape, velocity_init.shape)
    vmem = pl.BlockSpec(memory_space=pltpu.VMEM)
    hbm = pl.BlockSpec(memory_space=pltpu.HBM)
    f32 = jnp.float32
    limit = pltpu.CompilerParams(vmem_limit_bytes=(16 if plan.unrolled else 40) * MIB)
    inputs = [as_lines(x) for x in (velocity_init, driving, observed, log_friction, ice_mask)]

    def exchange(blocks):
        shaped = blocks.reshape(blocks.shape[0], 1, LANES)
        ranks = [
            m * plan.layer_size + part
            for part in reversed(range(plan.layer_size))
            for m in reversed(range(plan.map_size))
        ]
        return lax.all_to_all(
            shaped, ("map", "layer"), split_axis=0, concat_axis=0, tiled=True, axis_index_groups=[ranks]
        ).reshape(blocks.shape)

    packed = pl.pallas_call(
        functools.partial(pack_kernel, plan),
        out_shape=jax.ShapeDtypeStruct((plan.devices * plan.in_rows, LANES), f32),
        in_specs=[hbm] * 5,
        out_specs=vmem,
        scratch_shapes=[pltpu.VMEM(x.shape, x.dtype) for x in inputs]
        + [
            pltpu.SemaphoreType.DMA((VELOCITY_COPIES + 4,)),
        ],
        compiler_params=limit,
        name="pack",
    )(*(pltpu.with_memory_space_constraint(x, pltpu.HBM) for x in inputs))

    windows = exchange(packed)

    plane = (plan.layers, plan.map_size, LANES)
    solved = pl.pallas_call(
        functools.partial(solve_kernel, plan),
        out_shape=jax.ShapeDtypeStruct((plan.devices * plan.out_rows, LANES), f32),
        in_specs=[vmem],
        out_specs=vmem,
        scratch_shapes=[
            pltpu.VMEM((2,) + plane, f32),
            pltpu.VMEM(plane, f32),
            pltpu.VMEM((2,) + plane, f32),
            pltpu.VMEM((2,) + plane, f32),
            pltpu.VMEM((4,) + plane, f32),
            pltpu.VMEM((2,) + plane, f32),
            pltpu.VMEM((2,) + plane, f32),
            pltpu.VMEM((2, plan.layers, plan.map_size + 2 * PAD, LANES), f32),
            pltpu.VMEM((plan.layers, plan.map_size + 2 * PAD, LANES), f32),
        ],
        compiler_params=limit,
        name="solve",
    )(windows)

    back = exchange(solved)

    vel_lines, log_lines = inputs[0].reshape(2, -1, LANES), inputs[3]
    velocity, friction_new, misfit = pl.pallas_call(
        functools.partial(unpack_kernel, plan),
        out_shape=(
            jax.ShapeDtypeStruct(vel_lines.shape, f32),
            jax.ShapeDtypeStruct(log_lines.shape, f32),
            jax.ShapeDtypeStruct((1, 1), f32),
        ),
        in_specs=[vmem] * 2,
        out_specs=(hbm, hbm, hbm),
        scratch_shapes=[
            pltpu.VMEM(vel_lines.shape, f32),
            pltpu.VMEM(log_lines.shape, f32),
            pltpu.VMEM((1, 1), f32),
            pltpu.VMEM((plan.layer_size,) + log_lines.shape, f32),
            pltpu.SemaphoreType.DMA((4,)),
        ],
        compiler_params=limit,
        name="unpack",
    )(back, log_lines)
    return (
        from_lines(velocity, velocity_init.shape),
        from_lines(friction_new, log_friction.shape),
        misfit.reshape(()),
    )


def solution(mesh):
    in_specs = (
        P(None, "layer", "map", None),
        P(None, "map", "layer"),
        P(None, "map", "layer"),
        P("map", "layer"),
        P("map", "layer"),
    )
    out_specs = (P(None, "layer", "map", None), P("map", "layer"), P())
    return jax.shard_map(
        functools.partial(on_device, dict(mesh.shape)),
        mesh=mesh,
        in_specs=in_specs,
        out_specs=out_specs,
        check_vma=False,
    )
```

```python
import functools
import math

import jax
import jax.numpy as jnp
from jax import lax
from jax.experimental import pallas as pl
from jax.experimental.pallas import tpu as pltpu
from jax.sharding import PartitionSpec as P

strain_floor = 0.1
step_size = 0.5
LANES = 128
REACH = 5
BED_REACH = 3
MIB = 1 << 20
VELOCITY_COPIES = 4


class Plan:
    def __init__(self, mesh_shape, velocity_shape):
        self.map_size = mesh_shape["map"]
        self.layer_size = mesh_shape["layer"]
        self.devices = self.map_size * self.layer_size
        self.layers_here = velocity_shape[1]
        self.rows = velocity_shape[2]
        self.ny = velocity_shape[3]
        self.layers = self.layers_here * self.layer_size
        self.cols = self.ny // self.devices
        self.width = LANES // self.rows
        self.halo = (self.width - self.cols) // 2
        self.low = self.halo - REACH
        self.wide = self.cols + 2 * REACH
        self.half = self.wide // 2
        self.gap = self.low + self.wide
        self.local_cols = self.ny // self.layer_size
        self.per_chunk = LANES // self.cols
        self.chunks = self.ny // LANES
        self.column_count = self.rows * self.map_size * self.ny
        self.vel_rows = 2 * self.layers_here
        self.in_rows = self.vel_rows + 1
        self.left_at = self.gap
        self.right_at = self.gap + self.cols // 2 + 1
        self.out_rows = self.layers_here + 1
        self.unrolled = self.map_size <= 8
        assert self.width * self.rows == LANES and self.cols * self.per_chunk == LANES
        assert self.low >= 0 and self.wide % 2 == 0 and self.width - self.wide >= self.half
        assert 2 * self.cols <= self.width and self.local_cols % LANES == 0
        assert self.vel_rows == 8 and self.rows == 2 and 4 * self.cols <= LANES


def repeat(plan, count, body, carry=0):
    if plan.unrolled:
        for index in range(count):
            carry = body(index, carry)
        return carry
    return lax.fori_loop(0, count, body, carry)


def lane_roll(value, shift):
    shift = shift % LANES
    return value if shift == 0 else pltpu.roll(value, shift, 1)


def pack_kernel(
    plan, vel_hbm, driving_hbm, observed_hbm, log_hbm, mask_hbm, out_ref,
    vel_ref, driving_ref, observed_ref, log_ref, mask_ref, arrival,
):
    width, rows, cols, half = plan.width, plan.rows, plan.cols, plan.half
    piece = vel_ref.shape[0] // VELOCITY_COPIES
    spans = [pl.ds(n * piece, piece) for n in range(VELOCITY_COPIES)]
    pairs = [(vel_hbm.at[span, :], vel_ref.at[span, :]) for span in spans] + [
        (driving_hbm, driving_ref),
        (observed_hbm, observed_ref),
        (log_hbm, log_ref),
        (mask_hbm, mask_ref),
    ]
    copies = [pltpu.make_async_copy(pair[0], pair[1], arrival.at[n]) for n, pair in enumerate(pairs)]
    for copy in copies:
        copy.start()
    shape = (plan.vel_rows, LANES)
    lane = lax.broadcasted_iota(jnp.int32, shape, 1)
    sub = lax.broadcasted_iota(jnp.int32, shape, 0)
    in_gap = jnp.logical_not(jnp.logical_and(lane % width >= plan.low, lane % width < plan.gap))
    no_line = jnp.zeros((1, LANES), jnp.float32)

    def slide(part, start, length, place):
        step, offset = start // LANES, start % LANES
        value = part(step)
        if offset + length > LANES:
            after = part(step + 1)
            value = jnp.where(lax.broadcasted_iota(jnp.int32, value.shape, 1) >= offset, value, after)
        return lane_roll(value, place - offset)

    for copy in copies[:VELOCITY_COPIES]:
        copy.wait()

    def chunk_windows(i, carry):
        def velocity(r):
            def part(step):
                chunk = i + step
                if isinstance(chunk, int) and not 0 <= chunk < plan.chunks:
                    return jnp.zeros(shape, jnp.float32)
                at = chunk if isinstance(chunk, int) else jnp.clip(chunk, 0, plan.chunks - 1)
                value = vel_ref[pl.ds(at * rows + r, plan.vel_rows, stride=plan.chunks * rows), :]
                if isinstance(chunk, int):
                    return value
                return jnp.where(jnp.logical_and(chunk >= 0, chunk < plan.chunks), value, 0.0)

            return part

        for t in range(plan.per_chunk):
            block = None
            for r in range(rows):
                value = slide(velocity(r), plan.cols * t - plan.halo, width, r * width)
                block = value if block is None else jnp.where(lane >= r * width, value, block)
            at = (plan.chunks - 1 - i) * plan.per_chunk * plan.in_rows
            if not isinstance(at, int):
                at = pl.multiple_of(at, 8)
            at = at + (plan.per_chunk - 1 - t) * plan.in_rows
            out_ref[pl.ds(at, plan.vel_rows), :] = jnp.where(in_gap, 0.0, block)
            out_ref[pl.ds(at + plan.vel_rows, 1), :] = no_line
        return carry

    repeat(plan, plan.chunks, chunk_windows)
    for copy in copies[VELOCITY_COPIES:]:
        copy.wait()

    place = lax.axis_index("layer")
    local_chunks = plan.local_cols // LANES

    skip = local_chunks * rows
    no_block = jnp.zeros(shape, jnp.float32)

    def whole(ref, row):
        return jnp.broadcast_to(ref[row : row + 1, :], shape).astype(jnp.float32)

    def gap_part(r, step):
        at = step * rows + r
        observed = jnp.where(sub < 2, whole(observed_ref, at), whole(observed_ref, skip + at))
        return jnp.where(sub < 4, observed, jnp.where(sub < 6, whole(mask_ref, at), whole(log_ref, at)))

    def driving_part(r, step):
        at = step * rows + r
        return jnp.where(sub < 2, whole(driving_ref, at), whole(driving_ref, skip + at))

    def sequence(make):
        return [
            [no_block] + [make(r, step) for step in range(local_chunks)] + [no_block] for r in range(rows)
        ]

    gap_parts, driving_parts = sequence(gap_part), sequence(driving_part)
    own = plan.local_cols // cols
    spill = -(-REACH // cols)

    def column_block(q):
        start = q * cols
        block = None
        for r in range(rows):

            def in_gaps(step):
                return gap_parts[r][step + 1]

            def of_driving(step):
                return driving_parts[r][step + 1]

            at = r * width
            first = slide(in_gaps, start - REACH, half, (at + plan.gap) % LANES)
            second = slide(in_gaps, start - REACH + half, half, (at + plan.gap) % LANES)
            before = slide(of_driving, start - BED_REACH, BED_REACH, (at + plan.left_at) % LANES)
            after = slide(of_driving, start + cols, BED_REACH, (at + plan.right_at) % LANES)
            ahead = (lane + (LANES - plan.gap - at)) % LANES
            of_observed = sub < 4
            first = jnp.where(jnp.logical_and(of_observed, ahead < BED_REACH), before, first)
            second = jnp.where(jnp.logical_and(of_observed, ahead >= plan.right_at - plan.gap), after, second)
            value = jnp.where(sub % 2 == 0, first, second)
            ahead = (lane + (LANES - plan.gap)) % LANES
            block = value if block is None else jnp.where(ahead >= r * width, value, block)
        at = pl.multiple_of((plan.layer_size - 1 - place) * (own * plan.in_rows), 8) + (own - 1 - q) * plan.in_rows
        here = pl.ds(at, plan.vel_rows)
        out_ref[here, :] = jnp.where(in_gap, block, out_ref[here, :])
        if not 0 <= q < own:
            return
        line = None
        step, offset = start // LANES, start % LANES
        for r in range(rows):
            for c in range(2):
                row = c * skip + step * rows + r
                put = (2 * r + c) * cols
                value = lane_roll(driving_ref[row : row + 1, :], put - offset)
                line = value if line is None else jnp.where(lane[:1] >= put, value, line)
        out_ref[pl.ds(at + plan.vel_rows, 1), :] = line

    for q in range(own):
        column_block(q)

    @pl.when(place > 0)
    def _():
        for q in range(-spill, 0):
            column_block(q)

    @pl.when(place < plan.layer_size - 1)
    def _():
        for q in range(own, own + spill):
            column_block(q)


def solve_kernel(plan, in_ref, out_ref, field, eta_ref, side, rhs, faces, weight, gain):
    size, width, rows = plan.map_size, plan.width, plan.rows
    layers, here = plan.layers, plan.layers_here
    shape = (size, LANES)
    lane = lax.broadcasted_iota(jnp.int32, shape, 1)
    sub = lax.broadcasted_iota(jnp.int32, shape, 0)
    last_group = lane >= LANES - width
    first_group = lane < width
    x_end = jnp.logical_and(last_group, sub == 0)
    x_start = jnp.logical_and(first_group, sub == size - 1)

    def block_row(part, rows_of_block, row):
        first = (plan.layer_size - 1 - part) * size * rows_of_block
        return pl.ds(first + row, size, stride=rows_of_block)

    def arrived(part, row):
        return in_ref[block_row(part, plan.in_rows, row), :]

    def over_parts(row):
        total = arrived(0, row)
        for part in range(1, plan.layer_size):
            total = total + arrived(part, row)
        return total

    def moved(value, source, target):
        return lane_roll(value, target - source)

    def from_gap(halves):
        left, right = (moved(value, plan.gap, plan.low + h * plan.half) for h, value in enumerate(halves))
        return jnp.where(lane % width < plan.low + plan.half, left, right)

    def from_line(c):
        plane = None
        for r in range(rows):
            value = moved(line, (2 * r + c) * plan.cols, r * width + plan.halo)
            plane = value if plane is None else jnp.where(lane >= r * width, value, plane)
        return plane

    def driving_of(c, halves):
        left = moved(halves[0], plan.left_at, plan.halo - BED_REACH)
        right = moved(halves[1], plan.right_at, plan.halo + plan.cols)
        return jnp.where(centre, from_line(c), jnp.where(lane % width < plan.halo, left, right))

    def x_pair(value, edge):
        after = lane_roll(value, -width)
        before = after if 2 * width == LANES else lane_roll(value, width)
        after = jnp.where(last_group, pltpu.roll(after, 1, 0), after)
        before = jnp.where(first_group, pltpu.roll(before, size - 1, 0), before)
        return jnp.where(x_end, edge, after), jnp.where(x_start, edge, before)

    def y_pair(value):
        return lane_roll(value, -1), lane_roll(value, 1)

    def viscosity(rate):
        return jnp.exp2(jnp.log(strain_floor + rate) * (-1.0 / (3.0 * math.log(2.0))))

    for part in range(plan.layer_size):
        for c in range(2):
            for k in range(here):
                field[c, part * here + k] = arrived(part, c * here + k)
    line = over_parts(plan.vel_rows)
    gaps = [[over_parts(2 * n), over_parts(2 * n + 1)] for n in range(4)]
    reached = jnp.logical_and(lane % width >= plan.low, lane % width < plan.gap)
    centre = jnp.logical_and(lane % width >= plan.halo, lane % width < plan.halo + plan.cols)
    driving = [2.0 * driving_of(c, gaps[c]) for c in range(2)]
    observed = [from_gap(gaps[c]) for c in range(2)]
    mask = jnp.where(reached, from_gap(gaps[2]), 0.0)
    ice = mask != 0.0
    friction = jnp.where(mask == 1.0, jnp.exp(from_gap(gaps[3])), 0.0)

    def stencil(k, keep):
        u, v = field[0, k], field[1, k]
        u_east, u_west = x_pair(u, 0.0)
        v_east, v_west = x_pair(v, 0.0)
        u_north, u_south = y_pair(u)
        v_north, v_south = y_pair(v)
        stretch_x = u_east - u_west
        stretch_y = v_north - v_south
        shear = 0.5 * ((u_north - u_south) + (v_east - v_west))
        rate = 0.25 * (stretch_x * (stretch_x + stretch_y) + stretch_y * stretch_y + shear * shear)
        half_v = 0.5 * v
        eta = viscosity(rate)
        eta_edge = viscosity(0.25 * (u * u + half_v * half_v))
        eta_east, eta_west = x_pair(eta, eta_edge)
        eta_north, eta_south = y_pair(eta)
        east, west = eta + eta_east, eta + eta_west
        north, south = eta + eta_north, eta + eta_south
        along_x, along_y = east + west, north + south
        eta_ref[k] = eta
        side[0, k] = 4.0 * along_x + along_y
        side[1, k] = along_x + 4.0 * along_y
        rhs[0, k] = driving[0] + (4.0 * (east * u_east + west * u_west) + (north * u_north + south * u_south))
        rhs[1, k] = driving[1] + ((east * v_east + west * v_west) + 4.0 * (north * v_north + south * v_south))
        if keep:
            faces[0, k] = east
            faces[1, k] = west
            faces[2, k] = north
            faces[3, k] = south

    def coupling_of(k):
        return (2.0 * layers * layers) * (eta_ref[k] + eta_ref[k + 1])

    def reciprocal(value):
        guess = pl.reciprocal(value, approx=True)
        return guess * (2.0 - value * guess)

    middle = layers // 2
    zero = jnp.zeros(shape, jnp.float32)
    one = jnp.ones(shape, jnp.float32)

    def advance(k, coupling, carry):
        flux, value, total = carry
        across = reciprocal(coupling)
        new_flux, new_value, new_total = [], [], []
        for c in range(2):
            here_flux = flux[c] + side[c, k] * value[c]
            after = value[c] + across * here_flux
            here_total = total[c] + value[c] * rhs[c, k]
            weight[c, k] = value[c]
            gain[c, k] = reciprocal((coupling * value[c]) * after)
            rhs[c, k] = here_total
            new_flux.append(here_flux)
            new_value.append(after)
            new_total.append(here_total)
        return tuple(new_flux), tuple(new_value), tuple(new_total)

    def lower_step(k, carry):
        return advance(k, coupling_of(k), carry)

    def upper_step(k, carry):
        return advance(k, coupling_of(k - 1), carry)

    def fronts(step, carry):
        lower, upper = carry
        return lower_step(step, lower), upper_step(layers - 1 - step, upper)

    def outward(body, carry):
        def both(step, carry):
            return body(middle - 1 - step, 0, body(middle + 1 + step, 1, carry))

        carry = repeat(plan, layers - 1 - middle, both, carry)
        for k in range(2 * middle - layers, -1, -1):
            carry = body(k, 0, carry)
        return carry

    def sweep(keep):
        def stencil_body(k, carry):
            stencil(k, keep)
            return carry

        lower = ((2.0 * friction,) * 2, (one, one), (zero, zero))
        upper = ((zero, zero), (one, one), (zero, zero))
        if plan.unrolled:
            stencil(0, keep)
            stencil(layers - 1, keep)
            for step in range(layers - 1 - middle):
                stencil(step + 1, keep)
                if layers - 2 - step > step + 1:
                    stencil(layers - 2 - step, keep)
                lower, upper = fronts(step, (lower, upper))
        else:
            repeat(plan, layers, stencil_body)
            lower, upper = repeat(plan, layers - 1 - middle, fronts, (lower, upper))
        for k in range(layers - 1 - middle, middle):
            lower = lower_step(k, lower)
        joints, start = [], []
        for c in range(2):
            below, above = lower[1][c], upper[1][c]
            product = below * above
            inv = reciprocal(side[c, middle] * product + (lower[0][c] * above + upper[0][c] * below))
            joint = (below, above, product, inv, reciprocal(below), reciprocal(above))
            joints.append(joint)
            solved = join(joint, rhs[c, middle], lower[2][c], upper[2][c])
            field[c, middle] = jnp.where(ice, solved, 0.0)
            start.append((solved * joint[4], solved * joint[5]))

        def solved_layer(k, which, carry):
            new = list(carry)
            for c in range(2):
                scaled = carry[2 * which + c] + rhs[c, k] * gain[c, k]
                field[c, k] = jnp.where(ice, weight[c, k] * scaled, 0.0)
                new[2 * which + c] = scaled
            return tuple(new)

        outward(solved_layer, (start[0][0], start[1][0], start[0][1], start[1][1]))
        return joints

    def join(joint, right, lower_total, upper_total):
        below, above, product, inv, _, _ = joint
        return (right * product + (lower_total * above + upper_total * below)) * inv

    sweep(False)
    joints = sweep(True)
    base = [field[c, 0] for c in range(2)]
    top = [field[c, layers - 1] for c in range(2)]

    def send(k, carry):
        both = jnp.where(centre, field[0, k], lane_roll(field[1, k], plan.cols))
        out_ref[block_row(k // here, plan.out_rows, k % here), :] = both
        return carry

    repeat(plan, layers, send)

    mismatch = [jnp.where(ice, top[c] - observed[c], 0.0) for c in range(2)]
    source = [(2.0 * layers) * mismatch[c] for c in range(2)]

    def side_sum(k, value):
        east, west, north, south = (faces[n, k] for n in range(4))
        u_east, u_west = x_pair(value[0], 0.0)
        v_east, v_west = x_pair(value[1], 0.0)
        u_north, u_south = y_pair(value[0])
        v_north, v_south = y_pair(value[1])
        first = 4.0 * (east * u_east + west * u_west) + (north * u_north + south * u_south)
        second = (east * v_east + west * v_west) + 4.0 * (north * v_north + south * v_south)
        return first, second

    def side_sum(k, value):
        east, west, north, south = (faces[n, k] for n in range(4))
        u_east, u_west = x_pair(value[0], 0.0)
        v_east, v_west = x_pair(value[1], 0.0)
        u_north, u_south = y_pair(value[0])
        v_north, v_south = y_pair(value[1])
        first = 4.0 * (east * u_east + west * u_west) + (north * u_north + south * u_south)
        second = (east * v_east + west * v_west) + 4.0 * (north * v_north + south * v_south)
        return first, second

    below_scaled = tuple(source[c] * joints[c][3] for c in range(2))
    first_middle = tuple(below_scaled[c] * joints[c][0] for c in range(2))
    above_scaled = tuple(first_middle[c] * joints[c][5] for c in range(2))
    middle_sum = side_sum(middle, first_middle)

    def below_layer(k, carry):
        total, correction = carry
        added = side_sum(k, tuple(weight[c, k] * below_scaled[c] for c in range(2)))
        total = tuple(total[c] + weight[c, k] * added[c] for c in range(2))
        return total, tuple(correction[c] + total[c] * gain[c, k] for c in range(2))

    def above_layer(k, carry):
        total, scaled = carry
        scaled = tuple(scaled[c] + source[c] * gain[c, k] for c in range(2))
        added = side_sum(k, tuple(weight[c, k] * scaled[c] for c in range(2)))
        return tuple(total[c] + weight[c, k] * added[c] for c in range(2)), scaled

    def adjoint_layers(step, carry):
        below, above = carry
        return below_layer(step, below), above_layer(middle + 1 + step, above)

    nothing = (zero, zero)
    below, above = repeat(
        plan, layers - 1 - middle, adjoint_layers, ((nothing, nothing), (tuple(source), above_scaled))
    )
    for k in range(layers - 1 - middle, middle):
        below = below_layer(k, below)
    adjoint = tuple(
        join(joints[c], middle_sum[c], below[0][c], above[0][c]) * joints[c][4] + below[1][c] for c in range(2)
    )
    adjoint = [jnp.where(ice, adjoint[c], 0.0) for c in range(2)]
    gradient = -friction * (base[0] * adjoint[0] + base[1] * adjoint[1])

    def partial_sum(value):
        line = jnp.sum(jnp.where(centre, value, 0.0), axis=0, keepdims=True)
        folded = line
        for r in range(1, rows):
            folded = folded + lane_roll(line, r * width)
        return jnp.broadcast_to(lane_roll(folded, plan.cols), shape)

    misfit_line = partial_sum(mismatch[0] * mismatch[0] + mismatch[1] * mismatch[1])
    grad_line = partial_sum(gradient * gradient)
    in_first = jnp.logical_and(lane >= plan.halo + plan.cols, lane < plan.halo + 2 * plan.cols)
    last_row = jnp.where(centre, gradient, jnp.where(in_first, misfit_line, grad_line))
    for part in range(plan.layer_size):
        out_ref[block_row(part, plan.out_rows, here), :] = last_row


def unpack_kernel(
    plan, in_ref, log_ref, vel_hbm, friction_hbm, misfit_hbm,
    vel_ref, friction_ref, misfit_ref, grad_ref, leave,
):
    here, width, cols, rows = plan.layers_here, plan.width, plan.cols, plan.rows
    local_chunks = plan.local_cols // LANES

    total = jnp.sum(
        in_ref[pl.ds(here, plan.devices, stride=plan.out_rows), :], axis=0, keepdims=True
    )
    line_lane = lax.broadcasted_iota(jnp.int32, (1, LANES), 1)

    def summed(first):
        ahead = (line_lane + (LANES - first % LANES)) % LANES
        return jnp.sum(jnp.where(ahead < cols, total, 0.0), axis=1, keepdims=True)

    misfit_sum = summed(plan.halo + cols)
    grad_sum = summed(plan.halo + cols + width)
    scale = step_size / jnp.sqrt(grad_sum / plan.column_count + 1e-06)

    lane = lax.broadcasted_iota(jnp.int32, (plan.out_rows, LANES), 1)
    def chunk(c, i):
        at = (plan.chunks - 1 - i) * plan.per_chunk * plan.out_rows
        if not isinstance(at, int):
            at = pl.multiple_of(at, 8)
        turned = [
            lane_roll(in_ref[pl.ds(at + (plan.per_chunk - 1 - t) * plan.out_rows, plan.out_rows), :], t * cols)
            for t in range(plan.per_chunk)
        ]
        for r in range(rows):
            start = r * width + plan.halo + c * cols
            ahead = (lane + (LANES - start % LANES)) % LANES
            row = turned[0]
            for t in range(1, plan.per_chunk):
                row = jnp.where(ahead >= t * cols, turned[t], row)
            row = lane_roll(row, -start)
            vel_ref[c, pl.ds(i * rows + r, here, stride=plan.chunks * rows), :] = row[:here]
            if c == 0:
                owner, step = i // local_chunks, i % local_chunks
                grad_ref[owner, pl.ds(step * rows + r, 1), :] = row[here : here + 1]

    out = [pltpu.make_async_copy(vel_ref.at[c], vel_hbm.at[c], leave.at[c]) for c in range(2)]
    out.append(pltpu.make_async_copy(friction_ref, friction_hbm, leave.at[2]))
    out.append(pltpu.make_async_copy(misfit_ref, misfit_hbm, leave.at[3]))
    for c in range(2):

        def chunk_body(i, carry):
            chunk(c, i)
            return carry

        repeat(plan, plan.chunks, chunk_body)
        out[c].start()
    friction_ref[...] = log_ref[...] - grad_ref[lax.axis_index("layer")] * scale
    out[2].start()
    misfit_ref[...] = 0.5 * misfit_sum / plan.column_count
    out[3].start()
    for copy in out:
        copy.wait()


def as_lines(x):
    chunked = x.reshape(x.shape[:-1] + (x.shape[-1] // LANES, LANES))
    return jnp.swapaxes(chunked, -3, -2).reshape(-1, LANES)


def from_lines(lines, shape):
    chunked = lines.reshape(shape[:-2] + (shape[-1] // LANES, shape[-2], LANES))
    return jnp.swapaxes(chunked, -3, -2).reshape(shape)


def on_device(mesh_shape, velocity_init, driving, observed, log_friction, ice_mask):
    plan = Plan(mesh_shape, velocity_init.shape)
    vmem = pl.BlockSpec(memory_space=pltpu.VMEM)
    hbm = pl.BlockSpec(memory_space=pltpu.HBM)
    f32 = jnp.float32
    limit = pltpu.CompilerParams(vmem_limit_bytes=(16 if plan.unrolled else 40) * MIB)
    inputs = [as_lines(x) for x in (velocity_init, driving, observed, log_friction, ice_mask)]

    def exchange(blocks):
        shaped = blocks.reshape(blocks.shape[0], 1, LANES)
        ranks = [
            m * plan.layer_size + part
            for part in reversed(range(plan.layer_size))
            for m in reversed(range(plan.map_size))
        ]
        return lax.all_to_all(
            shaped, ("map", "layer"), split_axis=0, concat_axis=0, tiled=True, axis_index_groups=[ranks]
        ).reshape(blocks.shape)

    packed = pl.pallas_call(
        functools.partial(pack_kernel, plan),
        out_shape=jax.ShapeDtypeStruct((plan.devices * plan.in_rows, LANES), f32),
        in_specs=[hbm] * 5,
        out_specs=vmem,
        scratch_shapes=[pltpu.VMEM(x.shape, x.dtype) for x in inputs]
        + [
            pltpu.SemaphoreType.DMA((VELOCITY_COPIES + 4,)),
        ],
        compiler_params=limit,
        name="pack",
    )(*(pltpu.with_memory_space_constraint(x, pltpu.HBM) for x in inputs))

    windows = exchange(packed)

    plane = (plan.layers, plan.map_size, LANES)
    solved = pl.pallas_call(
        functools.partial(solve_kernel, plan),
        out_shape=jax.ShapeDtypeStruct((plan.devices * plan.out_rows, LANES), f32),
        in_specs=[vmem],
        out_specs=vmem,
        scratch_shapes=[
            pltpu.VMEM((2,) + plane, f32),
            pltpu.VMEM(plane, f32),
            pltpu.VMEM((2,) + plane, f32),
            pltpu.VMEM((2,) + plane, f32),
            pltpu.VMEM((4,) + plane, f32),
            pltpu.VMEM((2,) + plane, f32),
            pltpu.VMEM((2,) + plane, f32),
        ],
        compiler_params=limit,
        name="solve",
    )(windows)

    back = exchange(solved)

    vel_lines, log_lines = inputs[0].reshape(2, -1, LANES), inputs[3]
    velocity, friction_new, misfit = pl.pallas_call(
        functools.partial(unpack_kernel, plan),
        out_shape=(
            jax.ShapeDtypeStruct(vel_lines.shape, f32),
            jax.ShapeDtypeStruct(log_lines.shape, f32),
            jax.ShapeDtypeStruct((1, 1), f32),
        ),
        in_specs=[vmem] * 2,
        out_specs=(hbm, hbm, hbm),
        scratch_shapes=[
            pltpu.VMEM(vel_lines.shape, f32),
            pltpu.VMEM(log_lines.shape, f32),
            pltpu.VMEM((1, 1), f32),
            pltpu.VMEM((plan.layer_size,) + log_lines.shape, f32),
            pltpu.SemaphoreType.DMA((4,)),
        ],
        compiler_params=limit,
        name="unpack",
    )(back, log_lines)
    return (
        from_lines(velocity, velocity_init.shape),
        from_lines(friction_new, log_friction.shape),
        misfit.reshape(()),
    )


def solution(mesh):
    in_specs = (
        P(None, "layer", "map", None),
        P(None, "map", "layer"),
        P(None, "map", "layer"),
        P("map", "layer"),
        P("map", "layer"),
    )
    out_specs = (P(None, "layer", "map", None), P("map", "layer"), P())
    return jax.shard_map(
        functools.partial(on_device, dict(mesh.shape)),
        mesh=mesh,
        in_specs=in_specs,
        out_specs=out_specs,
        check_vma=False,
    )
```

```python
import functools
import math

import jax
import jax.numpy as jnp
from jax import lax
from jax.experimental import pallas as pl
from jax.experimental.pallas import tpu as pltpu
from jax.sharding import PartitionSpec as P

strain_floor = 0.1
step_size = 0.5
LANES = 128
REACH = 5
BED_REACH = 3
MIB = 1 << 20
VELOCITY_COPIES = 4


class Plan:
    def __init__(self, mesh_shape, velocity_shape):
        self.map_size = mesh_shape["map"]
        self.layer_size = mesh_shape["layer"]
        self.devices = self.map_size * self.layer_size
        self.layers_here = velocity_shape[1]
        self.rows = velocity_shape[2]
        self.ny = velocity_shape[3]
        self.layers = self.layers_here * self.layer_size
        self.cols = self.ny // self.devices
        self.width = LANES // self.rows
        self.halo = (self.width - self.cols) // 2
        self.low = self.halo - REACH
        self.wide = self.cols + 2 * REACH
        self.half = self.wide // 2
        self.gap = self.low + self.wide
        self.local_cols = self.ny // self.layer_size
        self.per_chunk = LANES // self.cols
        self.chunks = self.ny // LANES
        self.column_count = self.rows * self.map_size * self.ny
        self.vel_rows = 2 * self.layers_here
        self.in_rows = self.vel_rows + 1
        self.left_at = self.gap
        self.right_at = self.gap + self.cols // 2 + 1
        self.out_rows = self.layers_here + 1
        self.unrolled = self.map_size <= 8
        assert self.width * self.rows == LANES and self.cols * self.per_chunk == LANES
        assert self.low >= 0 and self.wide % 2 == 0 and self.width - self.wide >= self.half
        assert 2 * self.cols <= self.width and self.local_cols % LANES == 0
        assert self.vel_rows == 8 and self.rows == 2 and 4 * self.cols <= LANES


def repeat(plan, count, body, carry=0):
    if plan.unrolled:
        for index in range(count):
            carry = body(index, carry)
        return carry
    return lax.fori_loop(0, count, body, carry)


def lane_roll(value, shift):
    shift = shift % LANES
    return value if shift == 0 else pltpu.roll(value, shift, 1)


def pack_kernel(
    plan, vel_hbm, driving_hbm, observed_hbm, log_hbm, mask_hbm, out_ref,
    vel_ref, driving_ref, observed_ref, log_ref, mask_ref, arrival,
):
    width, rows, cols, half = plan.width, plan.rows, plan.cols, plan.half
    piece = vel_ref.shape[0] // VELOCITY_COPIES
    spans = [pl.ds(n * piece, piece) for n in range(VELOCITY_COPIES)]
    pairs = [(vel_hbm.at[span, :], vel_ref.at[span, :]) for span in spans] + [
        (driving_hbm, driving_ref),
        (observed_hbm, observed_ref),
        (log_hbm, log_ref),
        (mask_hbm, mask_ref),
    ]
    copies = [pltpu.make_async_copy(pair[0], pair[1], arrival.at[n]) for n, pair in enumerate(pairs)]
    for copy in copies:
        copy.start()
    shape = (plan.vel_rows, LANES)
    lane = lax.broadcasted_iota(jnp.int32, shape, 1)
    sub = lax.broadcasted_iota(jnp.int32, shape, 0)
    in_gap = jnp.logical_not(jnp.logical_and(lane % width >= plan.low, lane % width < plan.gap))
    no_line = jnp.zeros((1, LANES), jnp.float32)

    def slide(part, start, length, place):
        step, offset = start // LANES, start % LANES
        value = part(step)
        if offset + length > LANES:
            after = part(step + 1)
            value = jnp.where(lax.broadcasted_iota(jnp.int32, value.shape, 1) >= offset, value, after)
        return lane_roll(value, place - offset)

    for copy in copies[:VELOCITY_COPIES]:
        copy.wait()

    def chunk_windows(i, carry):
        def velocity(r):
            def part(step):
                chunk = i + step
                if isinstance(chunk, int) and not 0 <= chunk < plan.chunks:
                    return jnp.zeros(shape, jnp.float32)
                at = chunk if isinstance(chunk, int) else jnp.clip(chunk, 0, plan.chunks - 1)
                value = vel_ref[pl.ds(at * rows + r, plan.vel_rows, stride=plan.chunks * rows), :]
                if isinstance(chunk, int):
                    return value
                return jnp.where(jnp.logical_and(chunk >= 0, chunk < plan.chunks), value, 0.0)

            return part

        for t in range(plan.per_chunk):
            block = None
            for r in range(rows):
                value = slide(velocity(r), plan.cols * t - plan.halo, width, r * width)
                block = value if block is None else jnp.where(lane >= r * width, value, block)
            at = (plan.chunks - 1 - i) * plan.per_chunk * plan.in_rows
            if not isinstance(at, int):
                at = pl.multiple_of(at, 8)
            at = at + (plan.per_chunk - 1 - t) * plan.in_rows
            out_ref[pl.ds(at, plan.vel_rows), :] = jnp.where(in_gap, 0.0, block)
            out_ref[pl.ds(at + plan.vel_rows, 1), :] = no_line
        return carry

    repeat(plan, plan.chunks, chunk_windows)
    for copy in copies[VELOCITY_COPIES:]:
        copy.wait()

    place = lax.axis_index("layer")
    local_chunks = plan.local_cols // LANES

    skip = local_chunks * rows
    no_block = jnp.zeros(shape, jnp.float32)

    def whole(ref, row):
        return jnp.broadcast_to(ref[row : row + 1, :], shape).astype(jnp.float32)

    def gap_part(r, step):
        at = step * rows + r
        observed = jnp.where(sub < 2, whole(observed_ref, at), whole(observed_ref, skip + at))
        return jnp.where(sub < 4, observed, jnp.where(sub < 6, whole(mask_ref, at), whole(log_ref, at)))

    def driving_part(r, step):
        at = step * rows + r
        return jnp.where(sub < 2, whole(driving_ref, at), whole(driving_ref, skip + at))

    def sequence(make):
        return [
            [no_block] + [make(r, step) for step in range(local_chunks)] + [no_block] for r in range(rows)
        ]

    gap_parts, driving_parts = sequence(gap_part), sequence(driving_part)
    own = plan.local_cols // cols
    spill = -(-REACH // cols)

    def column_block(q):
        start = q * cols
        block = None
        for r in range(rows):

            def in_gaps(step):
                return gap_parts[r][step + 1]

            def of_driving(step):
                return driving_parts[r][step + 1]

            at = r * width
            first = slide(in_gaps, start - REACH, half, (at + plan.gap) % LANES)
            second = slide(in_gaps, start - REACH + half, half, (at + plan.gap) % LANES)
            before = slide(of_driving, start - BED_REACH, BED_REACH, (at + plan.left_at) % LANES)
            after = slide(of_driving, start + cols, BED_REACH, (at + plan.right_at) % LANES)
            ahead = (lane + (LANES - plan.gap - at)) % LANES
            of_observed = sub < 4
            first = jnp.where(jnp.logical_and(of_observed, ahead < BED_REACH), before, first)
            second = jnp.where(jnp.logical_and(of_observed, ahead >= plan.right_at - plan.gap), after, second)
            value = jnp.where(sub % 2 == 0, first, second)
            ahead = (lane + (LANES - plan.gap)) % LANES
            block = value if block is None else jnp.where(ahead >= r * width, value, block)
        at = pl.multiple_of((plan.layer_size - 1 - place) * (own * plan.in_rows), 8) + (own - 1 - q) * plan.in_rows
        here = pl.ds(at, plan.vel_rows)
        out_ref[here, :] = jnp.where(in_gap, block, out_ref[here, :])
        if not 0 <= q < own:
            return
        line = None
        step, offset = start // LANES, start % LANES
        for r in range(rows):
            for c in range(2):
                row = c * skip + step * rows + r
                put = (2 * r + c) * cols
                value = lane_roll(driving_ref[row : row + 1, :], put - offset)
                line = value if line is None else jnp.where(lane[:1] >= put, value, line)
        out_ref[pl.ds(at + plan.vel_rows, 1), :] = line

    for q in range(own):
        column_block(q)

    @pl.when(place > 0)
    def _():
        for q in range(-spill, 0):
            column_block(q)

    @pl.when(place < plan.layer_size - 1)
    def _():
        for q in range(own, own + spill):
            column_block(q)


def solve_kernel(plan, in_ref, out_ref, field, eta_ref, side, rhs, faces, weight, gain):
    size, width, rows = plan.map_size, plan.width, plan.rows
    layers, here = plan.layers, plan.layers_here
    shape = (size, LANES)
    lane = lax.broadcasted_iota(jnp.int32, shape, 1)
    sub = lax.broadcasted_iota(jnp.int32, shape, 0)
    last_group = lane >= LANES - width
    first_group = lane < width
    x_end = jnp.logical_and(last_group, sub == 0)
    x_start = jnp.logical_and(first_group, sub == size - 1)

    def block_row(part, rows_of_block, row):
        first = (plan.layer_size - 1 - part) * size * rows_of_block
        return pl.ds(first + row, size, stride=rows_of_block)

    def arrived(part, row):
        return in_ref[block_row(part, plan.in_rows, row), :]

    def moved(value, source, target):
        return lane_roll(value, target - source)

    def from_gap(halves):
        left, right = (moved(value, plan.gap, plan.low + h * plan.half) for h, value in enumerate(halves))
        return jnp.where(lane % width < plan.low + plan.half, left, right)

    def from_line(c):
        plane = None
        for r in range(rows):
            value = moved(line, (2 * r + c) * plan.cols, r * width + plan.halo)
            plane = value if plane is None else jnp.where(lane >= r * width, value, plane)
        return plane

    def driving_of(c, halves):
        left = moved(halves[0], plan.left_at, plan.halo - BED_REACH)
        right = moved(halves[1], plan.right_at, plan.halo + plan.cols)
        return jnp.where(centre, from_line(c), jnp.where(lane % width < plan.halo, left, right))

    def x_pair(value, edge):
        after = lane_roll(value, -width)
        before = after if 2 * width == LANES else lane_roll(value, width)
        after = jnp.where(last_group, pltpu.roll(after, 1, 0), after)
        before = jnp.where(first_group, pltpu.roll(before, size - 1, 0), before)
        return jnp.where(x_end, edge, after), jnp.where(x_start, edge, before)

    def y_pair(value):
        return lane_roll(value, -1), lane_roll(value, 1)

    def viscosity(rate):
        return jnp.exp2(jnp.log(strain_floor + rate) * (-1.0 / (3.0 * math.log(2.0))))

    sums = [None] * plan.in_rows
    for part in range(plan.layer_size):
        for row in range(plan.in_rows):
            value = arrived(part, row)
            if row < plan.vel_rows:
                field[row // here, part * here + row % here] = value
            sums[row] = value if part == 0 else sums[row] + value
    line = sums[plan.vel_rows]
    gaps = [sums[2 * n : 2 * n + 2] for n in range(4)]
    reached = jnp.logical_and(lane % width >= plan.low, lane % width < plan.gap)
    centre = jnp.logical_and(lane % width >= plan.halo, lane % width < plan.halo + plan.cols)
    driving = [2.0 * driving_of(c, gaps[c]) for c in range(2)]
    observed = [from_gap(gaps[c]) for c in range(2)]
    mask = jnp.where(reached, from_gap(gaps[2]), 0.0)
    ice = mask != 0.0
    friction = jnp.where(mask == 1.0, jnp.exp(from_gap(gaps[3])), 0.0)

    def stencil(k, keep):
        u, v = field[0, k], field[1, k]
        u_east, u_west = x_pair(u, 0.0)
        v_east, v_west = x_pair(v, 0.0)
        u_north, u_south = y_pair(u)
        v_north, v_south = y_pair(v)
        stretch_x = u_east - u_west
        stretch_y = v_north - v_south
        shear = 0.5 * ((u_north - u_south) + (v_east - v_west))
        rate = 0.25 * (stretch_x * (stretch_x + stretch_y) + stretch_y * stretch_y + shear * shear)
        half_v = 0.5 * v
        eta = viscosity(rate)
        eta_edge = viscosity(0.25 * (u * u + half_v * half_v))
        eta_east, eta_west = x_pair(eta, eta_edge)
        eta_north, eta_south = y_pair(eta)
        east, west = eta + eta_east, eta + eta_west
        north, south = eta + eta_north, eta + eta_south
        along_x, along_y = east + west, north + south
        eta_ref[k] = eta
        side[0, k] = 4.0 * along_x + along_y
        side[1, k] = along_x + 4.0 * along_y
        rhs[0, k] = driving[0] + (4.0 * (east * u_east + west * u_west) + (north * u_north + south * u_south))
        rhs[1, k] = driving[1] + ((east * v_east + west * v_west) + 4.0 * (north * v_north + south * v_south))
        if keep:
            faces[0, k] = east
            faces[1, k] = west
            faces[2, k] = north
            faces[3, k] = south

    def coupling_of(k):
        return (2.0 * layers * layers) * (eta_ref[k] + eta_ref[k + 1])

    def reciprocal(value):
        guess = pl.reciprocal(value, approx=True)
        return guess * (2.0 - value * guess)

    middle = layers // 2
    zero = jnp.zeros(shape, jnp.float32)
    one = jnp.ones(shape, jnp.float32)

    def advance(k, coupling, carry):
        flux, value, total = carry
        across = reciprocal(coupling)
        new_flux, new_value, new_total = [], [], []
        for c in range(2):
            here_flux = flux[c] + side[c, k] * value[c]
            after = value[c] + across * here_flux
            here_total = total[c] + value[c] * rhs[c, k]
            weight[c, k] = value[c]
            gain[c, k] = reciprocal((coupling * value[c]) * after)
            rhs[c, k] = here_total
            new_flux.append(here_flux)
            new_value.append(after)
            new_total.append(here_total)
        return tuple(new_flux), tuple(new_value), tuple(new_total)

    def lower_step(k, carry):
        return advance(k, coupling_of(k), carry)

    def upper_step(k, carry):
        return advance(k, coupling_of(k - 1), carry)

    def fronts(step, carry):
        lower, upper = carry
        return lower_step(step, lower), upper_step(layers - 1 - step, upper)

    def outward(body, carry):
        def both(step, carry):
            return body(middle - 1 - step, 0, body(middle + 1 + step, 1, carry))

        carry = repeat(plan, layers - 1 - middle, both, carry)
        for k in range(2 * middle - layers, -1, -1):
            carry = body(k, 0, carry)
        return carry

    def sweep(keep):
        def stencil_body(k, carry):
            stencil(k, keep)
            return carry

        lower = ((2.0 * friction,) * 2, (one, one), (zero, zero))
        upper = ((zero, zero), (one, one), (zero, zero))
        if plan.unrolled:
            stencil(0, keep)
            stencil(layers - 1, keep)
            for step in range(layers - 1 - middle):
                stencil(step + 1, keep)
                if layers - 2 - step > step + 1:
                    stencil(layers - 2 - step, keep)
                lower, upper = fronts(step, (lower, upper))
        else:
            repeat(plan, layers, stencil_body)
            lower, upper = repeat(plan, layers - 1 - middle, fronts, (lower, upper))
        for k in range(layers - 1 - middle, middle):
            lower = lower_step(k, lower)
        joints, start = [], []
        for c in range(2):
            below, above = lower[1][c], upper[1][c]
            product = below * above
            inv = reciprocal(side[c, middle] * product + (lower[0][c] * above + upper[0][c] * below))
            joint = (below, above, product, inv, reciprocal(below), reciprocal(above))
            joints.append(joint)
            solved = join(joint, rhs[c, middle], lower[2][c], upper[2][c])
            field[c, middle] = jnp.where(ice, solved, 0.0)
            start.append((solved * joint[4], solved * joint[5]))

        def solved_layer(k, which, carry):
            new = list(carry)
            for c in range(2):
                scaled = carry[2 * which + c] + rhs[c, k] * gain[c, k]
                field[c, k] = jnp.where(ice, weight[c, k] * scaled, 0.0)
                new[2 * which + c] = scaled
            return tuple(new)

        outward(solved_layer, (start[0][0], start[1][0], start[0][1], start[1][1]))
        return joints

    def join(joint, right, lower_total, upper_total):
        below, above, product, inv, _, _ = joint
        return (right * product + (lower_total * above + upper_total * below)) * inv

    sweep(False)
    joints = sweep(True)
    base = [field[c, 0] for c in range(2)]
    top = [field[c, layers - 1] for c in range(2)]

    def send(k, carry):
        both = jnp.where(centre, field[0, k], lane_roll(field[1, k], plan.cols))
        out_ref[block_row(k // here, plan.out_rows, k % here), :] = both
        return carry

    repeat(plan, layers, send)

    mismatch = [jnp.where(ice, top[c] - observed[c], 0.0) for c in range(2)]
    source = [(2.0 * layers) * mismatch[c] for c in range(2)]

    def side_sum(k, value):
        east, west, north, south = (faces[n, k] for n in range(4))
        u_east, u_west = x_pair(value[0], 0.0)
        v_east, v_west = x_pair(value[1], 0.0)
        u_north, u_south = y_pair(value[0])
        v_north, v_south = y_pair(value[1])
        first = 4.0 * (east * u_east + west * u_west) + (north * u_north + south * u_south)
        second = (east * v_east + west * v_west) + 4.0 * (north * v_north + south * v_south)
        return first, second

    def side_sum(k, value):
        east, west, north, south = (faces[n, k] for n in range(4))
        u_east, u_west = x_pair(value[0], 0.0)
        v_east, v_west = x_pair(value[1], 0.0)
        u_north, u_south = y_pair(value[0])
        v_north, v_south = y_pair(value[1])
        first = 4.0 * (east * u_east + west * u_west) + (north * u_north + south * u_south)
        second = (east * v_east + west * v_west) + 4.0 * (north * v_north + south * v_south)
        return first, second

    below_scaled = tuple(source[c] * joints[c][3] for c in range(2))
    first_middle = tuple(below_scaled[c] * joints[c][0] for c in range(2))
    above_scaled = tuple(first_middle[c] * joints[c][5] for c in range(2))
    middle_sum = side_sum(middle, first_middle)

    def below_layer(k, carry):
        total, correction = carry
        added = side_sum(k, tuple(weight[c, k] * below_scaled[c] for c in range(2)))
        total = tuple(total[c] + weight[c, k] * added[c] for c in range(2))
        return total, tuple(correction[c] + total[c] * gain[c, k] for c in range(2))

    def above_layer(k, carry):
        total, scaled = carry
        scaled = tuple(scaled[c] + source[c] * gain[c, k] for c in range(2))
        added = side_sum(k, tuple(weight[c, k] * scaled[c] for c in range(2)))
        return tuple(total[c] + weight[c, k] * added[c] for c in range(2)), scaled

    def adjoint_layers(step, carry):
        below, above = carry
        return below_layer(step, below), above_layer(middle + 1 + step, above)

    nothing = (zero, zero)
    below, above = repeat(
        plan, layers - 1 - middle, adjoint_layers, ((nothing, nothing), (tuple(source), above_scaled))
    )
    for k in range(layers - 1 - middle, middle):
        below = below_layer(k, below)
    adjoint = tuple(
        join(joints[c], middle_sum[c], below[0][c], above[0][c]) * joints[c][4] + below[1][c] for c in range(2)
    )
    adjoint = [jnp.where(ice, adjoint[c], 0.0) for c in range(2)]
    gradient = -friction * (base[0] * adjoint[0] + base[1] * adjoint[1])

    def partial_sum(value):
        line = jnp.sum(jnp.where(centre, value, 0.0), axis=0, keepdims=True)
        folded = line
        for r in range(1, rows):
            folded = folded + lane_roll(line, r * width)
        return jnp.broadcast_to(lane_roll(folded, plan.cols), shape)

    misfit_line = partial_sum(mismatch[0] * mismatch[0] + mismatch[1] * mismatch[1])
    grad_line = partial_sum(gradient * gradient)
    in_first = jnp.logical_and(lane >= plan.halo + plan.cols, lane < plan.halo + 2 * plan.cols)
    last_row = jnp.where(centre, gradient, jnp.where(in_first, misfit_line, grad_line))
    for part in range(plan.layer_size):
        out_ref[block_row(part, plan.out_rows, here), :] = last_row


def unpack_kernel(
    plan, in_ref, log_ref, vel_hbm, friction_hbm, misfit_hbm,
    vel_ref, friction_ref, misfit_ref, grad_ref, leave,
):
    here, width, cols, rows = plan.layers_here, plan.width, plan.cols, plan.rows
    local_chunks = plan.local_cols // LANES

    total = jnp.sum(
        in_ref[pl.ds(here, plan.devices, stride=plan.out_rows), :], axis=0, keepdims=True
    )
    line_lane = lax.broadcasted_iota(jnp.int32, (1, LANES), 1)

    def summed(first):
        ahead = (line_lane + (LANES - first % LANES)) % LANES
        return jnp.sum(jnp.where(ahead < cols, total, 0.0), axis=1, keepdims=True)

    misfit_sum = summed(plan.halo + cols)
    grad_sum = summed(plan.halo + cols + width)
    scale = step_size / jnp.sqrt(grad_sum / plan.column_count + 1e-06)

    lane = lax.broadcasted_iota(jnp.int32, (plan.out_rows, LANES), 1)
    def chunk(c, i):
        at = (plan.chunks - 1 - i) * plan.per_chunk * plan.out_rows
        if not isinstance(at, int):
            at = pl.multiple_of(at, 8)
        turned = [
            lane_roll(in_ref[pl.ds(at + (plan.per_chunk - 1 - t) * plan.out_rows, plan.out_rows), :], t * cols)
            for t in range(plan.per_chunk)
        ]
        for r in range(rows):
            start = r * width + plan.halo + c * cols
            ahead = (lane + (LANES - start % LANES)) % LANES
            row = turned[0]
            for t in range(1, plan.per_chunk):
                row = jnp.where(ahead >= t * cols, turned[t], row)
            row = lane_roll(row, -start)
            vel_ref[c, pl.ds(i * rows + r, here, stride=plan.chunks * rows), :] = row[:here]
            if c == 0:
                owner, step = i // local_chunks, i % local_chunks
                grad_ref[owner, pl.ds(step * rows + r, 1), :] = row[here : here + 1]

    out = [pltpu.make_async_copy(vel_ref.at[c], vel_hbm.at[c], leave.at[c]) for c in range(2)]
    out.append(pltpu.make_async_copy(friction_ref, friction_hbm, leave.at[2]))
    out.append(pltpu.make_async_copy(misfit_ref, misfit_hbm, leave.at[3]))
    for c in range(2):

        def chunk_body(i, carry):
            chunk(c, i)
            return carry

        repeat(plan, plan.chunks, chunk_body)
        out[c].start()
    friction_ref[...] = log_ref[...] - grad_ref[lax.axis_index("layer")] * scale
    out[2].start()
    misfit_ref[...] = 0.5 * misfit_sum / plan.column_count
    out[3].start()
    for copy in out:
        copy.wait()


def as_lines(x):
    chunked = x.reshape(x.shape[:-1] + (x.shape[-1] // LANES, LANES))
    return jnp.swapaxes(chunked, -3, -2).reshape(-1, LANES)


def from_lines(lines, shape):
    chunked = lines.reshape(shape[:-2] + (shape[-1] // LANES, shape[-2], LANES))
    return jnp.swapaxes(chunked, -3, -2).reshape(shape)


def on_device(mesh_shape, velocity_init, driving, observed, log_friction, ice_mask):
    plan = Plan(mesh_shape, velocity_init.shape)
    vmem = pl.BlockSpec(memory_space=pltpu.VMEM)
    hbm = pl.BlockSpec(memory_space=pltpu.HBM)
    f32 = jnp.float32
    limit = pltpu.CompilerParams(vmem_limit_bytes=(16 if plan.unrolled else 40) * MIB)
    inputs = [as_lines(x) for x in (velocity_init, driving, observed, log_friction, ice_mask)]

    def exchange(blocks):
        shaped = blocks.reshape(blocks.shape[0], 1, LANES)
        ranks = [
            m * plan.layer_size + part
            for part in reversed(range(plan.layer_size))
            for m in reversed(range(plan.map_size))
        ]
        return lax.all_to_all(
            shaped, ("map", "layer"), split_axis=0, concat_axis=0, tiled=True, axis_index_groups=[ranks]
        ).reshape(blocks.shape)

    packed = pl.pallas_call(
        functools.partial(pack_kernel, plan),
        out_shape=jax.ShapeDtypeStruct((plan.devices * plan.in_rows, LANES), f32),
        in_specs=[hbm] * 5,
        out_specs=vmem,
        scratch_shapes=[pltpu.VMEM(x.shape, x.dtype) for x in inputs]
        + [
            pltpu.SemaphoreType.DMA((VELOCITY_COPIES + 4,)),
        ],
        compiler_params=limit,
        name="pack",
    )(*(pltpu.with_memory_space_constraint(x, pltpu.HBM) for x in inputs))

    windows = exchange(packed)

    plane = (plan.layers, plan.map_size, LANES)
    solved = pl.pallas_call(
        functools.partial(solve_kernel, plan),
        out_shape=jax.ShapeDtypeStruct((plan.devices * plan.out_rows, LANES), f32),
        in_specs=[vmem],
        out_specs=vmem,
        scratch_shapes=[
            pltpu.VMEM((2,) + plane, f32),
            pltpu.VMEM(plane, f32),
            pltpu.VMEM((2,) + plane, f32),
            pltpu.VMEM((2,) + plane, f32),
            pltpu.VMEM((4,) + plane, f32),
            pltpu.VMEM((2,) + plane, f32),
            pltpu.VMEM((2,) + plane, f32),
        ],
        compiler_params=limit,
        name="solve",
    )(windows)

    back = exchange(solved)

    vel_lines, log_lines = inputs[0].reshape(2, -1, LANES), inputs[3]
    velocity, friction_new, misfit = pl.pallas_call(
        functools.partial(unpack_kernel, plan),
        out_shape=(
            jax.ShapeDtypeStruct(vel_lines.shape, f32),
            jax.ShapeDtypeStruct(log_lines.shape, f32),
            jax.ShapeDtypeStruct((1, 1), f32),
        ),
        in_specs=[vmem] * 2,
        out_specs=(hbm, hbm, hbm),
        scratch_shapes=[
            pltpu.VMEM(vel_lines.shape, f32),
            pltpu.VMEM(log_lines.shape, f32),
            pltpu.VMEM((1, 1), f32),
            pltpu.VMEM((plan.layer_size,) + log_lines.shape, f32),
            pltpu.SemaphoreType.DMA((4,)),
        ],
        compiler_params=limit,
        name="unpack",
    )(back, log_lines)
    return (
        from_lines(velocity, velocity_init.shape),
        from_lines(friction_new, log_friction.shape),
        misfit.reshape(()),
    )


def solution(mesh):
    in_specs = (
        P(None, "layer", "map", None),
        P(None, "map", "layer"),
        P(None, "map", "layer"),
        P("map", "layer"),
        P("map", "layer"),
    )
    out_specs = (P(None, "layer", "map", None), P("map", "layer"), P())
    return jax.shard_map(
        functools.partial(on_device, dict(mesh.shape)),
        mesh=mesh,
        in_specs=in_specs,
        out_specs=out_specs,
        check_vma=False,
    )
```

```python
import functools
import math

import jax
import jax.numpy as jnp
from jax import lax
from jax.experimental import pallas as pl
from jax.experimental.pallas import tpu as pltpu
from jax.sharding import PartitionSpec as P

strain_floor = 0.1
step_size = 0.5
LANES = 128
REACH = 5
TOP_REACH = 1
MIB = 1 << 20
VELOCITY_COPIES = 4


class Plan:
    def __init__(self, mesh_shape, velocity_shape):
        self.map_size = mesh_shape["map"]
        self.layer_size = mesh_shape["layer"]
        self.devices = self.map_size * self.layer_size
        self.layers_here = velocity_shape[1]
        self.rows = velocity_shape[2]
        self.ny = velocity_shape[3]
        self.layers = self.layers_here * self.layer_size
        self.cols = self.ny // self.devices
        self.width = LANES // self.rows
        self.halo = (self.width - self.cols) // 2
        self.low = self.halo - REACH
        self.wide = self.cols + 2 * REACH
        self.half = self.wide // 2
        self.gap = self.low + self.wide
        self.local_cols = self.ny // self.layer_size
        self.per_chunk = LANES // self.cols
        self.chunks = self.ny // LANES
        self.column_count = self.rows * self.map_size * self.ny
        self.vel_rows = 2 * self.layers_here
        self.in_rows = self.vel_rows
        self.left_at = self.gap
        self.right_at = self.gap + self.cols // 2 + 3
        self.out_rows = self.layers_here + 1
        self.unrolled = self.map_size <= 8
        assert self.width * self.rows == LANES and self.cols * self.per_chunk == LANES
        assert self.low >= 0 and self.wide % 2 == 0 and self.width - self.wide >= self.half
        assert 2 * self.cols <= self.width and self.local_cols % LANES == 0
        assert self.vel_rows == 8 and self.rows == 2


def repeat(plan, count, body, carry=0):
    if plan.unrolled:
        for index in range(count):
            carry = body(index, carry)
        return carry
    return lax.fori_loop(0, count, body, carry)


def lane_roll(value, shift):
    shift = shift % LANES
    return value if shift == 0 else pltpu.roll(value, shift, 1)


def pack_kernel(
    plan, vel_hbm, driving_hbm, observed_hbm, log_hbm, mask_hbm, out_ref,
    vel_ref, driving_ref, observed_ref, log_ref, mask_ref, arrival,
):
    width, rows, cols, half = plan.width, plan.rows, plan.cols, plan.half
    piece = vel_ref.shape[0] // VELOCITY_COPIES
    spans = [pl.ds(n * piece, piece) for n in range(VELOCITY_COPIES)]
    pairs = [(vel_hbm.at[span, :], vel_ref.at[span, :]) for span in spans] + [
        (driving_hbm, driving_ref),
        (observed_hbm, observed_ref),
        (log_hbm, log_ref),
        (mask_hbm, mask_ref),
    ]
    copies = [pltpu.make_async_copy(pair[0], pair[1], arrival.at[n]) for n, pair in enumerate(pairs)]
    for copy in copies:
        copy.start()
    shape = (plan.vel_rows, LANES)
    lane = lax.broadcasted_iota(jnp.int32, shape, 1)
    sub = lax.broadcasted_iota(jnp.int32, shape, 0)
    in_gap = jnp.logical_not(jnp.logical_and(lane % width >= plan.low, lane % width < plan.gap))

    def slide(part, start, length, place):
        step, offset = start // LANES, start % LANES
        value = part(step)
        if offset + length > LANES:
            after = part(step + 1)
            value = jnp.where(lax.broadcasted_iota(jnp.int32, value.shape, 1) >= offset, value, after)
        return lane_roll(value, place - offset)

    for copy in copies[:VELOCITY_COPIES]:
        copy.wait()

    def chunk_windows(i, carry):
        def velocity(r):
            def part(step):
                chunk = i + step
                if isinstance(chunk, int) and not 0 <= chunk < plan.chunks:
                    return jnp.zeros(shape, jnp.float32)
                at = chunk if isinstance(chunk, int) else jnp.clip(chunk, 0, plan.chunks - 1)
                value = vel_ref[pl.ds(at * rows + r, plan.vel_rows, stride=plan.chunks * rows), :]
                if isinstance(chunk, int):
                    return value
                return jnp.where(jnp.logical_and(chunk >= 0, chunk < plan.chunks), value, 0.0)

            return part

        for t in range(plan.per_chunk):
            block = None
            for r in range(rows):
                value = slide(velocity(r), plan.cols * t - plan.halo, width, r * width)
                block = value if block is None else jnp.where(lane >= r * width, value, block)
            at = (plan.chunks - 1 - i) * plan.per_chunk * plan.in_rows
            if not isinstance(at, int):
                at = pl.multiple_of(at, 8)
            at = at + (plan.per_chunk - 1 - t) * plan.in_rows
            out_ref[pl.ds(at, plan.vel_rows), :] = jnp.where(in_gap, 0.0, block)
        return carry

    repeat(plan, plan.chunks, chunk_windows)
    for copy in copies[VELOCITY_COPIES:]:
        copy.wait()

    place = lax.axis_index("layer")
    local_chunks = plan.local_cols // LANES

    skip = local_chunks * rows
    no_block = jnp.zeros(shape, jnp.float32)

    def whole(ref, row):
        return jnp.broadcast_to(ref[row : row + 1, :], shape).astype(jnp.float32)

    def gap_part(r, step):
        at = step * rows + r
        driving = jnp.where(sub < 2, whole(driving_ref, at), whole(driving_ref, skip + at))
        return jnp.where(sub < 4, driving, jnp.where(sub < 6, whole(mask_ref, at), whole(log_ref, at)))

    def observed_part(r, step):
        at = step * rows + r
        return jnp.where(sub < 2, whole(observed_ref, at), whole(observed_ref, skip + at))

    def sequence(make):
        return [
            [no_block] + [make(r, step) for step in range(local_chunks)] + [no_block] for r in range(rows)
        ]

    gap_parts, observed_parts = sequence(gap_part), sequence(observed_part)
    own = plan.local_cols // cols
    spill = -(-REACH // cols)

    def column_block(q):
        start = q * cols
        block = None
        for r in range(rows):

            def in_gaps(step):
                return gap_parts[r][step + 1]

            def of_observed(step):
                return observed_parts[r][step + 1]

            at = r * width
            first = slide(in_gaps, start - REACH, half, (at + plan.gap) % LANES)
            second = slide(in_gaps, start - REACH + half, half, (at + plan.gap) % LANES)
            before = slide(of_observed, start - TOP_REACH, TOP_REACH, (at + plan.left_at) % LANES)
            after = slide(of_observed, start + cols, TOP_REACH, (at + plan.right_at) % LANES)
            ahead = (lane + (LANES - plan.gap - at)) % LANES
            shared = sub < 4
            first = jnp.where(jnp.logical_and(shared, ahead < TOP_REACH), before, first)
            second = jnp.where(jnp.logical_and(shared, ahead >= plan.right_at - plan.gap), after, second)
            value = jnp.where(sub % 2 == 0, first, second)
            ahead = (lane + (LANES - plan.gap)) % LANES
            block = value if block is None else jnp.where(ahead >= r * width, value, block)
        at = pl.multiple_of((plan.layer_size - 1 - place) * (own * plan.in_rows), 8) + (own - 1 - q) * plan.in_rows
        here = pl.ds(at, plan.vel_rows)
        out_ref[here, :] = jnp.where(in_gap, block, out_ref[here, :])

    for q in range(own):
        column_block(q)

    @pl.when(place > 0)
    def _():
        for q in range(-spill, 0):
            column_block(q)

    @pl.when(place < plan.layer_size - 1)
    def _():
        for q in range(own, own + spill):
            column_block(q)


def solve_kernel(plan, in_ref, observed_hbm, out_ref, observed_ref, arrival, field, eta_ref, side, rhs, faces, weight, gain):
    copy = pltpu.make_async_copy(observed_hbm, observed_ref, arrival)
    copy.start()
    size, width, rows = plan.map_size, plan.width, plan.rows
    layers, here = plan.layers, plan.layers_here
    shape = (size, LANES)
    lane = lax.broadcasted_iota(jnp.int32, shape, 1)
    sub = lax.broadcasted_iota(jnp.int32, shape, 0)
    last_group = lane >= LANES - width
    first_group = lane < width
    x_end = jnp.logical_and(last_group, sub == 0)
    x_start = jnp.logical_and(first_group, sub == size - 1)

    def block_row(part, rows_of_block, row):
        first = (plan.layer_size - 1 - part) * size * rows_of_block
        return pl.ds(first + row, size, stride=rows_of_block)

    def arrived(part, row):
        return in_ref[block_row(part, plan.in_rows, row), :]

    def moved(value, source, target):
        return lane_roll(value, target - source)

    def from_gap(halves):
        left, right = (moved(value, plan.gap, plan.low + h * plan.half) for h, value in enumerate(halves))
        return jnp.where(lane % width < plan.low + plan.half, left, right)

    def own_observed(c):
        column = lax.axis_index("map") * plan.cols
        local_chunks = plan.local_cols // LANES
        plane = None
        for r in range(rows):
            row = (c * local_chunks + column // LANES) * rows + r
            value = observed_ref[pl.ds(row, size, stride=2 * local_chunks * rows), :]
            value = pltpu.roll(value, (r * width + plan.halo + LANES - column % LANES) % LANES, 1)
            plane = value if plane is None else jnp.where(lane >= r * width, value, plane)
        return plane

    def observed_of(c, halves):
        left = moved(halves[0], plan.left_at, plan.halo - TOP_REACH)
        right = moved(halves[1], plan.right_at, plan.halo + plan.cols)
        return jnp.where(centre, own_observed(c), jnp.where(lane % width < plan.halo, left, right))

    def x_pair(value, edge):
        after = lane_roll(value, -width)
        before = after if 2 * width == LANES else lane_roll(value, width)
        after = jnp.where(last_group, pltpu.roll(after, 1, 0), after)
        before = jnp.where(first_group, pltpu.roll(before, size - 1, 0), before)
        return jnp.where(x_end, edge, after), jnp.where(x_start, edge, before)

    def y_pair(value):
        return lane_roll(value, -1), lane_roll(value, 1)

    def viscosity(rate):
        return jnp.exp2(jnp.log(strain_floor + rate) * (-1.0 / (3.0 * math.log(2.0))))

    sums = [None] * plan.in_rows
    for part in range(plan.layer_size):
        for row in range(plan.in_rows):
            value = arrived(part, row)
            field[row // here, part * here + row % here] = value
            sums[row] = value if part == 0 else sums[row] + value
    gaps = [sums[2 * n : 2 * n + 2] for n in range(4)]
    reached = jnp.logical_and(lane % width >= plan.low, lane % width < plan.gap)
    centre = jnp.logical_and(lane % width >= plan.halo, lane % width < plan.halo + plan.cols)
    driving = [2.0 * from_gap(gaps[c]) for c in range(2)]
    mask = jnp.where(reached, from_gap(gaps[2]), 0.0)
    ice = mask != 0.0
    friction = jnp.where(mask == 1.0, jnp.exp(from_gap(gaps[3])), 0.0)

    def stencil(k, keep):
        u, v = field[0, k], field[1, k]
        u_east, u_west = x_pair(u, 0.0)
        v_east, v_west = x_pair(v, 0.0)
        u_north, u_south = y_pair(u)
        v_north, v_south = y_pair(v)
        stretch_x = u_east - u_west
        stretch_y = v_north - v_south
        shear = 0.5 * ((u_north - u_south) + (v_east - v_west))
        rate = 0.25 * (stretch_x * (stretch_x + stretch_y) + stretch_y * stretch_y + shear * shear)
        half_v = 0.5 * v
        eta = viscosity(rate)
        eta_edge = viscosity(0.25 * (u * u + half_v * half_v))
        eta_east, eta_west = x_pair(eta, eta_edge)
        eta_north, eta_south = y_pair(eta)
        east, west = eta + eta_east, eta + eta_west
        north, south = eta + eta_north, eta + eta_south
        along_x, along_y = east + west, north + south
        eta_ref[k] = eta
        side[0, k] = 4.0 * along_x + along_y
        side[1, k] = along_x + 4.0 * along_y
        rhs[0, k] = driving[0] + (4.0 * (east * u_east + west * u_west) + (north * u_north + south * u_south))
        rhs[1, k] = driving[1] + ((east * v_east + west * v_west) + 4.0 * (north * v_north + south * v_south))
        if keep:
            faces[0, k] = east
            faces[1, k] = west
            faces[2, k] = north
            faces[3, k] = south

    def coupling_of(k):
        return (2.0 * layers * layers) * (eta_ref[k] + eta_ref[k + 1])

    def reciprocal(value):
        guess = pl.reciprocal(value, approx=True)
        return guess * (2.0 - value * guess)

    middle = layers // 2
    zero = jnp.zeros(shape, jnp.float32)
    one = jnp.ones(shape, jnp.float32)

    def advance(k, coupling, carry):
        flux, value, total = carry
        across = reciprocal(coupling)
        new_flux, new_value, new_total = [], [], []
        for c in range(2):
            here_flux = flux[c] + side[c, k] * value[c]
            after = value[c] + across * here_flux
            here_total = total[c] + value[c] * rhs[c, k]
            weight[c, k] = value[c]
            gain[c, k] = reciprocal((coupling * value[c]) * after)
            rhs[c, k] = here_total
            new_flux.append(here_flux)
            new_value.append(after)
            new_total.append(here_total)
        return tuple(new_flux), tuple(new_value), tuple(new_total)

    def lower_step(k, carry):
        return advance(k, coupling_of(k), carry)

    def upper_step(k, carry):
        return advance(k, coupling_of(k - 1), carry)

    def fronts(step, carry):
        lower, upper = carry
        return lower_step(step, lower), upper_step(layers - 1 - step, upper)

    def outward(body, carry):
        def both(step, carry):
            return body(middle - 1 - step, 0, body(middle + 1 + step, 1, carry))

        carry = repeat(plan, layers - 1 - middle, both, carry)
        for k in range(2 * middle - layers, -1, -1):
            carry = body(k, 0, carry)
        return carry

    def sweep(keep):
        def stencil_body(k, carry):
            stencil(k, keep)
            return carry

        lower = ((2.0 * friction,) * 2, (one, one), (zero, zero))
        upper = ((zero, zero), (one, one), (zero, zero))
        if plan.unrolled:
            stencil(0, keep)
            stencil(layers - 1, keep)
            for step in range(layers - 1 - middle):
                stencil(step + 1, keep)
                if layers - 2 - step > step + 1:
                    stencil(layers - 2 - step, keep)
                lower, upper = fronts(step, (lower, upper))
        else:
            repeat(plan, layers, stencil_body)
            lower, upper = repeat(plan, layers - 1 - middle, fronts, (lower, upper))
        for k in range(layers - 1 - middle, middle):
            lower = lower_step(k, lower)
        joints, start = [], []
        for c in range(2):
            below, above = lower[1][c], upper[1][c]
            product = below * above
            inv = reciprocal(side[c, middle] * product + (lower[0][c] * above + upper[0][c] * below))
            joint = (below, above, product, inv, reciprocal(below), reciprocal(above))
            joints.append(joint)
            solved = join(joint, rhs[c, middle], lower[2][c], upper[2][c])
            field[c, middle] = jnp.where(ice, solved, 0.0)
            start.append((solved * joint[4], solved * joint[5]))

        def solved_layer(k, which, carry):
            new = list(carry)
            for c in range(2):
                scaled = carry[2 * which + c] + rhs[c, k] * gain[c, k]
                field[c, k] = jnp.where(ice, weight[c, k] * scaled, 0.0)
                new[2 * which + c] = scaled
            return tuple(new)

        outward(solved_layer, (start[0][0], start[1][0], start[0][1], start[1][1]))
        return joints

    def join(joint, right, lower_total, upper_total):
        below, above, product, inv, _, _ = joint
        return (right * product + (lower_total * above + upper_total * below)) * inv

    sweep(False)
    joints = sweep(True)
    base = [field[c, 0] for c in range(2)]
    top = [field[c, layers - 1] for c in range(2)]

    def send(k, carry):
        both = jnp.where(centre, field[0, k], lane_roll(field[1, k], plan.cols))
        out_ref[block_row(k // here, plan.out_rows, k % here), :] = both
        return carry

    repeat(plan, layers, send)

    copy.wait()
    mismatch = [jnp.where(ice, top[c] - observed_of(c, gaps[c]), 0.0) for c in range(2)]
    source = [(2.0 * layers) * mismatch[c] for c in range(2)]

    def side_sum(k, value):
        east, west, north, south = (faces[n, k] for n in range(4))
        u_east, u_west = x_pair(value[0], 0.0)
        v_east, v_west = x_pair(value[1], 0.0)
        u_north, u_south = y_pair(value[0])
        v_north, v_south = y_pair(value[1])
        first = 4.0 * (east * u_east + west * u_west) + (north * u_north + south * u_south)
        second = (east * v_east + west * v_west) + 4.0 * (north * v_north + south * v_south)
        return first, second

    def side_sum(k, value):
        east, west, north, south = (faces[n, k] for n in range(4))
        u_east, u_west = x_pair(value[0], 0.0)
        v_east, v_west = x_pair(value[1], 0.0)
        u_north, u_south = y_pair(value[0])
        v_north, v_south = y_pair(value[1])
        first = 4.0 * (east * u_east + west * u_west) + (north * u_north + south * u_south)
        second = (east * v_east + west * v_west) + 4.0 * (north * v_north + south * v_south)
        return first, second

    below_scaled = tuple(source[c] * joints[c][3] for c in range(2))
    first_middle = tuple(below_scaled[c] * joints[c][0] for c in range(2))
    above_scaled = tuple(first_middle[c] * joints[c][5] for c in range(2))
    middle_sum = side_sum(middle, first_middle)

    def below_layer(k, carry):
        total, correction = carry
        added = side_sum(k, tuple(weight[c, k] * below_scaled[c] for c in range(2)))
        total = tuple(total[c] + weight[c, k] * added[c] for c in range(2))
        return total, tuple(correction[c] + total[c] * gain[c, k] for c in range(2))

    def above_layer(k, carry):
        total, scaled = carry
        scaled = tuple(scaled[c] + source[c] * gain[c, k] for c in range(2))
        added = side_sum(k, tuple(weight[c, k] * scaled[c] for c in range(2)))
        return tuple(total[c] + weight[c, k] * added[c] for c in range(2)), scaled

    def adjoint_layers(step, carry):
        below, above = carry
        return below_layer(step, below), above_layer(middle + 1 + step, above)

    nothing = (zero, zero)
    below, above = repeat(
        plan, layers - 1 - middle, adjoint_layers, ((nothing, nothing), (tuple(source), above_scaled))
    )
    for k in range(layers - 1 - middle, middle):
        below = below_layer(k, below)
    adjoint = tuple(
        join(joints[c], middle_sum[c], below[0][c], above[0][c]) * joints[c][4] + below[1][c] for c in range(2)
    )
    adjoint = [jnp.where(ice, adjoint[c], 0.0) for c in range(2)]
    gradient = -friction * (base[0] * adjoint[0] + base[1] * adjoint[1])

    def partial_sum(value):
        line = jnp.sum(jnp.where(centre, value, 0.0), axis=0, keepdims=True)
        folded = line
        for r in range(1, rows):
            folded = folded + lane_roll(line, r * width)
        return jnp.broadcast_to(lane_roll(folded, plan.cols), shape)

    misfit_line = partial_sum(mismatch[0] * mismatch[0] + mismatch[1] * mismatch[1])
    grad_line = partial_sum(gradient * gradient)
    in_first = jnp.logical_and(lane >= plan.halo + plan.cols, lane < plan.halo + 2 * plan.cols)
    last_row = jnp.where(centre, gradient, jnp.where(in_first, misfit_line, grad_line))
    for part in range(plan.layer_size):
        out_ref[block_row(part, plan.out_rows, here), :] = last_row


def unpack_kernel(
    plan, in_ref, log_ref, vel_hbm, friction_hbm, misfit_hbm,
    vel_ref, friction_ref, misfit_ref, grad_ref, leave,
):
    here, width, cols, rows = plan.layers_here, plan.width, plan.cols, plan.rows
    local_chunks = plan.local_cols // LANES

    total = jnp.sum(
        in_ref[pl.ds(here, plan.devices, stride=plan.out_rows), :], axis=0, keepdims=True
    )
    line_lane = lax.broadcasted_iota(jnp.int32, (1, LANES), 1)

    def summed(first):
        ahead = (line_lane + (LANES - first % LANES)) % LANES
        return jnp.sum(jnp.where(ahead < cols, total, 0.0), axis=1, keepdims=True)

    misfit_sum = summed(plan.halo + cols)
    grad_sum = summed(plan.halo + cols + width)
    scale = step_size / jnp.sqrt(grad_sum / plan.column_count + 1e-06)

    lane = lax.broadcasted_iota(jnp.int32, (plan.out_rows, LANES), 1)
    def chunk(c, i):
        at = (plan.chunks - 1 - i) * plan.per_chunk * plan.out_rows
        if not isinstance(at, int):
            at = pl.multiple_of(at, 8)
        turned = [
            lane_roll(in_ref[pl.ds(at + (plan.per_chunk - 1 - t) * plan.out_rows, plan.out_rows), :], t * cols)
            for t in range(plan.per_chunk)
        ]
        for r in range(rows):
            start = r * width + plan.halo + c * cols
            ahead = (lane + (LANES - start % LANES)) % LANES
            row = turned[0]
            for t in range(1, plan.per_chunk):
                row = jnp.where(ahead >= t * cols, turned[t], row)
            row = lane_roll(row, -start)
            vel_ref[c, pl.ds(i * rows + r, here, stride=plan.chunks * rows), :] = row[:here]
            if c == 0:
                owner, step = i // local_chunks, i % local_chunks
                grad_ref[owner, pl.ds(step * rows + r, 1), :] = row[here : here + 1]

    out = [pltpu.make_async_copy(vel_ref.at[c], vel_hbm.at[c], leave.at[c]) for c in range(2)]
    out.append(pltpu.make_async_copy(friction_ref, friction_hbm, leave.at[2]))
    out.append(pltpu.make_async_copy(misfit_ref, misfit_hbm, leave.at[3]))
    for c in range(2):

        def chunk_body(i, carry):
            chunk(c, i)
            return carry

        repeat(plan, plan.chunks, chunk_body)
        out[c].start()
    friction_ref[...] = log_ref[...] - grad_ref[lax.axis_index("layer")] * scale
    out[2].start()
    misfit_ref[...] = 0.5 * misfit_sum / plan.column_count
    out[3].start()
    for copy in out:
        copy.wait()


def as_lines(x):
    chunked = x.reshape(x.shape[:-1] + (x.shape[-1] // LANES, LANES))
    return jnp.swapaxes(chunked, -3, -2).reshape(-1, LANES)


def from_lines(lines, shape):
    chunked = lines.reshape(shape[:-2] + (shape[-1] // LANES, shape[-2], LANES))
    return jnp.swapaxes(chunked, -3, -2).reshape(shape)


def on_device(mesh_shape, velocity_init, driving, observed, log_friction, ice_mask):
    plan = Plan(mesh_shape, velocity_init.shape)
    vmem = pl.BlockSpec(memory_space=pltpu.VMEM)
    hbm = pl.BlockSpec(memory_space=pltpu.HBM)
    f32 = jnp.float32
    limit = pltpu.CompilerParams(vmem_limit_bytes=(16 if plan.unrolled else 40) * MIB)
    inputs = [as_lines(x) for x in (velocity_init, driving, observed, log_friction, ice_mask)]

    def exchange(blocks):
        shaped = blocks.reshape(blocks.shape[0], 1, LANES)
        ranks = [
            m * plan.layer_size + part
            for part in reversed(range(plan.layer_size))
            for m in reversed(range(plan.map_size))
        ]
        return lax.all_to_all(
            shaped, ("map", "layer"), split_axis=0, concat_axis=0, tiled=True, axis_index_groups=[ranks]
        ).reshape(blocks.shape)

    packed = pl.pallas_call(
        functools.partial(pack_kernel, plan),
        out_shape=jax.ShapeDtypeStruct((plan.devices * plan.in_rows, LANES), f32),
        in_specs=[hbm] * 5,
        out_specs=vmem,
        scratch_shapes=[pltpu.VMEM(x.shape, x.dtype) for x in inputs]
        + [
            pltpu.SemaphoreType.DMA((VELOCITY_COPIES + 4,)),
        ],
        compiler_params=limit,
        name="pack",
    )(*(pltpu.with_memory_space_constraint(x, pltpu.HBM) for x in inputs))

    windows = exchange(packed)

    columns = [
        [m * plan.layer_size + part for m in reversed(range(plan.map_size))] for part in range(plan.layer_size)
    ]
    all_observed = lax.all_gather(inputs[2], ("map", "layer"), axis=0, tiled=True, axis_index_groups=columns)
    all_observed = pltpu.with_memory_space_constraint(all_observed, pltpu.HBM)

    plane = (plan.layers, plan.map_size, LANES)
    solved = pl.pallas_call(
        functools.partial(solve_kernel, plan),
        out_shape=jax.ShapeDtypeStruct((plan.devices * plan.out_rows, LANES), f32),
        in_specs=[vmem, hbm],
        out_specs=vmem,
        scratch_shapes=[
            pltpu.VMEM(all_observed.shape, f32),
            pltpu.SemaphoreType.DMA,
            pltpu.VMEM((2,) + plane, f32),
            pltpu.VMEM(plane, f32),
            pltpu.VMEM((2,) + plane, f32),
            pltpu.VMEM((2,) + plane, f32),
            pltpu.VMEM((4,) + plane, f32),
            pltpu.VMEM((2,) + plane, f32),
            pltpu.VMEM((2,) + plane, f32),
        ],
        compiler_params=limit,
        name="solve",
    )(windows, all_observed)

    back = exchange(solved)

    vel_lines, log_lines = inputs[0].reshape(2, -1, LANES), inputs[3]
    velocity, friction_new, misfit = pl.pallas_call(
        functools.partial(unpack_kernel, plan),
        out_shape=(
            jax.ShapeDtypeStruct(vel_lines.shape, f32),
            jax.ShapeDtypeStruct(log_lines.shape, f32),
            jax.ShapeDtypeStruct((1, 1), f32),
        ),
        in_specs=[vmem] * 2,
        out_specs=(hbm, hbm, hbm),
        scratch_shapes=[
            pltpu.VMEM(vel_lines.shape, f32),
            pltpu.VMEM(log_lines.shape, f32),
            pltpu.VMEM((1, 1), f32),
            pltpu.VMEM((plan.layer_size,) + log_lines.shape, f32),
            pltpu.SemaphoreType.DMA((4,)),
        ],
        compiler_params=limit,
        name="unpack",
    )(back, log_lines)
    return (
        from_lines(velocity, velocity_init.shape),
        from_lines(friction_new, log_friction.shape),
        misfit.reshape(()),
    )


def solution(mesh):
    in_specs = (
        P(None, "layer", "map", None),
        P(None, "map", "layer"),
        P(None, "map", "layer"),
        P("map", "layer"),
        P("map", "layer"),
    )
    out_specs = (P(None, "layer", "map", None), P("map", "layer"), P())
    return jax.shard_map(
        functools.partial(on_device, dict(mesh.shape)),
        mesh=mesh,
        in_specs=in_specs,
        out_specs=out_specs,
        check_vma=False,
    )
```

```python
import functools

import jax
import jax.numpy as jnp
from jax import lax
from jax.experimental import pallas as pl
from jax.experimental.pallas import tpu as pltpu
from jax.sharding import PartitionSpec as P

strain_floor = 0.1
step_size = 0.5
LANES = 128
REACH = 5
BED_REACH = 3
MIB = 1 << 20
VELOCITY_COPIES = 4


class Plan:
    def __init__(self, mesh_shape, velocity_shape):
        self.map_size = mesh_shape["map"]
        self.layer_size = mesh_shape["layer"]
        self.devices = self.map_size * self.layer_size
        self.layers_here = velocity_shape[1]
        self.rows = velocity_shape[2]
        self.ny = velocity_shape[3]
        self.layers = self.layers_here * self.layer_size
        self.cols = self.ny // self.devices
        self.width = LANES // self.rows
        self.halo = (self.width - self.cols) // 2
        self.low = self.halo - REACH
        self.wide = self.cols + 2 * REACH
        self.half = self.wide // 2
        self.gap = self.low + self.wide
        self.local_cols = self.ny // self.layer_size
        self.per_chunk = LANES // self.cols
        self.chunks = self.ny // LANES
        self.column_count = self.rows * self.map_size * self.ny
        self.vel_rows = 2 * self.layers_here
        self.in_rows = self.vel_rows + 1
        self.left_at = self.gap
        self.right_at = self.gap + self.cols // 2 + 1
        self.out_rows = self.layers_here + 1
        self.unrolled = self.map_size <= 8
        assert self.width * self.rows == LANES and self.cols * self.per_chunk == LANES
        assert self.low >= 0 and self.wide % 2 == 0 and self.width - self.wide >= self.half
        assert 2 * self.cols <= self.width and self.local_cols % LANES == 0
        assert self.vel_rows == 8 and self.rows == 2 and 4 * self.cols <= LANES


def repeat(plan, count, body, carry=0):
    if plan.unrolled:
        for index in range(count):
            carry = body(index, carry)
        return carry
    return lax.fori_loop(0, count, body, carry)


def lane_roll(value, shift):
    shift = shift % LANES
    return value if shift == 0 else pltpu.roll(value, shift, 1)


def pack_kernel(
    plan, vel_hbm, driving_hbm, observed_hbm, log_hbm, mask_hbm, out_ref,
    vel_ref, driving_ref, observed_ref, log_ref, mask_ref, arrival,
):
    width, rows, cols, half = plan.width, plan.rows, plan.cols, plan.half
    piece = vel_ref.shape[0] // VELOCITY_COPIES
    spans = [pl.ds(n * piece, piece) for n in range(VELOCITY_COPIES)]
    pairs = [(vel_hbm.at[span, :], vel_ref.at[span, :]) for span in spans] + [
        (driving_hbm, driving_ref),
        (observed_hbm, observed_ref),
        (log_hbm, log_ref),
        (mask_hbm, mask_ref),
    ]
    copies = [pltpu.make_async_copy(pair[0], pair[1], arrival.at[n]) for n, pair in enumerate(pairs)]
    for copy in copies:
        copy.start()
    shape = (plan.vel_rows, LANES)
    lane = lax.broadcasted_iota(jnp.int32, shape, 1)
    sub = lax.broadcasted_iota(jnp.int32, shape, 0)
    in_gap = jnp.logical_not(jnp.logical_and(lane % width >= plan.low, lane % width < plan.gap))
    no_line = jnp.zeros((1, LANES), jnp.float32)

    def slide(part, start, length, place):
        step, offset = start // LANES, start % LANES
        value = part(step)
        if offset + length > LANES:
            after = part(step + 1)
            value = jnp.where(lax.broadcasted_iota(jnp.int32, value.shape, 1) >= offset, value, after)
        return lane_roll(value, place - offset)

    for copy in copies[:VELOCITY_COPIES]:
        copy.wait()

    def chunk_windows(i, carry):
        def velocity(r):
            def part(step):
                chunk = i + step
                if isinstance(chunk, int) and not 0 <= chunk < plan.chunks:
                    return jnp.zeros(shape, jnp.float32)
                at = chunk if isinstance(chunk, int) else jnp.clip(chunk, 0, plan.chunks - 1)
                value = vel_ref[pl.ds(at * rows + r, plan.vel_rows, stride=plan.chunks * rows), :]
                if isinstance(chunk, int):
                    return value
                return jnp.where(jnp.logical_and(chunk >= 0, chunk < plan.chunks), value, 0.0)

            return part

        for t in range(plan.per_chunk):
            block = None
            for r in range(rows):
                value = slide(velocity(r), plan.cols * t - plan.halo, width, r * width)
                block = value if block is None else jnp.where(lane >= r * width, value, block)
            at = (plan.chunks - 1 - i) * plan.per_chunk * plan.in_rows
            if not isinstance(at, int):
                at = pl.multiple_of(at, 8)
            at = at + (plan.per_chunk - 1 - t) * plan.in_rows
            out_ref[pl.ds(at, plan.vel_rows), :] = jnp.where(in_gap, 0.0, block)
            out_ref[pl.ds(at + plan.vel_rows, 1), :] = no_line
        return carry

    repeat(plan, plan.chunks, chunk_windows)
    for copy in copies[VELOCITY_COPIES:]:
        copy.wait()

    place = lax.axis_index("layer")
    local_chunks = plan.local_cols // LANES

    skip = local_chunks * rows
    no_block = jnp.zeros(shape, jnp.float32)

    def whole(ref, row):
        return jnp.broadcast_to(ref[row : row + 1, :], shape).astype(jnp.float32)

    def gap_part(r, step):
        at = step * rows + r
        observed = jnp.where(sub < 2, whole(observed_ref, at), whole(observed_ref, skip + at))
        return jnp.where(sub < 4, observed, jnp.where(sub < 6, whole(mask_ref, at), whole(log_ref, at)))

    def driving_part(r, step):
        at = step * rows + r
        return jnp.where(sub < 2, whole(driving_ref, at), whole(driving_ref, skip + at))

    def sequence(make):
        return [
            [no_block] + [make(r, step) for step in range(local_chunks)] + [no_block] for r in range(rows)
        ]

    gap_parts, driving_parts = sequence(gap_part), sequence(driving_part)
    own = plan.local_cols // cols
    spill = -(-REACH // cols)

    def column_block(q):
        start = q * cols
        block = None
        for r in range(rows):

            def in_gaps(step):
                return gap_parts[r][step + 1]

            def of_driving(step):
                return driving_parts[r][step + 1]

            at = r * width
            first = slide(in_gaps, start - REACH, half, (at + plan.gap) % LANES)
            second = slide(in_gaps, start - REACH + half, half, (at + plan.gap) % LANES)
            before = slide(of_driving, start - BED_REACH, BED_REACH, (at + plan.left_at) % LANES)
            after = slide(of_driving, start + cols, BED_REACH, (at + plan.right_at) % LANES)
            ahead = (lane + (LANES - plan.gap - at)) % LANES
            of_observed = sub < 4
            first = jnp.where(jnp.logical_and(of_observed, ahead < BED_REACH), before, first)
            second = jnp.where(jnp.logical_and(of_observed, ahead >= plan.right_at - plan.gap), after, second)
            value = jnp.where(sub % 2 == 0, first, second)
            ahead = (lane + (LANES - plan.gap)) % LANES
            block = value if block is None else jnp.where(ahead >= r * width, value, block)
        at = pl.multiple_of((plan.layer_size - 1 - place) * (own * plan.in_rows), 8) + (own - 1 - q) * plan.in_rows
        here = pl.ds(at, plan.vel_rows)
        out_ref[here, :] = jnp.where(in_gap, block, out_ref[here, :])
        if not 0 <= q < own:
            return
        line = None
        step, offset = start // LANES, start % LANES
        for r in range(rows):
            for c in range(2):
                row = c * skip + step * rows + r
                put = (2 * r + c) * cols
                value = lane_roll(driving_ref[row : row + 1, :], put - offset)
                line = value if line is None else jnp.where(lane[:1] >= put, value, line)
        out_ref[pl.ds(at + plan.vel_rows, 1), :] = line

    for q in range(own):
        column_block(q)

    @pl.when(place > 0)
    def _():
        for q in range(-spill, 0):
            column_block(q)

    @pl.when(place < plan.layer_size - 1)
    def _():
        for q in range(own, own + spill):
            column_block(q)


def solve_kernel(plan, in_ref, out_ref, field, eta_ref, side, rhs, faces, weight, gain):
    size, width, rows = plan.map_size, plan.width, plan.rows
    layers, here = plan.layers, plan.layers_here
    shape = (size, LANES)
    lane = lax.broadcasted_iota(jnp.int32, shape, 1)
    sub = lax.broadcasted_iota(jnp.int32, shape, 0)
    last_group = lane >= LANES - width
    first_group = lane < width
    x_end = jnp.logical_and(last_group, sub == 0)
    x_start = jnp.logical_and(first_group, sub == size - 1)

    def block_row(part, rows_of_block, row):
        first = (plan.layer_size - 1 - part) * size * rows_of_block
        return pl.ds(first + row, size, stride=rows_of_block)

    def arrived(part, row):
        return in_ref[block_row(part, plan.in_rows, row), :]

    def moved(value, source, target):
        return lane_roll(value, target - source)

    def from_gap(halves):
        left, right = (moved(value, plan.gap, plan.low + h * plan.half) for h, value in enumerate(halves))
        return jnp.where(lane % width < plan.low + plan.half, left, right)

    def from_line(c):
        plane = None
        for r in range(rows):
            value = moved(line, (2 * r + c) * plan.cols, r * width + plan.halo)
            plane = value if plane is None else jnp.where(lane >= r * width, value, plane)
        return plane

    def driving_of(c, halves):
        left = moved(halves[0], plan.left_at, plan.halo - BED_REACH)
        right = moved(halves[1], plan.right_at, plan.halo + plan.cols)
        return jnp.where(centre, from_line(c), jnp.where(lane % width < plan.halo, left, right))

    def x_pair(value, edge):
        after = lane_roll(value, -width)
        before = after if 2 * width == LANES else lane_roll(value, width)
        after = jnp.where(last_group, pltpu.roll(after, 1, 0), after)
        before = jnp.where(first_group, pltpu.roll(before, size - 1, 0), before)
        return jnp.where(x_end, edge, after), jnp.where(x_start, edge, before)

    def y_pair(value):
        return lane_roll(value, -1), lane_roll(value, 1)

    unit = 2.0 / 4.0 ** (1.0 / 3.0)

    def viscosity(four_rates):
        return jnp.exp2(jnp.log2(4.0 * strain_floor + four_rates) * (-1.0 / 3.0))

    sums = [None] * plan.in_rows
    for part in range(plan.layer_size):
        for row in range(plan.in_rows):
            value = arrived(part, row)
            if row < plan.vel_rows:
                field[row // here, part * here + row % here] = value
            sums[row] = value if part == 0 else sums[row] + value
    line = sums[plan.vel_rows]
    gaps = [sums[2 * n : 2 * n + 2] for n in range(4)]
    reached = jnp.logical_and(lane % width >= plan.low, lane % width < plan.gap)
    centre = jnp.logical_and(lane % width >= plan.halo, lane % width < plan.halo + plan.cols)
    driving = [unit * driving_of(c, gaps[c]) for c in range(2)]
    observed = [from_gap(gaps[c]) for c in range(2)]
    mask = jnp.where(reached, from_gap(gaps[2]), 0.0)
    ice = mask != 0.0
    friction = jnp.where(mask == 1.0, jnp.exp(from_gap(gaps[3])), 0.0)

    def stencil(k, keep):
        u, v = field[0, k], field[1, k]
        u_east, u_west = x_pair(u, 0.0)
        v_east, v_west = x_pair(v, 0.0)
        u_north, u_south = y_pair(u)
        v_north, v_south = y_pair(v)
        stretch_x = u_east - u_west
        stretch_y = v_north - v_south
        shear = 0.5 * ((u_north - u_south) + (v_east - v_west))
        four_rates = stretch_x * (stretch_x + stretch_y) + (stretch_y * stretch_y + shear * shear)
        half_v = 0.5 * v
        eta = viscosity(four_rates)
        eta_edge = viscosity(u * u + half_v * half_v)
        eta_east, eta_west = x_pair(eta, eta_edge)
        eta_north, eta_south = y_pair(eta)
        east, west = eta + eta_east, eta + eta_west
        north, south = eta + eta_north, eta + eta_south
        along_x, along_y = east + west, north + south
        eta_ref[k] = eta
        side[0, k] = 4.0 * along_x + along_y
        side[1, k] = along_x + 4.0 * along_y
        rhs[0, k] = driving[0] + (4.0 * (east * u_east + west * u_west) + (north * u_north + south * u_south))
        rhs[1, k] = driving[1] + ((east * v_east + west * v_west) + 4.0 * (north * v_north + south * v_south))
        if keep:
            faces[0, k] = east
            faces[1, k] = west
            faces[2, k] = north
            faces[3, k] = south

    def coupling_of(k):
        return (2.0 * layers * layers) * (eta_ref[k] + eta_ref[k + 1])

    def reciprocal(value):
        guess = pl.reciprocal(value, approx=True)
        return guess * (2.0 - value * guess)

    middle = layers // 2
    zero = jnp.zeros(shape, jnp.float32)
    one = jnp.ones(shape, jnp.float32)

    def advance(k, coupling, carry):
        flux, value, total = carry
        across = reciprocal(coupling)
        new_flux, new_value, new_total = [], [], []
        for c in range(2):
            here_flux = flux[c] + side[c, k] * value[c]
            after = value[c] + across * here_flux
            here_total = total[c] + value[c] * rhs[c, k]
            weight[c, k] = value[c]
            gain[c, k] = reciprocal((coupling * value[c]) * after)
            rhs[c, k] = here_total
            new_flux.append(here_flux)
            new_value.append(after)
            new_total.append(here_total)
        return tuple(new_flux), tuple(new_value), tuple(new_total)

    def lower_step(k, carry):
        return advance(k, coupling_of(k), carry)

    def upper_step(k, carry):
        return advance(k, coupling_of(k - 1), carry)

    def fronts(step, carry):
        lower, upper = carry
        return lower_step(step, lower), upper_step(layers - 1 - step, upper)

    def outward(body, carry):
        def both(step, carry):
            return body(middle - 1 - step, 0, body(middle + 1 + step, 1, carry))

        carry = repeat(plan, layers - 1 - middle, both, carry)
        for k in range(2 * middle - layers, -1, -1):
            carry = body(k, 0, carry)
        return carry

    def sweep(keep):
        def stencil_body(k, carry):
            stencil(k, keep)
            return carry

        lower = ((unit * friction,) * 2, (one, one), (zero, zero))
        upper = ((zero, zero), (one, one), (zero, zero))
        if plan.unrolled:
            stencil(0, keep)
            stencil(layers - 1, keep)
            for step in range(layers - 1 - middle):
                stencil(step + 1, keep)
                if layers - 2 - step > step + 1:
                    stencil(layers - 2 - step, keep)
                lower, upper = fronts(step, (lower, upper))
        else:
            repeat(plan, layers, stencil_body)
            lower, upper = repeat(plan, layers - 1 - middle, fronts, (lower, upper))
        for k in range(layers - 1 - middle, middle):
            lower = lower_step(k, lower)
        joints, start = [], []
        for c in range(2):
            below, above = lower[1][c], upper[1][c]
            product = below * above
            inv = reciprocal(side[c, middle] * product + (lower[0][c] * above + upper[0][c] * below))
            joint = (below, above, product, inv, reciprocal(below), reciprocal(above))
            joints.append(joint)
            solved = join(joint, rhs[c, middle], lower[2][c], upper[2][c])
            field[c, middle] = jnp.where(ice, solved, 0.0)
            start.append((solved * joint[4], solved * joint[5]))

        def solved_layer(k, which, carry):
            new = list(carry)
            for c in range(2):
                scaled = carry[2 * which + c] + rhs[c, k] * gain[c, k]
                field[c, k] = jnp.where(ice, weight[c, k] * scaled, 0.0)
                new[2 * which + c] = scaled
            return tuple(new)

        outward(solved_layer, (start[0][0], start[1][0], start[0][1], start[1][1]))
        return joints

    def join(joint, right, lower_total, upper_total):
        below, above, product, inv, _, _ = joint
        return (right * product + (lower_total * above + upper_total * below)) * inv

    sweep(False)
    joints = sweep(True)
    base = [field[c, 0] for c in range(2)]
    top = [field[c, layers - 1] for c in range(2)]

    def send(k, carry):
        both = jnp.where(centre, field[0, k], lane_roll(field[1, k], plan.cols))
        out_ref[block_row(k // here, plan.out_rows, k % here), :] = both
        return carry

    repeat(plan, layers, send)

    mismatch = [jnp.where(ice, top[c] - observed[c], 0.0) for c in range(2)]
    source = [(unit * layers) * mismatch[c] for c in range(2)]

    def side_sum(k, value):
        east, west, north, south = (faces[n, k] for n in range(4))
        u_east, u_west = x_pair(value[0], 0.0)
        v_east, v_west = x_pair(value[1], 0.0)
        u_north, u_south = y_pair(value[0])
        v_north, v_south = y_pair(value[1])
        first = 4.0 * (east * u_east + west * u_west) + (north * u_north + south * u_south)
        second = (east * v_east + west * v_west) + 4.0 * (north * v_north + south * v_south)
        return first, second

    def side_sum(k, value):
        east, west, north, south = (faces[n, k] for n in range(4))
        u_east, u_west = x_pair(value[0], 0.0)
        v_east, v_west = x_pair(value[1], 0.0)
        u_north, u_south = y_pair(value[0])
        v_north, v_south = y_pair(value[1])
        first = 4.0 * (east * u_east + west * u_west) + (north * u_north + south * u_south)
        second = (east * v_east + west * v_west) + 4.0 * (north * v_north + south * v_south)
        return first, second

    below_scaled = tuple(source[c] * joints[c][3] for c in range(2))
    first_middle = tuple(below_scaled[c] * joints[c][0] for c in range(2))
    above_scaled = tuple(first_middle[c] * joints[c][5] for c in range(2))
    middle_sum = side_sum(middle, first_middle)

    def below_layer(k, carry):
        total, correction = carry
        added = side_sum(k, tuple(weight[c, k] * below_scaled[c] for c in range(2)))
        total = tuple(total[c] + weight[c, k] * added[c] for c in range(2))
        return total, tuple(correction[c] + total[c] * gain[c, k] for c in range(2))

    def above_layer(k, carry):
        total, scaled = carry
        scaled = tuple(scaled[c] + source[c] * gain[c, k] for c in range(2))
        added = side_sum(k, tuple(weight[c, k] * scaled[c] for c in range(2)))
        return tuple(total[c] + weight[c, k] * added[c] for c in range(2)), scaled

    def adjoint_layers(step, carry):
        below, above = carry
        return below_layer(step, below), above_layer(middle + 1 + step, above)

    nothing = (zero, zero)
    below, above = repeat(
        plan, layers - 1 - middle, adjoint_layers, ((nothing, nothing), (tuple(source), above_scaled))
    )
    for k in range(layers - 1 - middle, middle):
        below = below_layer(k, below)
    adjoint = tuple(
        join(joints[c], middle_sum[c], below[0][c], above[0][c]) * joints[c][4] + below[1][c] for c in range(2)
    )
    adjoint = [jnp.where(ice, adjoint[c], 0.0) for c in range(2)]
    gradient = -friction * (base[0] * adjoint[0] + base[1] * adjoint[1])

    def partial_sum(value):
        line = jnp.sum(jnp.where(centre, value, 0.0), axis=0, keepdims=True)
        folded = line
        for r in range(1, rows):
            folded = folded + lane_roll(line, r * width)
        return jnp.broadcast_to(lane_roll(folded, plan.cols), shape)

    misfit_line = partial_sum(mismatch[0] * mismatch[0] + mismatch[1] * mismatch[1])
    grad_line = partial_sum(gradient * gradient)
    in_first = jnp.logical_and(lane >= plan.halo + plan.cols, lane < plan.halo + 2 * plan.cols)
    last_row = jnp.where(centre, gradient, jnp.where(in_first, misfit_line, grad_line))
    for part in range(plan.layer_size):
        out_ref[block_row(part, plan.out_rows, here), :] = last_row


def unpack_kernel(
    plan, in_ref, log_ref, vel_hbm, friction_hbm, misfit_hbm,
    vel_ref, friction_ref, misfit_ref, grad_ref, leave,
):
    here, width, cols, rows = plan.layers_here, plan.width, plan.cols, plan.rows
    local_chunks = plan.local_cols // LANES

    total = jnp.sum(
        in_ref[pl.ds(here, plan.devices, stride=plan.out_rows), :], axis=0, keepdims=True
    )
    line_lane = lax.broadcasted_iota(jnp.int32, (1, LANES), 1)

    def summed(first):
        ahead = (line_lane + (LANES - first % LANES)) % LANES
        return jnp.sum(jnp.where(ahead < cols, total, 0.0), axis=1, keepdims=True)

    misfit_sum = summed(plan.halo + cols)
    grad_sum = summed(plan.halo + cols + width)
    scale = step_size / jnp.sqrt(grad_sum / plan.column_count + 1e-06)

    lane = lax.broadcasted_iota(jnp.int32, (plan.out_rows, LANES), 1)
    def chunk(c, i):
        at = (plan.chunks - 1 - i) * plan.per_chunk * plan.out_rows
        if not isinstance(at, int):
            at = pl.multiple_of(at, 8)
        turned = [
            lane_roll(in_ref[pl.ds(at + (plan.per_chunk - 1 - t) * plan.out_rows, plan.out_rows), :], t * cols)
            for t in range(plan.per_chunk)
        ]
        for r in range(rows):
            start = r * width + plan.halo + c * cols
            ahead = (lane + (LANES - start % LANES)) % LANES
            row = turned[0]
            for t in range(1, plan.per_chunk):
                row = jnp.where(ahead >= t * cols, turned[t], row)
            row = lane_roll(row, -start)
            vel_ref[c, pl.ds(i * rows + r, here, stride=plan.chunks * rows), :] = row[:here]
            if c == 0:
                owner, step = i // local_chunks, i % local_chunks
                grad_ref[owner, pl.ds(step * rows + r, 1), :] = row[here : here + 1]

    out = [pltpu.make_async_copy(vel_ref.at[c], vel_hbm.at[c], leave.at[c]) for c in range(2)]
    out.append(pltpu.make_async_copy(friction_ref, friction_hbm, leave.at[2]))
    out.append(pltpu.make_async_copy(misfit_ref, misfit_hbm, leave.at[3]))
    for c in range(2):

        def chunk_body(i, carry):
            chunk(c, i)
            return carry

        repeat(plan, plan.chunks, chunk_body)
        out[c].start()
    friction_ref[...] = log_ref[...] - grad_ref[lax.axis_index("layer")] * scale
    out[2].start()
    misfit_ref[...] = 0.5 * misfit_sum / plan.column_count
    out[3].start()
    for copy in out:
        copy.wait()


def as_lines(x):
    chunked = x.reshape(x.shape[:-1] + (x.shape[-1] // LANES, LANES))
    return jnp.swapaxes(chunked, -3, -2).reshape(-1, LANES)


def from_lines(lines, shape):
    chunked = lines.reshape(shape[:-2] + (shape[-1] // LANES, shape[-2], LANES))
    return jnp.swapaxes(chunked, -3, -2).reshape(shape)


def on_device(mesh_shape, velocity_init, driving, observed, log_friction, ice_mask):
    plan = Plan(mesh_shape, velocity_init.shape)
    vmem = pl.BlockSpec(memory_space=pltpu.VMEM)
    hbm = pl.BlockSpec(memory_space=pltpu.HBM)
    f32 = jnp.float32
    limit = pltpu.CompilerParams(vmem_limit_bytes=(16 if plan.unrolled else 40) * MIB)
    inputs = [as_lines(x) for x in (velocity_init, driving, observed, log_friction, ice_mask)]

    def exchange(blocks):
        shaped = blocks.reshape(blocks.shape[0], 1, LANES)
        ranks = [
            m * plan.layer_size + part
            for part in reversed(range(plan.layer_size))
            for m in reversed(range(plan.map_size))
        ]
        return lax.all_to_all(
            shaped, ("map", "layer"), split_axis=0, concat_axis=0, tiled=True, axis_index_groups=[ranks]
        ).reshape(blocks.shape)

    packed = pl.pallas_call(
        functools.partial(pack_kernel, plan),
        out_shape=jax.ShapeDtypeStruct((plan.devices * plan.in_rows, LANES), f32),
        in_specs=[hbm] * 5,
        out_specs=vmem,
        scratch_shapes=[pltpu.VMEM(x.shape, x.dtype) for x in inputs]
        + [
            pltpu.SemaphoreType.DMA((VELOCITY_COPIES + 4,)),
        ],
        compiler_params=limit,
        name="pack",
    )(*(pltpu.with_memory_space_constraint(x, pltpu.HBM) for x in inputs))

    windows = exchange(packed)

    plane = (plan.layers, plan.map_size, LANES)
    solved = pl.pallas_call(
        functools.partial(solve_kernel, plan),
        out_shape=jax.ShapeDtypeStruct((plan.devices * plan.out_rows, LANES), f32),
        in_specs=[vmem],
        out_specs=vmem,
        scratch_shapes=[
            pltpu.VMEM((2,) + plane, f32),
            pltpu.VMEM(plane, f32),
            pltpu.VMEM((2,) + plane, f32),
            pltpu.VMEM((2,) + plane, f32),
            pltpu.VMEM((4,) + plane, f32),
            pltpu.VMEM((2,) + plane, f32),
            pltpu.VMEM((2,) + plane, f32),
        ],
        compiler_params=limit,
        name="solve",
    )(windows)

    back = exchange(solved)

    vel_lines, log_lines = inputs[0].reshape(2, -1, LANES), inputs[3]
    velocity, friction_new, misfit = pl.pallas_call(
        functools.partial(unpack_kernel, plan),
        out_shape=(
            jax.ShapeDtypeStruct(vel_lines.shape, f32),
            jax.ShapeDtypeStruct(log_lines.shape, f32),
            jax.ShapeDtypeStruct((1, 1), f32),
        ),
        in_specs=[vmem] * 2,
        out_specs=(hbm, hbm, hbm),
        scratch_shapes=[
            pltpu.VMEM(vel_lines.shape, f32),
            pltpu.VMEM(log_lines.shape, f32),
            pltpu.VMEM((1, 1), f32),
            pltpu.VMEM((plan.layer_size,) + log_lines.shape, f32),
            pltpu.SemaphoreType.DMA((4,)),
        ],
        compiler_params=limit,
        name="unpack",
    )(back, log_lines)
    return (
        from_lines(velocity, velocity_init.shape),
        from_lines(friction_new, log_friction.shape),
        misfit.reshape(()),
    )


def solution(mesh):
    in_specs = (
        P(None, "layer", "map", None),
        P(None, "map", "layer"),
        P(None, "map", "layer"),
        P("map", "layer"),
        P("map", "layer"),
    )
    out_specs = (P(None, "layer", "map", None), P("map", "layer"), P())
    return jax.shard_map(
        functools.partial(on_device, dict(mesh.shape)),
        mesh=mesh,
        in_specs=in_specs,
        out_specs=out_specs,
        check_vma=False,
    )
```

```python
import functools

import jax
import jax.numpy as jnp
from jax import lax
from jax.experimental import pallas as pl
from jax.experimental.pallas import tpu as pltpu
from jax.sharding import PartitionSpec as P

strain_floor = 0.1
step_size = 0.5
LANES = 128
REACH = 5
BED_REACH = 3
MIB = 1 << 20
VELOCITY_COPIES = 4


class Plan:
    def __init__(self, mesh_shape, velocity_shape):
        self.map_size = mesh_shape["map"]
        self.layer_size = mesh_shape["layer"]
        self.devices = self.map_size * self.layer_size
        self.layers_here = velocity_shape[1]
        self.rows = velocity_shape[2]
        self.ny = velocity_shape[3]
        self.layers = self.layers_here * self.layer_size
        self.cols = self.ny // self.devices
        self.width = LANES // self.rows
        self.halo = (self.width - self.cols) // 2
        self.low = self.halo - REACH
        self.wide = self.cols + 2 * REACH
        self.half = self.wide // 2
        self.gap = self.low + self.wide
        self.local_cols = self.ny // self.layer_size
        self.per_chunk = LANES // self.cols
        self.chunks = self.ny // LANES
        self.column_count = self.rows * self.map_size * self.ny
        self.vel_rows = 2 * self.layers_here
        self.in_rows = self.vel_rows + 1
        self.left_at = self.gap
        self.right_at = self.gap + self.cols // 2 + 1
        self.out_rows = self.layers_here + 1
        self.unrolled = self.map_size <= 8
        assert self.width * self.rows == LANES and self.cols * self.per_chunk == LANES
        assert self.low >= 0 and self.wide % 2 == 0 and self.width - self.wide >= self.half
        assert 2 * self.cols <= self.width and self.local_cols % LANES == 0
        assert self.vel_rows == 8 and self.rows == 2 and 4 * self.cols <= LANES


def repeat(plan, count, body, carry=0):
    if plan.unrolled:
        for index in range(count):
            carry = body(index, carry)
        return carry
    return lax.fori_loop(0, count, body, carry)


def lane_roll(value, shift):
    shift = shift % LANES
    return value if shift == 0 else pltpu.roll(value, shift, 1)


def pack_kernel(
    plan, vel_hbm, driving_hbm, observed_hbm, log_hbm, mask_hbm, out_ref,
    vel_ref, driving_ref, observed_ref, log_ref, mask_ref, arrival,
):
    width, rows, cols, half = plan.width, plan.rows, plan.cols, plan.half
    piece = vel_ref.shape[0] // VELOCITY_COPIES
    spans = [pl.ds(n * piece, piece) for n in range(VELOCITY_COPIES)]
    pairs = [(vel_hbm.at[span, :], vel_ref.at[span, :]) for span in spans] + [
        (driving_hbm, driving_ref),
        (observed_hbm, observed_ref),
        (log_hbm, log_ref),
        (mask_hbm, mask_ref),
    ]
    copies = [pltpu.make_async_copy(pair[0], pair[1], arrival.at[n]) for n, pair in enumerate(pairs)]
    for copy in copies:
        copy.start()
    shape = (plan.vel_rows, LANES)
    lane = lax.broadcasted_iota(jnp.int32, shape, 1)
    sub = lax.broadcasted_iota(jnp.int32, shape, 0)
    in_gap = jnp.logical_not(jnp.logical_and(lane % width >= plan.low, lane % width < plan.gap))
    no_line = jnp.zeros((1, LANES), jnp.float32)

    def slide(part, start, length, place):
        step, offset = start // LANES, start % LANES
        value = part(step)
        if offset + length > LANES:
            after = part(step + 1)
            value = jnp.where(lax.broadcasted_iota(jnp.int32, value.shape, 1) >= offset, value, after)
        return lane_roll(value, place - offset)

    for copy in copies[:VELOCITY_COPIES]:
        copy.wait()

    def chunk_windows(i, carry):
        def velocity(r):
            def part(step):
                chunk = i + step
                at = jnp.clip(chunk, 0, plan.chunks - 1)
                value = vel_ref[pl.ds(at * rows + r, plan.vel_rows, stride=plan.chunks * rows), :]
                return jnp.where(jnp.logical_and(chunk >= 0, chunk < plan.chunks), value, 0.0)

            return part

        for t in range(plan.per_chunk):
            block = None
            for r in range(rows):
                value = slide(velocity(r), plan.cols * t - plan.halo, width, r * width)
                block = value if block is None else jnp.where(lane >= r * width, value, block)
            at = (plan.chunks - 1 - i) * plan.per_chunk * plan.in_rows
            at = pl.multiple_of(at, 4) + (plan.per_chunk - 1 - t) * plan.in_rows
            out_ref[pl.ds(at, plan.vel_rows), :] = jnp.where(in_gap, 0.0, block)
            out_ref[pl.ds(at + plan.vel_rows, 1), :] = no_line
        return carry

    lax.fori_loop(0, plan.chunks, chunk_windows, 0, unroll=2)
    for copy in copies[VELOCITY_COPIES:]:
        copy.wait()

    place = lax.axis_index("layer")
    local_chunks = plan.local_cols // LANES

    skip = local_chunks * rows
    no_block = jnp.zeros(shape, jnp.float32)

    def whole(ref, row):
        return jnp.broadcast_to(ref[row : row + 1, :], shape).astype(jnp.float32)

    def gap_part(r, step):
        at = step * rows + r
        observed = jnp.where(sub < 2, whole(observed_ref, at), whole(observed_ref, skip + at))
        return jnp.where(sub < 4, observed, jnp.where(sub < 6, whole(mask_ref, at), whole(log_ref, at)))

    def driving_part(r, step):
        at = step * rows + r
        return jnp.where(sub < 2, whole(driving_ref, at), whole(driving_ref, skip + at))

    def sequence(make):
        return [
            [no_block] + [make(r, step) for step in range(local_chunks)] + [no_block] for r in range(rows)
        ]

    gap_parts, driving_parts = sequence(gap_part), sequence(driving_part)
    own = plan.local_cols // cols
    spill = -(-REACH // cols)

    def column_block(q):
        start = q * cols
        block = None
        for r in range(rows):

            def in_gaps(step):
                return gap_parts[r][step + 1]

            def of_driving(step):
                return driving_parts[r][step + 1]

            at = r * width
            first = slide(in_gaps, start - REACH, half, (at + plan.gap) % LANES)
            second = slide(in_gaps, start - REACH + half, half, (at + plan.gap) % LANES)
            before = slide(of_driving, start - BED_REACH, BED_REACH, (at + plan.left_at) % LANES)
            after = slide(of_driving, start + cols, BED_REACH, (at + plan.right_at) % LANES)
            ahead = (lane + (LANES - plan.gap - at)) % LANES
            of_observed = sub < 4
            first = jnp.where(jnp.logical_and(of_observed, ahead < BED_REACH), before, first)
            second = jnp.where(jnp.logical_and(of_observed, ahead >= plan.right_at - plan.gap), after, second)
            value = jnp.where(sub % 2 == 0, first, second)
            ahead = (lane + (LANES - plan.gap)) % LANES
            block = value if block is None else jnp.where(ahead >= r * width, value, block)
        at = pl.multiple_of((plan.layer_size - 1 - place) * (own * plan.in_rows), 8) + (own - 1 - q) * plan.in_rows
        here = pl.ds(at, plan.vel_rows)
        out_ref[here, :] = jnp.where(in_gap, block, out_ref[here, :])
        if not 0 <= q < own:
            return
        line = None
        step, offset = start // LANES, start % LANES
        for r in range(rows):
            for c in range(2):
                row = c * skip + step * rows + r
                put = (2 * r + c) * cols
                value = lane_roll(driving_ref[row : row + 1, :], put - offset)
                line = value if line is None else jnp.where(lane[:1] >= put, value, line)
        out_ref[pl.ds(at + plan.vel_rows, 1), :] = line

    for q in range(own):
        column_block(q)

    @pl.when(place > 0)
    def _():
        for q in range(-spill, 0):
            column_block(q)

    @pl.when(place < plan.layer_size - 1)
    def _():
        for q in range(own, own + spill):
            column_block(q)


def solve_kernel(plan, in_ref, out_ref, field, eta_ref, side, rhs, faces, weight, gain):
    size, width, rows = plan.map_size, plan.width, plan.rows
    layers, here = plan.layers, plan.layers_here
    shape = (size, LANES)
    lane = lax.broadcasted_iota(jnp.int32, shape, 1)
    sub = lax.broadcasted_iota(jnp.int32, shape, 0)
    last_group = lane >= LANES - width
    first_group = lane < width
    x_end = jnp.logical_and(last_group, sub == 0)
    x_start = jnp.logical_and(first_group, sub == size - 1)

    def block_row(part, rows_of_block, row):
        first = (plan.layer_size - 1 - part) * size * rows_of_block
        return pl.ds(first + row, size, stride=rows_of_block)

    def arrived(part, row):
        return in_ref[block_row(part, plan.in_rows, row), :]

    def moved(value, source, target):
        return lane_roll(value, target - source)

    def from_gap(halves):
        left, right = (moved(value, plan.gap, plan.low + h * plan.half) for h, value in enumerate(halves))
        return jnp.where(lane % width < plan.low + plan.half, left, right)

    def from_line(c):
        plane = None
        for r in range(rows):
            value = moved(line, (2 * r + c) * plan.cols, r * width + plan.halo)
            plane = value if plane is None else jnp.where(lane >= r * width, value, plane)
        return plane

    def driving_of(c, halves):
        left = moved(halves[0], plan.left_at, plan.halo - BED_REACH)
        right = moved(halves[1], plan.right_at, plan.halo + plan.cols)
        return jnp.where(centre, from_line(c), jnp.where(lane % width < plan.halo, left, right))

    def x_pair(value, edge):
        after = lane_roll(value, -width)
        before = after if 2 * width == LANES else lane_roll(value, width)
        after = jnp.where(last_group, pltpu.roll(after, 1, 0), after)
        before = jnp.where(first_group, pltpu.roll(before, size - 1, 0), before)
        return jnp.where(x_end, edge, after), jnp.where(x_start, edge, before)

    def y_pair(value):
        return lane_roll(value, -1), lane_roll(value, 1)

    unit = 2.0 / 4.0 ** (1.0 / 3.0)

    def viscosity(four_rates):
        return jnp.exp2(jnp.log2(4.0 * strain_floor + four_rates) * (-1.0 / 3.0))

    sums = [None] * plan.in_rows
    for part in range(plan.layer_size):
        for row in range(plan.in_rows):
            value = arrived(part, row)
            if row < plan.vel_rows:
                field[row // here, part * here + row % here] = value
            sums[row] = value if part == 0 else sums[row] + value
    line = sums[plan.vel_rows]
    gaps = [sums[2 * n : 2 * n + 2] for n in range(4)]
    reached = jnp.logical_and(lane % width >= plan.low, lane % width < plan.gap)
    centre = jnp.logical_and(lane % width >= plan.halo, lane % width < plan.halo + plan.cols)
    driving = [unit * driving_of(c, gaps[c]) for c in range(2)]
    observed = [from_gap(gaps[c]) for c in range(2)]
    mask = jnp.where(reached, from_gap(gaps[2]), 0.0)
    ice = mask != 0.0
    friction = jnp.where(mask == 1.0, jnp.exp(from_gap(gaps[3])), 0.0)

    def stencil(k, keep):
        u, v = field[0, k], field[1, k]
        u_east, u_west = x_pair(u, 0.0)
        v_east, v_west = x_pair(v, 0.0)
        u_north, u_south = y_pair(u)
        v_north, v_south = y_pair(v)
        stretch_x = u_east - u_west
        stretch_y = v_north - v_south
        shear = 0.5 * ((u_north - u_south) + (v_east - v_west))
        four_rates = stretch_x * (stretch_x + stretch_y) + (stretch_y * stretch_y + shear * shear)
        half_v = 0.5 * v
        eta = viscosity(four_rates)
        eta_edge = viscosity(u * u + half_v * half_v)
        eta_east, eta_west = x_pair(eta, eta_edge)
        eta_north, eta_south = y_pair(eta)
        east, west = eta + eta_east, eta + eta_west
        north, south = eta + eta_north, eta + eta_south
        along_x, along_y = east + west, north + south
        eta_ref[k] = eta
        side[0, k] = 4.0 * along_x + along_y
        side[1, k] = along_x + 4.0 * along_y
        rhs[0, k] = driving[0] + (4.0 * (east * u_east + west * u_west) + (north * u_north + south * u_south))
        rhs[1, k] = driving[1] + ((east * v_east + west * v_west) + 4.0 * (north * v_north + south * v_south))
        if keep:
            faces[0, k] = east
            faces[1, k] = west
            faces[2, k] = north
            faces[3, k] = south

    def coupling_of(k):
        return (2.0 * layers * layers) * (eta_ref[k] + eta_ref[k + 1])

    def reciprocal(value):
        guess = pl.reciprocal(value, approx=True)
        return guess * (2.0 - value * guess)

    middle = layers // 2
    zero = jnp.zeros(shape, jnp.float32)
    one = jnp.ones(shape, jnp.float32)

    def advance(k, coupling, carry):
        flux, value, total = carry
        across = reciprocal(coupling)
        new_flux, new_value, new_total = [], [], []
        for c in range(2):
            here_flux = flux[c] + side[c, k] * value[c]
            after = value[c] + across * here_flux
            here_total = total[c] + value[c] * rhs[c, k]
            weight[c, k] = value[c]
            gain[c, k] = reciprocal((coupling * value[c]) * after)
            rhs[c, k] = here_total
            new_flux.append(here_flux)
            new_value.append(after)
            new_total.append(here_total)
        return tuple(new_flux), tuple(new_value), tuple(new_total)

    def lower_step(k, carry):
        return advance(k, coupling_of(k), carry)

    def upper_step(k, carry):
        return advance(k, coupling_of(k - 1), carry)

    def fronts(step, carry):
        lower, upper = carry
        return lower_step(step, lower), upper_step(layers - 1 - step, upper)

    def outward(body, carry):
        def both(step, carry):
            return body(middle - 1 - step, 0, body(middle + 1 + step, 1, carry))

        carry = repeat(plan, layers - 1 - middle, both, carry)
        for k in range(2 * middle - layers, -1, -1):
            carry = body(k, 0, carry)
        return carry

    def sweep(keep):
        def stencil_body(k, carry):
            stencil(k, keep)
            return carry

        lower = ((unit * friction,) * 2, (one, one), (zero, zero))
        upper = ((zero, zero), (one, one), (zero, zero))
        if plan.unrolled:
            stencil(0, keep)
            stencil(layers - 1, keep)
            for step in range(layers - 1 - middle):
                stencil(step + 1, keep)
                if layers - 2 - step > step + 1:
                    stencil(layers - 2 - step, keep)
                lower, upper = fronts(step, (lower, upper))
        else:
            repeat(plan, layers, stencil_body)
            lower, upper = repeat(plan, layers - 1 - middle, fronts, (lower, upper))
        for k in range(layers - 1 - middle, middle):
            lower = lower_step(k, lower)
        joints, start = [], []
        for c in range(2):
            below, above = lower[1][c], upper[1][c]
            product = below * above
            inv = reciprocal(side[c, middle] * product + (lower[0][c] * above + upper[0][c] * below))
            joint = (below, above, product, inv, reciprocal(below), reciprocal(above))
            joints.append(joint)
            solved = join(joint, rhs[c, middle], lower[2][c], upper[2][c])
            field[c, middle] = jnp.where(ice, solved, 0.0)
            start.append((solved * joint[4], solved * joint[5]))

        def solved_layer(k, which, carry):
            new = list(carry)
            for c in range(2):
                scaled = carry[2 * which + c] + rhs[c, k] * gain[c, k]
                field[c, k] = jnp.where(ice, weight[c, k] * scaled, 0.0)
                new[2 * which + c] = scaled
            return tuple(new)

        outward(solved_layer, (start[0][0], start[1][0], start[0][1], start[1][1]))
        return joints

    def join(joint, right, lower_total, upper_total):
        below, above, product, inv, _, _ = joint
        return (right * product + (lower_total * above + upper_total * below)) * inv

    sweep(False)
    joints = sweep(True)
    base = [field[c, 0] for c in range(2)]
    top = [field[c, layers - 1] for c in range(2)]

    def send(k, carry):
        both = jnp.where(centre, field[0, k], lane_roll(field[1, k], plan.cols))
        out_ref[block_row(k // here, plan.out_rows, k % here), :] = both
        return carry

    repeat(plan, layers, send)

    mismatch = [jnp.where(ice, top[c] - observed[c], 0.0) for c in range(2)]
    source = [(unit * layers) * mismatch[c] for c in range(2)]

    def side_sum(k, value):
        east, west, north, south = (faces[n, k] for n in range(4))
        u_east, u_west = x_pair(value[0], 0.0)
        v_east, v_west = x_pair(value[1], 0.0)
        u_north, u_south = y_pair(value[0])
        v_north, v_south = y_pair(value[1])
        first = 4.0 * (east * u_east + west * u_west) + (north * u_north + south * u_south)
        second = (east * v_east + west * v_west) + 4.0 * (north * v_north + south * v_south)
        return first, second

    def side_sum(k, value):
        east, west, north, south = (faces[n, k] for n in range(4))
        u_east, u_west = x_pair(value[0], 0.0)
        v_east, v_west = x_pair(value[1], 0.0)
        u_north, u_south = y_pair(value[0])
        v_north, v_south = y_pair(value[1])
        first = 4.0 * (east * u_east + west * u_west) + (north * u_north + south * u_south)
        second = (east * v_east + west * v_west) + 4.0 * (north * v_north + south * v_south)
        return first, second

    below_scaled = tuple(source[c] * joints[c][3] for c in range(2))
    first_middle = tuple(below_scaled[c] * joints[c][0] for c in range(2))
    above_scaled = tuple(first_middle[c] * joints[c][5] for c in range(2))
    middle_sum = side_sum(middle, first_middle)

    def below_layer(k, carry):
        total, correction = carry
        added = side_sum(k, tuple(weight[c, k] * below_scaled[c] for c in range(2)))
        total = tuple(total[c] + weight[c, k] * added[c] for c in range(2))
        return total, tuple(correction[c] + total[c] * gain[c, k] for c in range(2))

    def above_layer(k, carry):
        total, scaled = carry
        scaled = tuple(scaled[c] + source[c] * gain[c, k] for c in range(2))
        added = side_sum(k, tuple(weight[c, k] * scaled[c] for c in range(2)))
        return tuple(total[c] + weight[c, k] * added[c] for c in range(2)), scaled

    def adjoint_layers(step, carry):
        below, above = carry
        return below_layer(step, below), above_layer(middle + 1 + step, above)

    nothing = (zero, zero)
    below, above = repeat(
        plan, layers - 1 - middle, adjoint_layers, ((nothing, nothing), (tuple(source), above_scaled))
    )
    for k in range(layers - 1 - middle, middle):
        below = below_layer(k, below)
    adjoint = tuple(
        join(joints[c], middle_sum[c], below[0][c], above[0][c]) * joints[c][4] + below[1][c] for c in range(2)
    )
    adjoint = [jnp.where(ice, adjoint[c], 0.0) for c in range(2)]
    gradient = -friction * (base[0] * adjoint[0] + base[1] * adjoint[1])

    def partial_sum(value):
        line = jnp.sum(jnp.where(centre, value, 0.0), axis=0, keepdims=True)
        folded = line
        for r in range(1, rows):
            folded = folded + lane_roll(line, r * width)
        return jnp.broadcast_to(lane_roll(folded, plan.cols), shape)

    misfit_line = partial_sum(mismatch[0] * mismatch[0] + mismatch[1] * mismatch[1])
    grad_line = partial_sum(gradient * gradient)
    in_first = jnp.logical_and(lane >= plan.halo + plan.cols, lane < plan.halo + 2 * plan.cols)
    last_row = jnp.where(centre, gradient, jnp.where(in_first, misfit_line, grad_line))
    for part in range(plan.layer_size):
        out_ref[block_row(part, plan.out_rows, here), :] = last_row


def unpack_kernel(
    plan, in_ref, log_ref, vel_hbm, friction_hbm, misfit_hbm,
    vel_ref, friction_ref, misfit_ref, grad_ref, leave,
):
    here, width, cols, rows = plan.layers_here, plan.width, plan.cols, plan.rows
    local_chunks = plan.local_cols // LANES

    total = jnp.sum(
        in_ref[pl.ds(here, plan.devices, stride=plan.out_rows), :], axis=0, keepdims=True
    )
    line_lane = lax.broadcasted_iota(jnp.int32, (1, LANES), 1)

    def summed(first):
        ahead = (line_lane + (LANES - first % LANES)) % LANES
        return jnp.sum(jnp.where(ahead < cols, total, 0.0), axis=1, keepdims=True)

    misfit_sum = summed(plan.halo + cols)
    grad_sum = summed(plan.halo + cols + width)
    scale = step_size / jnp.sqrt(grad_sum / plan.column_count + 1e-06)

    lane = lax.broadcasted_iota(jnp.int32, (plan.out_rows, LANES), 1)
    def chunk(c, i):
        at = (plan.chunks - 1 - i) * plan.per_chunk * plan.out_rows
        if not isinstance(at, int):
            at = pl.multiple_of(at, 8)
        turned = [
            lane_roll(in_ref[pl.ds(at + (plan.per_chunk - 1 - t) * plan.out_rows, plan.out_rows), :], t * cols)
            for t in range(plan.per_chunk)
        ]
        for r in range(rows):
            start = r * width + plan.halo + c * cols
            ahead = (lane + (LANES - start % LANES)) % LANES
            row = turned[0]
            for t in range(1, plan.per_chunk):
                row = jnp.where(ahead >= t * cols, turned[t], row)
            row = lane_roll(row, -start)
            vel_ref[c, pl.ds(i * rows + r, here, stride=plan.chunks * rows), :] = row[:here]
            if c == 0:
                owner, step = i // local_chunks, i % local_chunks
                grad_ref[owner, pl.ds(step * rows + r, 1), :] = row[here : here + 1]

    out = [pltpu.make_async_copy(vel_ref.at[c], vel_hbm.at[c], leave.at[c]) for c in range(2)]
    out.append(pltpu.make_async_copy(friction_ref, friction_hbm, leave.at[2]))
    out.append(pltpu.make_async_copy(misfit_ref, misfit_hbm, leave.at[3]))
    for c in range(2):

        def chunk_body(i, carry):
            chunk(c, i)
            return carry

        repeat(plan, plan.chunks, chunk_body)
        out[c].start()
    friction_ref[...] = log_ref[...] - grad_ref[lax.axis_index("layer")] * scale
    out[2].start()
    misfit_ref[...] = 0.5 * misfit_sum / plan.column_count
    out[3].start()
    for copy in out:
        copy.wait()


def as_lines(x):
    chunked = x.reshape(x.shape[:-1] + (x.shape[-1] // LANES, LANES))
    return jnp.swapaxes(chunked, -3, -2).reshape(-1, LANES)


def from_lines(lines, shape):
    chunked = lines.reshape(shape[:-2] + (shape[-1] // LANES, shape[-2], LANES))
    return jnp.swapaxes(chunked, -3, -2).reshape(shape)


def on_device(mesh_shape, velocity_init, driving, observed, log_friction, ice_mask):
    plan = Plan(mesh_shape, velocity_init.shape)
    vmem = pl.BlockSpec(memory_space=pltpu.VMEM)
    hbm = pl.BlockSpec(memory_space=pltpu.HBM)
    f32 = jnp.float32
    limit = pltpu.CompilerParams(vmem_limit_bytes=(16 if plan.unrolled else 40) * MIB)
    inputs = [as_lines(x) for x in (velocity_init, driving, observed, log_friction, ice_mask)]

    def exchange(blocks):
        shaped = blocks.reshape(blocks.shape[0], 1, LANES)
        ranks = [
            m * plan.layer_size + part
            for part in reversed(range(plan.layer_size))
            for m in reversed(range(plan.map_size))
        ]
        return lax.all_to_all(
            shaped, ("map", "layer"), split_axis=0, concat_axis=0, tiled=True, axis_index_groups=[ranks]
        ).reshape(blocks.shape)

    packed = pl.pallas_call(
        functools.partial(pack_kernel, plan),
        out_shape=jax.ShapeDtypeStruct((plan.devices * plan.in_rows, LANES), f32),
        in_specs=[hbm] * 5,
        out_specs=vmem,
        scratch_shapes=[pltpu.VMEM(x.shape, x.dtype) for x in inputs]
        + [
            pltpu.SemaphoreType.DMA((VELOCITY_COPIES + 4,)),
        ],
        compiler_params=limit,
        name="pack",
    )(*(pltpu.with_memory_space_constraint(x, pltpu.HBM) for x in inputs))

    windows = exchange(packed)

    plane = (plan.layers, plan.map_size, LANES)
    solved = pl.pallas_call(
        functools.partial(solve_kernel, plan),
        out_shape=jax.ShapeDtypeStruct((plan.devices * plan.out_rows, LANES), f32),
        in_specs=[vmem],
        out_specs=vmem,
        scratch_shapes=[
            pltpu.VMEM((2,) + plane, f32),
            pltpu.VMEM(plane, f32),
            pltpu.VMEM((2,) + plane, f32),
            pltpu.VMEM((2,) + plane, f32),
            pltpu.VMEM((4,) + plane, f32),
            pltpu.VMEM((2,) + plane, f32),
            pltpu.VMEM((2,) + plane, f32),
        ],
        compiler_params=limit,
        name="solve",
    )(windows)

    back = exchange(solved)

    vel_lines, log_lines = inputs[0].reshape(2, -1, LANES), inputs[3]
    velocity, friction_new, misfit = pl.pallas_call(
        functools.partial(unpack_kernel, plan),
        out_shape=(
            jax.ShapeDtypeStruct(vel_lines.shape, f32),
            jax.ShapeDtypeStruct(log_lines.shape, f32),
            jax.ShapeDtypeStruct((1, 1), f32),
        ),
        in_specs=[vmem] * 2,
        out_specs=(hbm, hbm, hbm),
        scratch_shapes=[
            pltpu.VMEM(vel_lines.shape, f32),
            pltpu.VMEM(log_lines.shape, f32),
            pltpu.VMEM((1, 1), f32),
            pltpu.VMEM((plan.layer_size,) + log_lines.shape, f32),
            pltpu.SemaphoreType.DMA((4,)),
        ],
        compiler_params=limit,
        name="unpack",
    )(back, log_lines)
    return (
        from_lines(velocity, velocity_init.shape),
        from_lines(friction_new, log_friction.shape),
        misfit.reshape(()),
    )


def solution(mesh):
    in_specs = (
        P(None, "layer", "map", None),
        P(None, "map", "layer"),
        P(None, "map", "layer"),
        P("map", "layer"),
        P("map", "layer"),
    )
    out_specs = (P(None, "layer", "map", None), P("map", "layer"), P())
    return jax.shard_map(
        functools.partial(on_device, dict(mesh.shape)),
        mesh=mesh,
        in_specs=in_specs,
        out_specs=out_specs,
        check_vma=False,
    )
```

```python
import functools

import jax
import jax.numpy as jnp
from jax import lax
from jax.experimental import pallas as pl
from jax.experimental.pallas import tpu as pltpu
from jax.sharding import PartitionSpec as P

strain_floor = 0.1
step_size = 0.5
LANES = 128
REACH = 5
BED_REACH = 3
MIB = 1 << 20
VELOCITY_COPIES = 4


class Plan:
    def __init__(self, mesh_shape, velocity_shape):
        self.map_size = mesh_shape["map"]
        self.layer_size = mesh_shape["layer"]
        self.devices = self.map_size * self.layer_size
        self.layers_here = velocity_shape[1]
        self.rows = velocity_shape[2]
        self.ny = velocity_shape[3]
        self.layers = self.layers_here * self.layer_size
        self.cols = self.ny // self.devices
        self.width = LANES // self.rows
        self.halo = (self.width - self.cols) // 2
        self.low = self.halo - REACH
        self.wide = self.cols + 2 * REACH
        self.half = self.wide // 2
        self.gap = self.low + self.wide
        self.local_cols = self.ny // self.layer_size
        self.per_chunk = LANES // self.cols
        self.chunks = self.ny // LANES
        self.column_count = self.rows * self.map_size * self.ny
        self.vel_rows = 2 * self.layers_here
        self.in_rows = self.vel_rows + 1
        self.left_at = self.gap
        self.right_at = self.gap + self.cols // 2 + 1
        self.out_rows = self.layers_here + 1
        self.unrolled = self.map_size <= 8
        assert self.width * self.rows == LANES and self.cols * self.per_chunk == LANES
        assert self.low >= 0 and self.wide % 2 == 0 and self.width - self.wide >= self.half
        assert 2 * self.cols <= self.width and self.local_cols % LANES == 0
        assert self.vel_rows == 8 and self.rows == 2 and 4 * self.cols <= LANES


def repeat(plan, count, body, carry=0):
    if plan.unrolled:
        for index in range(count):
            carry = body(index, carry)
        return carry
    return lax.fori_loop(0, count, body, carry)


def lane_roll(value, shift):
    shift = shift % LANES
    return value if shift == 0 else pltpu.roll(value, shift, 1)


def pack_kernel(
    plan, vel_hbm, driving_hbm, observed_hbm, log_hbm, mask_hbm, out_ref,
    vel_ref, driving_ref, observed_ref, log_ref, mask_ref, arrival,
):
    width, rows, cols, half = plan.width, plan.rows, plan.cols, plan.half
    piece = vel_ref.shape[0] // VELOCITY_COPIES
    spans = [pl.ds(n * piece, piece) for n in range(VELOCITY_COPIES)]
    pairs = [(vel_hbm.at[span, :], vel_ref.at[span, :]) for span in spans] + [
        (driving_hbm, driving_ref),
        (observed_hbm, observed_ref),
        (log_hbm, log_ref),
        (mask_hbm, mask_ref),
    ]
    copies = [pltpu.make_async_copy(pair[0], pair[1], arrival.at[n]) for n, pair in enumerate(pairs)]
    for n, copy in enumerate(copies):
        copy.start(priority=1 if n >= VELOCITY_COPIES else n % 2)
    shape = (plan.vel_rows, LANES)
    lane = lax.broadcasted_iota(jnp.int32, shape, 1)
    sub = lax.broadcasted_iota(jnp.int32, shape, 0)
    in_gap = jnp.logical_not(jnp.logical_and(lane % width >= plan.low, lane % width < plan.gap))
    no_line = jnp.zeros((1, LANES), jnp.float32)

    def slide(part, start, length, place):
        step, offset = start // LANES, start % LANES
        value = part(step)
        if offset + length > LANES:
            after = part(step + 1)
            value = jnp.where(lax.broadcasted_iota(jnp.int32, value.shape, 1) >= offset, value, after)
        return lane_roll(value, place - offset)

    for copy in copies[:VELOCITY_COPIES]:
        copy.wait()

    def chunk_windows(i, carry):
        def velocity(r):
            def part(step):
                chunk = i + step
                if isinstance(chunk, int) and not 0 <= chunk < plan.chunks:
                    return jnp.zeros(shape, jnp.float32)
                at = chunk if isinstance(chunk, int) else jnp.clip(chunk, 0, plan.chunks - 1)
                value = vel_ref[pl.ds(at * rows + r, plan.vel_rows, stride=plan.chunks * rows), :]
                if isinstance(chunk, int):
                    return value
                return jnp.where(jnp.logical_and(chunk >= 0, chunk < plan.chunks), value, 0.0)

            return part

        for t in range(plan.per_chunk):
            block = None
            for r in range(rows):
                value = slide(velocity(r), plan.cols * t - plan.halo, width, r * width)
                block = value if block is None else jnp.where(lane >= r * width, value, block)
            at = (plan.chunks - 1 - i) * plan.per_chunk * plan.in_rows
            if not isinstance(at, int):
                at = pl.multiple_of(at, 8)
            at = at + (plan.per_chunk - 1 - t) * plan.in_rows
            out_ref[pl.ds(at, plan.vel_rows), :] = jnp.where(in_gap, 0.0, block)
            out_ref[pl.ds(at + plan.vel_rows, 1), :] = no_line
        return carry

    repeat(plan, plan.chunks, chunk_windows)
    for copy in copies[VELOCITY_COPIES:]:
        copy.wait()

    place = lax.axis_index("layer")
    local_chunks = plan.local_cols // LANES

    skip = local_chunks * rows
    no_block = jnp.zeros(shape, jnp.float32)

    def whole(ref, row):
        return jnp.broadcast_to(ref[row : row + 1, :], shape).astype(jnp.float32)

    def gap_part(r, step):
        at = step * rows + r
        observed = jnp.where(sub < 2, whole(observed_ref, at), whole(observed_ref, skip + at))
        return jnp.where(sub < 4, observed, jnp.where(sub < 6, whole(mask_ref, at), whole(log_ref, at)))

    def driving_part(r, step):
        at = step * rows + r
        return jnp.where(sub < 2, whole(driving_ref, at), whole(driving_ref, skip + at))

    def sequence(make):
        return [
            [no_block] + [make(r, step) for step in range(local_chunks)] + [no_block] for r in range(rows)
        ]

    gap_parts, driving_parts = sequence(gap_part), sequence(driving_part)
    own = plan.local_cols // cols
    spill = -(-REACH // cols)

    def column_block(q):
        start = q * cols
        block = None
        for r in range(rows):

            def in_gaps(step):
                return gap_parts[r][step + 1]

            def of_driving(step):
                return driving_parts[r][step + 1]

            at = r * width
            first = slide(in_gaps, start - REACH, half, (at + plan.gap) % LANES)
            second = slide(in_gaps, start - REACH + half, half, (at + plan.gap) % LANES)
            before = slide(of_driving, start - BED_REACH, BED_REACH, (at + plan.left_at) % LANES)
            after = slide(of_driving, start + cols, BED_REACH, (at + plan.right_at) % LANES)
            ahead = (lane + (LANES - plan.gap - at)) % LANES
            of_observed = sub < 4
            first = jnp.where(jnp.logical_and(of_observed, ahead < BED_REACH), before, first)
            second = jnp.where(jnp.logical_and(of_observed, ahead >= plan.right_at - plan.gap), after, second)
            value = jnp.where(sub % 2 == 0, first, second)
            ahead = (lane + (LANES - plan.gap)) % LANES
            block = value if block is None else jnp.where(ahead >= r * width, value, block)
        at = pl.multiple_of((plan.layer_size - 1 - place) * (own * plan.in_rows), 8) + (own - 1 - q) * plan.in_rows
        here = pl.ds(at, plan.vel_rows)
        out_ref[here, :] = jnp.where(in_gap, block, out_ref[here, :])
        if not 0 <= q < own:
            return
        line = None
        step, offset = start // LANES, start % LANES
        for r in range(rows):
            for c in range(2):
                row = c * skip + step * rows + r
                put = (2 * r + c) * cols
                value = lane_roll(driving_ref[row : row + 1, :], put - offset)
                line = value if line is None else jnp.where(lane[:1] >= put, value, line)
        out_ref[pl.ds(at + plan.vel_rows, 1), :] = line

    for q in range(own):
        column_block(q)

    @pl.when(place > 0)
    def _():
        for q in range(-spill, 0):
            column_block(q)

    @pl.when(place < plan.layer_size - 1)
    def _():
        for q in range(own, own + spill):
            column_block(q)


def solve_kernel(plan, in_ref, out_ref, field, eta_ref, side, rhs, faces, weight, gain):
    size, width, rows = plan.map_size, plan.width, plan.rows
    layers, here = plan.layers, plan.layers_here
    shape = (size, LANES)
    lane = lax.broadcasted_iota(jnp.int32, shape, 1)
    sub = lax.broadcasted_iota(jnp.int32, shape, 0)
    last_group = lane >= LANES - width
    first_group = lane < width
    x_end = jnp.logical_and(last_group, sub == 0)
    x_start = jnp.logical_and(first_group, sub == size - 1)

    def block_row(part, rows_of_block, row):
        first = (plan.layer_size - 1 - part) * size * rows_of_block
        return pl.ds(first + row, size, stride=rows_of_block)

    def arrived(part, row):
        return in_ref[block_row(part, plan.in_rows, row), :]

    def moved(value, source, target):
        return lane_roll(value, target - source)

    def from_gap(halves):
        left, right = (moved(value, plan.gap, plan.low + h * plan.half) for h, value in enumerate(halves))
        return jnp.where(lane % width < plan.low + plan.half, left, right)

    def from_line(c):
        plane = None
        for r in range(rows):
            value = moved(line, (2 * r + c) * plan.cols, r * width + plan.halo)
            plane = value if plane is None else jnp.where(lane >= r * width, value, plane)
        return plane

    def driving_of(c, halves):
        left = moved(halves[0], plan.left_at, plan.halo - BED_REACH)
        right = moved(halves[1], plan.right_at, plan.halo + plan.cols)
        return jnp.where(centre, from_line(c), jnp.where(lane % width < plan.halo, left, right))

    def x_pair(value, edge):
        after = lane_roll(value, -width)
        before = after if 2 * width == LANES else lane_roll(value, width)
        after = jnp.where(last_group, pltpu.roll(after, 1, 0), after)
        before = jnp.where(first_group, pltpu.roll(before, size - 1, 0), before)
        return jnp.where(x_end, edge, after), jnp.where(x_start, edge, before)

    def y_pair(value):
        return lane_roll(value, -1), lane_roll(value, 1)

    unit = 2.0 / 4.0 ** (1.0 / 3.0)

    def viscosity(four_rates):
        return jnp.exp2(jnp.log2(4.0 * strain_floor + four_rates) * (-1.0 / 3.0))

    sums = [None] * plan.in_rows
    for part in range(plan.layer_size):
        for row in range(plan.in_rows):
            value = arrived(part, row)
            if row < plan.vel_rows:
                field[row // here, part * here + row % here] = value
            sums[row] = value if part == 0 else sums[row] + value
    line = sums[plan.vel_rows]
    gaps = [sums[2 * n : 2 * n + 2] for n in range(4)]
    reached = jnp.logical_and(lane % width >= plan.low, lane % width < plan.gap)
    centre = jnp.logical_and(lane % width >= plan.halo, lane % width < plan.halo + plan.cols)
    driving = [unit * driving_of(c, gaps[c]) for c in range(2)]
    observed = [from_gap(gaps[c]) for c in range(2)]
    mask = jnp.where(reached, from_gap(gaps[2]), 0.0)
    ice = mask != 0.0
    friction = jnp.where(mask == 1.0, jnp.exp(from_gap(gaps[3])), 0.0)

    def stencil(k, keep):
        u, v = field[0, k], field[1, k]
        u_east, u_west = x_pair(u, 0.0)
        v_east, v_west = x_pair(v, 0.0)
        u_north, u_south = y_pair(u)
        v_north, v_south = y_pair(v)
        stretch_x = u_east - u_west
        stretch_y = v_north - v_south
        shear = 0.5 * ((u_north - u_south) + (v_east - v_west))
        four_rates = stretch_x * (stretch_x + stretch_y) + (stretch_y * stretch_y + shear * shear)
        half_v = 0.5 * v
        eta = viscosity(four_rates)
        eta_edge = viscosity(u * u + half_v * half_v)
        eta_east, eta_west = x_pair(eta, eta_edge)
        eta_north, eta_south = y_pair(eta)
        east, west = eta + eta_east, eta + eta_west
        north, south = eta + eta_north, eta + eta_south
        along_x, along_y = east + west, north + south
        eta_ref[k] = eta
        side[0, k] = 4.0 * along_x + along_y
        side[1, k] = along_x + 4.0 * along_y
        rhs[0, k] = driving[0] + (4.0 * (east * u_east + west * u_west) + (north * u_north + south * u_south))
        rhs[1, k] = driving[1] + ((east * v_east + west * v_west) + 4.0 * (north * v_north + south * v_south))
        if keep:
            faces[0, k] = east
            faces[1, k] = west
            faces[2, k] = north
            faces[3, k] = south

    def coupling_of(k):
        return (2.0 * layers * layers) * (eta_ref[k] + eta_ref[k + 1])

    def reciprocal(value):
        guess = pl.reciprocal(value, approx=True)
        return guess * (2.0 - value * guess)

    middle = layers // 2
    zero = jnp.zeros(shape, jnp.float32)
    one = jnp.ones(shape, jnp.float32)

    def advance(k, coupling, carry):
        flux, value, total = carry
        across = reciprocal(coupling)
        new_flux, new_value, new_total = [], [], []
        for c in range(2):
            here_flux = flux[c] + side[c, k] * value[c]
            after = value[c] + across * here_flux
            here_total = total[c] + value[c] * rhs[c, k]
            weight[c, k] = value[c]
            gain[c, k] = reciprocal((coupling * value[c]) * after)
            rhs[c, k] = here_total
            new_flux.append(here_flux)
            new_value.append(after)
            new_total.append(here_total)
        return tuple(new_flux), tuple(new_value), tuple(new_total)

    def lower_step(k, carry):
        return advance(k, coupling_of(k), carry)

    def upper_step(k, carry):
        return advance(k, coupling_of(k - 1), carry)

    def fronts(step, carry):
        lower, upper = carry
        return lower_step(step, lower), upper_step(layers - 1 - step, upper)

    def outward(body, carry):
        def both(step, carry):
            return body(middle - 1 - step, 0, body(middle + 1 + step, 1, carry))

        carry = repeat(plan, layers - 1 - middle, both, carry)
        for k in range(2 * middle - layers, -1, -1):
            carry = body(k, 0, carry)
        return carry

    def sweep(keep):
        def stencil_body(k, carry):
            stencil(k, keep)
            return carry

        lower = ((unit * friction,) * 2, (one, one), (zero, zero))
        upper = ((zero, zero), (one, one), (zero, zero))
        if plan.unrolled:
            stencil(0, keep)
            stencil(layers - 1, keep)
            for step in range(layers - 1 - middle):
                stencil(step + 1, keep)
                if layers - 2 - step > step + 1:
                    stencil(layers - 2 - step, keep)
                lower, upper = fronts(step, (lower, upper))
        else:
            repeat(plan, layers, stencil_body)
            lower, upper = repeat(plan, layers - 1 - middle, fronts, (lower, upper))
        for k in range(layers - 1 - middle, middle):
            lower = lower_step(k, lower)
        joints, start = [], []
        for c in range(2):
            below, above = lower[1][c], upper[1][c]
            product = below * above
            inv = reciprocal(side[c, middle] * product + (lower[0][c] * above + upper[0][c] * below))
            joint = (below, above, product, inv, reciprocal(below), reciprocal(above))
            joints.append(joint)
            solved = join(joint, rhs[c, middle], lower[2][c], upper[2][c])
            field[c, middle] = jnp.where(ice, solved, 0.0)
            start.append((solved * joint[4], solved * joint[5]))

        def solved_layer(k, which, carry):
            new = list(carry)
            for c in range(2):
                scaled = carry[2 * which + c] + rhs[c, k] * gain[c, k]
                field[c, k] = jnp.where(ice, weight[c, k] * scaled, 0.0)
                new[2 * which + c] = scaled
            return tuple(new)

        outward(solved_layer, (start[0][0], start[1][0], start[0][1], start[1][1]))
        return joints

    def join(joint, right, lower_total, upper_total):
        below, above, product, inv, _, _ = joint
        return (right * product + (lower_total * above + upper_total * below)) * inv

    sweep(False)
    joints = sweep(True)
    base = [field[c, 0] for c in range(2)]
    top = [field[c, layers - 1] for c in range(2)]

    def send(k, carry):
        both = jnp.where(centre, field[0, k], lane_roll(field[1, k], plan.cols))
        out_ref[block_row(k // here, plan.out_rows, k % here), :] = both
        return carry

    repeat(plan, layers, send)

    mismatch = [jnp.where(ice, top[c] - observed[c], 0.0) for c in range(2)]
    source = [(unit * layers) * mismatch[c] for c in range(2)]

    def side_sum(k, value):
        east, west, north, south = (faces[n, k] for n in range(4))
        u_east, u_west = x_pair(value[0], 0.0)
        v_east, v_west = x_pair(value[1], 0.0)
        u_north, u_south = y_pair(value[0])
        v_north, v_south = y_pair(value[1])
        first = 4.0 * (east * u_east + west * u_west) + (north * u_north + south * u_south)
        second = (east * v_east + west * v_west) + 4.0 * (north * v_north + south * v_south)
        return first, second

    def side_sum(k, value):
        east, west, north, south = (faces[n, k] for n in range(4))
        u_east, u_west = x_pair(value[0], 0.0)
        v_east, v_west = x_pair(value[1], 0.0)
        u_north, u_south = y_pair(value[0])
        v_north, v_south = y_pair(value[1])
        first = 4.0 * (east * u_east + west * u_west) + (north * u_north + south * u_south)
        second = (east * v_east + west * v_west) + 4.0 * (north * v_north + south * v_south)
        return first, second

    below_scaled = tuple(source[c] * joints[c][3] for c in range(2))
    first_middle = tuple(below_scaled[c] * joints[c][0] for c in range(2))
    above_scaled = tuple(first_middle[c] * joints[c][5] for c in range(2))
    middle_sum = side_sum(middle, first_middle)

    def below_layer(k, carry):
        total, correction = carry
        added = side_sum(k, tuple(weight[c, k] * below_scaled[c] for c in range(2)))
        total = tuple(total[c] + weight[c, k] * added[c] for c in range(2))
        return total, tuple(correction[c] + total[c] * gain[c, k] for c in range(2))

    def above_layer(k, carry):
        total, scaled = carry
        scaled = tuple(scaled[c] + source[c] * gain[c, k] for c in range(2))
        added = side_sum(k, tuple(weight[c, k] * scaled[c] for c in range(2)))
        return tuple(total[c] + weight[c, k] * added[c] for c in range(2)), scaled

    def adjoint_layers(step, carry):
        below, above = carry
        return below_layer(step, below), above_layer(middle + 1 + step, above)

    nothing = (zero, zero)
    below, above = repeat(
        plan, layers - 1 - middle, adjoint_layers, ((nothing, nothing), (tuple(source), above_scaled))
    )
    for k in range(layers - 1 - middle, middle):
        below = below_layer(k, below)
    adjoint = tuple(
        join(joints[c], middle_sum[c], below[0][c], above[0][c]) * joints[c][4] + below[1][c] for c in range(2)
    )
    adjoint = [jnp.where(ice, adjoint[c], 0.0) for c in range(2)]
    gradient = -friction * (base[0] * adjoint[0] + base[1] * adjoint[1])

    def partial_sum(value):
        line = jnp.sum(jnp.where(centre, value, 0.0), axis=0, keepdims=True)
        folded = line
        for r in range(1, rows):
            folded = folded + lane_roll(line, r * width)
        return jnp.broadcast_to(lane_roll(folded, plan.cols), shape)

    misfit_line = partial_sum(mismatch[0] * mismatch[0] + mismatch[1] * mismatch[1])
    grad_line = partial_sum(gradient * gradient)
    in_first = jnp.logical_and(lane >= plan.halo + plan.cols, lane < plan.halo + 2 * plan.cols)
    last_row = jnp.where(centre, gradient, jnp.where(in_first, misfit_line, grad_line))
    for part in range(plan.layer_size):
        out_ref[block_row(part, plan.out_rows, here), :] = last_row


def unpack_kernel(
    plan, in_ref, log_ref, vel_hbm, friction_hbm, misfit_hbm,
    vel_ref, friction_ref, misfit_ref, grad_ref, leave,
):
    here, width, cols, rows = plan.layers_here, plan.width, plan.cols, plan.rows
    local_chunks = plan.local_cols // LANES

    total = jnp.sum(
        in_ref[pl.ds(here, plan.devices, stride=plan.out_rows), :], axis=0, keepdims=True
    )
    line_lane = lax.broadcasted_iota(jnp.int32, (1, LANES), 1)

    def summed(first):
        ahead = (line_lane + (LANES - first % LANES)) % LANES
        return jnp.sum(jnp.where(ahead < cols, total, 0.0), axis=1, keepdims=True)

    misfit_sum = summed(plan.halo + cols)
    grad_sum = summed(plan.halo + cols + width)
    scale = step_size / jnp.sqrt(grad_sum / plan.column_count + 1e-06)

    lane = lax.broadcasted_iota(jnp.int32, (plan.out_rows, LANES), 1)
    def chunk(c, i):
        at = (plan.chunks - 1 - i) * plan.per_chunk * plan.out_rows
        if not isinstance(at, int):
            at = pl.multiple_of(at, 8)
        turned = [
            lane_roll(in_ref[pl.ds(at + (plan.per_chunk - 1 - t) * plan.out_rows, plan.out_rows), :], t * cols)
            for t in range(plan.per_chunk)
        ]
        for r in range(rows):
            start = r * width + plan.halo + c * cols
            ahead = (lane + (LANES - start % LANES)) % LANES
            row = turned[0]
            for t in range(1, plan.per_chunk):
                row = jnp.where(ahead >= t * cols, turned[t], row)
            row = lane_roll(row, -start)
            vel_ref[c, pl.ds(i * rows + r, here, stride=plan.chunks * rows), :] = row[:here]
            if c == 0:
                owner, step = i // local_chunks, i % local_chunks
                grad_ref[owner, pl.ds(step * rows + r, 1), :] = row[here : here + 1]

    out = [pltpu.make_async_copy(vel_ref.at[c], vel_hbm.at[c], leave.at[c]) for c in range(2)]
    out.append(pltpu.make_async_copy(friction_ref, friction_hbm, leave.at[2]))
    out.append(pltpu.make_async_copy(misfit_ref, misfit_hbm, leave.at[3]))
    for c in range(2):

        def chunk_body(i, carry):
            chunk(c, i)
            return carry

        repeat(plan, plan.chunks, chunk_body)
        out[c].start(priority=c)
    friction_ref[...] = log_ref[...] - grad_ref[lax.axis_index("layer")] * scale
    out[2].start(priority=1)
    misfit_ref[...] = 0.5 * misfit_sum / plan.column_count
    out[3].start(priority=1)
    for copy in out:
        copy.wait()


def as_lines(x):
    chunked = x.reshape(x.shape[:-1] + (x.shape[-1] // LANES, LANES))
    return jnp.swapaxes(chunked, -3, -2).reshape(-1, LANES)


def from_lines(lines, shape):
    chunked = lines.reshape(shape[:-2] + (shape[-1] // LANES, shape[-2], LANES))
    return jnp.swapaxes(chunked, -3, -2).reshape(shape)


def on_device(mesh_shape, velocity_init, driving, observed, log_friction, ice_mask):
    plan = Plan(mesh_shape, velocity_init.shape)
    vmem = pl.BlockSpec(memory_space=pltpu.VMEM)
    hbm = pl.BlockSpec(memory_space=pltpu.HBM)
    f32 = jnp.float32
    limit = pltpu.CompilerParams(vmem_limit_bytes=(16 if plan.unrolled else 40) * MIB)
    inputs = [as_lines(x) for x in (velocity_init, driving, observed, log_friction, ice_mask)]

    def exchange(blocks):
        shaped = blocks.reshape(blocks.shape[0], 1, LANES)
        ranks = [
            m * plan.layer_size + part
            for part in reversed(range(plan.layer_size))
            for m in reversed(range(plan.map_size))
        ]
        return lax.all_to_all(
            shaped, ("map", "layer"), split_axis=0, concat_axis=0, tiled=True, axis_index_groups=[ranks]
        ).reshape(blocks.shape)

    packed = pl.pallas_call(
        functools.partial(pack_kernel, plan),
        out_shape=jax.ShapeDtypeStruct((plan.devices * plan.in_rows, LANES), f32),
        in_specs=[hbm] * 5,
        out_specs=vmem,
        scratch_shapes=[pltpu.VMEM(x.shape, x.dtype) for x in inputs]
        + [
            pltpu.SemaphoreType.DMA((VELOCITY_COPIES + 4,)),
        ],
        compiler_params=limit,
        name="pack",
    )(*(pltpu.with_memory_space_constraint(x, pltpu.HBM) for x in inputs))

    windows = exchange(packed)

    plane = (plan.layers, plan.map_size, LANES)
    solved = pl.pallas_call(
        functools.partial(solve_kernel, plan),
        out_shape=jax.ShapeDtypeStruct((plan.devices * plan.out_rows, LANES), f32),
        in_specs=[vmem],
        out_specs=vmem,
        scratch_shapes=[
            pltpu.VMEM((2,) + plane, f32),
            pltpu.VMEM(plane, f32),
            pltpu.VMEM((2,) + plane, f32),
            pltpu.VMEM((2,) + plane, f32),
            pltpu.VMEM((4,) + plane, f32),
            pltpu.VMEM((2,) + plane, f32),
            pltpu.VMEM((2,) + plane, f32),
        ],
        compiler_params=limit,
        name="solve",
    )(windows)

    back = exchange(solved)

    vel_lines, log_lines = inputs[0].reshape(2, -1, LANES), inputs[3]
    velocity, friction_new, misfit = pl.pallas_call(
        functools.partial(unpack_kernel, plan),
        out_shape=(
            jax.ShapeDtypeStruct(vel_lines.shape, f32),
            jax.ShapeDtypeStruct(log_lines.shape, f32),
            jax.ShapeDtypeStruct((1, 1), f32),
        ),
        in_specs=[vmem] * 2,
        out_specs=(hbm, hbm, hbm),
        scratch_shapes=[
            pltpu.VMEM(vel_lines.shape, f32),
            pltpu.VMEM(log_lines.shape, f32),
            pltpu.VMEM((1, 1), f32),
            pltpu.VMEM((plan.layer_size,) + log_lines.shape, f32),
            pltpu.SemaphoreType.DMA((4,)),
        ],
        compiler_params=limit,
        name="unpack",
    )(back, log_lines)
    return (
        from_lines(velocity, velocity_init.shape),
        from_lines(friction_new, log_friction.shape),
        misfit.reshape(()),
    )


def solution(mesh):
    in_specs = (
        P(None, "layer", "map", None),
        P(None, "map", "layer"),
        P(None, "map", "layer"),
        P("map", "layer"),
        P("map", "layer"),
    )
    out_specs = (P(None, "layer", "map", None), P("map", "layer"), P())
    return jax.shard_map(
        functools.partial(on_device, dict(mesh.shape)),
        mesh=mesh,
        in_specs=in_specs,
        out_specs=out_specs,
        check_vma=False,
    )
```

```python
import functools

import jax
import jax.numpy as jnp
from jax import lax
from jax.experimental import pallas as pl
from jax.experimental.pallas import tpu as pltpu
from jax.sharding import PartitionSpec as P

strain_floor = 0.1
step_size = 0.5
LANES = 128
REACH = 5
BED_REACH = 3
MIB = 1 << 20
VELOCITY_COPIES = 4


class Plan:
    def __init__(self, mesh_shape, velocity_shape):
        self.map_size = mesh_shape["map"]
        self.layer_size = mesh_shape["layer"]
        self.devices = self.map_size * self.layer_size
        self.layers_here = velocity_shape[1]
        self.rows = velocity_shape[2]
        self.ny = velocity_shape[3]
        self.layers = self.layers_here * self.layer_size
        self.cols = self.ny // self.devices
        self.width = LANES // self.rows
        self.halo = (self.width - self.cols) // 2
        self.low = self.halo - REACH
        self.wide = self.cols + 2 * REACH
        self.half = self.wide // 2
        self.gap = self.low + self.wide
        self.local_cols = self.ny // self.layer_size
        self.per_chunk = LANES // self.cols
        self.chunks = self.ny // LANES
        self.column_count = self.rows * self.map_size * self.ny
        self.vel_rows = 2 * self.layers_here
        self.in_rows = self.vel_rows + 1
        self.left_at = self.gap
        self.right_at = self.gap + self.cols // 2 + 1
        self.out_rows = self.layers_here + 1
        self.unrolled = self.map_size <= 8
        assert self.width * self.rows == LANES and self.cols * self.per_chunk == LANES
        assert self.low >= 0 and self.wide % 2 == 0 and self.width - self.wide >= self.half
        assert 2 * self.cols <= self.width and self.local_cols % LANES == 0
        assert self.vel_rows == 8 and self.rows == 2 and 4 * self.cols <= LANES


def repeat(plan, count, body, carry=0):
    if plan.unrolled:
        for index in range(count):
            carry = body(index, carry)
        return carry
    return lax.fori_loop(0, count, body, carry)


def lane_roll(value, shift):
    shift = shift % LANES
    return value if shift == 0 else pltpu.roll(value, shift, 1)


def pack_kernel(
    plan, vel_hbm, driving_hbm, observed_hbm, log_hbm, mask_hbm, out_ref,
    vel_ref, driving_ref, observed_ref, log_ref, mask_ref, arrival,
):
    width, rows, cols, half = plan.width, plan.rows, plan.cols, plan.half
    piece = vel_ref.shape[0] // VELOCITY_COPIES
    spans = [pl.ds(n * piece, piece) for n in range(VELOCITY_COPIES)]
    pairs = [
        (driving_hbm, driving_ref),
        (observed_hbm, observed_ref),
        (log_hbm, log_ref),
        (mask_hbm, mask_ref),
    ] + [(vel_hbm.at[span, :], vel_ref.at[span, :]) for span in spans]
    copies = [pltpu.make_async_copy(pair[0], pair[1], arrival.at[n]) for n, pair in enumerate(pairs)]
    for copy in copies:
        copy.start()
    shape = (plan.vel_rows, LANES)
    lane = lax.broadcasted_iota(jnp.int32, shape, 1)
    sub = lax.broadcasted_iota(jnp.int32, shape, 0)
    in_gap = jnp.logical_not(jnp.logical_and(lane % width >= plan.low, lane % width < plan.gap))

    def slide(part, start, length, place):
        step, offset = start // LANES, start % LANES
        value = part(step)
        if offset + length > LANES:
            after = part(step + 1)
            value = jnp.where(lax.broadcasted_iota(jnp.int32, value.shape, 1) >= offset, value, after)
        return lane_roll(value, place - offset)

    out_ref[...] = jnp.zeros_like(out_ref)
    for copy in copies[:-VELOCITY_COPIES]:
        copy.wait()

    place = lax.axis_index("layer")
    local_chunks = plan.local_cols // LANES

    skip = local_chunks * rows
    no_block = jnp.zeros(shape, jnp.float32)

    def whole(ref, row):
        return jnp.broadcast_to(ref[row : row + 1, :], shape).astype(jnp.float32)

    def gap_part(r, step):
        at = step * rows + r
        observed = jnp.where(sub < 2, whole(observed_ref, at), whole(observed_ref, skip + at))
        return jnp.where(sub < 4, observed, jnp.where(sub < 6, whole(mask_ref, at), whole(log_ref, at)))

    def driving_part(r, step):
        at = step * rows + r
        return jnp.where(sub < 2, whole(driving_ref, at), whole(driving_ref, skip + at))

    def sequence(make):
        return [
            [no_block] + [make(r, step) for step in range(local_chunks)] + [no_block] for r in range(rows)
        ]

    gap_parts, driving_parts = sequence(gap_part), sequence(driving_part)
    own = plan.local_cols // cols
    spill = -(-REACH // cols)

    def column_block(q):
        start = q * cols
        block = None
        for r in range(rows):

            def in_gaps(step):
                return gap_parts[r][step + 1]

            def of_driving(step):
                return driving_parts[r][step + 1]

            at = r * width
            first = slide(in_gaps, start - REACH, half, (at + plan.gap) % LANES)
            second = slide(in_gaps, start - REACH + half, half, (at + plan.gap) % LANES)
            before = slide(of_driving, start - BED_REACH, BED_REACH, (at + plan.left_at) % LANES)
            after = slide(of_driving, start + cols, BED_REACH, (at + plan.right_at) % LANES)
            ahead = (lane + (LANES - plan.gap - at)) % LANES
            of_observed = sub < 4
            first = jnp.where(jnp.logical_and(of_observed, ahead < BED_REACH), before, first)
            second = jnp.where(jnp.logical_and(of_observed, ahead >= plan.right_at - plan.gap), after, second)
            value = jnp.where(sub % 2 == 0, first, second)
            ahead = (lane + (LANES - plan.gap)) % LANES
            block = value if block is None else jnp.where(ahead >= r * width, value, block)
        at = pl.multiple_of((plan.layer_size - 1 - place) * (own * plan.in_rows), 8) + (own - 1 - q) * plan.in_rows
        here = pl.ds(at, plan.vel_rows)
        out_ref[here, :] = block
        if not 0 <= q < own:
            return
        line = None
        step, offset = start // LANES, start % LANES
        for r in range(rows):
            for c in range(2):
                row = c * skip + step * rows + r
                put = (2 * r + c) * cols
                value = lane_roll(driving_ref[row : row + 1, :], put - offset)
                line = value if line is None else jnp.where(lane[:1] >= put, value, line)
        out_ref[pl.ds(at + plan.vel_rows, 1), :] = line

    for q in range(own):
        column_block(q)

    @pl.when(place > 0)
    def _():
        for q in range(-spill, 0):
            column_block(q)

    @pl.when(place < plan.layer_size - 1)
    def _():
        for q in range(own, own + spill):
            column_block(q)

    for copy in copies[-VELOCITY_COPIES:]:
        copy.wait()

    def chunk_windows(i, carry):
        def velocity(r):
            def part(step):
                chunk = i + step
                if isinstance(chunk, int) and not 0 <= chunk < plan.chunks:
                    return jnp.zeros(shape, jnp.float32)
                at = chunk if isinstance(chunk, int) else jnp.clip(chunk, 0, plan.chunks - 1)
                value = vel_ref[pl.ds(at * rows + r, plan.vel_rows, stride=plan.chunks * rows), :]
                if isinstance(chunk, int):
                    return value
                return jnp.where(jnp.logical_and(chunk >= 0, chunk < plan.chunks), value, 0.0)

            return part

        for t in range(plan.per_chunk):
            block = None
            for r in range(rows):
                value = slide(velocity(r), plan.cols * t - plan.halo, width, r * width)
                block = value if block is None else jnp.where(lane >= r * width, value, block)
            at = (plan.chunks - 1 - i) * plan.per_chunk * plan.in_rows
            if not isinstance(at, int):
                at = pl.multiple_of(at, 8)
            at = at + (plan.per_chunk - 1 - t) * plan.in_rows
            here = pl.ds(at, plan.vel_rows)
            out_ref[here, :] = jnp.where(in_gap, out_ref[here, :], block)
        return carry

    repeat(plan, plan.chunks, chunk_windows)


def solve_kernel(plan, in_ref, out_ref, field, eta_ref, side, rhs, faces, weight, gain):
    size, width, rows = plan.map_size, plan.width, plan.rows
    layers, here = plan.layers, plan.layers_here
    shape = (size, LANES)
    lane = lax.broadcasted_iota(jnp.int32, shape, 1)
    sub = lax.broadcasted_iota(jnp.int32, shape, 0)
    last_group = lane >= LANES - width
    first_group = lane < width
    x_end = jnp.logical_and(last_group, sub == 0)
    x_start = jnp.logical_and(first_group, sub == size - 1)

    def block_row(part, rows_of_block, row):
        first = (plan.layer_size - 1 - part) * size * rows_of_block
        return pl.ds(first + row, size, stride=rows_of_block)

    def arrived(part, row):
        return in_ref[block_row(part, plan.in_rows, row), :]

    def moved(value, source, target):
        return lane_roll(value, target - source)

    def from_gap(halves):
        left, right = (moved(value, plan.gap, plan.low + h * plan.half) for h, value in enumerate(halves))
        return jnp.where(lane % width < plan.low + plan.half, left, right)

    def from_line(c):
        plane = None
        for r in range(rows):
            value = moved(line, (2 * r + c) * plan.cols, r * width + plan.halo)
            plane = value if plane is None else jnp.where(lane >= r * width, value, plane)
        return plane

    def driving_of(c, halves):
        left = moved(halves[0], plan.left_at, plan.halo - BED_REACH)
        right = moved(halves[1], plan.right_at, plan.halo + plan.cols)
        return jnp.where(centre, from_line(c), jnp.where(lane % width < plan.halo, left, right))

    def x_pair(value, edge):
        after = lane_roll(value, -width)
        before = after if 2 * width == LANES else lane_roll(value, width)
        after = jnp.where(last_group, pltpu.roll(after, 1, 0), after)
        before = jnp.where(first_group, pltpu.roll(before, size - 1, 0), before)
        return jnp.where(x_end, edge, after), jnp.where(x_start, edge, before)

    def y_pair(value):
        return lane_roll(value, -1), lane_roll(value, 1)

    unit = 2.0 / 4.0 ** (1.0 / 3.0)

    def viscosity(four_rates):
        return jnp.exp2(jnp.log2(4.0 * strain_floor + four_rates) * (-1.0 / 3.0))

    sums = [None] * plan.in_rows
    for part in range(plan.layer_size):
        for row in range(plan.in_rows):
            value = arrived(part, row)
            if row < plan.vel_rows:
                field[row // here, part * here + row % here] = value
            sums[row] = value if part == 0 else sums[row] + value
    line = sums[plan.vel_rows]
    gaps = [sums[2 * n : 2 * n + 2] for n in range(4)]
    reached = jnp.logical_and(lane % width >= plan.low, lane % width < plan.gap)
    centre = jnp.logical_and(lane % width >= plan.halo, lane % width < plan.halo + plan.cols)
    driving = [unit * driving_of(c, gaps[c]) for c in range(2)]
    observed = [from_gap(gaps[c]) for c in range(2)]
    mask = jnp.where(reached, from_gap(gaps[2]), 0.0)
    ice = mask != 0.0
    friction = jnp.where(mask == 1.0, jnp.exp(from_gap(gaps[3])), 0.0)

    def stencil(k, keep):
        u, v = field[0, k], field[1, k]
        u_east, u_west = x_pair(u, 0.0)
        v_east, v_west = x_pair(v, 0.0)
        u_north, u_south = y_pair(u)
        v_north, v_south = y_pair(v)
        stretch_x = u_east - u_west
        stretch_y = v_north - v_south
        shear = 0.5 * ((u_north - u_south) + (v_east - v_west))
        four_rates = stretch_x * (stretch_x + stretch_y) + (stretch_y * stretch_y + shear * shear)
        half_v = 0.5 * v
        eta = viscosity(four_rates)
        eta_edge = viscosity(u * u + half_v * half_v)
        eta_east, eta_west = x_pair(eta, eta_edge)
        eta_north, eta_south = y_pair(eta)
        east, west = eta + eta_east, eta + eta_west
        north, south = eta + eta_north, eta + eta_south
        along_x, along_y = east + west, north + south
        eta_ref[k] = eta
        side[0, k] = 4.0 * along_x + along_y
        side[1, k] = along_x + 4.0 * along_y
        rhs[0, k] = driving[0] + (4.0 * (east * u_east + west * u_west) + (north * u_north + south * u_south))
        rhs[1, k] = driving[1] + ((east * v_east + west * v_west) + 4.0 * (north * v_north + south * v_south))
        if keep:
            faces[0, k] = east
            faces[1, k] = west
            faces[2, k] = north
            faces[3, k] = south

    def coupling_of(k):
        return (2.0 * layers * layers) * (eta_ref[k] + eta_ref[k + 1])

    def reciprocal(value):
        guess = pl.reciprocal(value, approx=True)
        return guess * (2.0 - value * guess)

    middle = layers // 2
    zero = jnp.zeros(shape, jnp.float32)
    one = jnp.ones(shape, jnp.float32)

    def advance(k, coupling, carry):
        flux, value, total = carry
        across = reciprocal(coupling)
        new_flux, new_value, new_total = [], [], []
        for c in range(2):
            here_flux = flux[c] + side[c, k] * value[c]
            after = value[c] + across * here_flux
            here_total = total[c] + value[c] * rhs[c, k]
            weight[c, k] = value[c]
            gain[c, k] = reciprocal((coupling * value[c]) * after)
            rhs[c, k] = here_total
            new_flux.append(here_flux)
            new_value.append(after)
            new_total.append(here_total)
        return tuple(new_flux), tuple(new_value), tuple(new_total)

    def lower_step(k, carry):
        return advance(k, coupling_of(k), carry)

    def upper_step(k, carry):
        return advance(k, coupling_of(k - 1), carry)

    def fronts(step, carry):
        lower, upper = carry
        return lower_step(step, lower), upper_step(layers - 1 - step, upper)

    def outward(body, carry):
        def both(step, carry):
            return body(middle - 1 - step, 0, body(middle + 1 + step, 1, carry))

        carry = repeat(plan, layers - 1 - middle, both, carry)
        for k in range(2 * middle - layers, -1, -1):
            carry = body(k, 0, carry)
        return carry

    def sweep(keep):
        def stencil_body(k, carry):
            stencil(k, keep)
            return carry

        lower = ((unit * friction,) * 2, (one, one), (zero, zero))
        upper = ((zero, zero), (one, one), (zero, zero))
        if plan.unrolled:
            stencil(0, keep)
            stencil(layers - 1, keep)
            for step in range(layers - 1 - middle):
                stencil(step + 1, keep)
                if layers - 2 - step > step + 1:
                    stencil(layers - 2 - step, keep)
                lower, upper = fronts(step, (lower, upper))
        else:
            repeat(plan, layers, stencil_body)
            lower, upper = repeat(plan, layers - 1 - middle, fronts, (lower, upper))
        for k in range(layers - 1 - middle, middle):
            lower = lower_step(k, lower)
        joints, start = [], []
        for c in range(2):
            below, above = lower[1][c], upper[1][c]
            product = below * above
            inv = reciprocal(side[c, middle] * product + (lower[0][c] * above + upper[0][c] * below))
            joint = (below, above, product, inv, reciprocal(below), reciprocal(above))
            joints.append(joint)
            solved = join(joint, rhs[c, middle], lower[2][c], upper[2][c])
            field[c, middle] = jnp.where(ice, solved, 0.0)
            start.append((solved * joint[4], solved * joint[5]))

        def solved_layer(k, which, carry):
            new = list(carry)
            for c in range(2):
                scaled = carry[2 * which + c] + rhs[c, k] * gain[c, k]
                field[c, k] = jnp.where(ice, weight[c, k] * scaled, 0.0)
                new[2 * which + c] = scaled
            return tuple(new)

        outward(solved_layer, (start[0][0], start[1][0], start[0][1], start[1][1]))
        return joints

    def join(joint, right, lower_total, upper_total):
        below, above, product, inv, _, _ = joint
        return (right * product + (lower_total * above + upper_total * below)) * inv

    sweep(False)
    joints = sweep(True)
    base = [field[c, 0] for c in range(2)]
    top = [field[c, layers - 1] for c in range(2)]

    def send(k, carry):
        both = jnp.where(centre, field[0, k], lane_roll(field[1, k], plan.cols))
        out_ref[block_row(k // here, plan.out_rows, k % here), :] = both
        return carry

    repeat(plan, layers, send)

    mismatch = [jnp.where(ice, top[c] - observed[c], 0.0) for c in range(2)]
    source = [(unit * layers) * mismatch[c] for c in range(2)]

    def side_sum(k, value):
        east, west, north, south = (faces[n, k] for n in range(4))
        u_east, u_west = x_pair(value[0], 0.0)
        v_east, v_west = x_pair(value[1], 0.0)
        u_north, u_south = y_pair(value[0])
        v_north, v_south = y_pair(value[1])
        first = 4.0 * (east * u_east + west * u_west) + (north * u_north + south * u_south)
        second = (east * v_east + west * v_west) + 4.0 * (north * v_north + south * v_south)
        return first, second

    def side_sum(k, value):
        east, west, north, south = (faces[n, k] for n in range(4))
        u_east, u_west = x_pair(value[0], 0.0)
        v_east, v_west = x_pair(value[1], 0.0)
        u_north, u_south = y_pair(value[0])
        v_north, v_south = y_pair(value[1])
        first = 4.0 * (east * u_east + west * u_west) + (north * u_north + south * u_south)
        second = (east * v_east + west * v_west) + 4.0 * (north * v_north + south * v_south)
        return first, second

    below_scaled = tuple(source[c] * joints[c][3] for c in range(2))
    first_middle = tuple(below_scaled[c] * joints[c][0] for c in range(2))
    above_scaled = tuple(first_middle[c] * joints[c][5] for c in range(2))
    middle_sum = side_sum(middle, first_middle)

    def below_layer(k, carry):
        total, correction = carry
        added = side_sum(k, tuple(weight[c, k] * below_scaled[c] for c in range(2)))
        total = tuple(total[c] + weight[c, k] * added[c] for c in range(2))
        return total, tuple(correction[c] + total[c] * gain[c, k] for c in range(2))

    def above_layer(k, carry):
        total, scaled = carry
        scaled = tuple(scaled[c] + source[c] * gain[c, k] for c in range(2))
        added = side_sum(k, tuple(weight[c, k] * scaled[c] for c in range(2)))
        return tuple(total[c] + weight[c, k] * added[c] for c in range(2)), scaled

    def adjoint_layers(step, carry):
        below, above = carry
        return below_layer(step, below), above_layer(middle + 1 + step, above)

    nothing = (zero, zero)
    below, above = repeat(
        plan, layers - 1 - middle, adjoint_layers, ((nothing, nothing), (tuple(source), above_scaled))
    )
    for k in range(layers - 1 - middle, middle):
        below = below_layer(k, below)
    adjoint = tuple(
        join(joints[c], middle_sum[c], below[0][c], above[0][c]) * joints[c][4] + below[1][c] for c in range(2)
    )
    adjoint = [jnp.where(ice, adjoint[c], 0.0) for c in range(2)]
    gradient = -friction * (base[0] * adjoint[0] + base[1] * adjoint[1])

    def partial_sum(value):
        line = jnp.sum(jnp.where(centre, value, 0.0), axis=0, keepdims=True)
        folded = line
        for r in range(1, rows):
            folded = folded + lane_roll(line, r * width)
        return jnp.broadcast_to(lane_roll(folded, plan.cols), shape)

    misfit_line = partial_sum(mismatch[0] * mismatch[0] + mismatch[1] * mismatch[1])
    grad_line = partial_sum(gradient * gradient)
    in_first = jnp.logical_and(lane >= plan.halo + plan.cols, lane < plan.halo + 2 * plan.cols)
    last_row = jnp.where(centre, gradient, jnp.where(in_first, misfit_line, grad_line))
    for part in range(plan.layer_size):
        out_ref[block_row(part, plan.out_rows, here), :] = last_row


def unpack_kernel(
    plan, in_ref, log_ref, vel_hbm, friction_hbm, misfit_hbm,
    vel_ref, friction_ref, misfit_ref, grad_ref, leave,
):
    here, width, cols, rows = plan.layers_here, plan.width, plan.cols, plan.rows
    local_chunks = plan.local_cols // LANES

    total = jnp.sum(
        in_ref[pl.ds(here, plan.devices, stride=plan.out_rows), :], axis=0, keepdims=True
    )
    line_lane = lax.broadcasted_iota(jnp.int32, (1, LANES), 1)

    def summed(first):
        ahead = (line_lane + (LANES - first % LANES)) % LANES
        return jnp.sum(jnp.where(ahead < cols, total, 0.0), axis=1, keepdims=True)

    misfit_sum = summed(plan.halo + cols)
    grad_sum = summed(plan.halo + cols + width)
    scale = step_size / jnp.sqrt(grad_sum / plan.column_count + 1e-06)

    lane = lax.broadcasted_iota(jnp.int32, (plan.out_rows, LANES), 1)
    def chunk(c, i):
        at = (plan.chunks - 1 - i) * plan.per_chunk * plan.out_rows
        if not isinstance(at, int):
            at = pl.multiple_of(at, 8)
        turned = [
            lane_roll(in_ref[pl.ds(at + (plan.per_chunk - 1 - t) * plan.out_rows, plan.out_rows), :], t * cols)
            for t in range(plan.per_chunk)
        ]
        for r in range(rows):
            start = r * width + plan.halo + c * cols
            ahead = (lane + (LANES - start % LANES)) % LANES
            row = turned[0]
            for t in range(1, plan.per_chunk):
                row = jnp.where(ahead >= t * cols, turned[t], row)
            row = lane_roll(row, -start)
            vel_ref[c, pl.ds(i * rows + r, here, stride=plan.chunks * rows), :] = row[:here]
            if c == 0:
                owner, step = i // local_chunks, i % local_chunks
                grad_ref[owner, pl.ds(step * rows + r, 1), :] = row[here : here + 1]

    out = [pltpu.make_async_copy(vel_ref.at[c], vel_hbm.at[c], leave.at[c]) for c in range(2)]
    out.append(pltpu.make_async_copy(friction_ref, friction_hbm, leave.at[2]))
    out.append(pltpu.make_async_copy(misfit_ref, misfit_hbm, leave.at[3]))
    for c in range(2):

        def chunk_body(i, carry):
            chunk(c, i)
            return carry

        repeat(plan, plan.chunks, chunk_body)
        out[c].start()
    friction_ref[...] = log_ref[...] - grad_ref[lax.axis_index("layer")] * scale
    out[2].start()
    misfit_ref[...] = 0.5 * misfit_sum / plan.column_count
    out[3].start()
    for copy in out:
        copy.wait()


def as_lines(x):
    chunked = x.reshape(x.shape[:-1] + (x.shape[-1] // LANES, LANES))
    return jnp.swapaxes(chunked, -3, -2).reshape(-1, LANES)


def from_lines(lines, shape):
    chunked = lines.reshape(shape[:-2] + (shape[-1] // LANES, shape[-2], LANES))
    return jnp.swapaxes(chunked, -3, -2).reshape(shape)


def on_device(mesh_shape, velocity_init, driving, observed, log_friction, ice_mask):
    plan = Plan(mesh_shape, velocity_init.shape)
    vmem = pl.BlockSpec(memory_space=pltpu.VMEM)
    hbm = pl.BlockSpec(memory_space=pltpu.HBM)
    f32 = jnp.float32
    limit = pltpu.CompilerParams(vmem_limit_bytes=(16 if plan.unrolled else 40) * MIB)
    inputs = [as_lines(x) for x in (velocity_init, driving, observed, log_friction, ice_mask)]

    def exchange(blocks):
        shaped = blocks.reshape(blocks.shape[0], 1, LANES)
        ranks = [
            m * plan.layer_size + part
            for part in reversed(range(plan.layer_size))
            for m in reversed(range(plan.map_size))
        ]
        return lax.all_to_all(
            shaped, ("map", "layer"), split_axis=0, concat_axis=0, tiled=True, axis_index_groups=[ranks]
        ).reshape(blocks.shape)

    packed = pl.pallas_call(
        functools.partial(pack_kernel, plan),
        out_shape=jax.ShapeDtypeStruct((plan.devices * plan.in_rows, LANES), f32),
        in_specs=[hbm] * 5,
        out_specs=vmem,
        scratch_shapes=[pltpu.VMEM(x.shape, x.dtype) for x in inputs]
        + [
            pltpu.SemaphoreType.DMA((VELOCITY_COPIES + 4,)),
        ],
        compiler_params=limit,
        name="pack",
    )(*(pltpu.with_memory_space_constraint(x, pltpu.HBM) for x in inputs))

    windows = exchange(packed)

    plane = (plan.layers, plan.map_size, LANES)
    solved = pl.pallas_call(
        functools.partial(solve_kernel, plan),
        out_shape=jax.ShapeDtypeStruct((plan.devices * plan.out_rows, LANES), f32),
        in_specs=[vmem],
        out_specs=vmem,
        scratch_shapes=[
            pltpu.VMEM((2,) + plane, f32),
            pltpu.VMEM(plane, f32),
            pltpu.VMEM((2,) + plane, f32),
            pltpu.VMEM((2,) + plane, f32),
            pltpu.VMEM((4,) + plane, f32),
            pltpu.VMEM((2,) + plane, f32),
            pltpu.VMEM((2,) + plane, f32),
        ],
        compiler_params=limit,
        name="solve",
    )(windows)

    back = exchange(solved)

    vel_lines, log_lines = inputs[0].reshape(2, -1, LANES), inputs[3]
    velocity, friction_new, misfit = pl.pallas_call(
        functools.partial(unpack_kernel, plan),
        out_shape=(
            jax.ShapeDtypeStruct(vel_lines.shape, f32),
            jax.ShapeDtypeStruct(log_lines.shape, f32),
            jax.ShapeDtypeStruct((1, 1), f32),
        ),
        in_specs=[vmem] * 2,
        out_specs=(hbm, hbm, hbm),
        scratch_shapes=[
            pltpu.VMEM(vel_lines.shape, f32),
            pltpu.VMEM(log_lines.shape, f32),
            pltpu.VMEM((1, 1), f32),
            pltpu.VMEM((plan.layer_size,) + log_lines.shape, f32),
            pltpu.SemaphoreType.DMA((4,)),
        ],
        compiler_params=limit,
        name="unpack",
    )(back, log_lines)
    return (
        from_lines(velocity, velocity_init.shape),
        from_lines(friction_new, log_friction.shape),
        misfit.reshape(()),
    )


def solution(mesh):
    in_specs = (
        P(None, "layer", "map", None),
        P(None, "map", "layer"),
        P(None, "map", "layer"),
        P("map", "layer"),
        P("map", "layer"),
    )
    out_specs = (P(None, "layer", "map", None), P("map", "layer"), P())
    return jax.shard_map(
        functools.partial(on_device, dict(mesh.shape)),
        mesh=mesh,
        in_specs=in_specs,
        out_specs=out_specs,
        check_vma=False,
    )
```

```python
import functools

import jax
import jax.numpy as jnp
from jax import lax
from jax.experimental import pallas as pl
from jax.experimental.pallas import tpu as pltpu
from jax.sharding import PartitionSpec as P

strain_floor = 0.1
step_size = 0.5
LANES = 128
REACH = 5
BED_REACH = 3
MIB = 1 << 20
VELOCITY_COPIES = 4


class Plan:
    def __init__(self, mesh_shape, velocity_shape):
        self.map_size = mesh_shape["map"]
        self.layer_size = mesh_shape["layer"]
        self.devices = self.map_size * self.layer_size
        self.layers_here = velocity_shape[1]
        self.rows = velocity_shape[2]
        self.ny = velocity_shape[3]
        self.layers = self.layers_here * self.layer_size
        self.cols = self.ny // self.devices
        self.width = LANES // self.rows
        self.halo = (self.width - self.cols) // 2
        self.low = self.halo - REACH
        self.wide = self.cols + 2 * REACH
        self.half = self.wide // 2
        self.gap = self.low + self.wide
        self.local_cols = self.ny // self.layer_size
        self.per_chunk = LANES // self.cols
        self.chunks = self.ny // LANES
        self.column_count = self.rows * self.map_size * self.ny
        self.vel_rows = 2 * self.layers_here
        self.in_rows = self.vel_rows + 1
        self.left_at = self.gap
        self.right_at = self.gap + self.cols // 2 + 1
        self.out_rows = self.layers_here + 1
        self.unrolled = self.map_size <= 8
        assert self.width * self.rows == LANES and self.cols * self.per_chunk == LANES
        assert self.low >= 0 and self.wide % 2 == 0 and self.width - self.wide >= self.half
        assert 2 * self.cols <= self.width and self.local_cols % LANES == 0
        assert self.vel_rows == 8 and self.rows == 2 and 4 * self.cols <= LANES


def repeat(plan, count, body, carry=0):
    if plan.unrolled:
        for index in range(count):
            carry = body(index, carry)
        return carry
    return lax.fori_loop(0, count, body, carry)


def lane_roll(value, shift):
    shift = shift % LANES
    return value if shift == 0 else pltpu.roll(value, shift, 1)


def pack_kernel(
    plan, vel_hbm, driving_hbm, observed_hbm, log_hbm, mask_hbm, out_ref,
    vel_ref, driving_ref, observed_ref, log_ref, mask_ref, arrival,
):
    width, rows, cols, half = plan.width, plan.rows, plan.cols, plan.half
    piece = vel_ref.shape[0] // VELOCITY_COPIES
    spans = [pl.ds(n * piece, piece) for n in range(VELOCITY_COPIES)]
    pairs = [
        (driving_hbm, driving_ref),
        (observed_hbm, observed_ref),
        (log_hbm, log_ref),
        (mask_hbm, mask_ref),
    ] + [(vel_hbm.at[span, :], vel_ref.at[span, :]) for span in spans]
    copies = [pltpu.make_async_copy(pair[0], pair[1], arrival.at[n]) for n, pair in enumerate(pairs)]
    for copy in copies:
        copy.start()
    shape = (plan.vel_rows, LANES)
    lane = lax.broadcasted_iota(jnp.int32, shape, 1)
    sub = lax.broadcasted_iota(jnp.int32, shape, 0)
    in_gap = jnp.logical_not(jnp.logical_and(lane % width >= plan.low, lane % width < plan.gap))

    def slide(part, start, length, place):
        step, offset = start // LANES, start % LANES
        value = part(step)
        if offset + length > LANES:
            after = part(step + 1)
            value = jnp.where(lax.broadcasted_iota(jnp.int32, value.shape, 1) >= offset, value, after)
        return lane_roll(value, place - offset)

    out_ref[...] = jnp.zeros_like(out_ref)
    for copy in copies[:-VELOCITY_COPIES]:
        copy.wait()

    place = lax.axis_index("layer")
    local_chunks = plan.local_cols // LANES

    skip = local_chunks * rows
    no_block = jnp.zeros(shape, jnp.float32)

    def whole(ref, row):
        return jnp.broadcast_to(ref[row : row + 1, :], shape).astype(jnp.float32)

    def gap_part(r, step):
        at = step * rows + r
        observed = jnp.where(sub < 2, whole(observed_ref, at), whole(observed_ref, skip + at))
        return jnp.where(sub < 4, observed, jnp.where(sub < 6, whole(mask_ref, at), whole(log_ref, at)))

    def driving_part(r, step):
        at = step * rows + r
        return jnp.where(sub < 2, whole(driving_ref, at), whole(driving_ref, skip + at))

    def sequence(make):
        return [
            [no_block] + [make(r, step) for step in range(local_chunks)] + [no_block] for r in range(rows)
        ]

    gap_parts, driving_parts = sequence(gap_part), sequence(driving_part)
    own = plan.local_cols // cols
    spill = -(-REACH // cols)

    def column_block(q):
        start = q * cols
        block = None
        for r in range(rows):

            def in_gaps(step):
                return gap_parts[r][step + 1]

            def of_driving(step):
                return driving_parts[r][step + 1]

            at = r * width
            first = slide(in_gaps, start - REACH, half, (at + plan.gap) % LANES)
            second = slide(in_gaps, start - REACH + half, half, (at + plan.gap) % LANES)
            before = slide(of_driving, start - BED_REACH, BED_REACH, (at + plan.left_at) % LANES)
            after = slide(of_driving, start + cols, BED_REACH, (at + plan.right_at) % LANES)
            ahead = (lane + (LANES - plan.gap - at)) % LANES
            of_observed = sub < 4
            first = jnp.where(jnp.logical_and(of_observed, ahead < BED_REACH), before, first)
            second = jnp.where(jnp.logical_and(of_observed, ahead >= plan.right_at - plan.gap), after, second)
            value = jnp.where(sub % 2 == 0, first, second)
            ahead = (lane + (LANES - plan.gap)) % LANES
            block = value if block is None else jnp.where(ahead >= r * width, value, block)
        at = pl.multiple_of((plan.layer_size - 1 - place) * (own * plan.in_rows), 8) + (own - 1 - q) * plan.in_rows
        here = pl.ds(at, plan.vel_rows)
        out_ref[here, :] = block
        if not 0 <= q < own:
            return
        line = None
        step, offset = start // LANES, start % LANES
        for r in range(rows):
            for c in range(2):
                row = c * skip + step * rows + r
                put = (2 * r + c) * cols
                value = lane_roll(driving_ref[row : row + 1, :], put - offset)
                line = value if line is None else jnp.where(lane[:1] >= put, value, line)
        out_ref[pl.ds(at + plan.vel_rows, 1), :] = line

    for q in range(own):
        column_block(q)

    @pl.when(place > 0)
    def _():
        for q in range(-spill, 0):
            column_block(q)

    @pl.when(place < plan.layer_size - 1)
    def _():
        for q in range(own, own + spill):
            column_block(q)

    for copy in copies[-VELOCITY_COPIES:]:
        copy.wait()

    kept = {}

    def chunk_windows(i, carry):
        seen = kept if plan.unrolled else {}

        def once(key, make):
            if key not in seen:
                seen[key] = make()
            return seen[key]

        def read(step, r):
            chunk = i + step
            if isinstance(chunk, int) and not 0 <= chunk < plan.chunks:
                return jnp.zeros(shape, jnp.float32)
            at = chunk if isinstance(chunk, int) else jnp.clip(chunk, 0, plan.chunks - 1)
            value = vel_ref[pl.ds(at * rows + r, plan.vel_rows, stride=plan.chunks * rows), :]
            if isinstance(chunk, int):
                return value
            return jnp.where(jnp.logical_and(chunk >= 0, chunk < plan.chunks), value, 0.0)

        def turned(step, r):
            name = i + step if plan.unrolled else step
            return once(("turned", name, r), lambda: lane_roll(read(step, r), r * width))

        def moved(step, r):
            if r == 0:
                return turned(step, 0)
            name = i + step if plan.unrolled else step
            return once(("moved", name, r), lambda: jnp.where(lane >= r * width, turned(step, r), turned(step - 1, r)))

        for t in range(plan.per_chunk):
            start = plan.cols * t - plan.halo
            step, offset = start // LANES, start % LANES
            block = None
            for r in range(rows):
                low, high = offset + r * width, offset + (r + 1) * width
                if high <= LANES:
                    value = moved(step, r)
                elif low >= LANES:
                    value = moved(step + 1, r)
                else:
                    value = jnp.where(lane >= offset, moved(step, r), moved(step + 1, r))
                ahead = (lane + (LANES - offset)) % LANES
                block = value if block is None else jnp.where(ahead >= r * width, value, block)
            block = lane_roll(block, -offset)
            at = (plan.chunks - 1 - i) * plan.per_chunk * plan.in_rows
            if not isinstance(at, int):
                at = pl.multiple_of(at, 8)
            at = at + (plan.per_chunk - 1 - t) * plan.in_rows
            here = pl.ds(at, plan.vel_rows)
            out_ref[here, :] = jnp.where(in_gap, out_ref[here, :], block)
        return carry

    repeat(plan, plan.chunks, chunk_windows)


def solve_kernel(plan, in_ref, out_ref, field, eta_ref, side, rhs, faces, weight, gain):
    size, width, rows = plan.map_size, plan.width, plan.rows
    layers, here = plan.layers, plan.layers_here
    shape = (size, LANES)
    lane = lax.broadcasted_iota(jnp.int32, shape, 1)
    sub = lax.broadcasted_iota(jnp.int32, shape, 0)
    last_group = lane >= LANES - width
    first_group = lane < width
    x_end = jnp.logical_and(last_group, sub == 0)
    x_start = jnp.logical_and(first_group, sub == size - 1)

    def block_row(part, rows_of_block, row):
        first = (plan.layer_size - 1 - part) * size * rows_of_block
        return pl.ds(first + row, size, stride=rows_of_block)

    def arrived(part, row):
        return in_ref[block_row(part, plan.in_rows, row), :]

    def moved(value, source, target):
        return lane_roll(value, target - source)

    def from_gap(halves):
        left, right = (moved(value, plan.gap, plan.low + h * plan.half) for h, value in enumerate(halves))
        return jnp.where(lane % width < plan.low + plan.half, left, right)

    def from_line(c):
        plane = None
        for r in range(rows):
            value = moved(line, (2 * r + c) * plan.cols, r * width + plan.halo)
            plane = value if plane is None else jnp.where(lane >= r * width, value, plane)
        return plane

    def driving_of(c, halves):
        left = moved(halves[0], plan.left_at, plan.halo - BED_REACH)
        right = moved(halves[1], plan.right_at, plan.halo + plan.cols)
        return jnp.where(centre, from_line(c), jnp.where(lane % width < plan.halo, left, right))

    def x_pair(value, edge):
        after = lane_roll(value, -width)
        before = after if 2 * width == LANES else lane_roll(value, width)
        after = jnp.where(last_group, pltpu.roll(after, 1, 0), after)
        before = jnp.where(first_group, pltpu.roll(before, size - 1, 0), before)
        return jnp.where(x_end, edge, after), jnp.where(x_start, edge, before)

    def y_pair(value):
        return lane_roll(value, -1), lane_roll(value, 1)

    unit = 2.0 / 4.0 ** (1.0 / 3.0)

    def viscosity(four_rates):
        return jnp.exp2(jnp.log2(4.0 * strain_floor + four_rates) * (-1.0 / 3.0))

    sums = [None] * plan.in_rows
    for part in range(plan.layer_size):
        for row in range(plan.in_rows):
            value = arrived(part, row)
            if row < plan.vel_rows:
                field[row // here, part * here + row % here] = value
            sums[row] = value if part == 0 else sums[row] + value
    line = sums[plan.vel_rows]
    gaps = [sums[2 * n : 2 * n + 2] for n in range(4)]
    reached = jnp.logical_and(lane % width >= plan.low, lane % width < plan.gap)
    centre = jnp.logical_and(lane % width >= plan.halo, lane % width < plan.halo + plan.cols)
    driving = [unit * driving_of(c, gaps[c]) for c in range(2)]
    observed = [from_gap(gaps[c]) for c in range(2)]
    mask = jnp.where(reached, from_gap(gaps[2]), 0.0)
    ice = mask != 0.0
    friction = jnp.where(mask == 1.0, jnp.exp(from_gap(gaps[3])), 0.0)

    def stencil(k, keep):
        u, v = field[0, k], field[1, k]
        u_east, u_west = x_pair(u, 0.0)
        v_east, v_west = x_pair(v, 0.0)
        u_north, u_south = y_pair(u)
        v_north, v_south = y_pair(v)
        stretch_x = u_east - u_west
        stretch_y = v_north - v_south
        shear = 0.5 * ((u_north - u_south) + (v_east - v_west))
        four_rates = stretch_x * (stretch_x + stretch_y) + (stretch_y * stretch_y + shear * shear)
        half_v = 0.5 * v
        eta = viscosity(four_rates)
        eta_edge = viscosity(u * u + half_v * half_v)
        eta_east, eta_west = x_pair(eta, eta_edge)
        eta_north, eta_south = y_pair(eta)
        east, west = eta + eta_east, eta + eta_west
        north, south = eta + eta_north, eta + eta_south
        along_x, along_y = east + west, north + south
        eta_ref[k] = eta
        side[0, k] = 4.0 * along_x + along_y
        side[1, k] = along_x + 4.0 * along_y
        rhs[0, k] = driving[0] + (4.0 * (east * u_east + west * u_west) + (north * u_north + south * u_south))
        rhs[1, k] = driving[1] + ((east * v_east + west * v_west) + 4.0 * (north * v_north + south * v_south))
        if keep:
            faces[0, k] = east
            faces[1, k] = west
            faces[2, k] = north
            faces[3, k] = south

    def coupling_of(k):
        return (2.0 * layers * layers) * (eta_ref[k] + eta_ref[k + 1])

    def reciprocal(value):
        guess = pl.reciprocal(value, approx=True)
        return guess * (2.0 - value * guess)

    middle = layers // 2
    zero = jnp.zeros(shape, jnp.float32)
    one = jnp.ones(shape, jnp.float32)

    def advance(k, coupling, carry):
        flux, value, total = carry
        across = reciprocal(coupling)
        new_flux, new_value, new_total = [], [], []
        for c in range(2):
            here_flux = flux[c] + side[c, k] * value[c]
            after = value[c] + across * here_flux
            here_total = total[c] + value[c] * rhs[c, k]
            weight[c, k] = value[c]
            gain[c, k] = reciprocal((coupling * value[c]) * after)
            rhs[c, k] = here_total
            new_flux.append(here_flux)
            new_value.append(after)
            new_total.append(here_total)
        return tuple(new_flux), tuple(new_value), tuple(new_total)

    def lower_step(k, carry):
        return advance(k, coupling_of(k), carry)

    def upper_step(k, carry):
        return advance(k, coupling_of(k - 1), carry)

    def fronts(step, carry):
        lower, upper = carry
        return lower_step(step, lower), upper_step(layers - 1 - step, upper)

    def outward(body, carry):
        def both(step, carry):
            return body(middle - 1 - step, 0, body(middle + 1 + step, 1, carry))

        carry = repeat(plan, layers - 1 - middle, both, carry)
        for k in range(2 * middle - layers, -1, -1):
            carry = body(k, 0, carry)
        return carry

    def sweep(keep):
        def stencil_body(k, carry):
            stencil(k, keep)
            return carry

        lower = ((unit * friction,) * 2, (one, one), (zero, zero))
        upper = ((zero, zero), (one, one), (zero, zero))
        if plan.unrolled:
            stencil(0, keep)
            stencil(layers - 1, keep)
            for step in range(layers - 1 - middle):
                stencil(step + 1, keep)
                if layers - 2 - step > step + 1:
                    stencil(layers - 2 - step, keep)
                lower, upper = fronts(step, (lower, upper))
        else:
            repeat(plan, layers, stencil_body)
            lower, upper = repeat(plan, layers - 1 - middle, fronts, (lower, upper))
        for k in range(layers - 1 - middle, middle):
            lower = lower_step(k, lower)
        joints, start = [], []
        for c in range(2):
            below, above = lower[1][c], upper[1][c]
            product = below * above
            inv = reciprocal(side[c, middle] * product + (lower[0][c] * above + upper[0][c] * below))
            joint = (below, above, product, inv, reciprocal(below), reciprocal(above))
            joints.append(joint)
            solved = join(joint, rhs[c, middle], lower[2][c], upper[2][c])
            field[c, middle] = jnp.where(ice, solved, 0.0)
            start.append((solved * joint[4], solved * joint[5]))

        def solved_layer(k, which, carry):
            new = list(carry)
            for c in range(2):
                scaled = carry[2 * which + c] + rhs[c, k] * gain[c, k]
                field[c, k] = jnp.where(ice, weight[c, k] * scaled, 0.0)
                new[2 * which + c] = scaled
            return tuple(new)

        outward(solved_layer, (start[0][0], start[1][0], start[0][1], start[1][1]))
        return joints

    def join(joint, right, lower_total, upper_total):
        below, above, product, inv, _, _ = joint
        return (right * product + (lower_total * above + upper_total * below)) * inv

    sweep(False)
    joints = sweep(True)
    base = [field[c, 0] for c in range(2)]
    top = [field[c, layers - 1] for c in range(2)]

    def send(k, carry):
        both = jnp.where(centre, field[0, k], lane_roll(field[1, k], plan.cols))
        out_ref[block_row(k // here, plan.out_rows, k % here), :] = both
        return carry

    repeat(plan, layers, send)

    mismatch = [jnp.where(ice, top[c] - observed[c], 0.0) for c in range(2)]
    source = [(unit * layers) * mismatch[c] for c in range(2)]

    def side_sum(k, value):
        east, west, north, south = (faces[n, k] for n in range(4))
        u_east, u_west = x_pair(value[0], 0.0)
        v_east, v_west = x_pair(value[1], 0.0)
        u_north, u_south = y_pair(value[0])
        v_north, v_south = y_pair(value[1])
        first = 4.0 * (east * u_east + west * u_west) + (north * u_north + south * u_south)
        second = (east * v_east + west * v_west) + 4.0 * (north * v_north + south * v_south)
        return first, second

    def side_sum(k, value):
        east, west, north, south = (faces[n, k] for n in range(4))
        u_east, u_west = x_pair(value[0], 0.0)
        v_east, v_west = x_pair(value[1], 0.0)
        u_north, u_south = y_pair(value[0])
        v_north, v_south = y_pair(value[1])
        first = 4.0 * (east * u_east + west * u_west) + (north * u_north + south * u_south)
        second = (east * v_east + west * v_west) + 4.0 * (north * v_north + south * v_south)
        return first, second

    below_scaled = tuple(source[c] * joints[c][3] for c in range(2))
    first_middle = tuple(below_scaled[c] * joints[c][0] for c in range(2))
    above_scaled = tuple(first_middle[c] * joints[c][5] for c in range(2))
    middle_sum = side_sum(middle, first_middle)

    def below_layer(k, carry):
        total, correction = carry
        added = side_sum(k, tuple(weight[c, k] * below_scaled[c] for c in range(2)))
        total = tuple(total[c] + weight[c, k] * added[c] for c in range(2))
        return total, tuple(correction[c] + total[c] * gain[c, k] for c in range(2))

    def above_layer(k, carry):
        total, scaled = carry
        scaled = tuple(scaled[c] + source[c] * gain[c, k] for c in range(2))
        added = side_sum(k, tuple(weight[c, k] * scaled[c] for c in range(2)))
        return tuple(total[c] + weight[c, k] * added[c] for c in range(2)), scaled

    def adjoint_layers(step, carry):
        below, above = carry
        return below_layer(step, below), above_layer(middle + 1 + step, above)

    nothing = (zero, zero)
    below, above = repeat(
        plan, layers - 1 - middle, adjoint_layers, ((nothing, nothing), (tuple(source), above_scaled))
    )
    for k in range(layers - 1 - middle, middle):
        below = below_layer(k, below)
    adjoint = tuple(
        join(joints[c], middle_sum[c], below[0][c], above[0][c]) * joints[c][4] + below[1][c] for c in range(2)
    )
    adjoint = [jnp.where(ice, adjoint[c], 0.0) for c in range(2)]
    gradient = -friction * (base[0] * adjoint[0] + base[1] * adjoint[1])

    def partial_sum(value):
        line = jnp.sum(jnp.where(centre, value, 0.0), axis=0, keepdims=True)
        folded = line
        for r in range(1, rows):
            folded = folded + lane_roll(line, r * width)
        return jnp.broadcast_to(lane_roll(folded, plan.cols), shape)

    misfit_line = partial_sum(mismatch[0] * mismatch[0] + mismatch[1] * mismatch[1])
    grad_line = partial_sum(gradient * gradient)
    in_first = jnp.logical_and(lane >= plan.halo + plan.cols, lane < plan.halo + 2 * plan.cols)
    last_row = jnp.where(centre, gradient, jnp.where(in_first, misfit_line, grad_line))
    for part in range(plan.layer_size):
        out_ref[block_row(part, plan.out_rows, here), :] = last_row


def unpack_kernel(
    plan, in_ref, log_ref, vel_hbm, friction_hbm, misfit_hbm,
    vel_ref, friction_ref, misfit_ref, grad_ref, leave,
):
    here, width, cols, rows = plan.layers_here, plan.width, plan.cols, plan.rows
    local_chunks = plan.local_cols // LANES

    total = jnp.sum(
        in_ref[pl.ds(here, plan.devices, stride=plan.out_rows), :], axis=0, keepdims=True
    )
    line_lane = lax.broadcasted_iota(jnp.int32, (1, LANES), 1)

    def summed(first):
        ahead = (line_lane + (LANES - first % LANES)) % LANES
        return jnp.sum(jnp.where(ahead < cols, total, 0.0), axis=1, keepdims=True)

    misfit_sum = summed(plan.halo + cols)
    grad_sum = summed(plan.halo + cols + width)
    scale = step_size / jnp.sqrt(grad_sum / plan.column_count + 1e-06)

    lane = lax.broadcasted_iota(jnp.int32, (plan.out_rows, LANES), 1)
    def chunk(c, i):
        at = (plan.chunks - 1 - i) * plan.per_chunk * plan.out_rows
        if not isinstance(at, int):
            at = pl.multiple_of(at, 8)
        turned = [
            lane_roll(in_ref[pl.ds(at + (plan.per_chunk - 1 - t) * plan.out_rows, plan.out_rows), :], t * cols)
            for t in range(plan.per_chunk)
        ]
        for r in range(rows):
            start = r * width + plan.halo + c * cols
            ahead = (lane + (LANES - start % LANES)) % LANES
            row = turned[0]
            for t in range(1, plan.per_chunk):
                row = jnp.where(ahead >= t * cols, turned[t], row)
            row = lane_roll(row, -start)
            vel_ref[c, pl.ds(i * rows + r, here, stride=plan.chunks * rows), :] = row[:here]
            if c == 0:
                owner, step = i // local_chunks, i % local_chunks
                grad_ref[owner, pl.ds(step * rows + r, 1), :] = row[here : here + 1]

    out = [pltpu.make_async_copy(vel_ref.at[c], vel_hbm.at[c], leave.at[c]) for c in range(2)]
    out.append(pltpu.make_async_copy(friction_ref, friction_hbm, leave.at[2]))
    out.append(pltpu.make_async_copy(misfit_ref, misfit_hbm, leave.at[3]))
    for c in range(2):

        def chunk_body(i, carry):
            chunk(c, i)
            return carry

        repeat(plan, plan.chunks, chunk_body)
        out[c].start()
    friction_ref[...] = log_ref[...] - grad_ref[lax.axis_index("layer")] * scale
    out[2].start()
    misfit_ref[...] = 0.5 * misfit_sum / plan.column_count
    out[3].start()
    for copy in out:
        copy.wait()


def as_lines(x):
    chunked = x.reshape(x.shape[:-1] + (x.shape[-1] // LANES, LANES))
    return jnp.swapaxes(chunked, -3, -2).reshape(-1, LANES)


def from_lines(lines, shape):
    chunked = lines.reshape(shape[:-2] + (shape[-1] // LANES, shape[-2], LANES))
    return jnp.swapaxes(chunked, -3, -2).reshape(shape)


def on_device(mesh_shape, velocity_init, driving, observed, log_friction, ice_mask):
    plan = Plan(mesh_shape, velocity_init.shape)
    vmem = pl.BlockSpec(memory_space=pltpu.VMEM)
    hbm = pl.BlockSpec(memory_space=pltpu.HBM)
    f32 = jnp.float32
    limit = pltpu.CompilerParams(vmem_limit_bytes=(16 if plan.unrolled else 40) * MIB)
    inputs = [as_lines(x) for x in (velocity_init, driving, observed, log_friction, ice_mask)]

    def exchange(blocks):
        shaped = blocks.reshape(blocks.shape[0], 1, LANES)
        ranks = [
            m * plan.layer_size + part
            for part in reversed(range(plan.layer_size))
            for m in reversed(range(plan.map_size))
        ]
        return lax.all_to_all(
            shaped, ("map", "layer"), split_axis=0, concat_axis=0, tiled=True, axis_index_groups=[ranks]
        ).reshape(blocks.shape)

    packed = pl.pallas_call(
        functools.partial(pack_kernel, plan),
        out_shape=jax.ShapeDtypeStruct((plan.devices * plan.in_rows, LANES), f32),
        in_specs=[hbm] * 5,
        out_specs=vmem,
        scratch_shapes=[pltpu.VMEM(x.shape, x.dtype) for x in inputs]
        + [
            pltpu.SemaphoreType.DMA((VELOCITY_COPIES + 4,)),
        ],
        compiler_params=limit,
        name="pack",
    )(*(pltpu.with_memory_space_constraint(x, pltpu.HBM) for x in inputs))

    windows = exchange(packed)

    plane = (plan.layers, plan.map_size, LANES)
    solved = pl.pallas_call(
        functools.partial(solve_kernel, plan),
        out_shape=jax.ShapeDtypeStruct((plan.devices * plan.out_rows, LANES), f32),
        in_specs=[vmem],
        out_specs=vmem,
        scratch_shapes=[
            pltpu.VMEM((2,) + plane, f32),
            pltpu.VMEM(plane, f32),
            pltpu.VMEM((2,) + plane, f32),
            pltpu.VMEM((2,) + plane, f32),
            pltpu.VMEM((4,) + plane, f32),
            pltpu.VMEM((2,) + plane, f32),
            pltpu.VMEM((2,) + plane, f32),
        ],
        compiler_params=limit,
        name="solve",
    )(windows)

    back = exchange(solved)

    vel_lines, log_lines = inputs[0].reshape(2, -1, LANES), inputs[3]
    velocity, friction_new, misfit = pl.pallas_call(
        functools.partial(unpack_kernel, plan),
        out_shape=(
            jax.ShapeDtypeStruct(vel_lines.shape, f32),
            jax.ShapeDtypeStruct(log_lines.shape, f32),
            jax.ShapeDtypeStruct((1, 1), f32),
        ),
        in_specs=[vmem] * 2,
        out_specs=(hbm, hbm, hbm),
        scratch_shapes=[
            pltpu.VMEM(vel_lines.shape, f32),
            pltpu.VMEM(log_lines.shape, f32),
            pltpu.VMEM((1, 1), f32),
            pltpu.VMEM((plan.layer_size,) + log_lines.shape, f32),
            pltpu.SemaphoreType.DMA((4,)),
        ],
        compiler_params=limit,
        name="unpack",
    )(back, log_lines)
    return (
        from_lines(velocity, velocity_init.shape),
        from_lines(friction_new, log_friction.shape),
        misfit.reshape(()),
    )


def solution(mesh):
    in_specs = (
        P(None, "layer", "map", None),
        P(None, "map", "layer"),
        P(None, "map", "layer"),
        P("map", "layer"),
        P("map", "layer"),
    )
    out_specs = (P(None, "layer", "map", None), P("map", "layer"), P())
    return jax.shard_map(
        functools.partial(on_device, dict(mesh.shape)),
        mesh=mesh,
        in_specs=in_specs,
        out_specs=out_specs,
        check_vma=False,
    )
```

```python
import functools

import jax
import jax.numpy as jnp
from jax import lax
from jax.experimental import pallas as pl
from jax.experimental.pallas import tpu as pltpu
from jax.sharding import PartitionSpec as P

strain_floor = 0.1
step_size = 0.5
LANES = 128
REACH = 5
BED_REACH = 3
MIB = 1 << 20
VELOCITY_COPIES = 4


class Plan:
    def __init__(self, mesh_shape, velocity_shape):
        self.map_size = mesh_shape["map"]
        self.layer_size = mesh_shape["layer"]
        self.devices = self.map_size * self.layer_size
        self.layers_here = velocity_shape[1]
        self.rows = velocity_shape[2]
        self.ny = velocity_shape[3]
        self.layers = self.layers_here * self.layer_size
        self.cols = self.ny // self.devices
        self.width = LANES // self.rows
        self.halo = (self.width - self.cols) // 2
        self.low = self.halo - REACH
        self.wide = self.cols + 2 * REACH
        self.half = self.wide // 2
        self.gap = self.low + self.wide
        self.local_cols = self.ny // self.layer_size
        self.per_chunk = LANES // self.cols
        self.chunks = self.ny // LANES
        self.column_count = self.rows * self.map_size * self.ny
        self.vel_rows = 2 * self.layers_here
        self.in_rows = self.vel_rows + 1
        self.left_at = self.gap
        self.right_at = self.gap + self.cols // 2 + 1
        self.out_rows = self.layers_here + 1
        self.unrolled = self.map_size <= 8
        assert self.width * self.rows == LANES and self.cols * self.per_chunk == LANES
        assert self.low >= 0 and self.wide % 2 == 0 and self.width - self.wide >= self.half
        assert 2 * self.cols <= self.width and self.local_cols % LANES == 0
        assert self.vel_rows == 8 and self.rows == 2 and 4 * self.cols <= LANES


def repeat(plan, count, body, carry=0):
    if plan.unrolled:
        for index in range(count):
            carry = body(index, carry)
        return carry
    return lax.fori_loop(0, count, body, carry)


def lane_roll(value, shift):
    shift = shift % LANES
    return value if shift == 0 else pltpu.roll(value, shift, 1)


def pack_kernel(
    plan, vel_hbm, driving_hbm, observed_hbm, log_hbm, mask_hbm, out_ref,
    vel_ref, driving_ref, observed_ref, log_ref, mask_ref, arrival,
):
    width, rows, cols, half = plan.width, plan.rows, plan.cols, plan.half
    piece = vel_ref.shape[0] // VELOCITY_COPIES
    spans = [pl.ds(n * piece, piece) for n in range(VELOCITY_COPIES)]
    pairs = [
        (driving_hbm, driving_ref),
        (observed_hbm, observed_ref),
        (log_hbm, log_ref),
        (mask_hbm, mask_ref),
    ] + [(vel_hbm.at[span, :], vel_ref.at[span, :]) for span in spans]
    copies = [pltpu.make_async_copy(pair[0], pair[1], arrival.at[n]) for n, pair in enumerate(pairs)]
    for copy in copies:
        copy.start()
    shape = (plan.vel_rows, LANES)
    lane = lax.broadcasted_iota(jnp.int32, shape, 1)
    sub = lax.broadcasted_iota(jnp.int32, shape, 0)
    in_gap = jnp.logical_not(jnp.logical_and(lane % width >= plan.low, lane % width < plan.gap))

    def slide(part, start, length, place):
        step, offset = start // LANES, start % LANES
        value = part(step)
        if offset + length > LANES:
            after = part(step + 1)
            value = jnp.where(lax.broadcasted_iota(jnp.int32, value.shape, 1) >= offset, value, after)
        return lane_roll(value, place - offset)

    out_ref[...] = jnp.zeros_like(out_ref)
    for copy in copies[:-VELOCITY_COPIES]:
        copy.wait()

    place = lax.axis_index("layer")
    local_chunks = plan.local_cols // LANES

    skip = local_chunks * rows
    no_block = jnp.zeros(shape, jnp.float32)

    def whole(ref, row):
        return jnp.broadcast_to(ref[row : row + 1, :], shape).astype(jnp.float32)

    def gap_part(r, step):
        at = step * rows + r
        observed = jnp.where(sub < 2, whole(observed_ref, at), whole(observed_ref, skip + at))
        return jnp.where(sub < 4, observed, jnp.where(sub < 6, whole(mask_ref, at), whole(log_ref, at)))

    def driving_part(r, step):
        at = step * rows + r
        return jnp.where(sub < 2, whole(driving_ref, at), whole(driving_ref, skip + at))

    def sequence(make):
        return [
            [no_block] + [make(r, step) for step in range(local_chunks)] + [no_block] for r in range(rows)
        ]

    gap_parts, driving_parts = sequence(gap_part), sequence(driving_part)
    own = plan.local_cols // cols
    spill = -(-REACH // cols)

    def column_block(q):
        start = q * cols
        block = None
        for r in range(rows):

            def in_gaps(step):
                return gap_parts[r][step + 1]

            def of_driving(step):
                return driving_parts[r][step + 1]

            at = r * width
            first = slide(in_gaps, start - REACH, half, (at + plan.gap) % LANES)
            second = slide(in_gaps, start - REACH + half, half, (at + plan.gap) % LANES)
            before = slide(of_driving, start - BED_REACH, BED_REACH, (at + plan.left_at) % LANES)
            after = slide(of_driving, start + cols, BED_REACH, (at + plan.right_at) % LANES)
            ahead = (lane + (LANES - plan.gap - at)) % LANES
            of_observed = sub < 4
            first = jnp.where(jnp.logical_and(of_observed, ahead < BED_REACH), before, first)
            second = jnp.where(jnp.logical_and(of_observed, ahead >= plan.right_at - plan.gap), after, second)
            value = jnp.where(sub % 2 == 0, first, second)
            ahead = (lane + (LANES - plan.gap)) % LANES
            block = value if block is None else jnp.where(ahead >= r * width, value, block)
        at = pl.multiple_of((plan.layer_size - 1 - place) * (own * plan.in_rows), 8) + (own - 1 - q) * plan.in_rows
        here = pl.ds(at, plan.vel_rows)
        out_ref[here, :] = block
        if not 0 <= q < own:
            return
        line = None
        step, offset = start // LANES, start % LANES
        for r in range(rows):
            for c in range(2):
                row = c * skip + step * rows + r
                put = (2 * r + c) * cols
                value = lane_roll(driving_ref[row : row + 1, :], put - offset)
                line = value if line is None else jnp.where(lane[:1] >= put, value, line)
        out_ref[pl.ds(at + plan.vel_rows, 1), :] = line

    for q in range(own):
        column_block(q)

    @pl.when(place > 0)
    def _():
        for q in range(-spill, 0):
            column_block(q)

    @pl.when(place < plan.layer_size - 1)
    def _():
        for q in range(own, own + spill):
            column_block(q)

    for copy in copies[-VELOCITY_COPIES:]:
        copy.wait()

    def chunk_windows(i, carry):
        def velocity(r):
            def part(step):
                chunk = i + step
                if isinstance(chunk, int) and not 0 <= chunk < plan.chunks:
                    return jnp.zeros(shape, jnp.float32)
                at = chunk if isinstance(chunk, int) else jnp.clip(chunk, 0, plan.chunks - 1)
                value = vel_ref[pl.ds(at * rows + r, plan.vel_rows, stride=plan.chunks * rows), :]
                if isinstance(chunk, int):
                    return value
                return jnp.where(jnp.logical_and(chunk >= 0, chunk < plan.chunks), value, 0.0)

            return part

        for t in range(plan.per_chunk):
            block = None
            for r in range(rows):
                value = slide(velocity(r), plan.cols * t - plan.halo, width, r * width)
                block = value if block is None else jnp.where(lane >= r * width, value, block)
            at = (plan.chunks - 1 - i) * plan.per_chunk * plan.in_rows
            if not isinstance(at, int):
                at = pl.multiple_of(at, 8)
            at = at + (plan.per_chunk - 1 - t) * plan.in_rows
            here = pl.ds(at, plan.vel_rows)
            out_ref[here, :] = jnp.where(in_gap, out_ref[here, :], block)
        return carry

    repeat(plan, plan.chunks, chunk_windows)


def solve_kernel(plan, in_ref, out_ref, field, eta_ref, side, rhs, faces, weight, gain):
    size, width, rows = plan.map_size, plan.width, plan.rows
    layers, here = plan.layers, plan.layers_here
    shape = (size, LANES)
    lane = lax.broadcasted_iota(jnp.int32, shape, 1)
    sub = lax.broadcasted_iota(jnp.int32, shape, 0)
    last_group = lane >= LANES - width
    first_group = lane < width
    x_end = jnp.logical_and(last_group, sub == 0)
    x_start = jnp.logical_and(first_group, sub == size - 1)

    def block_row(part, rows_of_block, row):
        first = (plan.layer_size - 1 - part) * size * rows_of_block
        return pl.ds(first + row, size, stride=rows_of_block)

    def arrived(part, row):
        return in_ref[block_row(part, plan.in_rows, row), :]

    def moved(value, source, target):
        return lane_roll(value, target - source)

    def from_gap(halves):
        left, right = (moved(value, plan.gap, plan.low + h * plan.half) for h, value in enumerate(halves))
        return jnp.where(lane % width < plan.low + plan.half, left, right)

    def from_line(c):
        plane = None
        for r in range(rows):
            value = moved(line, (2 * r + c) * plan.cols, r * width + plan.halo)
            plane = value if plane is None else jnp.where(lane >= r * width, value, plane)
        return plane

    def driving_of(c, halves):
        left = moved(halves[0], plan.left_at, plan.halo - BED_REACH)
        right = moved(halves[1], plan.right_at, plan.halo + plan.cols)
        return jnp.where(centre, from_line(c), jnp.where(lane % width < plan.halo, left, right))

    def x_pair(value, edge):
        after = lane_roll(value, -width)
        before = after if 2 * width == LANES else lane_roll(value, width)
        after = jnp.where(last_group, pltpu.roll(after, 1, 0), after)
        before = jnp.where(first_group, pltpu.roll(before, size - 1, 0), before)
        return jnp.where(x_end, edge, after), jnp.where(x_start, edge, before)

    def y_pair(value):
        return lane_roll(value, -1), lane_roll(value, 1)

    unit = 2.0 / 4.0 ** (1.0 / 3.0)

    def viscosity(four_rates):
        return jnp.exp2(jnp.log2(4.0 * strain_floor + four_rates) * (-1.0 / 3.0))

    sums = [None] * plan.in_rows
    for part in range(plan.layer_size):
        for row in range(plan.in_rows):
            value = arrived(part, row)
            if row < plan.vel_rows:
                field[row // here, part * here + row % here] = value
            sums[row] = value if part == 0 else sums[row] + value
    line = sums[plan.vel_rows]
    gaps = [sums[2 * n : 2 * n + 2] for n in range(4)]
    reached = jnp.logical_and(lane % width >= plan.low, lane % width < plan.gap)
    centre = jnp.logical_and(lane % width >= plan.halo, lane % width < plan.halo + plan.cols)
    driving = [unit * driving_of(c, gaps[c]) for c in range(2)]
    observed = [from_gap(gaps[c]) for c in range(2)]
    mask = jnp.where(reached, from_gap(gaps[2]), 0.0)
    ice = mask != 0.0
    friction = jnp.where(mask == 1.0, jnp.exp(from_gap(gaps[3])), 0.0)

    def stencil(k, keep):
        u, v = field[0, k], field[1, k]
        u_east, u_west = x_pair(u, 0.0)
        v_east, v_west = x_pair(v, 0.0)
        u_north, u_south = y_pair(u)
        v_north, v_south = y_pair(v)
        stretch_x = u_east - u_west
        stretch_y = v_north - v_south
        shear = 0.5 * ((u_north - u_south) + (v_east - v_west))
        four_rates = stretch_x * (stretch_x + stretch_y) + (stretch_y * stretch_y + shear * shear)
        half_v = 0.5 * v
        eta = viscosity(four_rates)
        eta_edge = viscosity(u * u + half_v * half_v)
        eta_east, eta_west = x_pair(eta, eta_edge)
        eta_north, eta_south = y_pair(eta)
        east, west = eta + eta_east, eta + eta_west
        north, south = eta + eta_north, eta + eta_south
        along_x, along_y = east + west, north + south
        eta_ref[k] = eta
        side[0, k] = 4.0 * along_x + along_y
        side[1, k] = along_x + 4.0 * along_y
        rhs[0, k] = driving[0] + (4.0 * (east * u_east + west * u_west) + (north * u_north + south * u_south))
        rhs[1, k] = driving[1] + ((east * v_east + west * v_west) + 4.0 * (north * v_north + south * v_south))
        if keep:
            faces[0, k] = east
            faces[1, k] = west
            faces[2, k] = north
            faces[3, k] = south

    def coupling_of(k):
        return (2.0 * layers * layers) * (eta_ref[k] + eta_ref[k + 1])

    def reciprocal(value):
        guess = pl.reciprocal(value, approx=True)
        return guess * (2.0 - value * guess)

    middle = layers // 2
    zero = jnp.zeros(shape, jnp.float32)
    one = jnp.ones(shape, jnp.float32)

    def advance(k, coupling, carry):
        flux, value, total = carry
        across = reciprocal(coupling)
        new_flux, new_value, new_total, product = [], [], [], []
        for c in range(2):
            here_flux = flux[c] + side[c, k] * value[c]
            after = value[c] + across * here_flux
            here_total = total[c] + value[c] * rhs[c, k]
            weight[c, k] = value[c]
            product.append((coupling * value[c]) * after)
            rhs[c, k] = here_total
            new_flux.append(here_flux)
            new_value.append(after)
            new_total.append(here_total)
        both = reciprocal(product[0] * product[1])
        gain[0, k] = both * product[1]
        gain[1, k] = both * product[0]
        return tuple(new_flux), tuple(new_value), tuple(new_total)

    def lower_step(k, carry):
        return advance(k, coupling_of(k), carry)

    def upper_step(k, carry):
        return advance(k, coupling_of(k - 1), carry)

    def fronts(step, carry):
        lower, upper = carry
        return lower_step(step, lower), upper_step(layers - 1 - step, upper)

    def outward(body, carry):
        def both(step, carry):
            return body(middle - 1 - step, 0, body(middle + 1 + step, 1, carry))

        carry = repeat(plan, layers - 1 - middle, both, carry)
        for k in range(2 * middle - layers, -1, -1):
            carry = body(k, 0, carry)
        return carry

    def sweep(keep):
        def stencil_body(k, carry):
            stencil(k, keep)
            return carry

        lower = ((unit * friction,) * 2, (one, one), (zero, zero))
        upper = ((zero, zero), (one, one), (zero, zero))
        if plan.unrolled:
            stencil(0, keep)
            stencil(layers - 1, keep)
            for step in range(layers - 1 - middle):
                stencil(step + 1, keep)
                if layers - 2 - step > step + 1:
                    stencil(layers - 2 - step, keep)
                lower, upper = fronts(step, (lower, upper))
        else:
            repeat(plan, layers, stencil_body)
            lower, upper = repeat(plan, layers - 1 - middle, fronts, (lower, upper))
        for k in range(layers - 1 - middle, middle):
            lower = lower_step(k, lower)
        joints, start = [], []
        for c in range(2):
            below, above = lower[1][c], upper[1][c]
            product = below * above
            inv = reciprocal(side[c, middle] * product + (lower[0][c] * above + upper[0][c] * below))
            joint = (below, above, product, inv, reciprocal(below), reciprocal(above))
            joints.append(joint)
            solved = join(joint, rhs[c, middle], lower[2][c], upper[2][c])
            field[c, middle] = jnp.where(ice, solved, 0.0)
            start.append((solved * joint[4], solved * joint[5]))

        def solved_layer(k, which, carry):
            new = list(carry)
            for c in range(2):
                scaled = carry[2 * which + c] + rhs[c, k] * gain[c, k]
                field[c, k] = jnp.where(ice, weight[c, k] * scaled, 0.0)
                new[2 * which + c] = scaled
            return tuple(new)

        outward(solved_layer, (start[0][0], start[1][0], start[0][1], start[1][1]))
        return joints

    def join(joint, right, lower_total, upper_total):
        below, above, product, inv, _, _ = joint
        return (right * product + (lower_total * above + upper_total * below)) * inv

    sweep(False)
    joints = sweep(True)
    base = [field[c, 0] for c in range(2)]
    top = [field[c, layers - 1] for c in range(2)]

    def send(k, carry):
        both = jnp.where(centre, field[0, k], lane_roll(field[1, k], plan.cols))
        out_ref[block_row(k // here, plan.out_rows, k % here), :] = both
        return carry

    repeat(plan, layers, send)

    mismatch = [jnp.where(ice, top[c] - observed[c], 0.0) for c in range(2)]
    source = [(unit * layers) * mismatch[c] for c in range(2)]

    def side_sum(k, value):
        east, west, north, south = (faces[n, k] for n in range(4))
        u_east, u_west = x_pair(value[0], 0.0)
        v_east, v_west = x_pair(value[1], 0.0)
        u_north, u_south = y_pair(value[0])
        v_north, v_south = y_pair(value[1])
        first = 4.0 * (east * u_east + west * u_west) + (north * u_north + south * u_south)
        second = (east * v_east + west * v_west) + 4.0 * (north * v_north + south * v_south)
        return first, second

    def side_sum(k, value):
        east, west, north, south = (faces[n, k] for n in range(4))
        u_east, u_west = x_pair(value[0], 0.0)
        v_east, v_west = x_pair(value[1], 0.0)
        u_north, u_south = y_pair(value[0])
        v_north, v_south = y_pair(value[1])
        first = 4.0 * (east * u_east + west * u_west) + (north * u_north + south * u_south)
        second = (east * v_east + west * v_west) + 4.0 * (north * v_north + south * v_south)
        return first, second

    below_scaled = tuple(source[c] * joints[c][3] for c in range(2))
    first_middle = tuple(below_scaled[c] * joints[c][0] for c in range(2))
    above_scaled = tuple(first_middle[c] * joints[c][5] for c in range(2))
    middle_sum = side_sum(middle, first_middle)

    def below_layer(k, carry):
        total, correction = carry
        added = side_sum(k, tuple(weight[c, k] * below_scaled[c] for c in range(2)))
        total = tuple(total[c] + weight[c, k] * added[c] for c in range(2))
        return total, tuple(correction[c] + total[c] * gain[c, k] for c in range(2))

    def above_layer(k, carry):
        total, scaled = carry
        scaled = tuple(scaled[c] + source[c] * gain[c, k] for c in range(2))
        added = side_sum(k, tuple(weight[c, k] * scaled[c] for c in range(2)))
        return tuple(total[c] + weight[c, k] * added[c] for c in range(2)), scaled

    def adjoint_layers(step, carry):
        below, above = carry
        return below_layer(step, below), above_layer(middle + 1 + step, above)

    nothing = (zero, zero)
    below, above = repeat(
        plan, layers - 1 - middle, adjoint_layers, ((nothing, nothing), (tuple(source), above_scaled))
    )
    for k in range(layers - 1 - middle, middle):
        below = below_layer(k, below)
    adjoint = tuple(
        join(joints[c], middle_sum[c], below[0][c], above[0][c]) * joints[c][4] + below[1][c] for c in range(2)
    )
    adjoint = [jnp.where(ice, adjoint[c], 0.0) for c in range(2)]
    gradient = -friction * (base[0] * adjoint[0] + base[1] * adjoint[1])

    def partial_sum(value):
        line = jnp.sum(jnp.where(centre, value, 0.0), axis=0, keepdims=True)
        folded = line
        for r in range(1, rows):
            folded = folded + lane_roll(line, r * width)
        return jnp.broadcast_to(lane_roll(folded, plan.cols), shape)

    misfit_line = partial_sum(mismatch[0] * mismatch[0] + mismatch[1] * mismatch[1])
    grad_line = partial_sum(gradient * gradient)
    in_first = jnp.logical_and(lane >= plan.halo + plan.cols, lane < plan.halo + 2 * plan.cols)
    last_row = jnp.where(centre, gradient, jnp.where(in_first, misfit_line, grad_line))
    for part in range(plan.layer_size):
        out_ref[block_row(part, plan.out_rows, here), :] = last_row


def unpack_kernel(
    plan, in_ref, log_ref, vel_hbm, friction_hbm, misfit_hbm,
    vel_ref, friction_ref, misfit_ref, grad_ref, leave,
):
    here, width, cols, rows = plan.layers_here, plan.width, plan.cols, plan.rows
    local_chunks = plan.local_cols // LANES

    total = jnp.sum(
        in_ref[pl.ds(here, plan.devices, stride=plan.out_rows), :], axis=0, keepdims=True
    )
    line_lane = lax.broadcasted_iota(jnp.int32, (1, LANES), 1)

    def summed(first):
        ahead = (line_lane + (LANES - first % LANES)) % LANES
        return jnp.sum(jnp.where(ahead < cols, total, 0.0), axis=1, keepdims=True)

    misfit_sum = summed(plan.halo + cols)
    grad_sum = summed(plan.halo + cols + width)
    scale = step_size / jnp.sqrt(grad_sum / plan.column_count + 1e-06)

    lane = lax.broadcasted_iota(jnp.int32, (plan.out_rows, LANES), 1)
    def chunk(c, i):
        at = (plan.chunks - 1 - i) * plan.per_chunk * plan.out_rows
        if not isinstance(at, int):
            at = pl.multiple_of(at, 8)
        turned = [
            lane_roll(in_ref[pl.ds(at + (plan.per_chunk - 1 - t) * plan.out_rows, plan.out_rows), :], t * cols)
            for t in range(plan.per_chunk)
        ]
        for r in range(rows):
            start = r * width + plan.halo + c * cols
            ahead = (lane + (LANES - start % LANES)) % LANES
            row = turned[0]
            for t in range(1, plan.per_chunk):
                row = jnp.where(ahead >= t * cols, turned[t], row)
            row = lane_roll(row, -start)
            vel_ref[c, pl.ds(i * rows + r, here, stride=plan.chunks * rows), :] = row[:here]
            if c == 0:
                owner, step = i // local_chunks, i % local_chunks
                grad_ref[owner, pl.ds(step * rows + r, 1), :] = row[here : here + 1]

    out = [pltpu.make_async_copy(vel_ref.at[c], vel_hbm.at[c], leave.at[c]) for c in range(2)]
    out.append(pltpu.make_async_copy(friction_ref, friction_hbm, leave.at[2]))
    out.append(pltpu.make_async_copy(misfit_ref, misfit_hbm, leave.at[3]))
    for c in range(2):

        def chunk_body(i, carry):
            chunk(c, i)
            return carry

        repeat(plan, plan.chunks, chunk_body)
        out[c].start()
    friction_ref[...] = log_ref[...] - grad_ref[lax.axis_index("layer")] * scale
    out[2].start()
    misfit_ref[...] = 0.5 * misfit_sum / plan.column_count
    out[3].start()
    for copy in out:
        copy.wait()


def as_lines(x):
    chunked = x.reshape(x.shape[:-1] + (x.shape[-1] // LANES, LANES))
    return jnp.swapaxes(chunked, -3, -2).reshape(-1, LANES)


def from_lines(lines, shape):
    chunked = lines.reshape(shape[:-2] + (shape[-1] // LANES, shape[-2], LANES))
    return jnp.swapaxes(chunked, -3, -2).reshape(shape)


def on_device(mesh_shape, velocity_init, driving, observed, log_friction, ice_mask):
    plan = Plan(mesh_shape, velocity_init.shape)
    vmem = pl.BlockSpec(memory_space=pltpu.VMEM)
    hbm = pl.BlockSpec(memory_space=pltpu.HBM)
    f32 = jnp.float32
    limit = pltpu.CompilerParams(vmem_limit_bytes=(16 if plan.unrolled else 40) * MIB)
    inputs = [as_lines(x) for x in (velocity_init, driving, observed, log_friction, ice_mask)]

    def exchange(blocks):
        shaped = blocks.reshape(blocks.shape[0], 1, LANES)
        ranks = [
            m * plan.layer_size + part
            for part in reversed(range(plan.layer_size))
            for m in reversed(range(plan.map_size))
        ]
        return lax.all_to_all(
            shaped, ("map", "layer"), split_axis=0, concat_axis=0, tiled=True, axis_index_groups=[ranks]
        ).reshape(blocks.shape)

    packed = pl.pallas_call(
        functools.partial(pack_kernel, plan),
        out_shape=jax.ShapeDtypeStruct((plan.devices * plan.in_rows, LANES), f32),
        in_specs=[hbm] * 5,
        out_specs=vmem,
        scratch_shapes=[pltpu.VMEM(x.shape, x.dtype) for x in inputs]
        + [
            pltpu.SemaphoreType.DMA((VELOCITY_COPIES + 4,)),
        ],
        compiler_params=limit,
        name="pack",
    )(*(pltpu.with_memory_space_constraint(x, pltpu.HBM) for x in inputs))

    windows = exchange(packed)

    plane = (plan.layers, plan.map_size, LANES)
    solved = pl.pallas_call(
        functools.partial(solve_kernel, plan),
        out_shape=jax.ShapeDtypeStruct((plan.devices * plan.out_rows, LANES), f32),
        in_specs=[vmem],
        out_specs=vmem,
        scratch_shapes=[
            pltpu.VMEM((2,) + plane, f32),
            pltpu.VMEM(plane, f32),
            pltpu.VMEM((2,) + plane, f32),
            pltpu.VMEM((2,) + plane, f32),
            pltpu.VMEM((4,) + plane, f32),
            pltpu.VMEM((2,) + plane, f32),
            pltpu.VMEM((2,) + plane, f32),
        ],
        compiler_params=limit,
        name="solve",
    )(windows)

    back = exchange(solved)

    vel_lines, log_lines = inputs[0].reshape(2, -1, LANES), inputs[3]
    velocity, friction_new, misfit = pl.pallas_call(
        functools.partial(unpack_kernel, plan),
        out_shape=(
            jax.ShapeDtypeStruct(vel_lines.shape, f32),
            jax.ShapeDtypeStruct(log_lines.shape, f32),
            jax.ShapeDtypeStruct((1, 1), f32),
        ),
        in_specs=[vmem] * 2,
        out_specs=(hbm, hbm, hbm),
        scratch_shapes=[
            pltpu.VMEM(vel_lines.shape, f32),
            pltpu.VMEM(log_lines.shape, f32),
            pltpu.VMEM((1, 1), f32),
            pltpu.VMEM((plan.layer_size,) + log_lines.shape, f32),
            pltpu.SemaphoreType.DMA((4,)),
        ],
        compiler_params=limit,
        name="unpack",
    )(back, log_lines)
    return (
        from_lines(velocity, velocity_init.shape),
        from_lines(friction_new, log_friction.shape),
        misfit.reshape(()),
    )


def solution(mesh):
    in_specs = (
        P(None, "layer", "map", None),
        P(None, "map", "layer"),
        P(None, "map", "layer"),
        P("map", "layer"),
        P("map", "layer"),
    )
    out_specs = (P(None, "layer", "map", None), P("map", "layer"), P())
    return jax.shard_map(
        functools.partial(on_device, dict(mesh.shape)),
        mesh=mesh,
        in_specs=in_specs,
        out_specs=out_specs,
        check_vma=False,
    )
```

```python
import functools

import jax
import jax.numpy as jnp
from jax import lax
from jax.experimental import pallas as pl
from jax.experimental.pallas import tpu as pltpu
from jax.sharding import PartitionSpec as P

strain_floor = 0.1
step_size = 0.5
LANES = 128
REACH = 5
BED_REACH = 3
MIB = 1 << 20
VELOCITY_COPIES = 4


class Plan:
    def __init__(self, mesh_shape, velocity_shape):
        self.map_size = mesh_shape["map"]
        self.layer_size = mesh_shape["layer"]
        self.devices = self.map_size * self.layer_size
        self.layers_here = velocity_shape[1]
        self.rows = velocity_shape[2]
        self.ny = velocity_shape[3]
        self.layers = self.layers_here * self.layer_size
        self.cols = self.ny // self.devices
        self.width = LANES // self.rows
        self.halo = (self.width - self.cols) // 2
        self.low = self.halo - REACH
        self.wide = self.cols + 2 * REACH
        self.half = self.wide // 2
        self.gap = self.low + self.wide
        self.local_cols = self.ny // self.layer_size
        self.per_chunk = LANES // self.cols
        self.chunks = self.ny // LANES
        self.column_count = self.rows * self.map_size * self.ny
        self.vel_rows = 2 * self.layers_here
        self.in_rows = self.vel_rows + 1
        self.left_at = self.gap
        self.right_at = self.gap + self.cols // 2 + 1
        self.out_rows = self.layers_here + 1
        self.unrolled = self.map_size <= 8
        assert self.width * self.rows == LANES and self.cols * self.per_chunk == LANES
        assert self.low >= 0 and self.wide % 2 == 0 and self.width - self.wide >= self.half
        assert 2 * self.cols <= self.width and self.local_cols % LANES == 0
        assert self.vel_rows == 8 and self.rows == 2 and 4 * self.cols <= LANES


def repeat(plan, count, body, carry=0):
    if plan.unrolled:
        for index in range(count):
            carry = body(index, carry)
        return carry
    return lax.fori_loop(0, count, body, carry)


def lane_roll(value, shift):
    shift = shift % LANES
    return value if shift == 0 else pltpu.roll(value, shift, 1)


def pack_kernel(
    plan, vel_hbm, driving_hbm, observed_hbm, log_hbm, mask_hbm, out_ref,
    vel_ref, driving_ref, observed_ref, log_ref, mask_ref, arrival,
):
    width, rows, cols, half = plan.width, plan.rows, plan.cols, plan.half
    piece = vel_ref.shape[0] // VELOCITY_COPIES
    spans = [pl.ds(n * piece, piece) for n in range(VELOCITY_COPIES)]
    pairs = [
        (driving_hbm, driving_ref),
        (observed_hbm, observed_ref),
        (log_hbm, log_ref),
        (mask_hbm, mask_ref),
    ] + [(vel_hbm.at[span, :], vel_ref.at[span, :]) for span in spans]
    copies = [pltpu.make_async_copy(pair[0], pair[1], arrival.at[n]) for n, pair in enumerate(pairs)]
    for copy in copies:
        copy.start()
    shape = (plan.vel_rows, LANES)
    lane = lax.broadcasted_iota(jnp.int32, shape, 1)
    sub = lax.broadcasted_iota(jnp.int32, shape, 0)
    in_gap = jnp.logical_not(jnp.logical_and(lane % width >= plan.low, lane % width < plan.gap))

    def slide(part, start, length, place):
        step, offset = start // LANES, start % LANES
        value = part(step)
        if offset + length > LANES:
            after = part(step + 1)
            value = jnp.where(lax.broadcasted_iota(jnp.int32, value.shape, 1) >= offset, value, after)
        return lane_roll(value, place - offset)

    out_ref[...] = jnp.zeros_like(out_ref)
    for copy in copies[:-VELOCITY_COPIES]:
        copy.wait()

    place = lax.axis_index("layer")
    local_chunks = plan.local_cols // LANES

    skip = local_chunks * rows
    no_block = jnp.zeros(shape, jnp.float32)

    def whole(ref, row):
        return jnp.broadcast_to(ref[row : row + 1, :], shape).astype(jnp.float32)

    def gap_part(r, step):
        at = step * rows + r
        observed = jnp.where(sub < 2, whole(observed_ref, at), whole(observed_ref, skip + at))
        return jnp.where(sub < 4, observed, jnp.where(sub < 6, whole(mask_ref, at), whole(log_ref, at)))

    def driving_part(r, step):
        at = step * rows + r
        return jnp.where(sub < 2, whole(driving_ref, at), whole(driving_ref, skip + at))

    def sequence(make):
        return [
            [no_block] + [make(r, step) for step in range(local_chunks)] + [no_block] for r in range(rows)
        ]

    gap_parts, driving_parts = sequence(gap_part), sequence(driving_part)
    own = plan.local_cols // cols
    spill = -(-REACH // cols)

    def column_block(q):
        start = q * cols
        block = None
        for r in range(rows):

            def in_gaps(step):
                return gap_parts[r][step + 1]

            def of_driving(step):
                return driving_parts[r][step + 1]

            at = r * width
            first = slide(in_gaps, start - REACH, half, (at + plan.gap) % LANES)
            second = slide(in_gaps, start - REACH + half, half, (at + plan.gap) % LANES)
            before = slide(of_driving, start - BED_REACH, BED_REACH, (at + plan.left_at) % LANES)
            after = slide(of_driving, start + cols, BED_REACH, (at + plan.right_at) % LANES)
            ahead = (lane + (LANES - plan.gap - at)) % LANES
            of_observed = sub < 4
            first = jnp.where(jnp.logical_and(of_observed, ahead < BED_REACH), before, first)
            second = jnp.where(jnp.logical_and(of_observed, ahead >= plan.right_at - plan.gap), after, second)
            value = jnp.where(sub % 2 == 0, first, second)
            ahead = (lane + (LANES - plan.gap)) % LANES
            block = value if block is None else jnp.where(ahead >= r * width, value, block)
        at = pl.multiple_of((plan.layer_size - 1 - place) * (own * plan.in_rows), 8) + (own - 1 - q) * plan.in_rows
        here = pl.ds(at, plan.vel_rows)
        out_ref[here, :] = block
        if not 0 <= q < own:
            return
        line = None
        step, offset = start // LANES, start % LANES
        for r in range(rows):
            for c in range(2):
                row = c * skip + step * rows + r
                put = (2 * r + c) * cols
                value = lane_roll(driving_ref[row : row + 1, :], put - offset)
                line = value if line is None else jnp.where(lane[:1] >= put, value, line)
        out_ref[pl.ds(at + plan.vel_rows, 1), :] = line

    for q in range(own):
        column_block(q)

    @pl.when(place > 0)
    def _():
        for q in range(-spill, 0):
            column_block(q)

    @pl.when(place < plan.layer_size - 1)
    def _():
        for q in range(own, own + spill):
            column_block(q)

    for copy in copies[-VELOCITY_COPIES:]:
        copy.wait()

    def chunk_windows(i, carry):
        def velocity(r):
            def part(step):
                chunk = i + step
                if isinstance(chunk, int) and not 0 <= chunk < plan.chunks:
                    return jnp.zeros(shape, jnp.float32)
                at = chunk if isinstance(chunk, int) else jnp.clip(chunk, 0, plan.chunks - 1)
                value = vel_ref[pl.ds(at * rows + r, plan.vel_rows, stride=plan.chunks * rows), :]
                if isinstance(chunk, int):
                    return value
                return jnp.where(jnp.logical_and(chunk >= 0, chunk < plan.chunks), value, 0.0)

            return part

        for t in range(plan.per_chunk):
            block = None
            for r in range(rows):
                value = slide(velocity(r), plan.cols * t - plan.halo, width, r * width)
                block = value if block is None else jnp.where(lane >= r * width, value, block)
            at = (plan.chunks - 1 - i) * plan.per_chunk * plan.in_rows
            if not isinstance(at, int):
                at = pl.multiple_of(at, 8)
            at = at + (plan.per_chunk - 1 - t) * plan.in_rows
            here = pl.ds(at, plan.vel_rows)
            out_ref[here, :] = jnp.where(in_gap, out_ref[here, :], block)
        return carry

    repeat(plan, plan.chunks, chunk_windows)


def solve_kernel(plan, in_ref, out_ref, field, eta_ref, side, rhs, faces, weight, gain):
    size, width, rows = plan.map_size, plan.width, plan.rows
    layers, here = plan.layers, plan.layers_here
    shape = (size, LANES)
    lane = lax.broadcasted_iota(jnp.int32, shape, 1)
    sub = lax.broadcasted_iota(jnp.int32, shape, 0)
    last_group = lane >= LANES - width
    first_group = lane < width
    x_end = jnp.logical_and(last_group, sub == 0)
    x_start = jnp.logical_and(first_group, sub == size - 1)

    def block_row(part, rows_of_block, row):
        first = (plan.layer_size - 1 - part) * size * rows_of_block
        return pl.ds(first + row, size, stride=rows_of_block)

    def arrived(part, row):
        return in_ref[block_row(part, plan.in_rows, row), :]

    def moved(value, source, target):
        return lane_roll(value, target - source)

    def from_gap(halves):
        left, right = (moved(value, plan.gap, plan.low + h * plan.half) for h, value in enumerate(halves))
        return jnp.where(lane % width < plan.low + plan.half, left, right)

    def from_line(c):
        plane = None
        for r in range(rows):
            value = moved(line, (2 * r + c) * plan.cols, r * width + plan.halo)
            plane = value if plane is None else jnp.where(lane >= r * width, value, plane)
        return plane

    def driving_of(c, halves):
        left = moved(halves[0], plan.left_at, plan.halo - BED_REACH)
        right = moved(halves[1], plan.right_at, plan.halo + plan.cols)
        return jnp.where(centre, from_line(c), jnp.where(lane % width < plan.halo, left, right))

    def x_pair(value, edge):
        after = lane_roll(value, -width)
        before = after if 2 * width == LANES else lane_roll(value, width)
        after = jnp.where(last_group, pltpu.roll(after, 1, 0), after)
        before = jnp.where(first_group, pltpu.roll(before, size - 1, 0), before)
        return jnp.where(x_end, edge, after), jnp.where(x_start, edge, before)

    def y_pair(value):
        return lane_roll(value, -1), lane_roll(value, 1)

    unit = 2.0 / 4.0 ** (1.0 / 3.0)

    def viscosity(four_rates):
        return jnp.exp2(jnp.log2(4.0 * strain_floor + four_rates) * (-1.0 / 3.0))

    sums = [None] * plan.in_rows
    for part in range(plan.layer_size):
        for row in range(plan.in_rows):
            value = arrived(part, row)
            if row < plan.vel_rows:
                field[row // here, part * here + row % here] = value
            sums[row] = value if part == 0 else sums[row] + value
    line = sums[plan.vel_rows]
    gaps = [sums[2 * n : 2 * n + 2] for n in range(4)]
    reached = jnp.logical_and(lane % width >= plan.low, lane % width < plan.gap)
    centre = jnp.logical_and(lane % width >= plan.halo, lane % width < plan.halo + plan.cols)
    driving = [unit * driving_of(c, gaps[c]) for c in range(2)]
    observed = [from_gap(gaps[c]) for c in range(2)]
    mask = jnp.where(reached, from_gap(gaps[2]), 0.0)
    ice = mask != 0.0
    friction = jnp.where(mask == 1.0, jnp.exp(from_gap(gaps[3])), 0.0)

    def stencil(k, keep):
        u, v = field[0, k], field[1, k]
        u_east, u_west = x_pair(u, 0.0)
        v_east, v_west = x_pair(v, 0.0)
        u_north, u_south = y_pair(u)
        v_north, v_south = y_pair(v)
        stretch_x = u_east - u_west
        stretch_y = v_north - v_south
        shear = 0.5 * ((u_north - u_south) + (v_east - v_west))
        four_rates = stretch_x * (stretch_x + stretch_y) + (stretch_y * stretch_y + shear * shear)
        half_v = 0.5 * v
        eta = viscosity(four_rates)
        eta_edge = viscosity(u * u + half_v * half_v)
        eta_east, eta_west = x_pair(eta, eta_edge)
        eta_north, eta_south = y_pair(eta)
        east, west = eta + eta_east, eta + eta_west
        north, south = eta + eta_north, eta + eta_south
        along_x, along_y = east + west, north + south
        eta_ref[k] = eta
        side[0, k] = 4.0 * along_x + along_y
        side[1, k] = along_x + 4.0 * along_y
        rhs[0, k] = driving[0] + (4.0 * (east * u_east + west * u_west) + (north * u_north + south * u_south))
        rhs[1, k] = driving[1] + ((east * v_east + west * v_west) + 4.0 * (north * v_north + south * v_south))
        if keep:
            faces[0, k] = east
            faces[1, k] = west
            faces[2, k] = north
            faces[3, k] = south

    def coupling_of(k):
        return (2.0 * layers * layers) * (eta_ref[k] + eta_ref[k + 1])

    def reciprocal(value):
        guess = pl.reciprocal(value, approx=True)
        return guess * (2.0 - value * guess)

    middle = layers // 2
    zero = jnp.zeros(shape, jnp.float32)
    one = jnp.ones(shape, jnp.float32)

    def advance(k, coupling, across, carry):
        flux, value, total = carry
        new_flux, new_value, new_total, product = [], [], [], []
        for c in range(2):
            here_flux = flux[c] + side[c, k] * value[c]
            after = value[c] + across * here_flux
            here_total = total[c] + value[c] * rhs[c, k]
            weight[c, k] = value[c]
            product.append((coupling * value[c]) * after)
            rhs[c, k] = here_total
            new_flux.append(here_flux)
            new_value.append(after)
            new_total.append(here_total)
        both = reciprocal(product[0] * product[1])
        gain[0, k] = both * product[1]
        gain[1, k] = both * product[0]
        return tuple(new_flux), tuple(new_value), tuple(new_total)

    def lower_step(k, carry):
        coupling = coupling_of(k)
        return advance(k, coupling, reciprocal(coupling), carry)

    def fronts(step, carry):
        low, high = step, layers - 1 - step
        under, over = coupling_of(low), coupling_of(high - 1)
        both = reciprocal(under * over)
        return advance(low, under, both * over, carry[0]), advance(high, over, both * under, carry[1])

    def outward(body, carry):
        def both(step, carry):
            return body(middle - 1 - step, 0, body(middle + 1 + step, 1, carry))

        carry = repeat(plan, layers - 1 - middle, both, carry)
        for k in range(2 * middle - layers, -1, -1):
            carry = body(k, 0, carry)
        return carry

    def sweep(keep):
        def stencil_body(k, carry):
            stencil(k, keep)
            return carry

        lower = ((unit * friction,) * 2, (one, one), (zero, zero))
        upper = ((zero, zero), (one, one), (zero, zero))
        if plan.unrolled:
            stencil(0, keep)
            stencil(layers - 1, keep)
            for step in range(layers - 1 - middle):
                stencil(step + 1, keep)
                if layers - 2 - step > step + 1:
                    stencil(layers - 2 - step, keep)
                lower, upper = fronts(step, (lower, upper))
        else:
            repeat(plan, layers, stencil_body)
            lower, upper = repeat(plan, layers - 1 - middle, fronts, (lower, upper))
        for k in range(layers - 1 - middle, middle):
            lower = lower_step(k, lower)
        joints, start = [], []
        for c in range(2):
            below, above = lower[1][c], upper[1][c]
            product = below * above
            inv = reciprocal(side[c, middle] * product + (lower[0][c] * above + upper[0][c] * below))
            both = reciprocal(product)
            joint = (below, above, product, inv, both * above, both * below)
            joints.append(joint)
            solved = join(joint, rhs[c, middle], lower[2][c], upper[2][c])
            field[c, middle] = jnp.where(ice, solved, 0.0)
            start.append((solved * joint[4], solved * joint[5]))

        def solved_layer(k, which, carry):
            new = list(carry)
            for c in range(2):
                scaled = carry[2 * which + c] + rhs[c, k] * gain[c, k]
                field[c, k] = jnp.where(ice, weight[c, k] * scaled, 0.0)
                new[2 * which + c] = scaled
            return tuple(new)

        outward(solved_layer, (start[0][0], start[1][0], start[0][1], start[1][1]))
        return joints

    def join(joint, right, lower_total, upper_total):
        below, above, product, inv, _, _ = joint
        return (right * product + (lower_total * above + upper_total * below)) * inv

    sweep(False)
    joints = sweep(True)
    base = [field[c, 0] for c in range(2)]
    top = [field[c, layers - 1] for c in range(2)]

    def send(k, carry):
        both = jnp.where(centre, field[0, k], lane_roll(field[1, k], plan.cols))
        out_ref[block_row(k // here, plan.out_rows, k % here), :] = both
        return carry

    repeat(plan, layers, send)

    mismatch = [jnp.where(ice, top[c] - observed[c], 0.0) for c in range(2)]
    source = [(unit * layers) * mismatch[c] for c in range(2)]

    def side_sum(k, value):
        east, west, north, south = (faces[n, k] for n in range(4))
        u_east, u_west = x_pair(value[0], 0.0)
        v_east, v_west = x_pair(value[1], 0.0)
        u_north, u_south = y_pair(value[0])
        v_north, v_south = y_pair(value[1])
        first = 4.0 * (east * u_east + west * u_west) + (north * u_north + south * u_south)
        second = (east * v_east + west * v_west) + 4.0 * (north * v_north + south * v_south)
        return first, second

    def side_sum(k, value):
        east, west, north, south = (faces[n, k] for n in range(4))
        u_east, u_west = x_pair(value[0], 0.0)
        v_east, v_west = x_pair(value[1], 0.0)
        u_north, u_south = y_pair(value[0])
        v_north, v_south = y_pair(value[1])
        first = 4.0 * (east * u_east + west * u_west) + (north * u_north + south * u_south)
        second = (east * v_east + west * v_west) + 4.0 * (north * v_north + south * v_south)
        return first, second

    below_scaled = tuple(source[c] * joints[c][3] for c in range(2))
    first_middle = tuple(below_scaled[c] * joints[c][0] for c in range(2))
    above_scaled = tuple(first_middle[c] * joints[c][5] for c in range(2))
    middle_sum = side_sum(middle, first_middle)

    def below_layer(k, carry):
        total, correction = carry
        added = side_sum(k, tuple(weight[c, k] * below_scaled[c] for c in range(2)))
        total = tuple(total[c] + weight[c, k] * added[c] for c in range(2))
        return total, tuple(correction[c] + total[c] * gain[c, k] for c in range(2))

    def above_layer(k, carry):
        total, scaled = carry
        scaled = tuple(scaled[c] + source[c] * gain[c, k] for c in range(2))
        added = side_sum(k, tuple(weight[c, k] * scaled[c] for c in range(2)))
        return tuple(total[c] + weight[c, k] * added[c] for c in range(2)), scaled

    def adjoint_layers(step, carry):
        below, above = carry
        return below_layer(step, below), above_layer(middle + 1 + step, above)

    nothing = (zero, zero)
    below, above = repeat(
        plan, layers - 1 - middle, adjoint_layers, ((nothing, nothing), (tuple(source), above_scaled))
    )
    for k in range(layers - 1 - middle, middle):
        below = below_layer(k, below)
    adjoint = tuple(
        join(joints[c], middle_sum[c], below[0][c], above[0][c]) * joints[c][4] + below[1][c] for c in range(2)
    )
    adjoint = [jnp.where(ice, adjoint[c], 0.0) for c in range(2)]
    gradient = -friction * (base[0] * adjoint[0] + base[1] * adjoint[1])

    def partial_sum(value):
        line = jnp.sum(jnp.where(centre, value, 0.0), axis=0, keepdims=True)
        folded = line
        for r in range(1, rows):
            folded = folded + lane_roll(line, r * width)
        return jnp.broadcast_to(lane_roll(folded, plan.cols), shape)

    misfit_line = partial_sum(mismatch[0] * mismatch[0] + mismatch[1] * mismatch[1])
    grad_line = partial_sum(gradient * gradient)
    in_first = jnp.logical_and(lane >= plan.halo + plan.cols, lane < plan.halo + 2 * plan.cols)
    last_row = jnp.where(centre, gradient, jnp.where(in_first, misfit_line, grad_line))
    for part in range(plan.layer_size):
        out_ref[block_row(part, plan.out_rows, here), :] = last_row


def unpack_kernel(
    plan, in_ref, log_ref, vel_hbm, friction_hbm, misfit_hbm,
    vel_ref, friction_ref, misfit_ref, grad_ref, leave,
):
    here, width, cols, rows = plan.layers_here, plan.width, plan.cols, plan.rows
    local_chunks = plan.local_cols // LANES

    total = jnp.sum(
        in_ref[pl.ds(here, plan.devices, stride=plan.out_rows), :], axis=0, keepdims=True
    )
    line_lane = lax.broadcasted_iota(jnp.int32, (1, LANES), 1)

    def summed(first):
        ahead = (line_lane + (LANES - first % LANES)) % LANES
        return jnp.sum(jnp.where(ahead < cols, total, 0.0), axis=1, keepdims=True)

    misfit_sum = summed(plan.halo + cols)
    grad_sum = summed(plan.halo + cols + width)
    scale = step_size / jnp.sqrt(grad_sum / plan.column_count + 1e-06)

    lane = lax.broadcasted_iota(jnp.int32, (plan.out_rows, LANES), 1)
    def chunk(c, i):
        at = (plan.chunks - 1 - i) * plan.per_chunk * plan.out_rows
        if not isinstance(at, int):
            at = pl.multiple_of(at, 8)
        turned = [
            lane_roll(in_ref[pl.ds(at + (plan.per_chunk - 1 - t) * plan.out_rows, plan.out_rows), :], t * cols)
            for t in range(plan.per_chunk)
        ]
        for r in range(rows):
            start = r * width + plan.halo + c * cols
            ahead = (lane + (LANES - start % LANES)) % LANES
            row = turned[0]
            for t in range(1, plan.per_chunk):
                row = jnp.where(ahead >= t * cols, turned[t], row)
            row = lane_roll(row, -start)
            vel_ref[c, pl.ds(i * rows + r, here, stride=plan.chunks * rows), :] = row[:here]
            if c == 0:
                owner, step = i // local_chunks, i % local_chunks
                grad_ref[owner, pl.ds(step * rows + r, 1), :] = row[here : here + 1]

    out = [pltpu.make_async_copy(vel_ref.at[c], vel_hbm.at[c], leave.at[c]) for c in range(2)]
    out.append(pltpu.make_async_copy(friction_ref, friction_hbm, leave.at[2]))
    out.append(pltpu.make_async_copy(misfit_ref, misfit_hbm, leave.at[3]))
    for c in range(2):

        def chunk_body(i, carry):
            chunk(c, i)
            return carry

        repeat(plan, plan.chunks, chunk_body)
        out[c].start()
    friction_ref[...] = log_ref[...] - grad_ref[lax.axis_index("layer")] * scale
    out[2].start()
    misfit_ref[...] = 0.5 * misfit_sum / plan.column_count
    out[3].start()
    for copy in out:
        copy.wait()


def as_lines(x):
    chunked = x.reshape(x.shape[:-1] + (x.shape[-1] // LANES, LANES))
    return jnp.swapaxes(chunked, -3, -2).reshape(-1, LANES)


def from_lines(lines, shape):
    chunked = lines.reshape(shape[:-2] + (shape[-1] // LANES, shape[-2], LANES))
    return jnp.swapaxes(chunked, -3, -2).reshape(shape)


def on_device(mesh_shape, velocity_init, driving, observed, log_friction, ice_mask):
    plan = Plan(mesh_shape, velocity_init.shape)
    vmem = pl.BlockSpec(memory_space=pltpu.VMEM)
    hbm = pl.BlockSpec(memory_space=pltpu.HBM)
    f32 = jnp.float32
    limit = pltpu.CompilerParams(vmem_limit_bytes=(16 if plan.unrolled else 40) * MIB)
    inputs = [as_lines(x) for x in (velocity_init, driving, observed, log_friction, ice_mask)]

    def exchange(blocks):
        shaped = blocks.reshape(blocks.shape[0], 1, LANES)
        ranks = [
            m * plan.layer_size + part
            for part in reversed(range(plan.layer_size))
            for m in reversed(range(plan.map_size))
        ]
        return lax.all_to_all(
            shaped, ("map", "layer"), split_axis=0, concat_axis=0, tiled=True, axis_index_groups=[ranks]
        ).reshape(blocks.shape)

    packed = pl.pallas_call(
        functools.partial(pack_kernel, plan),
        out_shape=jax.ShapeDtypeStruct((plan.devices * plan.in_rows, LANES), f32),
        in_specs=[hbm] * 5,
        out_specs=vmem,
        scratch_shapes=[pltpu.VMEM(x.shape, x.dtype) for x in inputs]
        + [
            pltpu.SemaphoreType.DMA((VELOCITY_COPIES + 4,)),
        ],
        compiler_params=limit,
        name="pack",
    )(*(pltpu.with_memory_space_constraint(x, pltpu.HBM) for x in inputs))

    windows = exchange(packed)

    plane = (plan.layers, plan.map_size, LANES)
    solved = pl.pallas_call(
        functools.partial(solve_kernel, plan),
        out_shape=jax.ShapeDtypeStruct((plan.devices * plan.out_rows, LANES), f32),
        in_specs=[vmem],
        out_specs=vmem,
        scratch_shapes=[
            pltpu.VMEM((2,) + plane, f32),
            pltpu.VMEM(plane, f32),
            pltpu.VMEM((2,) + plane, f32),
            pltpu.VMEM((2,) + plane, f32),
            pltpu.VMEM((4,) + plane, f32),
            pltpu.VMEM((2,) + plane, f32),
            pltpu.VMEM((2,) + plane, f32),
        ],
        compiler_params=limit,
        name="solve",
    )(windows)

    back = exchange(solved)

    vel_lines, log_lines = inputs[0].reshape(2, -1, LANES), inputs[3]
    velocity, friction_new, misfit = pl.pallas_call(
        functools.partial(unpack_kernel, plan),
        out_shape=(
            jax.ShapeDtypeStruct(vel_lines.shape, f32),
            jax.ShapeDtypeStruct(log_lines.shape, f32),
            jax.ShapeDtypeStruct((1, 1), f32),
        ),
        in_specs=[vmem] * 2,
        out_specs=(hbm, hbm, hbm),
        scratch_shapes=[
            pltpu.VMEM(vel_lines.shape, f32),
            pltpu.VMEM(log_lines.shape, f32),
            pltpu.VMEM((1, 1), f32),
            pltpu.VMEM((plan.layer_size,) + log_lines.shape, f32),
            pltpu.SemaphoreType.DMA((4,)),
        ],
        compiler_params=limit,
        name="unpack",
    )(back, log_lines)
    return (
        from_lines(velocity, velocity_init.shape),
        from_lines(friction_new, log_friction.shape),
        misfit.reshape(()),
    )


def solution(mesh):
    in_specs = (
        P(None, "layer", "map", None),
        P(None, "map", "layer"),
        P(None, "map", "layer"),
        P("map", "layer"),
        P("map", "layer"),
    )
    out_specs = (P(None, "layer", "map", None), P("map", "layer"), P())
    return jax.shard_map(
        functools.partial(on_device, dict(mesh.shape)),
        mesh=mesh,
        in_specs=in_specs,
        out_specs=out_specs,
        check_vma=False,
    )
```

```python
import functools

import jax
import jax.numpy as jnp
from jax import lax
from jax.experimental import pallas as pl
from jax.experimental.pallas import tpu as pltpu
from jax.sharding import PartitionSpec as P

strain_floor = 0.1
step_size = 0.5
LANES = 128
REACH = 5
BED_REACH = 3
MIB = 1 << 20
VELOCITY_COPIES = 2


class Plan:
    def __init__(self, mesh_shape, velocity_shape):
        self.map_size = mesh_shape["map"]
        self.layer_size = mesh_shape["layer"]
        self.devices = self.map_size * self.layer_size
        self.layers_here = velocity_shape[1]
        self.rows = velocity_shape[2]
        self.ny = velocity_shape[3]
        self.layers = self.layers_here * self.layer_size
        self.cols = self.ny // self.devices
        self.width = LANES // self.rows
        self.halo = (self.width - self.cols) // 2
        self.low = self.halo - REACH
        self.wide = self.cols + 2 * REACH
        self.half = self.wide // 2
        self.gap = self.low + self.wide
        self.local_cols = self.ny // self.layer_size
        self.per_chunk = LANES // self.cols
        self.chunks = self.ny // LANES
        self.column_count = self.rows * self.map_size * self.ny
        self.vel_rows = 2 * self.layers_here
        self.in_rows = self.vel_rows + 1
        self.left_at = self.gap
        self.right_at = self.gap + self.cols // 2 + 1
        self.out_rows = self.layers_here + 1
        self.unrolled = self.map_size <= 8
        assert self.width * self.rows == LANES and self.cols * self.per_chunk == LANES
        assert self.low >= 0 and self.wide % 2 == 0 and self.width - self.wide >= self.half
        assert 2 * self.cols <= self.width and self.local_cols % LANES == 0
        assert self.vel_rows == 8 and self.rows == 2 and 4 * self.cols <= LANES


def repeat(plan, count, body, carry=0):
    if plan.unrolled:
        for index in range(count):
            carry = body(index, carry)
        return carry
    return lax.fori_loop(0, count, body, carry)


def lane_roll(value, shift):
    shift = shift % LANES
    return value if shift == 0 else pltpu.roll(value, shift, 1)


def pack_kernel(
    plan, vel_hbm, driving_hbm, observed_hbm, log_hbm, mask_hbm, out_ref,
    vel_ref, driving_ref, observed_ref, log_ref, mask_ref, arrival,
):
    width, rows, cols, half = plan.width, plan.rows, plan.cols, plan.half
    piece = vel_ref.shape[0] // VELOCITY_COPIES
    spans = [pl.ds(n * piece, piece) for n in range(VELOCITY_COPIES)]
    pairs = [
        (driving_hbm, driving_ref),
        (observed_hbm, observed_ref),
        (log_hbm, log_ref),
        (mask_hbm, mask_ref),
    ] + [(vel_hbm.at[span, :], vel_ref.at[span, :]) for span in spans]
    copies = [pltpu.make_async_copy(pair[0], pair[1], arrival.at[n]) for n, pair in enumerate(pairs)]
    for copy in copies:
        copy.start()
    shape = (plan.vel_rows, LANES)
    lane = lax.broadcasted_iota(jnp.int32, shape, 1)
    sub = lax.broadcasted_iota(jnp.int32, shape, 0)
    in_gap = jnp.logical_not(jnp.logical_and(lane % width >= plan.low, lane % width < plan.gap))

    def slide(part, start, length, place):
        step, offset = start // LANES, start % LANES
        value = part(step)
        if offset + length > LANES:
            after = part(step + 1)
            value = jnp.where(lax.broadcasted_iota(jnp.int32, value.shape, 1) >= offset, value, after)
        return lane_roll(value, place - offset)

    out_ref[...] = jnp.zeros_like(out_ref)
    for copy in copies[:-VELOCITY_COPIES]:
        copy.wait()

    place = lax.axis_index("layer")
    local_chunks = plan.local_cols // LANES

    skip = local_chunks * rows
    no_block = jnp.zeros(shape, jnp.float32)

    def whole(ref, row):
        return jnp.broadcast_to(ref[row : row + 1, :], shape).astype(jnp.float32)

    def gap_part(r, step):
        at = step * rows + r
        observed = jnp.where(sub < 2, whole(observed_ref, at), whole(observed_ref, skip + at))
        return jnp.where(sub < 4, observed, jnp.where(sub < 6, whole(mask_ref, at), whole(log_ref, at)))

    def driving_part(r, step):
        at = step * rows + r
        return jnp.where(sub < 2, whole(driving_ref, at), whole(driving_ref, skip + at))

    def sequence(make):
        return [
            [no_block] + [make(r, step) for step in range(local_chunks)] + [no_block] for r in range(rows)
        ]

    gap_parts, driving_parts = sequence(gap_part), sequence(driving_part)
    own = plan.local_cols // cols
    spill = -(-REACH // cols)

    def column_block(q):
        start = q * cols
        block = None
        for r in range(rows):

            def in_gaps(step):
                return gap_parts[r][step + 1]

            def of_driving(step):
                return driving_parts[r][step + 1]

            at = r * width
            first = slide(in_gaps, start - REACH, half, (at + plan.gap) % LANES)
            second = slide(in_gaps, start - REACH + half, half, (at + plan.gap) % LANES)
            before = slide(of_driving, start - BED_REACH, BED_REACH, (at + plan.left_at) % LANES)
            after = slide(of_driving, start + cols, BED_REACH, (at + plan.right_at) % LANES)
            ahead = (lane + (LANES - plan.gap - at)) % LANES
            of_observed = sub < 4
            first = jnp.where(jnp.logical_and(of_observed, ahead < BED_REACH), before, first)
            second = jnp.where(jnp.logical_and(of_observed, ahead >= plan.right_at - plan.gap), after, second)
            value = jnp.where(sub % 2 == 0, first, second)
            ahead = (lane + (LANES - plan.gap)) % LANES
            block = value if block is None else jnp.where(ahead >= r * width, value, block)
        at = pl.multiple_of((plan.layer_size - 1 - place) * (own * plan.in_rows), 8) + (own - 1 - q) * plan.in_rows
        here = pl.ds(at, plan.vel_rows)
        out_ref[here, :] = block
        if not 0 <= q < own:
            return
        line = None
        step, offset = start // LANES, start % LANES
        for r in range(rows):
            for c in range(2):
                row = c * skip + step * rows + r
                put = (2 * r + c) * cols
                value = lane_roll(driving_ref[row : row + 1, :], put - offset)
                line = value if line is None else jnp.where(lane[:1] >= put, value, line)
        out_ref[pl.ds(at + plan.vel_rows, 1), :] = line

    for q in range(own):
        column_block(q)

    @pl.when(place > 0)
    def _():
        for q in range(-spill, 0):
            column_block(q)

    @pl.when(place < plan.layer_size - 1)
    def _():
        for q in range(own, own + spill):
            column_block(q)

    for copy in copies[-VELOCITY_COPIES:]:
        copy.wait()

    def chunk_windows(i, carry):
        def velocity(r):
            def part(step):
                chunk = i + step
                if isinstance(chunk, int) and not 0 <= chunk < plan.chunks:
                    return jnp.zeros(shape, jnp.float32)
                at = chunk if isinstance(chunk, int) else jnp.clip(chunk, 0, plan.chunks - 1)
                value = vel_ref[pl.ds(at * rows + r, plan.vel_rows, stride=plan.chunks * rows), :]
                if isinstance(chunk, int):
                    return value
                return jnp.where(jnp.logical_and(chunk >= 0, chunk < plan.chunks), value, 0.0)

            return part

        for t in range(plan.per_chunk):
            block = None
            for r in range(rows):
                value = slide(velocity(r), plan.cols * t - plan.halo, width, r * width)
                block = value if block is None else jnp.where(lane >= r * width, value, block)
            at = (plan.chunks - 1 - i) * plan.per_chunk * plan.in_rows
            if not isinstance(at, int):
                at = pl.multiple_of(at, 8)
            at = at + (plan.per_chunk - 1 - t) * plan.in_rows
            here = pl.ds(at, plan.vel_rows)
            out_ref[here, :] = jnp.where(in_gap, out_ref[here, :], block)
        return carry

    repeat(plan, plan.chunks, chunk_windows)


def solve_kernel(plan, in_ref, out_ref, field, eta_ref, side, rhs, faces, weight, gain):
    size, width, rows = plan.map_size, plan.width, plan.rows
    layers, here = plan.layers, plan.layers_here
    shape = (size, LANES)
    lane = lax.broadcasted_iota(jnp.int32, shape, 1)
    sub = lax.broadcasted_iota(jnp.int32, shape, 0)
    last_group = lane >= LANES - width
    first_group = lane < width
    x_end = jnp.logical_and(last_group, sub == 0)
    x_start = jnp.logical_and(first_group, sub == size - 1)

    def block_row(part, rows_of_block, row):
        first = (plan.layer_size - 1 - part) * size * rows_of_block
        return pl.ds(first + row, size, stride=rows_of_block)

    def arrived(part, row):
        return in_ref[block_row(part, plan.in_rows, row), :]

    def moved(value, source, target):
        return lane_roll(value, target - source)

    def from_gap(halves):
        left, right = (moved(value, plan.gap, plan.low + h * plan.half) for h, value in enumerate(halves))
        return jnp.where(lane % width < plan.low + plan.half, left, right)

    def from_line(c):
        plane = None
        for r in range(rows):
            value = moved(line, (2 * r + c) * plan.cols, r * width + plan.halo)
            plane = value if plane is None else jnp.where(lane >= r * width, value, plane)
        return plane

    def driving_of(c, halves):
        left = moved(halves[0], plan.left_at, plan.halo - BED_REACH)
        right = moved(halves[1], plan.right_at, plan.halo + plan.cols)
        return jnp.where(centre, from_line(c), jnp.where(lane % width < plan.halo, left, right))

    def x_pair(value, edge):
        after = lane_roll(value, -width)
        before = after if 2 * width == LANES else lane_roll(value, width)
        after = jnp.where(last_group, pltpu.roll(after, 1, 0), after)
        before = jnp.where(first_group, pltpu.roll(before, size - 1, 0), before)
        return jnp.where(x_end, edge, after), jnp.where(x_start, edge, before)

    def y_pair(value):
        return lane_roll(value, -1), lane_roll(value, 1)

    unit = 2.0 / 4.0 ** (1.0 / 3.0)

    def viscosity(four_rates):
        return jnp.exp2(jnp.log2(4.0 * strain_floor + four_rates) * (-1.0 / 3.0))

    sums = [None] * plan.in_rows
    for part in range(plan.layer_size):
        for row in range(plan.in_rows):
            value = arrived(part, row)
            if row < plan.vel_rows:
                field[row // here, part * here + row % here] = value
            sums[row] = value if part == 0 else sums[row] + value
    line = sums[plan.vel_rows]
    gaps = [sums[2 * n : 2 * n + 2] for n in range(4)]
    reached = jnp.logical_and(lane % width >= plan.low, lane % width < plan.gap)
    centre = jnp.logical_and(lane % width >= plan.halo, lane % width < plan.halo + plan.cols)
    driving = [unit * driving_of(c, gaps[c]) for c in range(2)]
    observed = [from_gap(gaps[c]) for c in range(2)]
    mask = jnp.where(reached, from_gap(gaps[2]), 0.0)
    ice = mask != 0.0
    friction = jnp.where(mask == 1.0, jnp.exp(from_gap(gaps[3])), 0.0)

    def stencil(k, keep):
        u, v = field[0, k], field[1, k]
        u_east, u_west = x_pair(u, 0.0)
        v_east, v_west = x_pair(v, 0.0)
        u_north, u_south = y_pair(u)
        v_north, v_south = y_pair(v)
        stretch_x = u_east - u_west
        stretch_y = v_north - v_south
        shear = 0.5 * ((u_north - u_south) + (v_east - v_west))
        four_rates = stretch_x * (stretch_x + stretch_y) + (stretch_y * stretch_y + shear * shear)
        half_v = 0.5 * v
        eta = viscosity(four_rates)
        eta_edge = viscosity(u * u + half_v * half_v)
        eta_east, eta_west = x_pair(eta, eta_edge)
        eta_north, eta_south = y_pair(eta)
        east, west = eta + eta_east, eta + eta_west
        north, south = eta + eta_north, eta + eta_south
        along_x, along_y = east + west, north + south
        eta_ref[k] = eta
        side[0, k] = 4.0 * along_x + along_y
        side[1, k] = along_x + 4.0 * along_y
        rhs[0, k] = driving[0] + (4.0 * (east * u_east + west * u_west) + (north * u_north + south * u_south))
        rhs[1, k] = driving[1] + ((east * v_east + west * v_west) + 4.0 * (north * v_north + south * v_south))
        if keep:
            faces[0, k] = east
            faces[1, k] = west
            faces[2, k] = north
            faces[3, k] = south

    def coupling_of(k):
        return (2.0 * layers * layers) * (eta_ref[k] + eta_ref[k + 1])

    def reciprocal(value):
        guess = pl.reciprocal(value, approx=True)
        return guess * (2.0 - value * guess)

    middle = layers // 2
    zero = jnp.zeros(shape, jnp.float32)
    one = jnp.ones(shape, jnp.float32)

    def advance(k, coupling, carry):
        flux, value, total = carry
        across = reciprocal(coupling)
        new_flux, new_value, new_total, product = [], [], [], []
        for c in range(2):
            here_flux = flux[c] + side[c, k] * value[c]
            after = value[c] + across * here_flux
            here_total = total[c] + value[c] * rhs[c, k]
            weight[c, k] = value[c]
            product.append((coupling * value[c]) * after)
            rhs[c, k] = here_total
            new_flux.append(here_flux)
            new_value.append(after)
            new_total.append(here_total)
        both = reciprocal(product[0] * product[1])
        gain[0, k] = both * product[1]
        gain[1, k] = both * product[0]
        return tuple(new_flux), tuple(new_value), tuple(new_total)

    def lower_step(k, carry):
        return advance(k, coupling_of(k), carry)

    def upper_step(k, carry):
        return advance(k, coupling_of(k - 1), carry)

    def fronts(step, carry):
        lower, upper = carry
        return lower_step(step, lower), upper_step(layers - 1 - step, upper)

    def outward(body, carry):
        def both(step, carry):
            return body(middle - 1 - step, 0, body(middle + 1 + step, 1, carry))

        carry = repeat(plan, layers - 1 - middle, both, carry)
        for k in range(2 * middle - layers, -1, -1):
            carry = body(k, 0, carry)
        return carry

    def sweep(keep):
        def stencil_body(k, carry):
            stencil(k, keep)
            return carry

        lower = ((unit * friction,) * 2, (one, one), (zero, zero))
        upper = ((zero, zero), (one, one), (zero, zero))
        if plan.unrolled:
            stencil(0, keep)
            stencil(layers - 1, keep)
            for step in range(layers - 1 - middle):
                stencil(step + 1, keep)
                if layers - 2 - step > step + 1:
                    stencil(layers - 2 - step, keep)
                lower, upper = fronts(step, (lower, upper))
        else:
            repeat(plan, layers, stencil_body)
            lower, upper = repeat(plan, layers - 1 - middle, fronts, (lower, upper))
        for k in range(layers - 1 - middle, middle):
            lower = lower_step(k, lower)
        joints, start = [], []
        for c in range(2):
            below, above = lower[1][c], upper[1][c]
            product = below * above
            inv = reciprocal(side[c, middle] * product + (lower[0][c] * above + upper[0][c] * below))
            joint = (below, above, product, inv, reciprocal(below), reciprocal(above))
            joints.append(joint)
            solved = join(joint, rhs[c, middle], lower[2][c], upper[2][c])
            field[c, middle] = jnp.where(ice, solved, 0.0)
            start.append((solved * joint[4], solved * joint[5]))

        def solved_layer(k, which, carry):
            new = list(carry)
            for c in range(2):
                scaled = carry[2 * which + c] + rhs[c, k] * gain[c, k]
                field[c, k] = jnp.where(ice, weight[c, k] * scaled, 0.0)
                new[2 * which + c] = scaled
            return tuple(new)

        outward(solved_layer, (start[0][0], start[1][0], start[0][1], start[1][1]))
        return joints

    def join(joint, right, lower_total, upper_total):
        below, above, product, inv, _, _ = joint
        return (right * product + (lower_total * above + upper_total * below)) * inv

    sweep(False)
    joints = sweep(True)
    base = [field[c, 0] for c in range(2)]
    top = [field[c, layers - 1] for c in range(2)]

    def send(k, carry):
        both = jnp.where(centre, field[0, k], lane_roll(field[1, k], plan.cols))
        out_ref[block_row(k // here, plan.out_rows, k % here), :] = both
        return carry

    repeat(plan, layers, send)

    mismatch = [jnp.where(ice, top[c] - observed[c], 0.0) for c in range(2)]
    source = [(unit * layers) * mismatch[c] for c in range(2)]

    def side_sum(k, value):
        east, west, north, south = (faces[n, k] for n in range(4))
        u_east, u_west = x_pair(value[0], 0.0)
        v_east, v_west = x_pair(value[1], 0.0)
        u_north, u_south = y_pair(value[0])
        v_north, v_south = y_pair(value[1])
        first = 4.0 * (east * u_east + west * u_west) + (north * u_north + south * u_south)
        second = (east * v_east + west * v_west) + 4.0 * (north * v_north + south * v_south)
        return first, second

    def side_sum(k, value):
        east, west, north, south = (faces[n, k] for n in range(4))
        u_east, u_west = x_pair(value[0], 0.0)
        v_east, v_west = x_pair(value[1], 0.0)
        u_north, u_south = y_pair(value[0])
        v_north, v_south = y_pair(value[1])
        first = 4.0 * (east * u_east + west * u_west) + (north * u_north + south * u_south)
        second = (east * v_east + west * v_west) + 4.0 * (north * v_north + south * v_south)
        return first, second

    below_scaled = tuple(source[c] * joints[c][3] for c in range(2))
    first_middle = tuple(below_scaled[c] * joints[c][0] for c in range(2))
    above_scaled = tuple(first_middle[c] * joints[c][5] for c in range(2))
    middle_sum = side_sum(middle, first_middle)

    def below_layer(k, carry):
        total, correction = carry
        added = side_sum(k, tuple(weight[c, k] * below_scaled[c] for c in range(2)))
        total = tuple(total[c] + weight[c, k] * added[c] for c in range(2))
        return total, tuple(correction[c] + total[c] * gain[c, k] for c in range(2))

    def above_layer(k, carry):
        total, scaled = carry
        scaled = tuple(scaled[c] + source[c] * gain[c, k] for c in range(2))
        added = side_sum(k, tuple(weight[c, k] * scaled[c] for c in range(2)))
        return tuple(total[c] + weight[c, k] * added[c] for c in range(2)), scaled

    def adjoint_layers(step, carry):
        below, above = carry
        return below_layer(step, below), above_layer(middle + 1 + step, above)

    nothing = (zero, zero)
    below, above = repeat(
        plan, layers - 1 - middle, adjoint_layers, ((nothing, nothing), (tuple(source), above_scaled))
    )
    for k in range(layers - 1 - middle, middle):
        below = below_layer(k, below)
    adjoint = tuple(
        join(joints[c], middle_sum[c], below[0][c], above[0][c]) * joints[c][4] + below[1][c] for c in range(2)
    )
    adjoint = [jnp.where(ice, adjoint[c], 0.0) for c in range(2)]
    gradient = -friction * (base[0] * adjoint[0] + base[1] * adjoint[1])

    def partial_sum(value):
        line = jnp.sum(jnp.where(centre, value, 0.0), axis=0, keepdims=True)
        folded = line
        for r in range(1, rows):
            folded = folded + lane_roll(line, r * width)
        return jnp.broadcast_to(lane_roll(folded, plan.cols), shape)

    misfit_line = partial_sum(mismatch[0] * mismatch[0] + mismatch[1] * mismatch[1])
    grad_line = partial_sum(gradient * gradient)
    in_first = jnp.logical_and(lane >= plan.halo + plan.cols, lane < plan.halo + 2 * plan.cols)
    last_row = jnp.where(centre, gradient, jnp.where(in_first, misfit_line, grad_line))
    for part in range(plan.layer_size):
        out_ref[block_row(part, plan.out_rows, here), :] = last_row


def unpack_kernel(
    plan, in_ref, log_ref, vel_hbm, friction_hbm, misfit_hbm,
    vel_ref, friction_ref, misfit_ref, grad_ref, leave,
):
    here, width, cols, rows = plan.layers_here, plan.width, plan.cols, plan.rows
    local_chunks = plan.local_cols // LANES

    total = jnp.sum(
        in_ref[pl.ds(here, plan.devices, stride=plan.out_rows), :], axis=0, keepdims=True
    )
    line_lane = lax.broadcasted_iota(jnp.int32, (1, LANES), 1)

    def summed(first):
        ahead = (line_lane + (LANES - first % LANES)) % LANES
        return jnp.sum(jnp.where(ahead < cols, total, 0.0), axis=1, keepdims=True)

    misfit_sum = summed(plan.halo + cols)
    grad_sum = summed(plan.halo + cols + width)
    scale = step_size / jnp.sqrt(grad_sum / plan.column_count + 1e-06)

    lane = lax.broadcasted_iota(jnp.int32, (plan.out_rows, LANES), 1)
    def chunk(c, i):
        at = (plan.chunks - 1 - i) * plan.per_chunk * plan.out_rows
        if not isinstance(at, int):
            at = pl.multiple_of(at, 8)
        turned = [
            lane_roll(in_ref[pl.ds(at + (plan.per_chunk - 1 - t) * plan.out_rows, plan.out_rows), :], t * cols)
            for t in range(plan.per_chunk)
        ]
        for r in range(rows):
            start = r * width + plan.halo + c * cols
            ahead = (lane + (LANES - start % LANES)) % LANES
            row = turned[0]
            for t in range(1, plan.per_chunk):
                row = jnp.where(ahead >= t * cols, turned[t], row)
            row = lane_roll(row, -start)
            vel_ref[c, pl.ds(i * rows + r, here, stride=plan.chunks * rows), :] = row[:here]
            if c == 0:
                owner, step = i // local_chunks, i % local_chunks
                grad_ref[owner, pl.ds(step * rows + r, 1), :] = row[here : here + 1]

    out = [pltpu.make_async_copy(vel_ref.at[c], vel_hbm.at[c], leave.at[c]) for c in range(2)]
    out.append(pltpu.make_async_copy(friction_ref, friction_hbm, leave.at[2]))
    out.append(pltpu.make_async_copy(misfit_ref, misfit_hbm, leave.at[3]))
    for c in range(2):

        def chunk_body(i, carry):
            chunk(c, i)
            return carry

        repeat(plan, plan.chunks, chunk_body)
        out[c].start()
    friction_ref[...] = log_ref[...] - grad_ref[lax.axis_index("layer")] * scale
    out[2].start()
    misfit_ref[...] = 0.5 * misfit_sum / plan.column_count
    out[3].start()
    for copy in out:
        copy.wait()


def as_lines(x):
    chunked = x.reshape(x.shape[:-1] + (x.shape[-1] // LANES, LANES))
    return jnp.swapaxes(chunked, -3, -2).reshape(-1, LANES)


def from_lines(lines, shape):
    chunked = lines.reshape(shape[:-2] + (shape[-1] // LANES, shape[-2], LANES))
    return jnp.swapaxes(chunked, -3, -2).reshape(shape)


def on_device(mesh_shape, velocity_init, driving, observed, log_friction, ice_mask):
    plan = Plan(mesh_shape, velocity_init.shape)
    vmem = pl.BlockSpec(memory_space=pltpu.VMEM)
    hbm = pl.BlockSpec(memory_space=pltpu.HBM)
    f32 = jnp.float32
    limit = pltpu.CompilerParams(vmem_limit_bytes=(16 if plan.unrolled else 40) * MIB)
    inputs = [as_lines(x) for x in (velocity_init, driving, observed, log_friction, ice_mask)]

    def exchange(blocks):
        shaped = blocks.reshape(blocks.shape[0], 1, LANES)
        ranks = [
            m * plan.layer_size + part
            for part in reversed(range(plan.layer_size))
            for m in reversed(range(plan.map_size))
        ]
        return lax.all_to_all(
            shaped, ("map", "layer"), split_axis=0, concat_axis=0, tiled=True, axis_index_groups=[ranks]
        ).reshape(blocks.shape)

    packed = pl.pallas_call(
        functools.partial(pack_kernel, plan),
        out_shape=jax.ShapeDtypeStruct((plan.devices * plan.in_rows, LANES), f32),
        in_specs=[hbm] * 5,
        out_specs=vmem,
        scratch_shapes=[pltpu.VMEM(x.shape, x.dtype) for x in inputs]
        + [
            pltpu.SemaphoreType.DMA((VELOCITY_COPIES + 4,)),
        ],
        compiler_params=limit,
        name="pack",
    )(*(pltpu.with_memory_space_constraint(x, pltpu.HBM) for x in inputs))

    windows = exchange(packed)

    plane = (plan.layers, plan.map_size, LANES)
    solved = pl.pallas_call(
        functools.partial(solve_kernel, plan),
        out_shape=jax.ShapeDtypeStruct((plan.devices * plan.out_rows, LANES), f32),
        in_specs=[vmem],
        out_specs=vmem,
        scratch_shapes=[
            pltpu.VMEM((2,) + plane, f32),
            pltpu.VMEM(plane, f32),
            pltpu.VMEM((2,) + plane, f32),
            pltpu.VMEM((2,) + plane, f32),
            pltpu.VMEM((4,) + plane, f32),
            pltpu.VMEM((2,) + plane, f32),
            pltpu.VMEM((2,) + plane, f32),
        ],
        compiler_params=limit,
        name="solve",
    )(windows)

    back = exchange(solved)

    vel_lines, log_lines = inputs[0].reshape(2, -1, LANES), inputs[3]
    velocity, friction_new, misfit = pl.pallas_call(
        functools.partial(unpack_kernel, plan),
        out_shape=(
            jax.ShapeDtypeStruct(vel_lines.shape, f32),
            jax.ShapeDtypeStruct(log_lines.shape, f32),
            jax.ShapeDtypeStruct((1, 1), f32),
        ),
        in_specs=[vmem] * 2,
        out_specs=(hbm, hbm, hbm),
        scratch_shapes=[
            pltpu.VMEM(vel_lines.shape, f32),
            pltpu.VMEM(log_lines.shape, f32),
            pltpu.VMEM((1, 1), f32),
            pltpu.VMEM((plan.layer_size,) + log_lines.shape, f32),
            pltpu.SemaphoreType.DMA((4,)),
        ],
        compiler_params=limit,
        name="unpack",
    )(back, log_lines)
    return (
        from_lines(velocity, velocity_init.shape),
        from_lines(friction_new, log_friction.shape),
        misfit.reshape(()),
    )


def solution(mesh):
    in_specs = (
        P(None, "layer", "map", None),
        P(None, "map", "layer"),
        P(None, "map", "layer"),
        P("map", "layer"),
        P("map", "layer"),
    )
    out_specs = (P(None, "layer", "map", None), P("map", "layer"), P())
    return jax.shard_map(
        functools.partial(on_device, dict(mesh.shape)),
        mesh=mesh,
        in_specs=in_specs,
        out_specs=out_specs,
        check_vma=False,
    )
```
